32 devices in a mesh: dp: 2 (over y), dom: 4 (over z), tensor: 4 (over x, core).
Axes of the slice: x: 2, y: 2, z: 4, core: 2. Of those that a mesh axis runs over, the one named last changes fastest.
Arguments:
- states: bfloat16 [2, 2048, 512], P('dp', 'dom'), may hold values from -60 to 60, as said below
- w_query: bfloat16 [512, 512], P(None, 'tensor'), as said below
- w_key: bfloat16 [512, 512], P(None, 'tensor'), as said below
- w_value: bfloat16 [512, 512], P(None, 'tensor'), may hold values from -0.25 to 0.25
- w_out: bfloat16 [512, 512], P('tensor'), may hold values from -0.25 to 0.25
- send_blocks: int32 [4, 4, 2], P('dom'), may hold values from 0 to 3
- neighbor_blocks: int32 [16, 3], P('dom'), may hold values from 0 to 11, as said below
- cotangent: bfloat16 [2, 2048, 512], P('dp', 'dom'), may hold values from -6 to 6
Outputs:
- update: bfloat16 [2, 2048, 512], P('dp', 'dom', 'tensor')
- branch_grad: bfloat16 [2, 2048, 512], P('dp', 'dom', 'tensor')
- grad_query: float32 [512, 512], P(None, 'tensor')
- grad_key: float32 [512, 512], P(None, 'tensor')
- grad_value: float32 [512, 512], P(None, 'tensor')
- grad_out: float32 [512, 512], P('tensor')
The draws below stay inside these ranges and needn't reach their ends.
Inputs may be any that keep to these rules, and one draw needn't show every extreme that they name: `neighbor_blocks`: entries index the pool of the row's own partition; every pool entry from 4 on is named by some row of that partition. `states`: real entries. `w_query`: real entries. `w_key`: real entries.
All inputs are finite; a program needn't handle non-finite values.
Results may differ from the reference program's by a relative error of at most 0.02.
The reference program's roundings to bfloat16 on the way count: a program that leaves them out, or rounds other values in their place, can miss the bound.
Values may be sent and summed in bfloat16 or wider, within the bound.
No kernel may reach another device: no remote copies, remote signals or barrier semaphores. Data moves between devices by JAX's collectives and lax.ppermute only.
A program may use at most 64 MiB of HBM per device.

```python
import math
import jax
import jax.numpy as jnp
from jax import lax

D = 512
HEADS = 8
BLK = 128
NB = 3
HOPS = 2
SEND = 2
BLK_DEV = 4
NOFF = 4
POOL = 12
PARTS_SIZE = 4
BLOCKS = 16
NODES = 2048
REPL = 2
N_TENSOR = 4


def query_key_pair(key):
    base_draw = jax.random.normal(jax.random.fold_in(key, 11), (D, D), jnp.float32) / math.sqrt(D)
    other_draw = jax.random.normal(jax.random.fold_in(key, 12), (D, D), jnp.float32) / math.sqrt(D)
    return (2.0 * base_draw, other_draw)


def draw_w_query(key, part):
    return query_key_pair(key)[0].astype(jnp.bfloat16)


def draw_w_key(key, part):
    return query_key_pair(key)[1].astype(jnp.bfloat16)


def draw_states(key, part):
    drawn_draw = jnp.clip(jax.random.normal(jax.random.fold_in(key, 31), (REPL, NODES, D), jnp.float32), -4.0, 4.0)
    return drawn_draw.astype(jnp.bfloat16)


def neighbor_rows(key):
    received = POOL - BLK_DEV
    length = BLK_DEV * NB
    covered = jax.random.permutation(jax.random.fold_in(key, 1), received) + BLK_DEV
    spares = jax.random.randint(jax.random.fold_in(key, 2), (length - received,), 0, POOL)
    listed = jnp.concatenate([covered.astype(jnp.int32), spares.astype(jnp.int32)])
    return jax.random.permutation(jax.random.fold_in(key, 3), listed).reshape(BLK_DEV, NB)


def draw_neighbor_blocks(key, part):
    key_list = jax.random.split(jax.random.fold_in(key, 41), PARTS_SIZE)
    return jax.vmap(neighbor_rows)(key_list).reshape(BLOCKS, NB).astype(jnp.int32)


def touch_ends(entries, rng, low, largest):
    longest = entries.shape.index(max(entries.shape))
    spots = []
    for shift in (0, 1):
        where = [jax.random.randint(jax.random.fold_in(rng, axis), (), 0, length) for axis, length in enumerate(entries.shape)]
        where[longest] = (where[longest] + shift) % entries.shape[longest]
        spots.append(tuple(where))
    return entries.at[spots[0]].set(low).at[spots[1]].set(largest)


def steps_of(own_key, shape, cuts, low, high):
    gain = 1.0
    for axis_at, parts in cuts:
        heights = jax.random.uniform(jax.random.fold_in(jax.random.fold_in(own_key, 6), axis_at), (parts,), jnp.float32, low / len(cuts), high / len(cuts))
        gain = gain * jnp.repeat(jnp.exp(heights), shape[axis_at] // parts).reshape((-1,) + (1,) * (len(shape) - 1 - axis_at))
    return gain


def scatter_about(own_key, extent, width, bound, pieces=(), kind=jnp.bfloat16):
    loudness = steps_of(own_key, extent, pieces, -0.22, 0.18) if pieces else 1.0
    values = jax.random.normal(own_key, extent, jnp.float32) * width * loudness
    return jnp.minimum(jnp.maximum(values, -bound), bound).astype(kind)


def setup_inputs(seed: int = 0) -> dict:
    keys = jax.random.split(jax.random.key(seed), 9)
    states = draw_states(jax.random.fold_in(keys[8], 71), 0)
    w_query = draw_w_query(jax.random.fold_in(keys[8], 71), 0)
    w_key = draw_w_key(jax.random.fold_in(keys[8], 71), 0)
    w_value = scatter_about(keys[3], (D, D), D ** -0.5, 0.25, ((1, 4),))
    w_out = scatter_about(keys[4], (D, D), D ** -0.5, 0.25, ((0, 4),))
    send_blocks = touch_ends(jax.random.randint(keys[5], (PARTS_SIZE, NOFF, SEND), 0, BLK_DEV), jax.random.fold_in(keys[5], 1), 0, BLK_DEV - 1).astype(jnp.int32)
    neighbor_blocks = draw_neighbor_blocks(jax.random.fold_in(keys[8], 71), 0)
    cotangent = scatter_about(keys[7], (REPL, NODES, D), 1.0, 6.0, ((0, 2), (1, 4)))
    return dict(states=states, w_query=w_query, w_key=w_key, w_value=w_value, w_out=w_out, send_blocks=send_blocks, neighbor_blocks=neighbor_blocks, cotangent=cotangent)


def offset_list(hops):
    result = []
    for section in range(1, hops + 1):
        result.append(section)
        result.append(-section)
    return result

def normalize(states):
    values = states.astype(jnp.float32)
    inverse = lax.rsqrt(lax.optimization_barrier(jnp.mean(values * values, axis=-1, keepdims=True)) + 1e-05)
    return (values * inverse, inverse)

def product(form, left, right):
    return jnp.einsum(form, left.astype(jnp.float32), right.astype(jnp.float32))

def rounded(values):
    return lax.optimization_barrier(values.astype(jnp.bfloat16)).astype(jnp.float32)

def attend(queries, key_pool, key_index, grad_heads, head_count):
    replicas, blocks, block_rows, widths = queries.shape
    head_size = widths // head_count
    shrink = 1.0 / math.sqrt(head_size)
    listed = key_index.shape[1]
    chosen = jnp.take(key_pool, key_index.reshape(-1), axis=1)
    chosen = chosen.reshape(replicas, blocks, listed * block_rows, 2, head_count, head_size)
    key_rows = chosen[:, :, :, 0]
    value_rows = chosen[:, :, :, 1]
    query_heads = queries.reshape(replicas, blocks, block_rows, head_count, head_size)
    grad_split = grad_heads.reshape(replicas, blocks, block_rows, head_count, head_size)
    scores = product('rbqhe,rbkhe->rbhqk', query_heads, key_rows) * shrink
    highest = lax.optimization_barrier(jnp.max(scores, axis=-1, keepdims=True))
    powers = jnp.exp(scores - highest)
    weights = powers / lax.optimization_barrier(jnp.sum(powers, axis=-1, keepdims=True))
    weights_low = weights.astype(jnp.bfloat16)
    mixed_rows = product('rbhqk,rbkhe->rbqhe', weights_low, value_rows).astype(jnp.bfloat16)
    prob_grad = product('rbqhe,rbkhe->rbhqk', grad_split, value_rows)
    score_grad = weights * (prob_grad - lax.optimization_barrier(jnp.sum(weights * prob_grad, axis=-1, keepdims=True)))
    score_low = (score_grad * shrink).astype(jnp.bfloat16)
    query_grad = product('rbhqk,rbkhe->rbqhe', score_low, key_rows).astype(jnp.bfloat16)
    key_grad = product('rbhqk,rbqhe->rbkhe', score_low, query_heads)
    value_grad = product('rbhqk,rbqhe->rbkhe', weights_low, grad_split)
    chosen_grad = jnp.stack([key_grad, value_grad], axis=3).reshape(replicas, blocks, listed, block_rows, 2 * widths)
    pool_size = key_pool.shape[1]
    chooser = (key_index[:, :, None] == jnp.arange(pool_size, dtype=jnp.int32)[None, None, :]).astype(jnp.float32)
    pool_grad = jnp.einsum('bnp,rbnqc->rpqc', chooser, chosen_grad, precision=lax.Precision.HIGHEST)
    return (mixed_rows.reshape(replicas, blocks, block_rows, widths), query_grad.reshape(replicas, blocks, block_rows, widths), pool_grad)

def reference(states, w_query, w_key, w_value, w_out, send_blocks, neighbor_blocks, cotangent):
    normed, inverse = normalize(states)
    unit_rows = normed.astype(jnp.bfloat16)
    flat_unit = unit_rows.reshape(-1, D)
    queries = jnp.dot(flat_unit, w_query, preferred_element_type=jnp.float32).astype(jnp.bfloat16)
    queries = queries.reshape(REPL, PARTS_SIZE, BLK_DEV, BLK, D)
    paired = jnp.dot(flat_unit, jnp.concatenate([w_key, w_value], axis=1), preferred_element_type=jnp.float32).astype(jnp.bfloat16)
    paired = paired.reshape(REPL, PARTS_SIZE, BLK_DEV, BLK, 2 * D)
    flat_cot = cotangent.reshape(-1, D)
    grad_heads = jnp.dot(flat_cot, w_out.T, preferred_element_type=jnp.float32).astype(jnp.bfloat16)
    grad_heads = grad_heads.reshape(REPL, PARTS_SIZE, BLK_DEV, BLK, D)
    offsets = offset_list(HOPS)

    def one_part(part):
        part = part.astype(jnp.int32)
        gathered = [paired[:, part]]
        for slot_group, distance in enumerate(offsets):
            source = (part - distance) % PARTS_SIZE
            picked = send_blocks[source, slot_group]
            gathered.append(jnp.take(paired[:, source], picked, axis=1))
        key_pool = jnp.concatenate(gathered, axis=1)
        near_list = lax.dynamic_slice_in_dim(neighbor_blocks, part * BLK_DEV, BLK_DEV, 0)
        key_index = jnp.concatenate([jnp.arange(BLK_DEV, dtype=jnp.int32)[:, None], near_list], axis=1)
        mixed_rows, query_grad, pool_grad = attend(queries[:, part], key_pool, key_index, grad_heads[:, part], HEADS)
        return (mixed_rows, query_grad, pool_grad[:, :BLK_DEV], pool_grad[:, BLK_DEV:].astype(jnp.bfloat16))
    mixed_rows, query_grad, own_grad, remote = lax.map(one_part, jnp.arange(PARTS_SIZE, dtype=jnp.int32))
    summed = jnp.transpose(own_grad, (0, 2, 1, 3, 4))
    remote = jnp.transpose(lax.optimization_barrier(remote), (0, 2, 1, 3, 4)).astype(jnp.float32)
    parts_all = jnp.arange(PARTS_SIZE, dtype=jnp.int32)
    for slot_group, distance in enumerate(offsets):
        owners = (parts_all - distance) % PARTS_SIZE
        picked = send_blocks[owners, slot_group]
        summed = summed.at[owners[:, None], picked].add(remote[:, slot_group * SEND:(slot_group + 1) * SEND])
    pair_grad = jnp.transpose(summed, (2, 0, 1, 3, 4)).astype(jnp.bfloat16).reshape(-1, 2 * D)
    key_grad = pair_grad[:, :D]
    value_grad = pair_grad[:, D:]
    flat_mixed = jnp.transpose(mixed_rows, (1, 0, 2, 3, 4)).reshape(-1, D)
    flat_query_grad = jnp.transpose(query_grad, (1, 0, 2, 3, 4)).reshape(-1, D)
    slab_width = D // N_TENSOR
    update_sum = jnp.zeros((flat_unit.shape[0], D), jnp.float32)
    unit_sum = jnp.zeros((flat_unit.shape[0], D), jnp.float32)
    for group in range(N_TENSOR):
        columns = slice(group * slab_width, (group + 1) * slab_width)
        update_sum = update_sum + rounded(jnp.dot(flat_mixed[:, columns], w_out[columns], preferred_element_type=jnp.float32))
        unit_term = jnp.dot(flat_query_grad[:, columns], w_query[:, columns].T, preferred_element_type=jnp.float32)
        unit_term = unit_term + jnp.dot(key_grad[:, columns], w_key[:, columns].T, preferred_element_type=jnp.float32)
        unit_term = unit_term + jnp.dot(value_grad[:, columns], w_value[:, columns].T, preferred_element_type=jnp.float32)
        unit_sum = unit_sum + rounded(unit_term)
    update = update_sum.astype(jnp.bfloat16).reshape(REPL, NODES, D)
    flat_normed = normed.reshape(-1, D)
    row_mean = lax.optimization_barrier(jnp.mean(unit_sum * flat_normed, axis=-1, keepdims=True))
    branch_grad = (inverse.reshape(-1, 1) * (unit_sum - flat_normed * row_mean)).astype(jnp.bfloat16)
    branch_grad = branch_grad.reshape(REPL, NODES, D)
    factor = 1.0 / math.sqrt(REPL * NODES)
    grad_query = jnp.dot(flat_unit.T, flat_query_grad, preferred_element_type=jnp.float32) * factor
    grad_key = jnp.dot(flat_unit.T, key_grad, preferred_element_type=jnp.float32) * factor
    grad_value = jnp.dot(flat_unit.T, value_grad, preferred_element_type=jnp.float32) * factor
    grad_out = jnp.dot(flat_mixed.T, flat_cot, preferred_element_type=jnp.float32) * factor
    return (update, branch_grad, grad_query, grad_key, grad_value, grad_out)
```

```python
import functools
import math

import jax
import jax.numpy as jnp
from jax import lax
from jax.experimental import pallas as pl
from jax.experimental.pallas import tpu as pltpu
from jax.sharding import PartitionSpec as P

BLK = 128
HOPS = 2
SEND = 2
HD = 64
PAD = 16
EPS = 1e-05
LIMIT = 48 * 1024 * 1024
F32 = jnp.float32
BF16 = jnp.bfloat16


def offset_list(hops):
    result = []
    for section in range(1, hops + 1):
        result.append(section)
        result.append(-section)
    return result


def piece_order(ranks, offsets):
    count = offsets * SEND
    share = count // ranks
    if share == SEND and offsets == 4:
        return [0, 1, 4, 5, 2, 3, 6, 7], share
    return list(range(count)), share


def nt(left, right):
    return lax.dot_general(left, right, (((1,), (1,)), ((), ())), preferred_element_type=F32)


def nn(left, right):
    return jnp.dot(left, right, preferred_element_type=F32)


def unit_of(rows):
    values = rows.astype(F32)
    return (values * lax.rsqrt(jnp.mean(values * values, axis=-1, keepdims=True) + EPS)).astype(BF16)


def block_at(index, size=BLK):
    return pl.ds(pl.multiple_of(index * size, size), size)


def pick_kernel(share, order_ref, place_ref, send_ref, states_ref, out_ref):
    for inner in range(share):
        block = send_ref[order_ref[place_ref[0] * share + inner]]
        out_ref[inner * BLK : (inner + 1) * BLK, :] = states_ref[block_at(block), :]


def pick_blocks(states, order, place, send, share):
    vmem = pl.BlockSpec(memory_space=pltpu.VMEM)
    smem = pl.BlockSpec(memory_space=pltpu.SMEM)
    return pl.pallas_call(
        functools.partial(pick_kernel, share),
        out_shape=jax.ShapeDtypeStruct((share * BLK, states.shape[1]), BF16),
        in_specs=[smem] * 3 + [vmem],
        out_specs=vmem,
        name="pick_blocks",
    )(order, place, send, states)


def layer_kernel(cfg, *refs):
    ranks, share, blocks, offsets, width = cfg
    place_ref, canon_ref, near_ref, states_ref = refs[:4]
    piece_refs = refs[4 : 4 + ranks]
    cot_ref, wq_ref, wk_ref, wv_ref, wo_ref = refs[4 + ranks : 9 + ranks]
    far_keep, far_send, own_keep, own_send, g_keep, g_send = refs[9 + ranks : 15 + ranks]
    unit_ref, k_ref, v_ref, kt_ref, vt_ref, ka_ref, va_ref, mixed_ref, dq_ref = refs[15 + ranks :]
    heads = width // HD
    received = offsets * SEND
    entries = blocks + received
    feats = states_ref.shape[1]
    slabs = feats // width
    sub = BLK // width
    group = SEND * BLK + PAD
    rank = place_ref[0]
    half = place_ref[1]
    odd = (rank & 1) == 1
    upper = rank >> 1

    chunk = 64
    for start in range(0, blocks * BLK, chunk):
        unit_ref[start : start + chunk, :] = unit_of(states_ref[start : start + chunk, :])
    for slot in range(ranks):
        for inner in range(share):
            base = pl.multiple_of((canon_ref[slot * share + inner] + blocks) * BLK, BLK)
            for start in range(0, BLK, chunk):
                source = inner * BLK + start
                unit_ref[pl.ds(pl.multiple_of(base + start, chunk), chunk), :] = unit_of(
                    piece_refs[slot][source : source + chunk, :]
                )

    wkv = jnp.concatenate([wk_ref[...], wv_ref[...]], axis=1)
    queries = nn(unit_ref[: blocks * BLK, :], wq_ref[...])
    grads = nt(cot_ref[...], wo_ref[...])
    for start in range(0, entries, blocks):
        paired = nn(unit_ref[start * BLK : (start + blocks) * BLK, :], wkv)
        for entry in range(blocks):
            rows = paired[entry * BLK : (entry + 1) * BLK]
            keys, values = rows[:, :width], rows[:, width:]
            at = start + entry
            k_ref[at * BLK : (at + 1) * BLK, :] = keys.astype(BF16)
            v_ref[at * BLK : (at + 1) * BLK, :] = values.astype(BF16)
            kt_ref[at] = keys.T.astype(BF16)
            vt_ref[at] = values.T.astype(BF16)
    ka_ref[...] = jnp.zeros_like(ka_ref)
    va_ref[...] = jnp.zeros_like(va_ref)

    lane_head = lax.broadcasted_iota(jnp.int32, (BLK, width), 1) // HD

    def by_head(rows):
        if heads == 1:
            return rows.astype(BF16)
        return jnp.concatenate(
            [jnp.where(lane_head == head, rows, 0.0) for head in range(heads)], axis=0
        ).astype(BF16)

    def diagonal(stacked):
        return jnp.concatenate(
            [
                stacked[head * HD : (head + 1) * HD, head * BLK : (head + 1) * BLK]
                for head in range(heads)
            ],
            axis=0,
        )

    shrink = 1.0 / math.sqrt(HD)
    near = near_ref.shape[1]
    mixed_t, dq_t = [], []
    for block in range(blocks):
        listed = [block] + [near_ref[block, n] for n in range(near)]
        keys = jnp.concatenate([k_ref[block_at(e), :] for e in listed], axis=0)
        values = jnp.concatenate([v_ref[block_at(e), :] for e in listed], axis=0)
        keys_t = jnp.concatenate([kt_ref[e] for e in listed], axis=1)
        values_t = jnp.concatenate([vt_ref[e] for e in listed], axis=1)
        q_all = by_head(queries[block * BLK : (block + 1) * BLK])
        g_all = by_head(grads[block * BLK : (block + 1) * BLK].astype(BF16).astype(F32))
        scores = nt(keys, q_all) * shrink
        powers = jnp.exp(scores - jnp.max(scores, axis=0, keepdims=True))
        weights = powers / jnp.sum(powers, axis=0, keepdims=True)
        low = weights.astype(BF16)
        mix = diagonal(nn(values_t, low))
        mixed_t.append(mix.astype(BF16))
        mixed_ref[block * BLK : (block + 1) * BLK, :] = mix.T.astype(BF16)
        prob = nt(values, g_all)
        drop = jnp.sum(weights * prob, axis=0, keepdims=True)
        score_low = (weights * (prob - drop) * shrink).astype(BF16)
        dq = diagonal(nn(keys_t, score_low))
        dq_t.append(dq.astype(BF16))
        dq_ref[block * BLK : (block + 1) * BLK, :] = dq.T.astype(BF16)
        dk = nn(score_low, q_all)
        dv = nn(low, g_all)
        for n, e in enumerate(listed):
            ka_ref[block_at(e), :] += dk[n * BLK : (n + 1) * BLK]
            va_ref[block_at(e), :] += dv[n * BLK : (n + 1) * BLK]

    ones = jnp.ones((16, feats), BF16)

    def put(keep_ref, send_ref, row, values):
        count = values.shape[0]
        for pair in range(slabs // 2):
            left = values[:, 2 * pair * width : (2 * pair + 1) * width]
            right = values[:, (2 * pair + 1) * width : (2 * pair + 2) * width]
            at = upper ^ pair
            keep_ref[at, row : row + count, :] = jnp.where(odd, right, left).astype(BF16)
            send_ref[at, row : row + count, :] = jnp.where(odd, left, right).astype(BF16)

    def put_dots(keep_ref, send_ref, row, dots):
        parts = []
        for dot in dots:
            for piece in range(sub):
                parts.append(dot[:1, piece * width : (piece + 1) * width])
        parts.append(jnp.zeros((PAD - len(parts), width), F32))
        rows = jnp.concatenate(parts, axis=0).astype(BF16)
        for pair in range(slabs // 2):
            keep_ref[pair, row : row + PAD, :] = rows
            send_ref[pair, row : row + PAD, :] = rows

    def row_dot(term, first):
        product = (term * unit_ref[first : first + BLK, :].astype(F32)).astype(BF16)
        return nt(ones, product)

    wkv_b = wkv
    for offset in range(offsets):
        first = (blocks + offset * SEND) * BLK
        both = jnp.concatenate(
            [ka_ref[first : first + SEND * BLK, :], va_ref[first : first + SEND * BLK, :]], axis=1
        ).astype(BF16)
        term = nt(both, wkv_b)
        put(far_keep, far_send, offset * group, term)
        dots = [
            row_dot(term[c * BLK : (c + 1) * BLK], first + c * BLK) for c in range(SEND)
        ]
        put_dots(far_keep, far_send, offset * group + SEND * BLK, dots)

    own_rows = blocks * BLK
    dots = []
    for pair in range(0, blocks, 2):
        first, last = pair * BLK, (pair + 2) * BLK
        both = jnp.concatenate([ka_ref[first:last, :], va_ref[first:last, :]], axis=1).astype(BF16)
        term = nt(both, wkv_b) + nt(dq_ref[first:last, :], wq_ref[...])
        put(own_keep, own_send, first, term)
        dots += [row_dot(term[c * BLK : (c + 1) * BLK], first + c * BLK) for c in range(2)]
        update = nn(mixed_ref[first:last, :], wo_ref[...])
        put(own_keep, own_send, own_rows + PAD + first, update)
    put_dots(own_keep, own_send, own_rows, dots)

    own_unit = unit_ref[:own_rows, :]
    grad_q = nn(jnp.concatenate(dq_t, axis=1), own_unit)
    grad_out = nn(jnp.concatenate(mixed_t, axis=1), cot_ref[...])

    def turned(ref):
        return jnp.concatenate(
            [ref[e * BLK : (e + 1) * BLK, :].T.astype(BF16) for e in range(entries)], axis=1
        )

    grad_k = nn(turned(ka_ref), unit_ref[...])
    grad_v = nn(turned(va_ref), unit_ref[...])
    second = half == 1
    g_keep[:width, :] = jnp.where(second, grad_v, grad_q).astype(BF16)
    g_keep[width:, :] = jnp.where(second, grad_out, grad_k).astype(BF16)
    g_send[:width, :] = jnp.where(second, grad_q, grad_v).astype(BF16)
    g_send[width:, :] = jnp.where(second, grad_k, grad_out).astype(BF16)


def run_layer(ranks, share, offsets, place, canon, near, states, pieces, cot, weights):
    rows, feats = states.shape
    blocks = rows // BLK
    width = weights[0].shape[1]
    entries = blocks + offsets * SEND
    pairs = feats // width // 2
    far_rows = offsets * (SEND * BLK + PAD)
    own_rows = 2 * rows + PAD
    vmem = pl.BlockSpec(memory_space=pltpu.VMEM)
    smem = pl.BlockSpec(memory_space=pltpu.SMEM)
    cfg = (ranks, share, blocks, offsets, width)
    shape = jax.ShapeDtypeStruct
    return pl.pallas_call(
        functools.partial(layer_kernel, cfg),
        out_shape=(
            shape((pairs, far_rows, width), BF16),
            shape((pairs, far_rows, width), BF16),
            shape((pairs, own_rows, width), BF16),
            shape((pairs, own_rows, width), BF16),
            shape((2 * width, feats), BF16),
            shape((2 * width, feats), BF16),
        ),
        in_specs=[smem] * 3 + [vmem] * (6 + ranks),
        out_specs=[vmem] * 6,
        scratch_shapes=[
            pltpu.VMEM((entries * BLK, feats), BF16),
            pltpu.VMEM((entries * BLK, width), BF16),
            pltpu.VMEM((entries * BLK, width), BF16),
            pltpu.VMEM((entries, width, BLK), BF16),
            pltpu.VMEM((entries, width, BLK), BF16),
            pltpu.VMEM((entries * BLK, width), F32),
            pltpu.VMEM((entries * BLK, width), F32),
            pltpu.VMEM((rows, width), BF16),
            pltpu.VMEM((rows, width), BF16),
        ],
        compiler_params=pltpu.CompilerParams(vmem_limit_bytes=LIMIT),
        name="layer",
    )(place, canon, near, states, *pieces, cot, *weights)


def finish_kernel(cfg, *refs):
    blocks, offsets, width, spread = cfg
    place_ref, send_ref, states_ref, mine_ref, other_ref = refs[:5]
    far_refs = refs[5 : 5 + len(spread)]
    update_ref, branch_ref, unit_ref = refs[5 + len(spread) :]
    own_rows = blocks * BLK
    sub = BLK // width
    group = SEND * BLK + PAD
    rank = place_ref[0]

    def both(first, last):
        return mine_ref[first:last, :].astype(F32) + other_ref[first:last, :].astype(F32)

    update_ref[...] = both(own_rows + PAD, 2 * own_rows + PAD).astype(BF16)
    unit_ref[...] = both(0, own_rows)
    dots = both(own_rows, own_rows + PAD)
    at_row = lax.broadcasted_iota(jnp.int32, (PAD, width), 0)
    for ref, members in zip(far_refs, spread):
        for position, offset in enumerate(members):
            first = position * group
            extra = ref[first + SEND * BLK : first + group, :].astype(F32)
            for c in range(SEND):
                block = send_ref[offset, c]
                rows = ref[first + c * BLK : first + (c + 1) * BLK, :].astype(F32)
                unit_ref[block_at(block), :] += rows
                for piece in range(sub):
                    line = extra[c * sub + piece : c * sub + piece + 1, :]
                    dots = dots + jnp.where(at_row == block * sub + piece, line, 0.0)
    feats = states_ref.shape[1]
    for block in range(blocks):
        rows = slice(block * BLK, (block + 1) * BLK)
        values = states_ref[rows, :].astype(F32)
        inverse = lax.rsqrt(jnp.mean(values * values, axis=-1, keepdims=True) + EPS)
        own = values[:, :width]
        for slab in range(1, feats // width):
            own = jnp.where(rank == slab, values[:, slab * width : (slab + 1) * width], own)
        line = jnp.concatenate(
            [dots[block * sub + piece : block * sub + piece + 1, :] for piece in range(sub)], axis=1
        )
        mean = jnp.broadcast_to(line * (1.0 / feats), (BLK, BLK)).T[:, :width]
        branch_ref[rows, :] = (inverse * (unit_ref[rows, :] - own * inverse * mean)).astype(BF16)


def run_finish(place, send, states, mine, other, far, spread):
    rows, feats = states.shape
    width = mine.shape[1]
    vmem = pl.BlockSpec(memory_space=pltpu.VMEM)
    smem = pl.BlockSpec(memory_space=pltpu.SMEM)
    shape = jax.ShapeDtypeStruct
    cfg = (rows // BLK, send.shape[0], width, spread)
    return pl.pallas_call(
        functools.partial(finish_kernel, cfg),
        out_shape=(shape((rows, width), BF16), shape((rows, width), BF16)),
        in_specs=[smem] * 2 + [vmem] * (3 + len(far)),
        out_specs=[vmem] * 2,
        scratch_shapes=[pltpu.VMEM((rows, width), F32)],
        compiler_params=pltpu.CompilerParams(vmem_limit_bytes=LIMIT),
        name="finish",
    )(place, send, states, mine, other, *far)


def grads_kernel(cfg, place_ref, *refs):
    parts, factor = cfg
    mine_refs = refs[:parts]
    other_refs = refs[parts : 2 * parts]
    q_ref, k_ref, v_ref, o_ref, all_ref = refs[2 * parts :]
    half = place_ref[1]
    dom = place_ref[2]
    size = mine_refs[0].shape[0]
    width = q_ref.shape[1]
    for group, side in ((mine_refs, half), (other_refs, 1 - half)):
        for step in range(parts):
            index = side * parts + ((dom + parts - step) & (parts - 1))
            all_ref[block_at(index, size), :] = group[step][...]
    for position, ref in enumerate((q_ref, k_ref, v_ref)):
        for start in range(0, ref.shape[0], BLK):
            rows = all_ref[position * width : (position + 1) * width, start : start + BLK]
            ref[start : start + BLK, :] = rows.astype(F32).T * factor
    o_ref[...] = all_ref[3 * width :, :].astype(F32) * factor


def run_grads(place, mine, other, factor):
    parts = len(mine)
    size, feats = mine[0].shape
    width = parts * size // 2
    vmem = pl.BlockSpec(memory_space=pltpu.VMEM)
    smem = pl.BlockSpec(memory_space=pltpu.SMEM)
    tall = jax.ShapeDtypeStruct((feats, width), F32)
    return pl.pallas_call(
        functools.partial(grads_kernel, (parts, factor)),
        out_shape=(tall, tall, tall, jax.ShapeDtypeStruct((width, feats), F32)),
        in_specs=[smem] + [vmem] * (2 * parts),
        out_specs=[vmem] * 4,
        scratch_shapes=[pltpu.VMEM((4 * width, feats), BF16)],
        compiler_params=pltpu.CompilerParams(vmem_limit_bytes=LIMIT),
        name="weight_grads",
    )(place, *mine, *other)


def swap(array, axis, bit):
    return lax.ppermute(array, axis, [(i, i ^ bit) for i in range(lax.axis_size(axis))])


def shifted(array, axis, distance):
    size = lax.axis_size(axis)
    return lax.ppermute(array, axis, [(i, (i + distance) % size) for i in range(size)])


def added(left, right):
    return (left.astype(F32) + right.astype(F32)).astype(BF16)


def scatter_rest(summed, bit, ranks):
    while summed.shape[0] > 1:
        keep, send = summed[0::2], summed[1::2]
        got = swap(send, "tensor", bit)
        bit *= 2
        if keep.shape[0] == 1:
            return keep[0], got[0]
        summed = added(keep, got)
    return summed[0], None


def body(states, w_query, w_key, w_value, w_out, send_blocks, neighbor_blocks, cotangent):
    replicas, node_count, feats = states.shape
    width = w_query.shape[1]
    ranks = lax.axis_size("tensor")
    parts = lax.axis_size("dom")
    offsets = offset_list(HOPS)
    order, share = piece_order(ranks, len(offsets))
    rank = lax.axis_index("tensor")
    half = lax.axis_index("dp")
    dom = lax.axis_index("dom")
    explicit = parts == 4 and lax.axis_size("dp") == 2
    place = jnp.stack([rank, half if explicit else jnp.zeros_like(half), dom]).astype(jnp.int32)
    table = [
        [order[(slot ^ r) * share + inner] for slot in range(ranks) for inner in range(share)]
        for r in range(ranks)
    ]
    canon = lax.dynamic_index_in_dim(jnp.asarray(table, jnp.int32), rank, 0, keepdims=False)
    flat_states = states.reshape(-1, feats)
    flat_cot = cotangent.reshape(-1, feats)

    leaving = pick_blocks(
        flat_states,
        jnp.asarray(order, jnp.int32),
        place,
        send_blocks.reshape(-1),
        share,
    )
    route = []
    for p in range(parts):
        for r in range(ranks):
            distance = offsets[order[r * share] // SEND]
            route.append((p * ranks + r, ((p + distance) % parts) * ranks + r))
    pieces = [lax.ppermute(leaving, ("dom", "tensor"), route)]
    bit = 1
    levels = []
    while bit < ranks:
        levels.append(bit)
        bit *= 2
    held = {0: pieces[0]}
    for bit in reversed(levels):
        for slot in list(held):
            held[slot ^ bit] = swap(held[slot], "tensor", bit)
    pieces = [held[slot] for slot in range(ranks)]

    far_keep, far_send, own_keep, own_send, g_keep, g_send = run_layer(
        ranks,
        share,
        len(offsets),
        place,
        canon,
        neighbor_blocks,
        flat_states,
        pieces,
        flat_cot,
        (w_query, w_key, w_value, w_out),
    )

    far_got = swap(far_send, "tensor", 1)
    g_got = swap(g_send, "dp", 1) if explicit else None
    own_got = swap(own_send, "tensor", 1)
    far_mine, far_other = scatter_rest(added(far_keep, far_got), 2, ranks)
    far_sum = far_mine if far_other is None else added(far_mine, far_other)
    own_mine, own_other = scatter_rest(added(own_keep, own_got), 2, ranks)
    if own_other is None:
        own_other = jnp.zeros_like(own_mine)

    group = SEND * BLK + PAD
    spread = []
    for index, distance in enumerate(offsets):
        for members in spread:
            if (offsets[members[0]] - distance) % parts == 0 and members[-1] == index - 1:
                members.append(index)
                break
        else:
            spread.append([index])
    far = [
        shifted(
            far_sum[members[0] * group : (members[-1] + 1) * group], "dom", -offsets[members[0]]
        )
        for members in spread
    ]
    spread = tuple(tuple(members) for members in spread)

    total_rows = replicas * node_count * lax.axis_size("dp") * parts
    factor = 1.0 / math.sqrt(total_rows)
    if explicit:
        quarters = added(g_keep, g_got).reshape(parts, -1, feats)
        mine = lax.dynamic_index_in_dim(quarters, dom, 0, keepdims=False).astype(F32)
        for step in range(1, parts):
            leaving = lax.dynamic_index_in_dim(quarters, (dom + step) % parts, 0, keepdims=False)
            mine = mine + shifted(leaving, "dom", step).astype(F32)
        mine = mine.astype(BF16)
        chunks = [mine] + [shifted(mine, "dom", step) for step in range(1, parts)]
        others = [swap(chunk, "dp", 1) for chunk in chunks]
        grads = run_grads(place, chunks, others, factor)
    else:
        summed = lax.psum(
            jnp.concatenate([g_keep, g_send]).astype(F32), ("dp", "dom")
        ).reshape(4, width, feats)
        grads = (
            summed[0].T * factor,
            summed[1].T * factor,
            summed[2].T * factor,
            summed[3] * factor,
        )
    update, branch = run_finish(
        place, send_blocks[0], flat_states, own_mine, own_other, far, spread
    )
    shape = (replicas, node_count, width)
    return (update.reshape(shape), branch.reshape(shape), *grads)


def solution(mesh):
    placed = (
        P("dp", "dom", None),
        P(None, "tensor"),
        P(None, "tensor"),
        P(None, "tensor"),
        P("tensor", None),
        P("dom", None, None),
        P("dom", None),
        P("dp", "dom", None),
    )
    return jax.shard_map(
        body,
        mesh=mesh,
        in_specs=placed,
        out_specs=(
            P("dp", "dom", "tensor"),
            P("dp", "dom", "tensor"),
            P(None, "tensor"),
            P(None, "tensor"),
            P(None, "tensor"),
            P("tensor", None),
        ),
        check_vma=False,
    )
```

```python
import functools
import math

import jax
import jax.numpy as jnp
from jax import lax
from jax.experimental import pallas as pl
from jax.experimental.pallas import tpu as pltpu
from jax.sharding import PartitionSpec as P

BLK = 128
HOPS = 2
SEND = 2
HD = 64
PAD = 16
EPS = 1e-05
LIMIT = 24 * 1024 * 1024
SMALL = 8 * 1024 * 1024
CHUNK = 64
F32 = jnp.float32
BF16 = jnp.bfloat16


def offset_list(hops):
    result = []
    for section in range(1, hops + 1):
        result.append(section)
        result.append(-section)
    return result


def piece_order(ranks, offsets):
    count = offsets * SEND
    share = count // ranks
    if share == SEND and offsets == 4:
        return [0, 1, 4, 5, 2, 3, 6, 7], share
    return list(range(count)), share


def nt(left, right):
    return lax.dot_general(left, right, (((1,), (1,)), ((), ())), preferred_element_type=F32)


def nn(left, right):
    return jnp.dot(left, right, preferred_element_type=F32)


def unit_of(rows):
    values = rows.astype(F32)
    return (values * lax.rsqrt(jnp.mean(values * values, axis=-1, keepdims=True) + EPS)).astype(BF16)


def block_at(index, size=BLK):
    return pl.ds(pl.multiple_of(index * size, size), size)


def rank_piece(rank, ranks, share, inner):
    if share == SEND and ranks == 4:
        return ((rank & 1) * 2 + (rank >> 1)) * SEND + inner
    return rank * share + inner


def pick_kernel(ranks, share, send_ref, states_ref, *refs):
    outs, sems = refs[:-1], refs[-1]
    rank = lax.axis_index("tensor")
    copies = []
    for inner, out_ref in enumerate(outs):
        piece = rank_piece(rank, ranks, share, inner)
        block = send_ref[piece % SEND, piece // SEND]
        copies.append(
            pltpu.make_async_copy(states_ref.at[block_at(block), :], out_ref, sems.at[inner])
        )
        copies[-1].start()
    for copy in copies:
        copy.wait()


def pick_blocks(states, send, ranks, share):
    anywhere = pl.BlockSpec(memory_space=pl.ANY)
    return pl.pallas_call(
        functools.partial(pick_kernel, ranks, share),
        out_shape=[jax.ShapeDtypeStruct((BLK, states.shape[1]), BF16)] * share,
        in_specs=[pl.BlockSpec(memory_space=pltpu.SMEM), anywhere],
        out_specs=[anywhere] * share,
        scratch_shapes=[pltpu.SemaphoreType.DMA((share,))],
        compiler_params=pltpu.CompilerParams(vmem_limit_bytes=SMALL),
        name="pick_blocks",
    )(send, states)


def by_head(rows, heads):
    if heads == 1:
        return rows.astype(BF16)
    lane_head = lax.broadcasted_iota(jnp.int32, rows.shape, 1) // HD
    return jnp.concatenate(
        [jnp.where(lane_head == head, rows, 0.0) for head in range(heads)], axis=0
    ).astype(BF16)


def diagonal(stacked, heads):
    return jnp.concatenate(
        [
            stacked[head * HD : (head + 1) * HD, head * BLK : (head + 1) * BLK]
            for head in range(heads)
        ],
        axis=0,
    )


def put_pairs(paired, at, width, k_ref, v_ref, kt_ref, vt_ref):
    for index, entry in enumerate(at):
        rows = paired[index * BLK : (index + 1) * BLK]
        keys, values = rows[:, :width], rows[:, width:]
        k_ref[block_at(entry), :] = keys.astype(BF16)
        v_ref[block_at(entry), :] = values.astype(BF16)
        kt_ref[entry] = keys.T.astype(BF16)
        vt_ref[entry] = values.T.astype(BF16)


def own_kernel(states_ref, cot_ref, wq_ref, wk_ref, wv_ref, wo_ref, *refs):
    unit_ref, q_ref, g_ref, k_ref, v_ref, kt_ref, vt_ref = refs
    rows = states_ref.shape[0]
    width = wq_ref.shape[1]
    heads = width // HD
    tall = heads * BLK
    for start in range(0, rows, CHUNK):
        unit_ref[start : start + CHUNK, :] = unit_of(states_ref[start : start + CHUNK, :])
    unit = unit_ref[...]
    queries = nn(unit, wq_ref[...])
    grads = nt(cot_ref[...], wo_ref[...])
    for block in range(rows // BLK):
        q_ref[block * tall : (block + 1) * tall, :] = by_head(
            queries[block * BLK : (block + 1) * BLK], heads
        )
        g_ref[block * tall : (block + 1) * tall, :] = by_head(
            grads[block * BLK : (block + 1) * BLK], heads
        )
    paired = nn(unit, jnp.concatenate([wk_ref[...], wv_ref[...]], axis=1))
    put_pairs(paired, range(rows // BLK), width, k_ref, v_ref, kt_ref, vt_ref)


def run_own(states, cot, weights):
    rows, feats = states.shape
    width = weights[0].shape[1]
    blocks = rows // BLK
    tall = blocks * (width // HD) * BLK
    vmem = pl.BlockSpec(memory_space=pltpu.VMEM)
    shape = jax.ShapeDtypeStruct
    return pl.pallas_call(
        own_kernel,
        out_shape=(
            shape((rows, feats), BF16),
            shape((tall, width), BF16),
            shape((tall, width), BF16),
            shape((rows, width), BF16),
            shape((rows, width), BF16),
            shape((blocks, width, BLK), BF16),
            shape((blocks, width, BLK), BF16),
        ),
        in_specs=[vmem] * 6,
        out_specs=[vmem] * 7,
        compiler_params=pltpu.CompilerParams(vmem_limit_bytes=LIMIT),
        cost_estimate=pl.CostEstimate(
            flops=8 * rows * feats * width, bytes_accessed=6 * rows * feats, transcendentals=0
        ),
        name="own_rows",
    )(states, cot, *weights)


def attend_kernel(cfg, near_ref, *refs):
    ranks, share, blocks, offsets, width = cfg
    count = ranks * share
    piece_refs = refs[:count]
    own_refs = refs[count : count + 7]
    wk_ref, wv_ref = refs[count + 7 : count + 9]
    pool_ref, both_ref, dq_ref, mixed_ref = refs[count + 9 : count + 13]
    k_ref, v_ref, kt_ref, vt_ref, ka_ref, va_ref = refs[count + 13 :]
    q_ref, g_ref, k_own, v_own, kt_own, vt_own = own_refs[1:]
    heads = width // HD
    tall = heads * BLK
    entries = blocks + offsets * SEND
    rank = lax.axis_index("tensor")

    own_rows = blocks * BLK
    k_ref[:own_rows, :] = k_own[...]
    v_ref[:own_rows, :] = v_own[...]
    kt_ref[:blocks] = kt_own[...]
    vt_ref[:blocks] = vt_own[...]
    wkv = jnp.concatenate([wk_ref[...], wv_ref[...]], axis=1)
    for slot in range(ranks):
        for inner in range(share):
            entry = rank_piece(rank ^ slot, ranks, share, inner)
            base = pl.multiple_of(entry * BLK, BLK)
            source = piece_refs[slot * share + inner]
            for start in range(0, BLK, CHUNK):
                rows = unit_of(source[start : start + CHUNK, :])
                pool_ref[pl.ds(pl.multiple_of(base + start, CHUNK), CHUNK), :] = rows
    for start in range(blocks, entries, blocks):
        first = (start - blocks) * BLK
        paired = nn(pool_ref[first : first + blocks * BLK, :], wkv)
        put_pairs(
            paired, range(start, start + blocks), width, k_ref, v_ref, kt_ref, vt_ref
        )
    ka_ref[...] = jnp.zeros_like(ka_ref)
    va_ref[...] = jnp.zeros_like(va_ref)

    shrink = 1.0 / math.sqrt(HD)
    near = near_ref.shape[1]
    for block in range(blocks):
        listed = [block] + [near_ref[block, n] for n in range(near)]
        keys = jnp.concatenate([k_ref[block_at(e), :] for e in listed], axis=0)
        values = jnp.concatenate([v_ref[block_at(e), :] for e in listed], axis=0)
        keys_t = jnp.concatenate([kt_ref[e] for e in listed], axis=1)
        values_t = jnp.concatenate([vt_ref[e] for e in listed], axis=1)
        q_all = q_ref[block * tall : (block + 1) * tall, :]
        g_all = g_ref[block * tall : (block + 1) * tall, :]
        scores = nt(keys, q_all) * shrink
        powers = jnp.exp(scores - jnp.max(scores, axis=0, keepdims=True))
        weights = powers * (1.0 / jnp.sum(powers, axis=0, keepdims=True))
        low = weights.astype(BF16)
        mix = diagonal(nn(values_t, low), heads)
        mixed_ref[block * BLK : (block + 1) * BLK, :] = mix.T.astype(BF16)
        prob = nt(values, g_all)
        drop = jnp.sum(weights * prob, axis=0, keepdims=True)
        score_low = (weights * (prob - drop) * shrink).astype(BF16)
        dq = diagonal(nn(keys_t, score_low), heads)
        dq_ref[block * BLK : (block + 1) * BLK, :] = dq.T.astype(BF16)
        dk = nn(score_low, q_all)
        dv = nn(low, g_all)
        for n, e in enumerate(listed):
            ka_ref[block_at(e), :] += dk[n * BLK : (n + 1) * BLK]
            va_ref[block_at(e), :] += dv[n * BLK : (n + 1) * BLK]

    both_ref[:, :width] = ka_ref[...].astype(BF16)
    both_ref[:, width:] = va_ref[...].astype(BF16)


def grad_terms_kernel(explicit, unit_ref, pool_ref, both_ref, dq_ref, mixed_ref, cot_ref, *refs):
    g_keep, g_send = refs
    rows, width = dq_ref.shape
    half = lax.axis_index("dp") if explicit else 0

    def turned(ref, first, last):
        parts = [
            ref[start : start + BLK, :].astype(F32).T.astype(BF16)
            for start in range(first, last, BLK)
        ]
        return jnp.concatenate(parts, axis=1)

    unit = unit_ref[...]
    grad_q = nn(turned(dq_ref, 0, rows), unit)
    grad_out = nn(turned(mixed_ref, 0, rows), cot_ref[...])
    grad_kv = nn(turned(both_ref, 0, rows), unit)
    grad_kv = grad_kv + nn(turned(both_ref, rows, both_ref.shape[0]), pool_ref[...])
    grad_k, grad_v = grad_kv[:width], grad_kv[width:]
    second = jnp.equal(half, 1)
    g_keep[:width, :] = jnp.where(second, grad_v, grad_q).astype(BF16)
    g_keep[width:, :] = jnp.where(second, grad_out, grad_k).astype(BF16)
    g_send[:width, :] = jnp.where(second, grad_q, grad_v).astype(BF16)
    g_send[width:, :] = jnp.where(second, grad_k, grad_out).astype(BF16)


def run_grad_terms(explicit, unit, pool, both, dq, mixed, cot):
    rows, feats = cot.shape
    width = dq.shape[1]
    vmem = pl.BlockSpec(memory_space=pltpu.VMEM)
    side = jax.ShapeDtypeStruct((2 * width, feats), BF16)
    return pl.pallas_call(
        functools.partial(grad_terms_kernel, explicit),
        out_shape=(side, side),
        in_specs=[vmem] * 6,
        out_specs=[vmem] * 2,
        compiler_params=pltpu.CompilerParams(vmem_limit_bytes=LIMIT),
        cost_estimate=pl.CostEstimate(
            flops=16 * rows * feats * width, bytes_accessed=8 * rows * feats, transcendentals=0
        ),
        name="grad_terms",
    )(unit, pool, both, dq, mixed, cot)


def run_attend(ranks, share, offsets, near, pieces, own, w_key, w_value):
    rows, feats = own[0].shape
    blocks = rows // BLK
    width = w_key.shape[1]
    received = offsets * SEND
    entries = blocks + received
    vmem = pl.BlockSpec(memory_space=pltpu.VMEM)
    smem = pl.BlockSpec(memory_space=pltpu.SMEM)
    cfg = (ranks, share, blocks, offsets, width)
    shape = jax.ShapeDtypeStruct
    return pl.pallas_call(
        functools.partial(attend_kernel, cfg),
        out_shape=(
            shape((received * BLK, feats), BF16),
            shape((entries * BLK, 2 * width), BF16),
            shape((rows, width), BF16),
            shape((rows, width), BF16),
        ),
        in_specs=[smem] + [vmem] * (len(pieces) + 9),
        out_specs=[vmem] * 4,
        scratch_shapes=[
            pltpu.VMEM((entries * BLK, width), BF16),
            pltpu.VMEM((entries * BLK, width), BF16),
            pltpu.VMEM((entries, width, BLK), BF16),
            pltpu.VMEM((entries, width, BLK), BF16),
            pltpu.VMEM((entries * BLK, width), F32),
            pltpu.VMEM((entries * BLK, width), F32),
        ],
        compiler_params=pltpu.CompilerParams(vmem_limit_bytes=LIMIT),
        cost_estimate=pl.CostEstimate(
            flops=64 * rows * feats * width, bytes_accessed=12 * rows * feats, transcendentals=0
        ),
        name="attention",
    )(near, *pieces, *own, w_key, w_value)


def terms_kernel(cfg, *refs):
    blocks, offsets, width = cfg
    unit_ref, pool_ref, both_ref, dq_ref, mixed_ref, wq_ref, wk_ref, wv_ref, wo_ref = refs[:9]
    far_keep, far_send, own_keep, own_send = refs[9:]
    feats = unit_ref.shape[1]
    slabs = feats // width
    sub = BLK // width
    group = SEND * BLK + PAD
    rank = lax.axis_index("tensor")
    odd = (rank & 1) == 1
    upper = rank >> 1
    ones = jnp.ones((16, feats), BF16)
    wkv = jnp.concatenate([wk_ref[...], wv_ref[...]], axis=1)

    def put(keep_ref, send_ref, row, values):
        count = values.shape[0]
        for pair in range(slabs // 2):
            left = values[:, 2 * pair * width : (2 * pair + 1) * width]
            right = values[:, (2 * pair + 1) * width : (2 * pair + 2) * width]
            at = upper ^ pair
            keep_ref[at, row : row + count, :] = jnp.where(odd, right, left).astype(BF16)
            send_ref[at, row : row + count, :] = jnp.where(odd, left, right).astype(BF16)

    def put_dots(keep_ref, send_ref, row, dots):
        parts = []
        for dot in dots:
            for piece in range(sub):
                parts.append(dot[:1, piece * width : (piece + 1) * width])
        parts.append(jnp.zeros((PAD - len(parts), width), F32))
        rows = jnp.concatenate(parts, axis=0).astype(BF16)
        for pair in range(slabs // 2):
            keep_ref[pair, row : row + PAD, :] = rows
            send_ref[pair, row : row + PAD, :] = rows

    def row_dot(term, ref, first):
        product = (term * ref[first : first + BLK, :].astype(F32)).astype(BF16)
        return nt(ones, product)

    own_rows = blocks * BLK
    for offset in range(offsets):
        first = offset * SEND * BLK
        term = nt(both_ref[own_rows + first : own_rows + first + SEND * BLK, :], wkv)
        put(far_keep, far_send, offset * group, term)
        dots = [
            row_dot(term[c * BLK : (c + 1) * BLK], pool_ref, first + c * BLK)
            for c in range(SEND)
        ]
        put_dots(far_keep, far_send, offset * group + SEND * BLK, dots)

    dots = []
    for pair in range(0, blocks, 2):
        first, last = pair * BLK, (pair + 2) * BLK
        term = nt(both_ref[first:last, :], wkv) + nt(dq_ref[first:last, :], wq_ref[...])
        put(own_keep, own_send, first, term)
        dots += [
            row_dot(term[c * BLK : (c + 1) * BLK], unit_ref, first + c * BLK) for c in range(2)
        ]
        update = nn(mixed_ref[first:last, :], wo_ref[...])
        put(own_keep, own_send, own_rows + PAD + first, update)
    put_dots(own_keep, own_send, own_rows, dots)


def run_terms(offsets, unit, pool, both, dq, mixed, weights):
    rows, feats = unit.shape
    width = dq.shape[1]
    pairs = feats // width // 2
    far_rows = offsets * (SEND * BLK + PAD)
    own_rows = 2 * rows + PAD
    vmem = pl.BlockSpec(memory_space=pltpu.VMEM)
    shape = jax.ShapeDtypeStruct
    far = shape((pairs, far_rows, width), BF16)
    own = shape((pairs, own_rows, width), BF16)
    return pl.pallas_call(
        functools.partial(terms_kernel, (rows // BLK, offsets, width)),
        out_shape=(far, far, own, own),
        in_specs=[vmem] * 9,
        out_specs=[vmem] * 4,
        compiler_params=pltpu.CompilerParams(vmem_limit_bytes=LIMIT),
        cost_estimate=pl.CostEstimate(
            flops=14 * rows * feats * width, bytes_accessed=8 * rows * feats, transcendentals=0
        ),
        name="group_terms",
    )(unit, pool, both, dq, mixed, *weights)


def returns_kernel(bounds, keep_ref, got_ref, last_ref, *outs):
    for (first, last), out_ref in zip(bounds, outs):
        total = keep_ref[0, first:last, :].astype(F32) + got_ref[0, first:last, :].astype(F32)
        out_ref[...] = (total + last_ref[first:last, :].astype(F32)).astype(BF16)


def run_returns(bounds, keep, got, last):
    vmem = pl.BlockSpec(memory_space=pltpu.VMEM)
    width = keep.shape[2]
    return pl.pallas_call(
        functools.partial(returns_kernel, bounds),
        out_shape=[jax.ShapeDtypeStruct((b - a, width), BF16) for a, b in bounds],
        in_specs=[vmem] * 3,
        out_specs=[vmem] * len(bounds),
        compiler_params=pltpu.CompilerParams(vmem_limit_bytes=SMALL),
        name="returned_terms",
    )(keep, got, last)


def split_kernel(parts, keep_ref, got_ref, mine_ref, *outs):
    dom = lax.axis_index("dom")
    size = mine_ref.shape[0]
    for step in range(parts):
        at = block_at((dom + step) & (parts - 1), size)
        total = keep_ref[at, :].astype(F32) + got_ref[at, :].astype(F32)
        if step == 0:
            mine_ref[...] = total
        else:
            outs[step - 1][...] = total.astype(BF16)


def run_split(parts, keep, got):
    vmem = pl.BlockSpec(memory_space=pltpu.VMEM)
    size, feats = keep.shape[0] // parts, keep.shape[1]
    shape = jax.ShapeDtypeStruct
    return pl.pallas_call(
        functools.partial(split_kernel, parts),
        out_shape=[shape((size, feats), F32)] + [shape((size, feats), BF16)] * (parts - 1),
        in_specs=[vmem] * 2,
        out_specs=[vmem] * parts,
        compiler_params=pltpu.CompilerParams(vmem_limit_bytes=SMALL),
        name="split_grads",
    )(keep, got)


def finish_kernel(cfg, *refs):
    blocks, offsets, width, spread = cfg
    send_ref, states_ref, keep_ref, got_ref, last_ref = refs[:5]
    far_refs = refs[5 : 5 + len(spread)]
    update_ref, branch_ref, unit_ref = refs[5 + len(spread) :]
    own_rows = blocks * BLK
    sub = BLK // width
    group = SEND * BLK + PAD
    rank = lax.axis_index("tensor")

    def both(first, last):
        total = keep_ref[0, first:last, :].astype(F32) + got_ref[0, first:last, :].astype(F32)
        return total + last_ref[first:last, :].astype(F32)

    update_ref[...] = both(own_rows + PAD, 2 * own_rows + PAD).astype(BF16)
    unit_ref[...] = both(0, own_rows)
    dots = both(own_rows, own_rows + PAD)
    at_row = lax.broadcasted_iota(jnp.int32, (PAD, width), 0)
    for ref, members in zip(far_refs, spread):
        for position, offset in enumerate(members):
            first = position * group
            extra = ref[first + SEND * BLK : first + group, :].astype(F32)
            for c in range(SEND):
                block = send_ref[c, offset]
                rows = ref[first + c * BLK : first + (c + 1) * BLK, :].astype(F32)
                unit_ref[block_at(block), :] += rows
                for piece in range(sub):
                    line = extra[c * sub + piece : c * sub + piece + 1, :]
                    dots = dots + jnp.where(at_row == block * sub + piece, line, 0.0)
    feats = states_ref.shape[1]
    for block in range(blocks):
        rows = slice(block * BLK, (block + 1) * BLK)
        values = states_ref[rows, :].astype(F32)
        inverse = lax.rsqrt(jnp.mean(values * values, axis=-1, keepdims=True) + EPS)
        own = values[:, :width]
        for slab in range(1, feats // width):
            own = jnp.where(rank == slab, values[:, slab * width : (slab + 1) * width], own)
        line = jnp.concatenate(
            [dots[block * sub + piece : block * sub + piece + 1, :] for piece in range(sub)], axis=1
        )
        mean = jnp.broadcast_to(line * (1.0 / feats), (BLK, BLK)).T[:, :width]
        branch_ref[rows, :] = (inverse * (unit_ref[rows, :] - own * inverse * mean)).astype(BF16)


def run_finish(send, states, keep, got, last, far, spread):
    rows, feats = states.shape
    width = last.shape[1]
    vmem = pl.BlockSpec(memory_space=pltpu.VMEM)
    smem = pl.BlockSpec(memory_space=pltpu.SMEM)
    shape = jax.ShapeDtypeStruct
    cfg = (rows // BLK, send.shape[1], width, spread)
    return pl.pallas_call(
        functools.partial(finish_kernel, cfg),
        out_shape=(shape((rows, width), BF16), shape((rows, width), BF16)),
        in_specs=[smem] + [vmem] * (4 + len(far)),
        out_specs=[vmem] * 2,
        scratch_shapes=[pltpu.VMEM((rows, width), F32)],
        compiler_params=pltpu.CompilerParams(vmem_limit_bytes=SMALL),
        name="finish",
    )(send, states, keep, got, last, *far)


def grads_kernel(cfg, *refs):
    parts, factor = cfg
    mine_refs = refs[:parts]
    other_refs = refs[parts : 2 * parts]
    q_ref, k_ref, v_ref, o_ref, all_ref = refs[2 * parts :]
    half = lax.axis_index("dp")
    dom = lax.axis_index("dom")
    size = mine_refs[0].shape[0]
    width = q_ref.shape[1]
    for group, side in ((mine_refs, half), (other_refs, 1 - half)):
        for step in range(parts):
            index = side * parts + ((dom + parts - step) & (parts - 1))
            all_ref[block_at(index, size), :] = group[step][...]
    for position, ref in enumerate((q_ref, k_ref, v_ref)):
        for start in range(0, ref.shape[0], BLK):
            rows = all_ref[position * width : (position + 1) * width, start : start + BLK]
            ref[start : start + BLK, :] = rows.astype(F32).T * factor
    o_ref[...] = all_ref[3 * width :, :].astype(F32) * factor


def run_grads(mine, other, factor):
    parts = len(mine)
    size, feats = mine[0].shape
    width = parts * size // 2
    vmem = pl.BlockSpec(memory_space=pltpu.VMEM)
    tall = jax.ShapeDtypeStruct((feats, width), F32)
    return pl.pallas_call(
        functools.partial(grads_kernel, (parts, factor)),
        out_shape=(tall, tall, tall, jax.ShapeDtypeStruct((width, feats), F32)),
        in_specs=[vmem] * (2 * parts),
        out_specs=[vmem] * 4,
        scratch_shapes=[pltpu.VMEM((4 * width, feats), BF16)],
        compiler_params=pltpu.CompilerParams(vmem_limit_bytes=SMALL),
        name="weight_grads",
    )(*mine, *other)


def swap(array, axis, bit):
    return lax.ppermute(array, axis, [(i, i ^ bit) for i in range(lax.axis_size(axis))])


def shifted(array, axis, distance):
    size = lax.axis_size(axis)
    return lax.ppermute(array, axis, [(i, (i + distance) % size) for i in range(size)])


def added(left, right):
    return (left.astype(F32) + right.astype(F32)).astype(BF16)


def after(values, *earlier):
    held = lax.optimization_barrier((values, earlier))
    return held[0]


def narrow(keep, got, bit):
    while keep.shape[0] > 2:
        summed = added(keep, got)
        keep, send = summed[0::2], summed[1::2]
        got = swap(send, "tensor", bit)
        bit *= 2
    return keep, got, bit


def body(states, w_query, w_key, w_value, w_out, send_blocks, neighbor_blocks, cotangent):
    replicas, node_count, feats = states.shape
    width = w_query.shape[1]
    ranks = lax.axis_size("tensor")
    parts = lax.axis_size("dom")
    explicit = parts == 4 and lax.axis_size("dp") == 2
    offsets = offset_list(HOPS)
    order, share = piece_order(ranks, len(offsets))
    send = send_blocks[0].T
    weights = (w_query, w_key, w_value, w_out)
    flat_states = states.reshape(-1, feats)
    flat_cot = cotangent.reshape(-1, feats)

    leaving = pick_blocks(flat_states, send, ranks, share)
    route = []
    for p in range(parts):
        for r in range(ranks):
            distance = offsets[order[r * share] // SEND]
            route.append((p * ranks + r, ((p + distance) % parts) * ranks + r))
    levels = []
    bit = 1
    while bit < ranks:
        levels.append(bit)
        bit *= 2
    arrived = [lax.ppermute(block, ("dom", "tensor"), route) for block in leaving]
    own = run_own(flat_states, flat_cot, weights)
    arrived[0] = after(arrived[0], own)
    pieces = [None] * (ranks * share)
    for inner in range(share):
        if inner:
            arrived[inner] = after(arrived[inner], pieces[share + inner - 1])
        held = {0: arrived[inner]}
        for bit in reversed(levels):
            for slot in list(held):
                held[slot ^ bit] = swap(held[slot], "tensor", bit)
        for slot in range(ranks):
            pieces[slot * share + inner] = held[slot]

    pool, both, dq, mixed = run_attend(
        ranks,
        share,
        len(offsets),
        neighbor_blocks,
        pieces,
        own,
        w_key,
        w_value,
    )
    unit = own[0]
    far_keep, far_send, own_keep, own_send = run_terms(
        len(offsets), unit, pool, both, dq, mixed, weights
    )
    far_got = swap(far_send, "tensor", 1)
    g_keep, g_send = run_grad_terms(explicit, unit, pool, both, dq, mixed, flat_cot)
    g_got = swap(g_send, "dp", 1) if explicit else None
    own_got = swap(own_send, "tensor", 1)
    far_keep, far_got, bit = narrow(far_keep, far_got, 2)
    own_keep, own_got, bit = narrow(own_keep, own_got, 2)
    far_out = added(far_keep[1], far_got[1])
    far_last = swap(far_out, "tensor", bit)
    own_got = after(own_got, far_out)
    own_out = added(own_keep[1], own_got[1])
    own_last = swap(own_out, "tensor", bit)

    group = SEND * BLK + PAD
    spread = []
    for index, distance in enumerate(offsets):
        for members in spread:
            if (offsets[members[0]] - distance) % parts == 0 and members[-1] == index - 1:
                members.append(index)
                break
        else:
            spread.append([index])
    spread = tuple(tuple(members) for members in spread)
    bounds = tuple((members[0] * group, (members[-1] + 1) * group) for members in spread)

    total_rows = replicas * node_count * lax.axis_size("dp") * parts
    factor = 1.0 / math.sqrt(total_rows)
    if explicit:
        g_got = after(g_got, own_out)
        mine, *leaving = run_split(parts, g_keep, g_got)
        arrived = [shifted(part, "dom", step + 1) for step, part in enumerate(leaving)]
    far_sums = run_returns(bounds, far_keep, far_got, far_last)
    far = [
        shifted(part, "dom", -offsets[members[0]]) for part, members in zip(far_sums, spread)
    ]
    if explicit:
        arrived = after(arrived, far_sums)
        for part in arrived:
            mine = mine + part.astype(F32)
        mine = mine.astype(BF16)
        chunks = [mine] + [shifted(mine, "dom", step) for step in range(1, parts)]
        others = [swap(chunk, "dp", 1) for chunk in chunks]
        grads = run_grads(chunks, others, factor)
    else:
        summed = lax.psum(
            jnp.concatenate([g_keep, g_send]).astype(F32), ("dp", "dom")
        ).reshape(4, width, feats)
        grads = (
            summed[0].T * factor,
            summed[1].T * factor,
            summed[2].T * factor,
            summed[3] * factor,
        )
    update, branch = run_finish(send, flat_states, own_keep, own_got, own_last, far, spread)
    shape = (replicas, node_count, width)
    return (update.reshape(shape), branch.reshape(shape), *grads)


def solution(mesh):
    placed = (
        P("dp", "dom", None),
        P(None, "tensor"),
        P(None, "tensor"),
        P(None, "tensor"),
        P("tensor", None),
        P("dom", None, None),
        P("dom", None),
        P("dp", "dom", None),
    )
    return jax.shard_map(
        body,
        mesh=mesh,
        in_specs=placed,
        out_specs=(
            P("dp", "dom", "tensor"),
            P("dp", "dom", "tensor"),
            P(None, "tensor"),
            P(None, "tensor"),
            P(None, "tensor"),
            P("tensor", None),
        ),
        check_vma=False,
    )
```

```python
import functools
import math

import jax
import jax.numpy as jnp
from jax import lax
from jax.experimental import pallas as pl
from jax.experimental.pallas import tpu as pltpu
from jax.sharding import PartitionSpec as P

BLK = 128
HOPS = 2
SEND = 2
HD = 64
PAD = 16
EPS = 1e-05
LIMIT = 24 * 1024 * 1024
SMALL = 8 * 1024 * 1024
CHUNK = 64
F32 = jnp.float32
BF16 = jnp.bfloat16


def offset_list(hops):
    result = []
    for section in range(1, hops + 1):
        result.append(section)
        result.append(-section)
    return result


def piece_order(ranks, offsets):
    count = offsets * SEND
    share = count // ranks
    if share == SEND and offsets == 4:
        return [0, 1, 4, 5, 2, 3, 6, 7], share
    return list(range(count)), share


def nt(left, right):
    return lax.dot_general(left, right, (((1,), (1,)), ((), ())), preferred_element_type=F32)


def nn(left, right):
    return jnp.dot(left, right, preferred_element_type=F32)


def unit_of(rows):
    values = rows.astype(F32)
    return (values * lax.rsqrt(jnp.mean(values * values, axis=-1, keepdims=True) + EPS)).astype(BF16)


def block_at(index, size=BLK):
    return pl.ds(pl.multiple_of(index * size, size), size)


def rank_piece(rank, ranks, share, inner):
    if share == SEND and ranks == 4:
        return ((rank & 1) * 2 + (rank >> 1)) * SEND + inner
    return rank * share + inner


def in_hbm(*arrays):
    return [pltpu.with_memory_space_constraint(array, pltpu.HBM) for array in arrays]


def pick_kernel(ranks, share, send_ref, states_ref, *refs):
    outs, table, sems = refs[:share], refs[share], refs[share + 1]
    rank = lax.axis_index("tensor")
    fetch = pltpu.make_async_copy(send_ref, table, sems.at[share])
    fetch.start()
    fetch.wait()
    copies = []
    for inner, out_ref in enumerate(outs):
        piece = rank_piece(rank, ranks, share, inner)
        block = table[piece % SEND, piece // SEND]
        copies.append(
            pltpu.make_async_copy(states_ref.at[block_at(block), :], out_ref, sems.at[inner])
        )
        copies[-1].start()
    for copy in copies:
        copy.wait()


def pick_blocks(states, send, ranks, share):
    far = pl.BlockSpec(memory_space=pltpu.HBM)
    vmem = pl.BlockSpec(memory_space=pltpu.VMEM)
    return pl.pallas_call(
        functools.partial(pick_kernel, ranks, share),
        out_shape=[jax.ShapeDtypeStruct((BLK, states.shape[1]), BF16)] * share,
        in_specs=[far, far],
        out_specs=[vmem] * share,
        scratch_shapes=[
            pltpu.SMEM(send.shape, jnp.int32),
            pltpu.SemaphoreType.DMA((share + 1,)),
        ],
        compiler_params=pltpu.CompilerParams(vmem_limit_bytes=SMALL),
        name="pick_blocks",
    )(*in_hbm(send, states))


def by_head(rows, heads):
    if heads == 1:
        return rows.astype(BF16)
    lane_head = lax.broadcasted_iota(jnp.int32, rows.shape, 1) // HD
    return jnp.concatenate(
        [jnp.where(lane_head == head, rows, 0.0) for head in range(heads)], axis=0
    ).astype(BF16)


def diagonal(stacked, heads):
    return jnp.concatenate(
        [
            stacked[head * HD : (head + 1) * HD, head * BLK : (head + 1) * BLK]
            for head in range(heads)
        ],
        axis=0,
    )


def put_pairs(paired, at, width, k_ref, v_ref, kt_ref, vt_ref):
    for index, entry in enumerate(at):
        rows = paired[index * BLK : (index + 1) * BLK]
        keys, values = rows[:, :width], rows[:, width:]
        k_ref[block_at(entry), :] = keys.astype(BF16)
        v_ref[block_at(entry), :] = values.astype(BF16)
        kt_ref[entry] = keys.T.astype(BF16)
        vt_ref[entry] = values.T.astype(BF16)


def own_kernel(*refs):
    sources = refs[:6]
    unit_ref, q_ref, g_ref, k_ref, v_ref, kt_ref, vt_ref, slab_ref, inverse_ref = refs[6:15]
    held, states_ref, sems = refs[15:20], refs[20], refs[21]
    cot_ref, wq_ref, wk_ref, wv_ref, wo_ref = held
    copies = []
    for index, (source, target) in enumerate(zip(sources, (states_ref,) + tuple(held))):
        copies.append(pltpu.make_async_copy(source, target, sems.at[index]))
        copies[-1].start()
    rows, feats = states_ref.shape
    width = wq_ref.shape[1]
    heads = width // HD
    tall = heads * BLK
    rank = lax.axis_index("tensor")
    copies[0].wait()
    for start in range(0, rows, CHUNK):
        values = states_ref[start : start + CHUNK, :].astype(F32)
        inverse = lax.rsqrt(jnp.mean(values * values, axis=-1, keepdims=True) + EPS)
        normed = values * inverse
        unit_ref[start : start + CHUNK, :] = normed.astype(BF16)
        slab = normed[:, :width]
        for index in range(1, feats // width):
            slab = jnp.where(rank == index, normed[:, index * width : (index + 1) * width], slab)
        slab_ref[start : start + CHUNK, :] = slab
        inverse_ref[start : start + CHUNK, :] = jnp.broadcast_to(inverse, slab.shape)
    for copy in copies[1:]:
        copy.wait()
    unit = unit_ref[...]
    queries = nn(unit, wq_ref[...])
    grads = nt(cot_ref[...], wo_ref[...])
    for block in range(rows // BLK):
        q_ref[block * tall : (block + 1) * tall, :] = by_head(
            queries[block * BLK : (block + 1) * BLK], heads
        )
        g_ref[block * tall : (block + 1) * tall, :] = by_head(
            grads[block * BLK : (block + 1) * BLK], heads
        )
    paired = nn(unit, jnp.concatenate([wk_ref[...], wv_ref[...]], axis=1))
    put_pairs(paired, range(rows // BLK), width, k_ref, v_ref, kt_ref, vt_ref)


def run_own(states, cot, weights):
    rows, feats = states.shape
    width = weights[0].shape[1]
    blocks = rows // BLK
    tall = blocks * (width // HD) * BLK
    vmem = pl.BlockSpec(memory_space=pltpu.VMEM)
    far = pl.BlockSpec(memory_space=pltpu.HBM)
    shape = jax.ShapeDtypeStruct
    return pl.pallas_call(
        own_kernel,
        out_shape=(
            shape((rows, feats), BF16),
            shape((tall, width), BF16),
            shape((tall, width), BF16),
            shape((rows, width), BF16),
            shape((rows, width), BF16),
            shape((blocks, width, BLK), BF16),
            shape((blocks, width, BLK), BF16),
            shape((rows, width), F32),
            shape((rows, width), F32),
            shape(cot.shape, BF16),
            *[shape(w.shape, BF16) for w in weights],
        ),
        in_specs=[far] * 6,
        out_specs=[vmem] * 14,
        scratch_shapes=[pltpu.VMEM((rows, feats), BF16), pltpu.SemaphoreType.DMA((6,))],
        compiler_params=pltpu.CompilerParams(vmem_limit_bytes=LIMIT),
        cost_estimate=pl.CostEstimate(
            flops=8 * rows * feats * width, bytes_accessed=6 * rows * feats, transcendentals=0
        ),
        name="own_rows",
    )(*in_hbm(states, cot, *weights))


def attend_kernel(cfg, near_ref, *refs):
    ranks, share, blocks, offsets, width = cfg
    count = ranks * share
    piece_refs = refs[:count]
    own_refs = refs[count : count + 7]
    wk_ref, wv_ref = refs[count + 7 : count + 9]
    pool_ref, both_ref, dq_ref, mixed_ref = refs[count + 9 : count + 13]
    k_ref, v_ref, kt_ref, vt_ref, ka_ref, va_ref, dk_ref, dv_ref = refs[count + 13 : count + 21]
    near_table, near_sem = refs[count + 21 :]
    fetch = pltpu.make_async_copy(near_ref, near_table, near_sem)
    fetch.start()
    q_ref, g_ref, k_own, v_own, kt_own, vt_own = own_refs[1:]
    heads = width // HD
    tall = heads * BLK
    entries = blocks + offsets * SEND
    rank = lax.axis_index("tensor")

    own_rows = blocks * BLK
    k_ref[:own_rows, :] = k_own[...]
    v_ref[:own_rows, :] = v_own[...]
    kt_ref[:blocks] = kt_own[...]
    vt_ref[:blocks] = vt_own[...]
    wkv = jnp.concatenate([wk_ref[...], wv_ref[...]], axis=1)
    for slot in range(ranks):
        for inner in range(share):
            entry = rank_piece(rank ^ slot, ranks, share, inner)
            base = pl.multiple_of(entry * BLK, BLK)
            source = piece_refs[slot * share + inner]
            for start in range(0, BLK, CHUNK):
                rows = unit_of(source[start : start + CHUNK, :])
                pool_ref[pl.ds(pl.multiple_of(base + start, CHUNK), CHUNK), :] = rows
    for start in range(blocks, entries, blocks):
        first = (start - blocks) * BLK
        paired = nn(pool_ref[first : first + blocks * BLK, :], wkv)
        put_pairs(
            paired, range(start, start + blocks), width, k_ref, v_ref, kt_ref, vt_ref
        )

    shrink = 1.0 / math.sqrt(HD)
    near = near_ref.shape[1]
    fetch.wait()
    for block in range(blocks):
        listed = [block] + [near_table[block, n] for n in range(near)]
        keys = jnp.concatenate([k_ref[block_at(e), :] for e in listed], axis=0)
        values = jnp.concatenate([v_ref[block_at(e), :] for e in listed], axis=0)
        keys_t = jnp.concatenate([kt_ref[e] for e in listed], axis=1)
        values_t = jnp.concatenate([vt_ref[e] for e in listed], axis=1)
        q_all = q_ref[block * tall : (block + 1) * tall, :]
        g_all = g_ref[block * tall : (block + 1) * tall, :]
        scores = nt(keys, q_all) * shrink
        powers = jnp.exp(scores - jnp.max(scores, axis=0, keepdims=True))
        weights = powers * (1.0 / jnp.sum(powers, axis=0, keepdims=True))
        low = weights.astype(BF16)
        mix = diagonal(nn(values_t, low), heads)
        mixed_ref[block * BLK : (block + 1) * BLK, :] = mix.T.astype(BF16)
        prob = nt(values, g_all)
        drop = jnp.sum(weights * prob, axis=0, keepdims=True)
        score_low = (weights * (prob - drop) * shrink).astype(BF16)
        dq = diagonal(nn(keys_t, score_low), heads)
        dq_ref[block * BLK : (block + 1) * BLK, :] = dq.T.astype(BF16)
        dk = nn(score_low, q_all)
        dv = nn(low, g_all)
        ka_ref[block * BLK : (block + 1) * BLK, :] = dk[:BLK]
        va_ref[block * BLK : (block + 1) * BLK, :] = dv[:BLK]
        dk_ref[block] = dk[BLK:]
        dv_ref[block] = dv[BLK:]

    ka_ref[own_rows:, :] = jnp.zeros((entries * BLK - own_rows, width), F32)
    va_ref[own_rows:, :] = jnp.zeros((entries * BLK - own_rows, width), F32)
    for block in range(blocks):
        for n in range(near):
            entry = block_at(near_table[block, n])
            ka_ref[entry, :] += dk_ref[block, n * BLK : (n + 1) * BLK]
            va_ref[entry, :] += dv_ref[block, n * BLK : (n + 1) * BLK]

    both_ref[:, :width] = ka_ref[...].astype(BF16)
    both_ref[:, width:] = va_ref[...].astype(BF16)


def grad_terms_kernel(unit_ref, pool_ref, both_ref, dq_ref, mixed_ref, cot_ref, g_ref):
    rows, width = dq_ref.shape
    def turned(ref, first, last):
        parts = [
            ref[start : start + BLK, :].astype(F32).T.astype(BF16)
            for start in range(first, last, BLK)
        ]
        return jnp.concatenate(parts, axis=1)

    unit = unit_ref[...]
    g_ref[:width, :] = nn(turned(dq_ref, 0, rows), unit).astype(BF16)
    grad_kv = nn(turned(both_ref, 0, rows), unit)
    grad_kv = grad_kv + nn(turned(both_ref, rows, both_ref.shape[0]), pool_ref[...])
    g_ref[width : 3 * width, :] = grad_kv.astype(BF16)
    g_ref[3 * width :, :] = nn(turned(mixed_ref, 0, rows), cot_ref[...]).astype(BF16)


def run_grad_terms(unit, pool, both, dq, mixed, cot):
    rows, feats = cot.shape
    width = dq.shape[1]
    vmem = pl.BlockSpec(memory_space=pltpu.VMEM)
    return pl.pallas_call(
        grad_terms_kernel,
        out_shape=jax.ShapeDtypeStruct((4 * width, feats), BF16),
        in_specs=[vmem] * 6,
        out_specs=vmem,
        compiler_params=pltpu.CompilerParams(vmem_limit_bytes=LIMIT),
        cost_estimate=pl.CostEstimate(
            flops=16 * rows * feats * width, bytes_accessed=8 * rows * feats, transcendentals=0
        ),
        name="grad_terms",
    )(unit, pool, both, dq, mixed, cot)


def run_attend(ranks, share, offsets, near, pieces, own, w_key, w_value):
    rows, feats = own[0].shape
    blocks = rows // BLK
    width = w_key.shape[1]
    received = offsets * SEND
    entries = blocks + received
    vmem = pl.BlockSpec(memory_space=pltpu.VMEM)
    far = pl.BlockSpec(memory_space=pltpu.HBM)
    cfg = (ranks, share, blocks, offsets, width)
    shape = jax.ShapeDtypeStruct
    return pl.pallas_call(
        functools.partial(attend_kernel, cfg),
        out_shape=(
            shape((received * BLK, feats), BF16),
            shape((entries * BLK, 2 * width), BF16),
            shape((rows, width), BF16),
            shape((rows, width), BF16),
        ),
        in_specs=[far] + [vmem] * (len(pieces) + 9),
        out_specs=[vmem] * 4,
        scratch_shapes=[
            pltpu.VMEM((entries * BLK, width), BF16),
            pltpu.VMEM((entries * BLK, width), BF16),
            pltpu.VMEM((entries, width, BLK), BF16),
            pltpu.VMEM((entries, width, BLK), BF16),
            pltpu.VMEM((entries * BLK, width), F32),
            pltpu.VMEM((entries * BLK, width), F32),
            pltpu.VMEM((blocks, near.shape[1] * BLK, width), F32),
            pltpu.VMEM((blocks, near.shape[1] * BLK, width), F32),
            pltpu.SMEM(near.shape, jnp.int32),
            pltpu.SemaphoreType.DMA(()),
        ],
        compiler_params=pltpu.CompilerParams(vmem_limit_bytes=LIMIT),
        cost_estimate=pl.CostEstimate(
            flops=64 * rows * feats * width, bytes_accessed=12 * rows * feats, transcendentals=0
        ),
        name="attention",
    )(*in_hbm(near), *pieces, *own, w_key, w_value)


def terms_kernel(cfg, *refs):
    blocks, offsets, width = cfg
    unit_ref, pool_ref, both_ref, dq_ref, mixed_ref, wq_ref, wk_ref, wv_ref, wo_ref = refs[:9]
    far_keep, far_send, own_keep, own_send = refs[9:]
    feats = unit_ref.shape[1]
    slabs = feats // width
    sub = BLK // width
    group = SEND * BLK + PAD
    rank = lax.axis_index("tensor")
    odd = (rank & 1) == 1
    upper = rank >> 1
    ones = jnp.ones((16, feats), BF16)
    wkv = jnp.concatenate([wk_ref[...], wv_ref[...]], axis=1)

    def put(keep_ref, send_ref, row, values):
        count = values.shape[0]
        for pair in range(slabs // 2):
            left = values[:, 2 * pair * width : (2 * pair + 1) * width]
            right = values[:, (2 * pair + 1) * width : (2 * pair + 2) * width]
            at = upper ^ pair
            keep_ref[at, row : row + count, :] = jnp.where(odd, right, left).astype(BF16)
            send_ref[at, row : row + count, :] = jnp.where(odd, left, right).astype(BF16)

    def put_dots(keep_ref, send_ref, row, dots):
        parts = []
        for dot in dots:
            for piece in range(sub):
                parts.append(dot[:1, piece * width : (piece + 1) * width])
        parts.append(jnp.zeros((PAD - len(parts), width), F32))
        rows = jnp.concatenate(parts, axis=0).astype(BF16)
        for pair in range(slabs // 2):
            keep_ref[pair, row : row + PAD, :] = rows
            send_ref[pair, row : row + PAD, :] = rows

    def row_dot(term, ref, first):
        product = (term * ref[first : first + BLK, :].astype(F32)).astype(BF16)
        return nt(ones, product)

    own_rows = blocks * BLK
    for offset in range(offsets):
        first = offset * SEND * BLK
        term = nt(both_ref[own_rows + first : own_rows + first + SEND * BLK, :], wkv)
        put(far_keep, far_send, offset * group, term)
        dots = [
            row_dot(term[c * BLK : (c + 1) * BLK], pool_ref, first + c * BLK)
            for c in range(SEND)
        ]
        put_dots(far_keep, far_send, offset * group + SEND * BLK, dots)

    dots = []
    for pair in range(0, blocks, 2):
        first, last = pair * BLK, (pair + 2) * BLK
        term = nt(both_ref[first:last, :], wkv) + nt(dq_ref[first:last, :], wq_ref[...])
        put(own_keep, own_send, first, term)
        dots += [
            row_dot(term[c * BLK : (c + 1) * BLK], unit_ref, first + c * BLK) for c in range(2)
        ]
        update = nn(mixed_ref[first:last, :], wo_ref[...])
        put(own_keep, own_send, own_rows + PAD + first, update)
    put_dots(own_keep, own_send, own_rows, dots)


def run_terms(offsets, unit, pool, both, dq, mixed, weights):
    rows, feats = unit.shape
    width = dq.shape[1]
    pairs = feats // width // 2
    far_rows = offsets * (SEND * BLK + PAD)
    own_rows = 2 * rows + PAD
    vmem = pl.BlockSpec(memory_space=pltpu.VMEM)
    shape = jax.ShapeDtypeStruct
    far = shape((pairs, far_rows, width), BF16)
    own = shape((pairs, own_rows, width), BF16)
    return pl.pallas_call(
        functools.partial(terms_kernel, (rows // BLK, offsets, width)),
        out_shape=(far, far, own, own),
        in_specs=[vmem] * 9,
        out_specs=[vmem] * 4,
        compiler_params=pltpu.CompilerParams(vmem_limit_bytes=LIMIT),
        cost_estimate=pl.CostEstimate(
            flops=14 * rows * feats * width, bytes_accessed=8 * rows * feats, transcendentals=0
        ),
        name="group_terms",
    )(unit, pool, both, dq, mixed, *weights)


def returns_kernel(bounds, keep_ref, got_ref, last_ref, *outs):
    for (first, last), out_ref in zip(bounds, outs):
        total = keep_ref[0, first:last, :].astype(F32) + got_ref[0, first:last, :].astype(F32)
        out_ref[...] = (total + last_ref[first:last, :].astype(F32)).astype(BF16)


def run_returns(bounds, keep, got, last):
    vmem = pl.BlockSpec(memory_space=pltpu.VMEM)
    width = keep.shape[2]
    return pl.pallas_call(
        functools.partial(returns_kernel, bounds),
        out_shape=[jax.ShapeDtypeStruct((b - a, width), BF16) for a, b in bounds],
        in_specs=[vmem] * 3,
        out_specs=[vmem] * len(bounds),
        compiler_params=pltpu.CompilerParams(vmem_limit_bytes=SMALL),
        name="returned_terms",
    )(keep, got, last)


def own_sum_kernel(keep_ref, got_ref, last_ref, update_ref, unit_ref):
    rows = update_ref.shape[0]

    def total(first, last):
        both = keep_ref[0, first:last, :].astype(F32) + got_ref[0, first:last, :].astype(F32)
        return both + last_ref[first:last, :].astype(F32)

    unit_ref[...] = total(0, rows + PAD)
    update_ref[...] = total(rows + PAD, 2 * rows + PAD).astype(BF16)


def run_own_sum(rows, keep, got, last):
    width = last.shape[1]
    vmem = pl.BlockSpec(memory_space=pltpu.VMEM)
    shape = jax.ShapeDtypeStruct
    return pl.pallas_call(
        own_sum_kernel,
        out_shape=(shape((rows, width), BF16), shape((rows + PAD, width), F32)),
        in_specs=[vmem] * 3,
        out_specs=[vmem] * 2,
        compiler_params=pltpu.CompilerParams(vmem_limit_bytes=SMALL),
        name="own_sum",
    )(keep, got, last)


def finish_kernel(cfg, *refs):
    blocks, offsets, width, feats, spread = cfg
    send_ref, sum_ref, slab_ref, inverse_ref = refs[:4]
    far_refs = refs[4 : 4 + len(spread)]
    branch_ref, unit_ref, table, sem = refs[4 + len(spread) :]
    fetch = pltpu.make_async_copy(send_ref, table, sem)
    fetch.start()
    own_rows = blocks * BLK
    sub = BLK // width
    group = SEND * BLK + PAD

    unit_ref[...] = sum_ref[:own_rows, :]
    dots = sum_ref[own_rows:, :]
    at_row = lax.broadcasted_iota(jnp.int32, (PAD, width), 0)
    fetch.wait()
    for ref, members in zip(far_refs, spread):
        for position, offset in enumerate(members):
            first = position * group
            extra = ref[first + SEND * BLK : first + group, :].astype(F32)
            for c in range(SEND):
                block = table[c, offset]
                rows = ref[first + c * BLK : first + (c + 1) * BLK, :].astype(F32)
                unit_ref[block_at(block), :] += rows
                for piece in range(sub):
                    line = extra[c * sub + piece : c * sub + piece + 1, :]
                    dots = dots + jnp.where(at_row == block * sub + piece, line, 0.0)
    for block in range(blocks):
        rows = slice(block * BLK, (block + 1) * BLK)
        line = jnp.concatenate(
            [dots[block * sub + piece : block * sub + piece + 1, :] for piece in range(sub)], axis=1
        )
        mean = jnp.broadcast_to(line * (1.0 / feats), (BLK, BLK)).T[:, :width]
        branch = inverse_ref[rows, :] * (unit_ref[rows, :] - slab_ref[rows, :] * mean)
        branch_ref[rows, :] = branch.astype(BF16)


def run_finish(feats, send, own_sum, slab, inverse, far, spread):
    rows, width = slab.shape
    vmem = pl.BlockSpec(memory_space=pltpu.VMEM)
    hbm = pl.BlockSpec(memory_space=pltpu.HBM)
    cfg = (rows // BLK, send.shape[1], width, feats, spread)
    return pl.pallas_call(
        functools.partial(finish_kernel, cfg),
        out_shape=jax.ShapeDtypeStruct((rows, width), BF16),
        in_specs=[hbm] + [vmem] * (3 + len(far)),
        out_specs=vmem,
        scratch_shapes=[
            pltpu.VMEM((rows, width), F32),
            pltpu.SMEM(send.shape, jnp.int32),
            pltpu.SemaphoreType.DMA(()),
        ],
        compiler_params=pltpu.CompilerParams(vmem_limit_bytes=SMALL),
        name="finish",
    )(*in_hbm(send), own_sum, slab, inverse, *far)


def grads_kernel(factor, all_ref, q_ref, k_ref, v_ref, o_ref):
    width = q_ref.shape[1]
    for position, ref in enumerate((q_ref, k_ref, v_ref)):
        for start in range(0, ref.shape[0], BLK):
            rows = all_ref[position * width : (position + 1) * width, start : start + BLK]
            ref[start : start + BLK, :] = rows.astype(F32).T * factor
    o_ref[...] = all_ref[3 * width :, :].astype(F32) * factor


def run_grads(gathered, factor):
    feats = gathered.shape[1]
    width = gathered.shape[0] // 4
    vmem = pl.BlockSpec(memory_space=pltpu.VMEM)
    tall = jax.ShapeDtypeStruct((feats, width), F32)
    return pl.pallas_call(
        functools.partial(grads_kernel, factor),
        out_shape=(tall, tall, tall, jax.ShapeDtypeStruct((width, feats), F32)),
        in_specs=[vmem],
        out_specs=[vmem] * 4,
        compiler_params=pltpu.CompilerParams(vmem_limit_bytes=SMALL),
        name="weight_grads",
    )(gathered)


def swap(array, axis, bit):
    return lax.ppermute(array, axis, [(i, i ^ bit) for i in range(lax.axis_size(axis))])


def shifted(array, axis, distance):
    size = lax.axis_size(axis)
    return lax.ppermute(array, axis, [(i, (i + distance) % size) for i in range(size)])


def added(left, right):
    return (left.astype(F32) + right.astype(F32)).astype(BF16)


def after(values, *earlier):
    held = lax.optimization_barrier((values, earlier))
    return held[0]


def narrow(keep, got, bit):
    while keep.shape[0] > 2:
        summed = added(keep, got)
        keep, send = summed[0::2], summed[1::2]
        got = swap(send, "tensor", bit)
        bit *= 2
    return keep, got, bit


def body(states, w_query, w_key, w_value, w_out, send_blocks, neighbor_blocks, cotangent):
    replicas, node_count, feats = states.shape
    width = w_query.shape[1]
    ranks = lax.axis_size("tensor")
    parts = lax.axis_size("dom")
    team = lax.axis_size("dp") * parts
    direct = (4 * width) % (team * PAD) == 0 and team <= 16
    offsets = offset_list(HOPS)
    order, share = piece_order(ranks, len(offsets))
    send = send_blocks[0].T
    weights = (w_query, w_key, w_value, w_out)
    flat_states = states.reshape(-1, feats)
    flat_cot = cotangent.reshape(-1, feats)

    leaving = pick_blocks(flat_states, send, ranks, share)
    route = []
    for p in range(parts):
        for r in range(ranks):
            distance = offsets[order[r * share] // SEND]
            route.append((p * ranks + r, ((p + distance) % parts) * ranks + r))
    levels = []
    bit = 1
    while bit < ranks:
        levels.append(bit)
        bit *= 2
    arrived = [lax.ppermute(block, ("dom", "tensor"), route) for block in leaving]
    own = run_own(flat_states, flat_cot, weights)
    arrived[0] = after(arrived[0], own[0])
    pieces = [None] * (ranks * share)
    for inner in range(share):
        if inner:
            arrived[inner] = after(arrived[inner], pieces[share + inner - 1])
        held = {0: arrived[inner]}
        for bit in reversed(levels):
            for slot in list(held):
                held[slot ^ bit] = swap(held[slot], "tensor", bit)
        for slot in range(ranks):
            pieces[slot * share + inner] = held[slot]
    unit, slab, inverse, cot = own[0], own[7], own[8], own[9]
    weights = own[10:]
    pool, both, dq, mixed = run_attend(
        ranks, share, len(offsets), neighbor_blocks, pieces, own[:7], weights[1], weights[2]
    )
    far_keep, far_send, own_keep, own_send = run_terms(
        len(offsets), unit, pool, both, dq, mixed, weights
    )
    far_got = swap(far_send, "tensor", 1)
    g_terms = run_grad_terms(unit, pool, both, dq, mixed, cot)
    own_got = swap(own_send, "tensor", 1)
    far_keep, far_got, bit = narrow(far_keep, far_got, 2)
    own_keep, own_got, bit = narrow(own_keep, own_got, 2)
    far_out = added(far_keep[1], far_got[1])
    far_last = swap(far_out, "tensor", bit)
    own_got = after(own_got, far_out)
    own_out = added(own_keep[1], own_got[1])
    own_last = swap(own_out, "tensor", bit)

    group = SEND * BLK + PAD
    spread = []
    for index, distance in enumerate(offsets):
        for members in spread:
            if (offsets[members[0]] - distance) % parts == 0 and members[-1] == index - 1:
                members.append(index)
                break
        else:
            spread.append([index])
    spread = tuple(tuple(members) for members in spread)
    bounds = tuple((members[0] * group, (members[-1] + 1) * group) for members in spread)

    total_rows = replicas * node_count * lax.axis_size("dp") * parts
    factor = 1.0 / math.sqrt(total_rows)
    if direct:
        g_terms = after(g_terms, own_out).reshape(team, -1, feats)
        spans = lax.all_to_all(g_terms, ("dp", "dom"), 0, 0)
        span = jnp.sum(spans.astype(F32), axis=0).astype(BF16)
    far_sums = run_returns(bounds, far_keep, far_got, far_last)
    far = [
        shifted(part, "dom", -offsets[members[0]]) for part, members in zip(far_sums, spread)
    ]
    update, own_sum = run_own_sum(replicas * node_count, own_keep, own_got, own_last)
    if direct:
        span = after(span, far_sums)
        copies = jnp.broadcast_to(span[None], (team,) + span.shape)
        gathered = lax.all_to_all(copies, ("dp", "dom"), 0, 0).reshape(-1, feats)
        grads = run_grads(gathered, factor)
    else:
        grads = run_grads(lax.psum(g_terms.astype(F32), ("dp", "dom")), factor)
    branch = run_finish(feats, send, own_sum, slab, inverse, far, spread)
    shape = (replicas, node_count, width)
    return (update.reshape(shape), branch.reshape(shape), *grads)


def solution(mesh):
    placed = (
        P("dp", "dom", None),
        P(None, "tensor"),
        P(None, "tensor"),
        P(None, "tensor"),
        P("tensor", None),
        P("dom", None, None),
        P("dom", None),
        P("dp", "dom", None),
    )
    return jax.shard_map(
        body,
        mesh=mesh,
        in_specs=placed,
        out_specs=(
            P("dp", "dom", "tensor"),
            P("dp", "dom", "tensor"),
            P(None, "tensor"),
            P(None, "tensor"),
            P(None, "tensor"),
            P("tensor", None),
        ),
        check_vma=False,
    )
```

```python
import functools
import math

import jax
import jax.numpy as jnp
from jax import lax
from jax.experimental import pallas as pl
from jax.experimental.pallas import tpu as pltpu
from jax.sharding import PartitionSpec as P

BLK = 128
HOPS = 2
SEND = 2
NEAR = 2
HD = 64
PAD = 16
EPS = 1e-05
LIMIT = 24 * 1024 * 1024
SMALL = 8 * 1024 * 1024
CHUNK = 64
F32 = jnp.float32
BF16 = jnp.bfloat16


def offset_list(hops):
    result = []
    for section in range(1, hops + 1):
        result.append(section)
        result.append(-section)
    return result


def piece_order(ranks, offsets):
    count = offsets * SEND
    share = count // ranks
    if share == SEND and offsets == 4:
        return [0, 1, 4, 5, 2, 3, 6, 7], share
    return list(range(count)), share


def nt(left, right):
    return lax.dot_general(left, right, (((1,), (1,)), ((), ())), preferred_element_type=F32)


def nn(left, right):
    return jnp.dot(left, right, preferred_element_type=F32)


def unit_of(rows):
    values = rows.astype(F32)
    return (values * lax.rsqrt(jnp.mean(values * values, axis=-1, keepdims=True) + EPS)).astype(BF16)


def block_at(index, size=BLK):
    return pl.ds(pl.multiple_of(index * size, size), size)


def rank_piece(rank, ranks, share, inner):
    if share == SEND and ranks == 4:
        return ((rank & 1) * 2 + (rank >> 1)) * SEND + inner
    return rank * share + inner


def in_hbm(*arrays):
    return [pltpu.with_memory_space_constraint(array, pltpu.HBM) for array in arrays]


def pick_kernel(ranks, share, send_ref, states_ref, *refs):
    outs, table, sems = refs[:share], refs[share], refs[share + 1]
    rank = lax.axis_index("tensor")
    fetch = pltpu.make_async_copy(send_ref, table, sems.at[share])
    fetch.start()
    fetch.wait()
    copies = []
    for inner, out_ref in enumerate(outs):
        piece = rank_piece(rank, ranks, share, inner)
        block = table[piece % SEND, piece // SEND]
        copies.append(
            pltpu.make_async_copy(states_ref.at[block_at(block), :], out_ref, sems.at[inner])
        )
        copies[-1].start()
    for copy in copies:
        copy.wait()


def pick_blocks(states, send, ranks, share):
    far = pl.BlockSpec(memory_space=pltpu.HBM)
    vmem = pl.BlockSpec(memory_space=pltpu.VMEM)
    return pl.pallas_call(
        functools.partial(pick_kernel, ranks, share),
        out_shape=[jax.ShapeDtypeStruct((BLK, states.shape[1]), BF16)] * share,
        in_specs=[far, far],
        out_specs=[vmem] * share,
        scratch_shapes=[
            pltpu.SMEM(send.shape, jnp.int32),
            pltpu.SemaphoreType.DMA((share + 1,)),
        ],
        compiler_params=pltpu.CompilerParams(vmem_limit_bytes=SMALL),
        name="pick_blocks",
    )(*in_hbm(send, states))


def by_head(rows, heads):
    if heads == 1:
        return rows.astype(BF16)
    lane_head = lax.broadcasted_iota(jnp.int32, rows.shape, 1) // HD
    return jnp.concatenate(
        [jnp.where(lane_head == head, rows, 0.0) for head in range(heads)], axis=0
    ).astype(BF16)


def diagonal(stacked, heads):
    return jnp.concatenate(
        [
            stacked[head * HD : (head + 1) * HD, head * BLK : (head + 1) * BLK]
            for head in range(heads)
        ],
        axis=0,
    )


def put_pairs(paired, at, width, k_ref, v_ref, kt_ref, vt_ref):
    for index, entry in enumerate(at):
        rows = paired[index * BLK : (index + 1) * BLK]
        keys, values = rows[:, :width], rows[:, width:]
        k_ref[block_at(entry), :] = keys.astype(BF16)
        v_ref[block_at(entry), :] = values.astype(BF16)
        kt_ref[entry] = keys.T.astype(BF16)
        vt_ref[entry] = values.T.astype(BF16)


def own_kernel(*refs):
    sources = refs[:6]
    unit_ref, q_ref, g_ref, k_ref, v_ref, kt_ref, vt_ref, slab_ref, inverse_ref = refs[6:15]
    held, states_ref, sems = refs[15:20], refs[20], refs[21]
    cot_ref, wq_ref, wk_ref, wv_ref, wo_ref = held
    copies = []
    for index, (source, target) in enumerate(zip(sources, (states_ref,) + tuple(held))):
        copies.append(pltpu.make_async_copy(source, target, sems.at[index]))
        copies[-1].start()
    rows, feats = states_ref.shape
    width = wq_ref.shape[1]
    heads = width // HD
    tall = heads * BLK
    rank = lax.axis_index("tensor")
    copies[0].wait()
    for start in range(0, rows, CHUNK):
        values = states_ref[start : start + CHUNK, :].astype(F32)
        inverse = lax.rsqrt(jnp.mean(values * values, axis=-1, keepdims=True) + EPS)
        normed = values * inverse
        unit_ref[start : start + CHUNK, :] = normed.astype(BF16)
        slab = normed[:, :width]
        for index in range(1, feats // width):
            slab = jnp.where(rank == index, normed[:, index * width : (index + 1) * width], slab)
        slab_ref[start : start + CHUNK, :] = slab
        inverse_ref[start : start + CHUNK, :] = jnp.broadcast_to(inverse, slab.shape)
    for copy in copies[1:]:
        copy.wait()
    unit = unit_ref[...]
    queries = nn(unit, wq_ref[...])
    grads = nt(cot_ref[...], wo_ref[...])
    for block in range(rows // BLK):
        q_ref[block * tall : (block + 1) * tall, :] = by_head(
            queries[block * BLK : (block + 1) * BLK], heads
        )
        g_ref[block * tall : (block + 1) * tall, :] = by_head(
            grads[block * BLK : (block + 1) * BLK], heads
        )
    paired = nn(unit, jnp.concatenate([wk_ref[...], wv_ref[...]], axis=1))
    put_pairs(paired, range(rows // BLK), width, k_ref, v_ref, kt_ref, vt_ref)


def run_own(states, cot, weights):
    rows, feats = states.shape
    width = weights[0].shape[1]
    blocks = rows // BLK
    tall = blocks * (width // HD) * BLK
    vmem = pl.BlockSpec(memory_space=pltpu.VMEM)
    far = pl.BlockSpec(memory_space=pltpu.HBM)
    shape = jax.ShapeDtypeStruct
    return pl.pallas_call(
        own_kernel,
        out_shape=(
            shape((rows, feats), BF16),
            shape((tall, width), BF16),
            shape((tall, width), BF16),
            shape((rows, width), BF16),
            shape((rows, width), BF16),
            shape((blocks, width, BLK), BF16),
            shape((blocks, width, BLK), BF16),
            shape((rows, width), F32),
            shape((rows, width), F32),
            shape(cot.shape, BF16),
            *[shape(w.shape, BF16) for w in weights],
        ),
        in_specs=[far] * 6,
        out_specs=[vmem] * 14,
        scratch_shapes=[pltpu.VMEM((rows, feats), BF16), pltpu.SemaphoreType.DMA((6,))],
        compiler_params=pltpu.CompilerParams(vmem_limit_bytes=LIMIT),
        cost_estimate=pl.CostEstimate(
            flops=8 * rows * feats * width, bytes_accessed=6 * rows * feats, transcendentals=0
        ),
        name="own_rows",
    )(*in_hbm(states, cot, *weights))


def attend_kernel(cfg, near_ref, *refs):
    ranks, share, blocks, offsets, width = cfg
    count = ranks * share
    piece_refs = refs[:count]
    own_refs = refs[count : count + 7]
    wk_ref, wv_ref = refs[count + 7 : count + 9]
    pool_ref, both_ref, dq_ref, mixed_ref, own_sum = refs[count + 9 : count + 14]
    back_refs = refs[count + 14 : count + 14 + NEAR]
    refs = refs[count + 14 + NEAR :]
    k_ref, v_ref, kt_ref, vt_ref, ka_ref, va_ref, dk_ref, dv_ref, near_table, near_sem = refs
    fetch = pltpu.make_async_copy(near_ref, near_table, near_sem)
    fetch.start()
    q_ref, g_ref, k_own, v_own, kt_own, vt_own = own_refs[1:]
    heads = width // HD
    tall = heads * BLK
    entries = blocks + offsets * SEND
    rank = lax.axis_index("tensor")

    own_rows = blocks * BLK
    k_ref[:own_rows, :] = k_own[...]
    v_ref[:own_rows, :] = v_own[...]
    kt_ref[:blocks] = kt_own[...]
    vt_ref[:blocks] = vt_own[...]
    wkv = jnp.concatenate([wk_ref[...], wv_ref[...]], axis=1)
    for slot in range(ranks):
        for inner in range(share):
            entry = rank_piece(rank ^ slot, ranks, share, inner)
            base = pl.multiple_of(entry * BLK, BLK)
            source = piece_refs[slot * share + inner]
            for start in range(0, BLK, CHUNK):
                rows = unit_of(source[start : start + CHUNK, :])
                pool_ref[pl.ds(pl.multiple_of(base + start, CHUNK), CHUNK), :] = rows
    for start in range(blocks, entries, blocks):
        first = (start - blocks) * BLK
        paired = nn(pool_ref[first : first + blocks * BLK, :], wkv)
        put_pairs(
            paired, range(start, start + blocks), width, k_ref, v_ref, kt_ref, vt_ref
        )

    shrink = 1.0 / math.sqrt(HD)
    near = near_ref.shape[1]
    fetch.wait()
    for block in range(blocks):
        listed = [block] + [near_table[block, n] for n in range(near)]
        keys = jnp.concatenate([k_ref[block_at(e), :] for e in listed], axis=0)
        values = jnp.concatenate([v_ref[block_at(e), :] for e in listed], axis=0)
        keys_t = jnp.concatenate([kt_ref[e] for e in listed], axis=1)
        values_t = jnp.concatenate([vt_ref[e] for e in listed], axis=1)
        q_all = q_ref[block * tall : (block + 1) * tall, :]
        g_all = g_ref[block * tall : (block + 1) * tall, :]
        scores = nt(keys, q_all) * shrink
        powers = jnp.exp(scores - jnp.max(scores, axis=0, keepdims=True))
        weights = powers * (1.0 / jnp.sum(powers, axis=0, keepdims=True))
        low = weights.astype(BF16)
        mix = diagonal(nn(values_t, low), heads)
        mixed_ref[block * BLK : (block + 1) * BLK, :] = mix.T.astype(BF16)
        prob = nt(values, g_all)
        drop = jnp.sum(weights * prob, axis=0, keepdims=True)
        score_low = (weights * (prob - drop) * shrink).astype(BF16)
        dq = diagonal(nn(keys_t, score_low), heads)
        dq_ref[block * BLK : (block + 1) * BLK, :] = dq.T.astype(BF16)
        dk = nn(score_low, q_all)
        dv = nn(low, g_all)
        ka_ref[block * BLK : (block + 1) * BLK, :] = dk[:BLK]
        va_ref[block * BLK : (block + 1) * BLK, :] = dv[:BLK]
        dk_ref[block] = dk[BLK:]
        dv_ref[block] = dv[BLK:]

    ka_ref[own_rows:, :] = jnp.zeros((entries * BLK - own_rows, width), F32)
    va_ref[own_rows:, :] = jnp.zeros((entries * BLK - own_rows, width), F32)
    for block in range(blocks):
        for n in range(near):
            entry = block_at(near_table[block, n])
            ka_ref[entry, :] += dk_ref[block, n * BLK : (n + 1) * BLK]
            va_ref[entry, :] += dv_ref[block, n * BLK : (n + 1) * BLK]

    both_ref[:, :width] = ka_ref[...].astype(BF16)
    both_ref[:, width:] = va_ref[...].astype(BF16)
    own_sum[:, :width] = ka_ref[:own_rows, :]
    own_sum[:, width:] = va_ref[:own_rows, :]
    for offset, back_ref in enumerate(back_refs):
        first = own_rows + offset * SEND * BLK
        back_ref[...] = both_ref[first : first + SEND * BLK, :]


def grad_terms_kernel(explicit, unit_ref, pool_ref, both_ref, dq_ref, mixed_ref, cot_ref, *refs):
    g_keep, g_send = refs
    rows, width = dq_ref.shape
    half = lax.axis_index("dp") if explicit else 0

    def turned(ref, first, last):
        parts = [
            ref[start : start + BLK, :].astype(F32).T.astype(BF16)
            for start in range(first, last, BLK)
        ]
        return jnp.concatenate(parts, axis=1)

    unit = unit_ref[...]
    grad_q = nn(turned(dq_ref, 0, rows), unit)
    grad_out = nn(turned(mixed_ref, 0, rows), cot_ref[...])
    grad_kv = nn(turned(both_ref, 0, rows), unit)
    grad_kv = grad_kv + nn(turned(both_ref, rows, both_ref.shape[0]), pool_ref[...])
    grad_k, grad_v = grad_kv[:width], grad_kv[width:]
    second = jnp.equal(half, 1)
    g_keep[:width, :] = jnp.where(second, grad_v, grad_q).astype(BF16)
    g_keep[width:, :] = jnp.where(second, grad_out, grad_k).astype(BF16)
    g_send[:width, :] = jnp.where(second, grad_q, grad_v).astype(BF16)
    g_send[width:, :] = jnp.where(second, grad_k, grad_out).astype(BF16)


def run_grad_terms(explicit, unit, pool, both, dq, mixed, cot):
    rows, feats = cot.shape
    width = dq.shape[1]
    vmem = pl.BlockSpec(memory_space=pltpu.VMEM)
    side = jax.ShapeDtypeStruct((2 * width, feats), BF16)
    return pl.pallas_call(
        functools.partial(grad_terms_kernel, explicit),
        out_shape=(side, side),
        in_specs=[vmem] * 6,
        out_specs=[vmem] * 2,
        compiler_params=pltpu.CompilerParams(vmem_limit_bytes=LIMIT),
        cost_estimate=pl.CostEstimate(
            flops=16 * rows * feats * width, bytes_accessed=8 * rows * feats, transcendentals=0
        ),
        name="grad_terms",
    )(unit, pool, both, dq, mixed, cot)


def run_attend(ranks, share, offsets, near, pieces, own, w_key, w_value):
    rows, feats = own[0].shape
    blocks = rows // BLK
    width = w_key.shape[1]
    received = offsets * SEND
    entries = blocks + received
    vmem = pl.BlockSpec(memory_space=pltpu.VMEM)
    far = pl.BlockSpec(memory_space=pltpu.HBM)
    cfg = (ranks, share, blocks, offsets, width)
    shape = jax.ShapeDtypeStruct
    return pl.pallas_call(
        functools.partial(attend_kernel, cfg),
        out_shape=(
            shape((received * BLK, feats), BF16),
            shape((entries * BLK, 2 * width), BF16),
            shape((rows, width), BF16),
            shape((rows, width), BF16),
            shape((rows, 2 * width), F32),
            *[shape((SEND * BLK, 2 * width), BF16)] * NEAR,
        ),
        in_specs=[far] + [vmem] * (len(pieces) + 9),
        out_specs=[vmem] * (5 + NEAR),
        scratch_shapes=[
            pltpu.VMEM((entries * BLK, width), BF16),
            pltpu.VMEM((entries * BLK, width), BF16),
            pltpu.VMEM((entries, width, BLK), BF16),
            pltpu.VMEM((entries, width, BLK), BF16),
            pltpu.VMEM((entries * BLK, width), F32),
            pltpu.VMEM((entries * BLK, width), F32),
            pltpu.VMEM((blocks, near.shape[1] * BLK, width), F32),
            pltpu.VMEM((blocks, near.shape[1] * BLK, width), F32),
            pltpu.SMEM(near.shape, jnp.int32),
            pltpu.SemaphoreType.DMA(()),
        ],
        compiler_params=pltpu.CompilerParams(vmem_limit_bytes=LIMIT),
        cost_estimate=pl.CostEstimate(
            flops=64 * rows * feats * width, bytes_accessed=12 * rows * feats, transcendentals=0
        ),
        name="attention",
    )(*in_hbm(near), *pieces, *own, w_key, w_value)


def put(odd, upper, keep_ref, send_ref, row, values):
    count, width = values.shape[0], keep_ref.shape[2]
    for pair in range(values.shape[1] // width // 2):
        left = values[:, 2 * pair * width : (2 * pair + 1) * width]
        right = values[:, (2 * pair + 1) * width : (2 * pair + 2) * width]
        at = upper ^ pair
        keep_ref[at, row : row + count, :] = jnp.where(odd, right, left).astype(BF16)
        send_ref[at, row : row + count, :] = jnp.where(odd, left, right).astype(BF16)


def put_dots(keep_ref, send_ref, row, dots):
    width = keep_ref.shape[2]
    parts = []
    for dot in dots:
        for piece in range(BLK // width):
            parts.append(dot[:1, piece * width : (piece + 1) * width])
    parts.append(jnp.zeros((PAD - len(parts), width), F32))
    rows = jnp.concatenate(parts, axis=0).astype(BF16)
    for pair in range(keep_ref.shape[0]):
        keep_ref[pair, row : row + PAD, :] = rows
        send_ref[pair, row : row + PAD, :] = rows


def row_dot(term, ref, first):
    ones = jnp.ones((16, ref.shape[1]), BF16)
    product = (term * ref[first : first + BLK, :].astype(F32)).astype(BF16)
    return nt(ones, product)


def far_terms_kernel(blocks, pool_ref, both_ref, wk_ref, wv_ref, *refs):
    count = len(refs) // 2
    keeps, sends = refs[:count], refs[count:]
    rank = lax.axis_index("tensor")
    odd, upper = (rank & 1) == 1, rank >> 1
    wkv = jnp.concatenate([wk_ref[...], wv_ref[...]], axis=1)
    for index in range(count):
        first = (NEAR + index) * SEND * BLK
        source = blocks * BLK + first
        term = nt(both_ref[source : source + SEND * BLK, :], wkv)
        put(odd, upper, keeps[index], sends[index], 0, term)
        dots = [
            row_dot(term[c * BLK : (c + 1) * BLK], pool_ref, first + c * BLK)
            for c in range(SEND)
        ]
        put_dots(keeps[index], sends[index], SEND * BLK, dots)


def run_far_terms(blocks, count, pool, both, w_key, w_value):
    feats, width = w_key.shape
    vmem = pl.BlockSpec(memory_space=pltpu.VMEM)
    far = jax.ShapeDtypeStruct((feats // width // 2, SEND * BLK + PAD, width), BF16)
    return pl.pallas_call(
        functools.partial(far_terms_kernel, blocks),
        out_shape=[far] * (2 * count),
        in_specs=[vmem] * 4,
        out_specs=[vmem] * (2 * count),
        compiler_params=pltpu.CompilerParams(vmem_limit_bytes=LIMIT),
        cost_estimate=pl.CostEstimate(
            flops=8 * count * SEND * BLK * feats * width, bytes_accessed=2000000, transcendentals=0
        ),
        name="far_terms",
    )(pool, both, w_key, w_value)


def own_terms_kernel(send_ref, sum_ref, *refs):
    back_refs = refs[:NEAR]
    unit_ref, dq_ref, mixed_ref, wq_ref, wk_ref, wv_ref, wo_ref = refs[NEAR : NEAR + 7]
    keep_ref, out_ref, total_ref, table, sem = refs[NEAR + 7 :]
    fetch = pltpu.make_async_copy(send_ref, table, sem)
    fetch.start()
    rank = lax.axis_index("tensor")
    odd, upper = (rank & 1) == 1, rank >> 1
    rows = unit_ref.shape[0]
    for first in range(0, rows, 2 * BLK):
        update = nn(mixed_ref[first : first + 2 * BLK, :], wo_ref[...])
        put(odd, upper, keep_ref, out_ref, rows + PAD + first, update)
    total_ref[...] = sum_ref[...]
    fetch.wait()
    for offset, back_ref in enumerate(back_refs):
        for c in range(SEND):
            at = block_at(table[c, offset])
            total_ref[at, :] += back_ref[c * BLK : (c + 1) * BLK, :].astype(F32)
    wkv = jnp.concatenate([wk_ref[...], wv_ref[...]], axis=1)
    dots = []
    for first in range(0, rows, 2 * BLK):
        last = first + 2 * BLK
        term = nt(total_ref[first:last, :].astype(BF16), wkv)
        term = term + nt(dq_ref[first:last, :], wq_ref[...])
        put(odd, upper, keep_ref, out_ref, first, term)
        dots += [
            row_dot(term[c * BLK : (c + 1) * BLK], unit_ref, first + c * BLK) for c in range(2)
        ]
    put_dots(keep_ref, out_ref, rows, dots)


def run_own_terms(send, own_sum, backs, unit, dq, mixed, weights):
    rows, feats = unit.shape
    width = dq.shape[1]
    vmem = pl.BlockSpec(memory_space=pltpu.VMEM)
    hbm = pl.BlockSpec(memory_space=pltpu.HBM)
    own = jax.ShapeDtypeStruct((feats // width // 2, 2 * rows + PAD, width), BF16)
    return pl.pallas_call(
        own_terms_kernel,
        out_shape=(own, own),
        in_specs=[hbm] + [vmem] * (8 + len(backs)),
        out_specs=[vmem] * 2,
        scratch_shapes=[
            pltpu.VMEM((rows, 2 * width), F32),
            pltpu.SMEM(send.shape, jnp.int32),
            pltpu.SemaphoreType.DMA(()),
        ],
        compiler_params=pltpu.CompilerParams(vmem_limit_bytes=LIMIT),
        cost_estimate=pl.CostEstimate(
            flops=8 * rows * feats * width, bytes_accessed=4000000, transcendentals=0
        ),
        name="own_terms",
    )(*in_hbm(send), own_sum, *backs, unit, dq, mixed, *weights)


def relay_kernel(*refs):
    count = len(refs) // 2
    out_ref = refs[-1]
    size = refs[0].shape[1]
    for index in range(count):
        total = refs[index][1].astype(F32) + refs[count + index][1].astype(F32)
        out_ref[index * size : (index + 1) * size, :] = total.astype(BF16)


def run_relay(keeps, gots):
    vmem = pl.BlockSpec(memory_space=pltpu.VMEM)
    _, size, width = keeps[0].shape
    return pl.pallas_call(
        relay_kernel,
        out_shape=jax.ShapeDtypeStruct((len(keeps) * size, width), BF16),
        in_specs=[vmem] * (2 * len(keeps)),
        out_specs=vmem,
        compiler_params=pltpu.CompilerParams(vmem_limit_bytes=SMALL),
        name="relayed_terms",
    )(*keeps, *gots)


def returns_kernel(count, bounds, *refs):
    keeps, gots = refs[:count], refs[count : 2 * count]
    last_ref, outs = refs[2 * count], refs[2 * count + 1 :]
    size = keeps[0].shape[1]
    for (first, last), out_ref in zip(bounds, outs):
        for index in range(first, last):
            total = keeps[index][0].astype(F32) + gots[index][0].astype(F32)
            total = total + last_ref[index * size : (index + 1) * size, :].astype(F32)
            out_ref[(index - first) * size : (index - first + 1) * size, :] = total.astype(BF16)


def run_returns(bounds, keeps, gots, last):
    vmem = pl.BlockSpec(memory_space=pltpu.VMEM)
    _, size, width = keeps[0].shape
    return pl.pallas_call(
        functools.partial(returns_kernel, len(keeps), bounds),
        out_shape=[jax.ShapeDtypeStruct(((b - a) * size, width), BF16) for a, b in bounds],
        in_specs=[vmem] * (2 * len(keeps) + 1),
        out_specs=[vmem] * len(bounds),
        compiler_params=pltpu.CompilerParams(vmem_limit_bytes=SMALL),
        name="returned_terms",
    )(*keeps, *gots, last)


def split_kernel(parts, keep_ref, got_ref, mine_ref, *outs):
    dom = lax.axis_index("dom")
    size = mine_ref.shape[0]
    for step in range(parts):
        at = block_at((dom + step) & (parts - 1), size)
        total = keep_ref[at, :].astype(F32) + got_ref[at, :].astype(F32)
        if step == 0:
            mine_ref[...] = total
        else:
            outs[step - 1][...] = total.astype(BF16)


def run_split(parts, keep, got):
    vmem = pl.BlockSpec(memory_space=pltpu.VMEM)
    size, feats = keep.shape[0] // parts, keep.shape[1]
    shape = jax.ShapeDtypeStruct
    return pl.pallas_call(
        functools.partial(split_kernel, parts),
        out_shape=[shape((size, feats), F32)] + [shape((size, feats), BF16)] * (parts - 1),
        in_specs=[vmem] * 2,
        out_specs=[vmem] * parts,
        compiler_params=pltpu.CompilerParams(vmem_limit_bytes=SMALL),
        name="split_grads",
    )(keep, got)


def own_sum_kernel(keep_ref, got_ref, last_ref, update_ref, unit_ref):
    rows = update_ref.shape[0]

    def total(first, last):
        both = keep_ref[0, first:last, :].astype(F32) + got_ref[0, first:last, :].astype(F32)
        return both + last_ref[first:last, :].astype(F32)

    unit_ref[...] = total(0, rows + PAD)
    update_ref[...] = total(rows + PAD, 2 * rows + PAD).astype(BF16)


def run_own_sum(rows, keep, got, last):
    width = last.shape[1]
    vmem = pl.BlockSpec(memory_space=pltpu.VMEM)
    shape = jax.ShapeDtypeStruct
    return pl.pallas_call(
        own_sum_kernel,
        out_shape=(shape((rows, width), BF16), shape((rows + PAD, width), F32)),
        in_specs=[vmem] * 3,
        out_specs=[vmem] * 2,
        compiler_params=pltpu.CompilerParams(vmem_limit_bytes=SMALL),
        name="own_sum",
    )(keep, got, last)


def finish_kernel(cfg, *refs):
    blocks, offsets, width, feats, spread = cfg
    send_ref, sum_ref, slab_ref, inverse_ref = refs[:4]
    far_refs = refs[4 : 4 + len(spread)]
    branch_ref, unit_ref, table, sem = refs[4 + len(spread) :]
    fetch = pltpu.make_async_copy(send_ref, table, sem)
    fetch.start()
    own_rows = blocks * BLK
    sub = BLK // width
    group = SEND * BLK + PAD

    unit_ref[...] = sum_ref[:own_rows, :]
    dots = sum_ref[own_rows:, :]
    at_row = lax.broadcasted_iota(jnp.int32, (PAD, width), 0)
    fetch.wait()
    for ref, members in zip(far_refs, spread):
        for position, offset in enumerate(members):
            first = position * group
            extra = ref[first + SEND * BLK : first + group, :].astype(F32)
            for c in range(SEND):
                block = table[c, offset]
                rows = ref[first + c * BLK : first + (c + 1) * BLK, :].astype(F32)
                unit_ref[block_at(block), :] += rows
                for piece in range(sub):
                    line = extra[c * sub + piece : c * sub + piece + 1, :]
                    dots = dots + jnp.where(at_row == block * sub + piece, line, 0.0)
    for block in range(blocks):
        rows = slice(block * BLK, (block + 1) * BLK)
        line = jnp.concatenate(
            [dots[block * sub + piece : block * sub + piece + 1, :] for piece in range(sub)], axis=1
        )
        mean = jnp.broadcast_to(line * (1.0 / feats), (BLK, BLK)).T[:, :width]
        branch = inverse_ref[rows, :] * (unit_ref[rows, :] - slab_ref[rows, :] * mean)
        branch_ref[rows, :] = branch.astype(BF16)


def run_finish(feats, send, own_sum, slab, inverse, far, spread):
    rows, width = slab.shape
    vmem = pl.BlockSpec(memory_space=pltpu.VMEM)
    hbm = pl.BlockSpec(memory_space=pltpu.HBM)
    cfg = (rows // BLK, send.shape[1], width, feats, spread)
    return pl.pallas_call(
        functools.partial(finish_kernel, cfg),
        out_shape=jax.ShapeDtypeStruct((rows, width), BF16),
        in_specs=[hbm] + [vmem] * (3 + len(far)),
        out_specs=vmem,
        scratch_shapes=[
            pltpu.VMEM((rows, width), F32),
            pltpu.SMEM(send.shape, jnp.int32),
            pltpu.SemaphoreType.DMA(()),
        ],
        compiler_params=pltpu.CompilerParams(vmem_limit_bytes=SMALL),
        name="finish",
    )(*in_hbm(send), own_sum, slab, inverse, *far)


def grads_kernel(cfg, *refs):
    parts, factor = cfg
    mine_refs = refs[:parts]
    other_refs = refs[parts : 2 * parts]
    q_ref, k_ref, v_ref, o_ref, all_ref = refs[2 * parts :]
    half = lax.axis_index("dp")
    dom = lax.axis_index("dom")
    size = mine_refs[0].shape[0]
    width = q_ref.shape[1]
    for group, side in ((mine_refs, half), (other_refs, 1 - half)):
        for step in range(parts):
            index = side * parts + ((dom + parts - step) & (parts - 1))
            all_ref[block_at(index, size), :] = group[step][...]
    for position, ref in enumerate((q_ref, k_ref, v_ref)):
        for start in range(0, ref.shape[0], BLK):
            rows = all_ref[position * width : (position + 1) * width, start : start + BLK]
            ref[start : start + BLK, :] = rows.astype(F32).T * factor
    o_ref[...] = all_ref[3 * width :, :].astype(F32) * factor


def run_grads(mine, other, factor):
    parts = len(mine)
    size, feats = mine[0].shape
    width = parts * size // 2
    vmem = pl.BlockSpec(memory_space=pltpu.VMEM)
    tall = jax.ShapeDtypeStruct((feats, width), F32)
    return pl.pallas_call(
        functools.partial(grads_kernel, (parts, factor)),
        out_shape=(tall, tall, tall, jax.ShapeDtypeStruct((width, feats), F32)),
        in_specs=[vmem] * (2 * parts),
        out_specs=[vmem] * 4,
        scratch_shapes=[pltpu.VMEM((4 * width, feats), BF16)],
        compiler_params=pltpu.CompilerParams(vmem_limit_bytes=SMALL),
        name="weight_grads",
    )(*mine, *other)


def swap(array, axis, bit):
    return lax.ppermute(array, axis, [(i, i ^ bit) for i in range(lax.axis_size(axis))])


def shifted(array, axis, distance):
    size = lax.axis_size(axis)
    return lax.ppermute(array, axis, [(i, (i + distance) % size) for i in range(size)])


def added(left, right):
    return (left.astype(F32) + right.astype(F32)).astype(BF16)


def after(values, *earlier):
    held = lax.optimization_barrier((values, earlier))
    return held[0]


def narrow(keep, got, bit):
    while keep.shape[0] > 2:
        summed = added(keep, got)
        keep, send = summed[0::2], summed[1::2]
        got = swap(send, "tensor", bit)
        bit *= 2
    return keep, got, bit


def body(states, w_query, w_key, w_value, w_out, send_blocks, neighbor_blocks, cotangent):
    replicas, node_count, feats = states.shape
    width = w_query.shape[1]
    ranks = lax.axis_size("tensor")
    parts = lax.axis_size("dom")
    explicit = parts == 4 and lax.axis_size("dp") == 2
    offsets = offset_list(HOPS)
    order, share = piece_order(ranks, len(offsets))
    send = send_blocks[0].T
    weights = (w_query, w_key, w_value, w_out)
    flat_states = states.reshape(-1, feats)
    flat_cot = cotangent.reshape(-1, feats)

    leaving = pick_blocks(flat_states, send, ranks, share)
    route = []
    for p in range(parts):
        for r in range(ranks):
            distance = offsets[order[r * share] // SEND]
            route.append((p * ranks + r, ((p + distance) % parts) * ranks + r))
    levels = []
    bit = 1
    while bit < ranks:
        levels.append(bit)
        bit *= 2
    arrived = [lax.ppermute(block, ("dom", "tensor"), route) for block in leaving]
    own = run_own(flat_states, flat_cot, weights)
    arrived[0] = after(arrived[0], own[0])
    pieces = [None] * (ranks * share)
    for inner in range(share):
        if inner:
            arrived[inner] = after(arrived[inner], pieces[share + inner - 1])
        held = {0: arrived[inner]}
        for bit in reversed(levels):
            for slot in list(held):
                held[slot ^ bit] = swap(held[slot], "tensor", bit)
        for slot in range(ranks):
            pieces[slot * share + inner] = held[slot]
    unit, slab, inverse, cot = own[0], own[7], own[8], own[9]
    weights = own[10:]
    pool, both, dq, mixed, own_part, *backs = run_attend(
        ranks, share, len(offsets), neighbor_blocks, pieces, own[:7], weights[1], weights[2]
    )
    backs = [shifted(back, "dom", -distance) for back, distance in zip(backs, offsets)]

    count = len(offsets) - NEAR
    terms = run_far_terms(node_count // BLK, count, pool, both, weights[1], weights[2])
    g_keep, g_send = run_grad_terms(
        explicit, unit, pool, both, after(dq, terms[0]), mixed, cot
    )
    g_got = swap(g_send, "dp", 1) if explicit else None
    far = [
        narrow(keep, swap(part, "tensor", 1), 2) for keep, part in zip(terms[:count], terms[count:])
    ]
    bit = far[0][2]
    keeps, gots = [item[0] for item in far], after([item[1] for item in far], g_send)
    far_last = swap(run_relay(keeps, gots), "tensor", bit)
    joined = (offsets[NEAR] - offsets[NEAR + 1]) % parts == 0
    bounds = ((0, 2),) if joined else ((0, 1), (1, 2))
    far_last = after(far_last, backs)
    far_sums = run_returns(bounds, keeps, gots, far_last)
    spread = tuple(tuple(range(NEAR + first, NEAR + last)) for first, last in bounds)
    returned = [
        shifted(part, "dom", -offsets[members[0]]) for part, members in zip(far_sums, spread)
    ]

    backs = after(backs, far_sums, g_got) if explicit else backs
    own_keep, own_out = run_own_terms(send, own_part, backs, unit, dq, mixed, weights)
    own_keep, own_got, bit = narrow(own_keep, swap(own_out, "tensor", 1), 2)
    own_out = added(own_keep[1], own_got[1])
    own_last = swap(own_out, "tensor", bit)

    total_rows = replicas * node_count * lax.axis_size("dp") * parts
    factor = 1.0 / math.sqrt(total_rows)
    if explicit:
        mine, *leaving = run_split(parts, g_keep, g_got)
        passed = [shifted(part, "dom", step + 1) for step, part in enumerate(leaving)]
        for part in after(passed, own_out):
            mine = mine + part.astype(F32)
        mine = mine.astype(BF16)
        chunks = [mine] + [shifted(mine, "dom", step) for step in range(1, parts)]
        others = [swap(chunk, "dp", 1) for chunk in chunks]
        grads = run_grads(chunks, others, factor)
    else:
        summed = lax.psum(
            jnp.concatenate([g_keep, g_send]).astype(F32), ("dp", "dom")
        ).reshape(4, width, feats)
        grads = (
            summed[0].T * factor,
            summed[1].T * factor,
            summed[2].T * factor,
            summed[3] * factor,
        )
    update, own_sum = run_own_sum(replicas * node_count, own_keep, own_got, own_last)
    branch = run_finish(feats, send, own_sum, slab, inverse, returned, spread)
    shape = (replicas, node_count, width)
    return (update.reshape(shape), branch.reshape(shape), *grads)


def solution(mesh):
    placed = (
        P("dp", "dom", None),
        P(None, "tensor"),
        P(None, "tensor"),
        P(None, "tensor"),
        P("tensor", None),
        P("dom", None, None),
        P("dom", None),
        P("dp", "dom", None),
    )
    return jax.shard_map(
        body,
        mesh=mesh,
        in_specs=placed,
        out_specs=(
            P("dp", "dom", "tensor"),
            P("dp", "dom", "tensor"),
            P(None, "tensor"),
            P(None, "tensor"),
            P(None, "tensor"),
            P("tensor", None),
        ),
        check_vma=False,
    )
```

```python
import functools
import math

import jax
import jax.numpy as jnp
from jax import lax
from jax.experimental import pallas as pl
from jax.experimental.pallas import tpu as pltpu
from jax.sharding import PartitionSpec as P

BLK = 128
HOPS = 2
SEND = 2
HD = 64
PAD = 16
EPS = 1e-05
LIMIT = 24 * 1024 * 1024
SMALL = 8 * 1024 * 1024
CHUNK = 64
BRIEF = pl.CostEstimate(flops=1, bytes_accessed=1, transcendentals=0)
F32 = jnp.float32
BF16 = jnp.bfloat16


def offset_list(hops):
    result = []
    for section in range(1, hops + 1):
        result.append(section)
        result.append(-section)
    return result


def piece_order(ranks, offsets):
    count = offsets * SEND
    share = count // ranks
    if share == SEND and offsets == 4:
        return [0, 1, 4, 5, 2, 3, 6, 7], share
    return list(range(count)), share


def nt(left, right):
    return lax.dot_general(left, right, (((1,), (1,)), ((), ())), preferred_element_type=F32)


def nn(left, right):
    return jnp.dot(left, right, preferred_element_type=F32)


def unit_of(rows):
    values = rows.astype(F32)
    return (values * lax.rsqrt(jnp.mean(values * values, axis=-1, keepdims=True) + EPS)).astype(BF16)


def block_at(index, size=BLK):
    return pl.ds(pl.multiple_of(index * size, size), size)


def rank_piece(rank, ranks, share, inner):
    if share == SEND and ranks == 4:
        return ((rank & 1) * 2 + (rank >> 1)) * SEND + inner
    return rank * share + inner


def in_hbm(*arrays):
    return [pltpu.with_memory_space_constraint(array, pltpu.HBM) for array in arrays]


def pick_kernel(ranks, share, send_ref, states_ref, *refs):
    outs, table, sems = refs[:share], refs[share], refs[share + 1]
    rank = lax.axis_index("tensor")
    fetch = pltpu.make_async_copy(send_ref, table, sems.at[share])
    fetch.start()
    fetch.wait()
    copies = []
    for inner, out_ref in enumerate(outs):
        piece = rank_piece(rank, ranks, share, inner)
        block = table[piece % SEND, piece // SEND]
        copies.append(
            pltpu.make_async_copy(states_ref.at[block_at(block), :], out_ref, sems.at[inner])
        )
        copies[-1].start()
    for copy in copies:
        copy.wait()


def pick_blocks(states, send, ranks, share):
    far = pl.BlockSpec(memory_space=pltpu.HBM)
    vmem = pl.BlockSpec(memory_space=pltpu.VMEM)
    return pl.pallas_call(
        functools.partial(pick_kernel, ranks, share),
        out_shape=[jax.ShapeDtypeStruct((BLK, states.shape[1]), BF16)] * share,
        in_specs=[far, far],
        out_specs=[vmem] * share,
        scratch_shapes=[
            pltpu.SMEM(send.shape, jnp.int32),
            pltpu.SemaphoreType.DMA((share + 1,)),
        ],
        compiler_params=pltpu.CompilerParams(vmem_limit_bytes=SMALL),
        cost_estimate=BRIEF,
        name="pick_blocks",
    )(*in_hbm(send, states))


def by_head(rows, heads):
    if heads == 1:
        return rows.astype(BF16)
    lane_head = lax.broadcasted_iota(jnp.int32, rows.shape, 1) // HD
    return jnp.concatenate(
        [jnp.where(lane_head == head, rows, 0.0) for head in range(heads)], axis=0
    ).astype(BF16)


def diagonal(stacked, heads):
    return jnp.concatenate(
        [
            stacked[head * HD : (head + 1) * HD, head * BLK : (head + 1) * BLK]
            for head in range(heads)
        ],
        axis=0,
    )


def put_pairs(paired, at, width, k_ref, v_ref, kt_ref, vt_ref):
    for index, entry in enumerate(at):
        rows = paired[index * BLK : (index + 1) * BLK]
        keys, values = rows[:, :width], rows[:, width:]
        k_ref[block_at(entry), :] = keys.astype(BF16)
        v_ref[block_at(entry), :] = values.astype(BF16)
        kt_ref[entry] = keys.T.astype(BF16)
        vt_ref[entry] = values.T.astype(BF16)


def own_kernel(*refs):
    sources = refs[:6]
    unit_ref, q_ref, g_ref, k_ref, v_ref, kt_ref, vt_ref, slab_ref, inverse_ref = refs[6:15]
    held, states_ref, sems = refs[15:20], refs[20], refs[21]
    cot_ref, wq_ref, wk_ref, wv_ref, wo_ref = held
    copies = []
    for index, (source, target) in enumerate(zip(sources, (states_ref,) + tuple(held))):
        copies.append(pltpu.make_async_copy(source, target, sems.at[index]))
        copies[-1].start()
    rows, feats = states_ref.shape
    width = wq_ref.shape[1]
    heads = width // HD
    tall = heads * BLK
    rank = lax.axis_index("tensor")
    copies[0].wait()
    for start in range(0, rows, CHUNK):
        values = states_ref[start : start + CHUNK, :].astype(F32)
        inverse = lax.rsqrt(jnp.mean(values * values, axis=-1, keepdims=True) + EPS)
        normed = values * inverse
        unit_ref[start : start + CHUNK, :] = normed.astype(BF16)
        slab = normed[:, :width]
        for index in range(1, feats // width):
            slab = jnp.where(rank == index, normed[:, index * width : (index + 1) * width], slab)
        slab_ref[start : start + CHUNK, :] = slab
        inverse_ref[start : start + CHUNK, :] = jnp.broadcast_to(inverse, slab.shape)
    for copy in copies[1:]:
        copy.wait()
    unit = unit_ref[...]
    queries = nn(unit, wq_ref[...])
    grads = nt(cot_ref[...], wo_ref[...])
    for block in range(rows // BLK):
        q_ref[block * tall : (block + 1) * tall, :] = by_head(
            queries[block * BLK : (block + 1) * BLK], heads
        )
        g_ref[block * tall : (block + 1) * tall, :] = by_head(
            grads[block * BLK : (block + 1) * BLK], heads
        )
    paired = nn(unit, jnp.concatenate([wk_ref[...], wv_ref[...]], axis=1))
    put_pairs(paired, range(rows // BLK), width, k_ref, v_ref, kt_ref, vt_ref)


def run_own(states, cot, weights):
    rows, feats = states.shape
    width = weights[0].shape[1]
    blocks = rows // BLK
    tall = blocks * (width // HD) * BLK
    vmem = pl.BlockSpec(memory_space=pltpu.VMEM)
    far = pl.BlockSpec(memory_space=pltpu.HBM)
    shape = jax.ShapeDtypeStruct
    return pl.pallas_call(
        own_kernel,
        out_shape=(
            shape((rows, feats), BF16),
            shape((tall, width), BF16),
            shape((tall, width), BF16),
            shape((rows, width), BF16),
            shape((rows, width), BF16),
            shape((blocks, width, BLK), BF16),
            shape((blocks, width, BLK), BF16),
            shape((rows, width), F32),
            shape((rows, width), F32),
            shape(cot.shape, BF16),
            *[shape(w.shape, BF16) for w in weights],
        ),
        in_specs=[far] * 6,
        out_specs=[vmem] * 14,
        scratch_shapes=[pltpu.VMEM((rows, feats), BF16), pltpu.SemaphoreType.DMA((6,))],
        compiler_params=pltpu.CompilerParams(vmem_limit_bytes=LIMIT),
        cost_estimate=BRIEF,
        name="own_rows",
    )(*in_hbm(states, cot, *weights))


def attend_kernel(cfg, near_ref, *refs):
    ranks, share, blocks, offsets, width = cfg
    count = ranks * share
    piece_refs = refs[:count]
    own_refs = refs[count : count + 7]
    wk_ref, wv_ref = refs[count + 7 : count + 9]
    pool_ref, both_ref, dq_ref, mixed_ref = refs[count + 9 : count + 13]
    refs = refs[count + 13 :]
    k_ref, v_ref, kt_ref, vt_ref, ka_ref, va_ref, dk_ref, dv_ref, near_table, near_sem = refs
    fetch = pltpu.make_async_copy(near_ref, near_table, near_sem)
    fetch.start()
    q_ref, g_ref, k_own, v_own, kt_own, vt_own = own_refs[1:]
    heads = width // HD
    tall = heads * BLK
    entries = blocks + offsets * SEND
    rank = lax.axis_index("tensor")

    own_rows = blocks * BLK
    k_ref[:own_rows, :] = k_own[...]
    v_ref[:own_rows, :] = v_own[...]
    kt_ref[:blocks] = kt_own[...]
    vt_ref[:blocks] = vt_own[...]
    wkv = jnp.concatenate([wk_ref[...], wv_ref[...]], axis=1)
    for slot in range(ranks):
        for inner in range(share):
            entry = rank_piece(rank ^ slot, ranks, share, inner)
            base = pl.multiple_of(entry * BLK, BLK)
            source = piece_refs[slot * share + inner]
            for start in range(0, BLK, CHUNK):
                rows = unit_of(source[start : start + CHUNK, :])
                pool_ref[pl.ds(pl.multiple_of(base + start, CHUNK), CHUNK), :] = rows
    for start in range(blocks, entries, blocks):
        first = (start - blocks) * BLK
        paired = nn(pool_ref[first : first + blocks * BLK, :], wkv)
        put_pairs(
            paired, range(start, start + blocks), width, k_ref, v_ref, kt_ref, vt_ref
        )

    shrink = 1.0 / math.sqrt(HD)
    near = near_ref.shape[1]
    fetch.wait()
    for block in range(blocks):
        listed = [block] + [near_table[block, n] for n in range(near)]
        keys = jnp.concatenate([k_ref[block_at(e), :] for e in listed], axis=0)
        values = jnp.concatenate([v_ref[block_at(e), :] for e in listed], axis=0)
        keys_t = jnp.concatenate([kt_ref[e] for e in listed], axis=1)
        values_t = jnp.concatenate([vt_ref[e] for e in listed], axis=1)
        q_all = q_ref[block * tall : (block + 1) * tall, :]
        g_all = g_ref[block * tall : (block + 1) * tall, :]
        scores = nt(keys, q_all) * shrink
        powers = jnp.exp(scores - jnp.max(scores, axis=0, keepdims=True))
        weights = powers * (1.0 / jnp.sum(powers, axis=0, keepdims=True))
        low = weights.astype(BF16)
        mix = diagonal(nn(values_t, low), heads)
        mixed_ref[block * BLK : (block + 1) * BLK, :] = mix.T.astype(BF16)
        prob = nt(values, g_all)
        drop = jnp.sum(weights * prob, axis=0, keepdims=True)
        score_low = (weights * (prob - drop) * shrink).astype(BF16)
        dq = diagonal(nn(keys_t, score_low), heads)
        dq_ref[block * BLK : (block + 1) * BLK, :] = dq.T.astype(BF16)
        dk = nn(score_low, q_all)
        dv = nn(low, g_all)
        ka_ref[block * BLK : (block + 1) * BLK, :] = dk[:BLK]
        va_ref[block * BLK : (block + 1) * BLK, :] = dv[:BLK]
        dk_ref[block] = dk[BLK:]
        dv_ref[block] = dv[BLK:]

    ka_ref[own_rows:, :] = jnp.zeros((entries * BLK - own_rows, width), F32)
    va_ref[own_rows:, :] = jnp.zeros((entries * BLK - own_rows, width), F32)
    for block in range(blocks):
        for n in range(near):
            entry = block_at(near_table[block, n])
            ka_ref[entry, :] += dk_ref[block, n * BLK : (n + 1) * BLK]
            va_ref[entry, :] += dv_ref[block, n * BLK : (n + 1) * BLK]

    both_ref[:, :width] = ka_ref[...].astype(BF16)
    both_ref[:, width:] = va_ref[...].astype(BF16)


def grad_terms_kernel(explicit, unit_ref, pool_ref, both_ref, dq_ref, mixed_ref, cot_ref, *refs):
    first_keep, first_send, second_keep, second_send = refs
    rows, width = dq_ref.shape

    def turned(ref, first, last):
        parts = [
            ref[start : start + BLK, :].astype(F32).T.astype(BF16)
            for start in range(first, last, BLK)
        ]
        return jnp.concatenate(parts, axis=1)

    unit = unit_ref[...]
    grad_q = nn(turned(dq_ref, 0, rows), unit)
    grad_out = nn(turned(mixed_ref, 0, rows), cot_ref[...])
    grad_kv = nn(turned(both_ref, 0, rows), unit)
    grad_kv = grad_kv + nn(turned(both_ref, rows, both_ref.shape[0]), pool_ref[...])
    grad_k, grad_v = grad_kv[:width], grad_kv[width:]
    by_dp = jnp.equal(lax.axis_index("dp") if explicit else 0, 1)
    by_dom = jnp.equal(lax.axis_index("dom") & 1 if explicit else 0, 1)
    first_keep[...] = jnp.where(by_dp, grad_k, grad_q).astype(BF16)
    first_send[...] = jnp.where(by_dp, grad_q, grad_k).astype(BF16)
    second_keep[...] = jnp.where(by_dom, grad_out, grad_v).astype(BF16)
    second_send[...] = jnp.where(by_dom, grad_v, grad_out).astype(BF16)


def run_grad_terms(explicit, unit, pool, both, dq, mixed, cot):
    rows, feats = cot.shape
    width = dq.shape[1]
    vmem = pl.BlockSpec(memory_space=pltpu.VMEM)
    return pl.pallas_call(
        functools.partial(grad_terms_kernel, explicit),
        out_shape=[jax.ShapeDtypeStruct((width, feats), BF16)] * 4,
        in_specs=[vmem] * 6,
        out_specs=[vmem] * 4,
        compiler_params=pltpu.CompilerParams(vmem_limit_bytes=LIMIT),
        cost_estimate=BRIEF,
        name="grad_terms",
    )(unit, pool, both, dq, mixed, cot)


def run_attend(ranks, share, offsets, near, pieces, own, w_key, w_value):
    rows, feats = own[0].shape
    blocks = rows // BLK
    width = w_key.shape[1]
    received = offsets * SEND
    entries = blocks + received
    vmem = pl.BlockSpec(memory_space=pltpu.VMEM)
    far = pl.BlockSpec(memory_space=pltpu.HBM)
    cfg = (ranks, share, blocks, offsets, width)
    shape = jax.ShapeDtypeStruct
    return pl.pallas_call(
        functools.partial(attend_kernel, cfg),
        out_shape=(
            shape((received * BLK, feats), BF16),
            shape((entries * BLK, 2 * width), BF16),
            shape((rows, width), BF16),
            shape((rows, width), BF16),
        ),
        in_specs=[far] + [vmem] * (len(pieces) + 9),
        out_specs=[vmem] * 4,
        scratch_shapes=[
            pltpu.VMEM((entries * BLK, width), BF16),
            pltpu.VMEM((entries * BLK, width), BF16),
            pltpu.VMEM((entries, width, BLK), BF16),
            pltpu.VMEM((entries, width, BLK), BF16),
            pltpu.VMEM((entries * BLK, width), F32),
            pltpu.VMEM((entries * BLK, width), F32),
            pltpu.VMEM((blocks, near.shape[1] * BLK, width), F32),
            pltpu.VMEM((blocks, near.shape[1] * BLK, width), F32),
            pltpu.SMEM(near.shape, jnp.int32),
            pltpu.SemaphoreType.DMA(()),
        ],
        compiler_params=pltpu.CompilerParams(vmem_limit_bytes=LIMIT),
        cost_estimate=BRIEF,
        name="attention",
    )(*in_hbm(near), *pieces, *own, w_key, w_value)


def put(odd, upper, keep_ref, send_ref, row, values):
    count, width = values.shape[0], keep_ref.shape[2]
    for pair in range(values.shape[1] // width // 2):
        left = values[:, 2 * pair * width : (2 * pair + 1) * width]
        right = values[:, (2 * pair + 1) * width : (2 * pair + 2) * width]
        at = upper ^ pair
        keep_ref[at, row : row + count, :] = jnp.where(odd, right, left).astype(BF16)
        send_ref[at, row : row + count, :] = jnp.where(odd, left, right).astype(BF16)


def put_dots(keep_ref, send_ref, row, dots):
    width = keep_ref.shape[2]
    parts = []
    for dot in dots:
        for piece in range(BLK // width):
            parts.append(dot[:1, piece * width : (piece + 1) * width])
    parts.append(jnp.zeros((PAD - len(parts), width), F32))
    rows = jnp.concatenate(parts, axis=0).astype(BF16)
    for pair in range(keep_ref.shape[0]):
        keep_ref[pair, row : row + PAD, :] = rows
        send_ref[pair, row : row + PAD, :] = rows


def row_dot(term, ref, first):
    ones = jnp.ones((16, ref.shape[1]), BF16)
    product = (term * ref[first : first + BLK, :].astype(F32)).astype(BF16)
    return nt(ones, product)


def far_terms_kernel(blocks, pool_ref, both_ref, wk_ref, wv_ref, *refs):
    count = len(refs) // 2
    keeps, sends = refs[:count], refs[count:]
    rank = lax.axis_index("tensor")
    odd, upper = (rank & 1) == 1, rank >> 1
    wkv = jnp.concatenate([wk_ref[...], wv_ref[...]], axis=1)
    for index in range(count):
        first = index * SEND * BLK
        source = blocks * BLK + first
        term = nt(both_ref[source : source + SEND * BLK, :], wkv)
        put(odd, upper, keeps[index], sends[index], 0, term)
        dots = [
            row_dot(term[c * BLK : (c + 1) * BLK], pool_ref, first + c * BLK)
            for c in range(SEND)
        ]
        put_dots(keeps[index], sends[index], SEND * BLK, dots)


def run_far_terms(blocks, count, pool, both, w_key, w_value):
    feats, width = w_key.shape
    vmem = pl.BlockSpec(memory_space=pltpu.VMEM)
    far = jax.ShapeDtypeStruct((feats // width // 2, SEND * BLK + PAD, width), BF16)
    return pl.pallas_call(
        functools.partial(far_terms_kernel, blocks),
        out_shape=[far] * (2 * count),
        in_specs=[vmem] * 4,
        out_specs=[vmem] * (2 * count),
        compiler_params=pltpu.CompilerParams(vmem_limit_bytes=LIMIT),
        cost_estimate=BRIEF,
        name="far_terms",
    )(pool, both, w_key, w_value)


def own_terms_kernel(both_ref, unit_ref, dq_ref, mixed_ref, *refs):
    wq_ref, wk_ref, wv_ref, wo_ref = refs[:4]
    count = len(refs[4:]) // 4
    unit_keeps, unit_sends, update_keeps, update_sends = [
        refs[4 + group * count : 4 + (group + 1) * count] for group in range(4)
    ]
    rank = lax.axis_index("tensor")
    odd, upper = (rank & 1) == 1, rank >> 1
    wkv = jnp.concatenate([wk_ref[...], wv_ref[...]], axis=1)
    for index in range(count):
        first, last = 2 * index * BLK, (2 * index + 2) * BLK
        update = nn(mixed_ref[first:last, :], wo_ref[...])
        put(odd, upper, update_keeps[index], update_sends[index], 0, update)
        term = nt(both_ref[first:last, :], wkv) + nt(dq_ref[first:last, :], wq_ref[...])
        put(odd, upper, unit_keeps[index], unit_sends[index], 0, term)
        dots = [
            row_dot(term[c * BLK : (c + 1) * BLK], unit_ref, first + c * BLK) for c in range(2)
        ]
        put_dots(unit_keeps[index], unit_sends[index], 2 * BLK, dots)


def run_own_terms(both, unit, dq, mixed, weights):
    rows, feats = unit.shape
    width = dq.shape[1]
    count, pairs = rows // BLK // 2, feats // width // 2
    vmem = pl.BlockSpec(memory_space=pltpu.VMEM)
    terms = [jax.ShapeDtypeStruct((pairs, 2 * BLK + PAD, width), BF16)] * (2 * count)
    updates = [jax.ShapeDtypeStruct((pairs, 2 * BLK, width), BF16)] * (2 * count)
    return pl.pallas_call(
        own_terms_kernel,
        out_shape=terms + updates,
        in_specs=[vmem] * 8,
        out_specs=[vmem] * (4 * count),
        compiler_params=pltpu.CompilerParams(vmem_limit_bytes=LIMIT),
        cost_estimate=BRIEF,
        name="own_terms",
    )(both, unit, dq, mixed, *weights)


def relay_kernel(*refs):
    count = len(refs) // 2
    out_ref = refs[-1]
    size = refs[0].shape[1]
    for index in range(count):
        total = refs[index][1].astype(F32) + refs[count + index][1].astype(F32)
        out_ref[index * size : (index + 1) * size, :] = total.astype(BF16)


def run_relay(keeps, gots):
    vmem = pl.BlockSpec(memory_space=pltpu.VMEM)
    _, size, width = keeps[0].shape
    return pl.pallas_call(
        relay_kernel,
        out_shape=jax.ShapeDtypeStruct((len(keeps) * size, width), BF16),
        in_specs=[vmem] * (2 * len(keeps)),
        out_specs=vmem,
        compiler_params=pltpu.CompilerParams(vmem_limit_bytes=SMALL),
        cost_estimate=BRIEF,
        name="relayed_terms",
    )(*keeps, *gots)


def returns_kernel(count, bounds, *refs):
    keeps, gots = refs[:count], refs[count : 2 * count]
    last_ref, outs = refs[2 * count], refs[2 * count + 1 :]
    size = keeps[0].shape[1]
    for (first, last), out_ref in zip(bounds, outs):
        for index in range(first, last):
            total = keeps[index][0].astype(F32) + gots[index][0].astype(F32)
            total = total + last_ref[index * size : (index + 1) * size, :].astype(F32)
            out_ref[(index - first) * size : (index - first + 1) * size, :] = total.astype(BF16)


def run_returns(bounds, keeps, gots, last):
    vmem = pl.BlockSpec(memory_space=pltpu.VMEM)
    _, size, width = keeps[0].shape
    return pl.pallas_call(
        functools.partial(returns_kernel, len(keeps), bounds),
        out_shape=[jax.ShapeDtypeStruct(((b - a) * size, width), BF16) for a, b in bounds],
        in_specs=[vmem] * (2 * len(keeps) + 1),
        out_specs=[vmem] * len(bounds),
        compiler_params=pltpu.CompilerParams(vmem_limit_bytes=SMALL),
        cost_estimate=BRIEF,
        name="returned_terms",
    )(*keeps, *gots, last)


def my_bits():
    dom = lax.axis_index("dom")
    return lax.axis_index("dp"), dom & 1, dom >> 1


def halve_kernel(bits, *refs):
    count = len(bits)
    ins, outs = refs[: 2 * count], refs[2 * count :]
    mine = my_bits()
    size = ins[0].shape[0] // 2
    joint = len(outs) == 2
    for index, bit in enumerate(bits):
        keep_ref, got_ref = ins[2 * index : 2 * index + 2]
        for side, name in enumerate((mine[bit], 1 - mine[bit])):
            at = block_at(name, size)
            total = (keep_ref[at, :].astype(F32) + got_ref[at, :].astype(F32)).astype(BF16)
            if joint:
                outs[side][index * size : (index + 1) * size, :] = total
            else:
                outs[2 * index + side][...] = total


def run_halve(bits, joint, *arrays):
    vmem = pl.BlockSpec(memory_space=pltpu.VMEM)
    rows, feats = arrays[0].shape
    count = len(bits)
    if joint:
        outs = [jax.ShapeDtypeStruct((count * rows // 2, feats), BF16)] * 2
    else:
        outs = [jax.ShapeDtypeStruct((rows // 2, feats), BF16)] * (2 * count)
    return pl.pallas_call(
        functools.partial(halve_kernel, bits),
        out_shape=outs,
        in_specs=[vmem] * len(arrays),
        out_specs=[vmem] * len(outs),
        compiler_params=pltpu.CompilerParams(vmem_limit_bytes=SMALL),
        cost_estimate=BRIEF,
        name="halve_grads",
    )(*arrays)


def join_kernel(bits, *refs):
    count = len(bits)
    outs = refs[-count:]
    mine = my_bits()
    size = outs[0].shape[0] // 2
    for index, bit in enumerate(bits):
        if len(refs) - count == 2:
            first = index * size
            held, got = refs[0][first : first + size, :], refs[1][first : first + size, :]
        else:
            held, got = refs[2 * index][...], refs[2 * index + 1][...]
        outs[index][block_at(mine[bit], size), :] = held
        outs[index][block_at(1 - mine[bit], size), :] = got


def run_join(bits, *arrays):
    vmem = pl.BlockSpec(memory_space=pltpu.VMEM)
    count = len(bits)
    rows, feats = arrays[0].shape
    rows = rows * len(arrays) // count
    return pl.pallas_call(
        functools.partial(join_kernel, bits),
        out_shape=[jax.ShapeDtypeStruct((rows, feats), BF16)] * count,
        in_specs=[vmem] * len(arrays),
        out_specs=[vmem] * count,
        compiler_params=pltpu.CompilerParams(vmem_limit_bytes=SMALL),
        cost_estimate=BRIEF,
        name="join_grads",
    )(*arrays)


def own_sum_kernel(*refs):
    count = (len(refs) - 4) // 4
    keeps, gots = refs[:count], refs[count : 2 * count]
    more_keeps, more_gots = refs[2 * count : 3 * count], refs[3 * count : 4 * count]
    last_ref, more_ref, update_ref, unit_ref = refs[4 * count :]
    width = update_ref.shape[1]
    size = keeps[0].shape[1]
    dots = []
    for index in range(count):
        rows = slice(2 * index * BLK, 2 * (index + 1) * BLK)
        total = keeps[index][0].astype(F32) + gots[index][0].astype(F32)
        total = total + last_ref[index * size : (index + 1) * size, :].astype(F32)
        unit_ref[rows, :] = total[: 2 * BLK]
        dots.append(total[2 * BLK : 2 * BLK + 2 * (BLK // width)])
        total = more_keeps[index][0].astype(F32) + more_gots[index][0].astype(F32)
        update_ref[rows, :] = (total + more_ref[rows, :].astype(F32)).astype(BF16)
    lines = sum(dot.shape[0] for dot in dots)
    dots.append(jnp.zeros((PAD - lines, width), F32))
    unit_ref[2 * count * BLK :, :] = jnp.concatenate(dots, axis=0)


def run_own_sum(rows, *arrays):
    width = arrays[-1].shape[1]
    vmem = pl.BlockSpec(memory_space=pltpu.VMEM)
    shape = jax.ShapeDtypeStruct
    return pl.pallas_call(
        own_sum_kernel,
        out_shape=(shape((rows, width), BF16), shape((rows + PAD, width), F32)),
        in_specs=[vmem] * len(arrays),
        out_specs=[vmem] * 2,
        compiler_params=pltpu.CompilerParams(vmem_limit_bytes=SMALL),
        cost_estimate=BRIEF,
        name="own_sum",
    )(*arrays)


def finish_kernel(cfg, *refs):
    blocks, offsets, width, feats, spread = cfg
    send_ref, sum_ref, slab_ref, inverse_ref = refs[:4]
    far_refs = refs[4 : 4 + len(spread)]
    branch_ref, unit_ref, table, sem = refs[4 + len(spread) :]
    fetch = pltpu.make_async_copy(send_ref, table, sem)
    fetch.start()
    own_rows = blocks * BLK
    sub = BLK // width
    group = SEND * BLK + PAD

    unit_ref[...] = sum_ref[:own_rows, :]
    dots = sum_ref[own_rows:, :]
    at_row = lax.broadcasted_iota(jnp.int32, (PAD, width), 0)
    fetch.wait()
    for ref, members in zip(far_refs, spread):
        for position, offset in enumerate(members):
            first = position * group
            extra = ref[first + SEND * BLK : first + group, :].astype(F32)
            for c in range(SEND):
                block = table[c, offset]
                rows = ref[first + c * BLK : first + (c + 1) * BLK, :].astype(F32)
                unit_ref[block_at(block), :] += rows
                for piece in range(sub):
                    line = extra[c * sub + piece : c * sub + piece + 1, :]
                    dots = dots + jnp.where(at_row == block * sub + piece, line, 0.0)
    for block in range(blocks):
        rows = slice(block * BLK, (block + 1) * BLK)
        line = jnp.concatenate(
            [dots[block * sub + piece : block * sub + piece + 1, :] for piece in range(sub)], axis=1
        )
        mean = jnp.broadcast_to(line * (1.0 / feats), (BLK, BLK)).T[:, :width]
        branch = inverse_ref[rows, :] * (unit_ref[rows, :] - slab_ref[rows, :] * mean)
        branch_ref[rows, :] = branch.astype(BF16)


def run_finish(feats, send, own_sum, slab, inverse, far, spread):
    rows, width = slab.shape
    vmem = pl.BlockSpec(memory_space=pltpu.VMEM)
    hbm = pl.BlockSpec(memory_space=pltpu.HBM)
    cfg = (rows // BLK, send.shape[1], width, feats, spread)
    return pl.pallas_call(
        functools.partial(finish_kernel, cfg),
        out_shape=jax.ShapeDtypeStruct((rows, width), BF16),
        in_specs=[hbm] + [vmem] * (3 + len(far)),
        out_specs=vmem,
        scratch_shapes=[
            pltpu.VMEM((rows, width), F32),
            pltpu.SMEM(send.shape, jnp.int32),
            pltpu.SemaphoreType.DMA(()),
        ],
        compiler_params=pltpu.CompilerParams(vmem_limit_bytes=SMALL),
        cost_estimate=BRIEF,
        name="finish",
    )(*in_hbm(send), own_sum, slab, inverse, *far)


def grads_kernel(factor, *refs):
    first_held, first_got, second_held, second_got, q_ref, k_ref, v_ref, o_ref = refs
    dp, low, _ = my_bits()
    first, second = jnp.equal(dp, 1), jnp.equal(low, 1)

    def picked(flag, left, right, start):
        columns = slice(start, start + BLK)
        return jnp.where(flag, left[:, columns].astype(F32), right[:, columns].astype(F32)) * factor

    for start in range(0, q_ref.shape[0], BLK):
        rows = slice(start, start + BLK)
        q_ref[rows, :] = picked(first, first_got, first_held, start).T
        k_ref[rows, :] = picked(first, first_held, first_got, start).T
        v_ref[rows, :] = picked(second, second_got, second_held, start).T
        o_ref[:, rows] = picked(second, second_held, second_got, start)


def run_grads(factor, *arrays):
    width, feats = arrays[0].shape
    vmem = pl.BlockSpec(memory_space=pltpu.VMEM)
    tall = jax.ShapeDtypeStruct((feats, width), F32)
    return pl.pallas_call(
        functools.partial(grads_kernel, factor),
        out_shape=(tall, tall, tall, jax.ShapeDtypeStruct((width, feats), F32)),
        in_specs=[vmem] * 4,
        out_specs=[vmem] * 4,
        compiler_params=pltpu.CompilerParams(vmem_limit_bytes=SMALL),
        cost_estimate=BRIEF,
        name="weight_grads",
    )(*arrays)


def swap(array, axis, bit):
    return lax.ppermute(array, axis, [(i, i ^ bit) for i in range(lax.axis_size(axis))])


def shifted(array, axis, distance):
    size = lax.axis_size(axis)
    return lax.ppermute(array, axis, [(i, (i + distance) % size) for i in range(size)])


def added(left, right):
    return (left.astype(F32) + right.astype(F32)).astype(BF16)


def after(values, *earlier):
    held = lax.optimization_barrier((values, earlier))
    return held[0]


def narrow(keep, got, bit):
    while keep.shape[0] > 2:
        summed = added(keep, got)
        keep, send = summed[0::2], summed[1::2]
        got = swap(send, "tensor", bit)
        bit *= 2
    return keep, got, bit


def body(states, w_query, w_key, w_value, w_out, send_blocks, neighbor_blocks, cotangent):
    replicas, node_count, feats = states.shape
    width = w_query.shape[1]
    ranks = lax.axis_size("tensor")
    parts = lax.axis_size("dom")
    explicit = parts == 4 and lax.axis_size("dp") == 2
    offsets = offset_list(HOPS)
    order, share = piece_order(ranks, len(offsets))
    send = send_blocks[0].T
    weights = (w_query, w_key, w_value, w_out)
    flat_states = states.reshape(-1, feats)
    flat_cot = cotangent.reshape(-1, feats)

    leaving = pick_blocks(flat_states, send, ranks, share)
    route = []
    for p in range(parts):
        for r in range(ranks):
            distance = offsets[order[r * share] // SEND]
            route.append((p * ranks + r, ((p + distance) % parts) * ranks + r))
    levels = []
    bit = 1
    while bit < ranks:
        levels.append(bit)
        bit *= 2
    arrived = [lax.ppermute(block, ("dom", "tensor"), route) for block in leaving]
    own = run_own(flat_states, flat_cot, weights)
    arrived[0] = after(arrived[0], own[0])
    pieces = [None] * (ranks * share)
    for inner in range(share):
        if inner:
            arrived[inner] = after(arrived[inner], pieces[share + inner - 1])
        held = {0: arrived[inner]}
        for bit in reversed(levels):
            for slot in list(held):
                held[slot ^ bit] = swap(held[slot], "tensor", bit)
        for slot in range(ranks):
            pieces[slot * share + inner] = held[slot]
    unit, slab, inverse, cot = own[0], own[7], own[8], own[9]
    weights = own[10:]
    pool, both, dq, mixed = run_attend(
        ranks, share, len(offsets), neighbor_blocks, pieces, own[:7], weights[1], weights[2]
    )
    total_rows = replicas * node_count * lax.axis_size("dp") * parts
    factor = 1.0 / math.sqrt(total_rows)

    count = len(offsets)
    terms = run_far_terms(node_count // BLK, count, pool, both, weights[1], weights[2])
    halves = run_grad_terms(explicit, unit, pool, both, after(dq, terms[0]), mixed, cot)
    if explicit:
        first, second = swap(halves[1], "dp", 1), swap(halves[3], "dom", 1)
    far = [
        narrow(keep, swap(part, "tensor", 1), 2) for keep, part in zip(terms[:count], terms[count:])
    ]
    bit = far[0][2]

    sums = {}

    def relay(start, *earlier):
        keeps = [far[start][0], far[start + 1][0]]
        gots = after([far[start][1], far[start + 1][1]], *earlier)
        held = run_relay(keeps, gots)
        return keeps, gots, held, swap(held, "tensor", bit)

    def give_back(start, keeps, gots, last):
        joined = (offsets[start] - offsets[start + 1]) % parts == 0
        bounds = ((0, 2),) if joined else ((0, 1), (1, 2))
        out = run_returns(bounds, keeps, gots, last)
        for (low, high), part in zip(bounds, out):
            members = tuple(range(start + low, start + high))
            sums[members] = shifted(part, "dom", -offsets[members[0]])
        return out

    far_keeps, far_gots, held, far_last = relay(2, halves[0])
    near_keeps, near_gots, held, near_last = relay(0, held)
    if explicit:
        first = after(first, held)
        halves = run_halve((1, 0), False, halves[0], first, halves[2], second)
        first, second = swap(halves[1], "dom", 1), swap(halves[3], "dp", 1)
        far_last = after(far_last, halves[0])
    far_out = give_back(2, far_keeps, far_gots, far_last)
    if explicit:
        first = after(first, far_out)
        keep, leave = run_halve((2, 2), True, halves[0], first, halves[2], second)
        got = swap(leave, "dom", 2)
        near_last = after(near_last, keep)
        dq = after(dq, keep)
    own_out = run_own_terms(both, unit, dq, mixed, weights)
    size = len(own_out) // 4
    own = []
    for start in (0, 2 * size):
        pairs = zip(own_out[start : start + size], own_out[start + size : start + 2 * size])
        pairs = [narrow(keep, swap(part, "tensor", 1), 2) for keep, part in pairs]
        own.append([[item[0] for item in pairs], [item[1] for item in pairs]])
    near_out = give_back(0, near_keeps, near_gots, near_last)
    own_held = [run_relay(keeps, after(gots, near_out)) for keeps, gots in own]
    own_last = [swap(held, "tensor", bit) for held in own_held]
    if explicit:
        total = added(keep, after(got, own_held))
        got = swap(total, "dom", 2)
        got = after(got, [part for members, part in sums.items() if members[0] >= 2])
        held = run_join((2, 2), total, got)
        first, second = swap(held[0], "dom", 1), swap(held[1], "dp", 1)
        own_last = after(own_last, held)
    parts_of = [array for keeps, gots in own for array in keeps + gots]
    update, own_sum = run_own_sum(replicas * node_count, *parts_of, *own_last)
    if explicit:
        first = after(first, own_sum, list(sums.values()))
        held = run_join((1, 0), held[0], first, held[1], second)
        first, second = swap(held[0], "dp", 1), swap(held[1], "dom", 1)
    branch = run_finish(feats, send, own_sum, slab, inverse, list(sums.values()), tuple(sums))
    if explicit:
        first = after(first, branch)
        grads = run_grads(factor, held[0], first, held[1], second)
    else:
        summed = [lax.psum(half.astype(F32), ("dp", "dom")) * factor for half in halves]
        grads = (summed[0].T, summed[1].T, summed[2].T, summed[3])
    shape = (replicas, node_count, width)
    return (update.reshape(shape), branch.reshape(shape), *grads)


def solution(mesh):
    placed = (
        P("dp", "dom", None),
        P(None, "tensor"),
        P(None, "tensor"),
        P(None, "tensor"),
        P("tensor", None),
        P("dom", None, None),
        P("dom", None),
        P("dp", "dom", None),
    )
    return jax.shard_map(
        body,
        mesh=mesh,
        in_specs=placed,
        out_specs=(
            P("dp", "dom", "tensor"),
            P("dp", "dom", "tensor"),
            P(None, "tensor"),
            P(None, "tensor"),
            P(None, "tensor"),
            P("tensor", None),
        ),
        check_vma=False,
    )
```

```python
import functools
import math

import jax
import jax.numpy as jnp
from jax import lax
from jax.experimental import pallas as pl
from jax.experimental.pallas import tpu as pltpu
from jax.sharding import PartitionSpec as P

BLK = 128
HOPS = 2
SEND = 2
HD = 64
PAD = 16
EPS = 1e-05
LIMIT = 24 * 1024 * 1024
SMALL = 8 * 1024 * 1024
CHUNK = 64
BRIEF = pl.CostEstimate(flops=1, bytes_accessed=1, transcendentals=0)
F32 = jnp.float32
BF16 = jnp.bfloat16


def offset_list(hops):
    result = []
    for section in range(1, hops + 1):
        result.append(section)
        result.append(-section)
    return result


def piece_order(ranks, offsets):
    count = offsets * SEND
    share = count // ranks
    if share == SEND and offsets == 4:
        return [0, 1, 4, 5, 2, 3, 6, 7], share
    return list(range(count)), share


def nt(left, right):
    return lax.dot_general(left, right, (((1,), (1,)), ((), ())), preferred_element_type=F32)


def nn(left, right):
    return jnp.dot(left, right, preferred_element_type=F32)


def unit_of(rows):
    values = rows.astype(F32)
    return (values * lax.rsqrt(jnp.mean(values * values, axis=-1, keepdims=True) + EPS)).astype(BF16)


def block_at(index, size=BLK):
    return pl.ds(pl.multiple_of(index * size, size), size)


def rank_piece(rank, ranks, share, inner):
    if share == SEND and ranks == 4:
        return ((rank & 1) * 2 + (rank >> 1)) * SEND + inner
    return rank * share + inner


def in_hbm(*arrays):
    return [pltpu.with_memory_space_constraint(array, pltpu.HBM) for array in arrays]


def pick_kernel(ranks, share, send_ref, states_ref, *refs):
    outs, table, sems = refs[:share], refs[share], refs[share + 1]
    rank = lax.axis_index("tensor")
    fetch = pltpu.make_async_copy(send_ref, table, sems.at[share])
    fetch.start()
    fetch.wait()
    copies = []
    for inner, out_ref in enumerate(outs):
        piece = rank_piece(rank, ranks, share, inner)
        block = table[piece % SEND, piece // SEND]
        copies.append(
            pltpu.make_async_copy(states_ref.at[block_at(block), :], out_ref, sems.at[inner])
        )
        copies[-1].start()
    for copy in copies:
        copy.wait()


def pick_blocks(states, send, ranks, share):
    far = pl.BlockSpec(memory_space=pltpu.HBM)
    vmem = pl.BlockSpec(memory_space=pltpu.VMEM)
    return pl.pallas_call(
        functools.partial(pick_kernel, ranks, share),
        out_shape=[jax.ShapeDtypeStruct((BLK, states.shape[1]), BF16)] * share,
        in_specs=[far, far],
        out_specs=[vmem] * share,
        scratch_shapes=[
            pltpu.SMEM(send.shape, jnp.int32),
            pltpu.SemaphoreType.DMA((share + 1,)),
        ],
        compiler_params=pltpu.CompilerParams(vmem_limit_bytes=SMALL),
        cost_estimate=BRIEF,
        name="pick_blocks",
    )(*in_hbm(send, states))


def by_head(rows, heads):
    if heads == 1:
        return rows.astype(BF16)
    lane_head = lax.broadcasted_iota(jnp.int32, rows.shape, 1) // HD
    return jnp.concatenate(
        [jnp.where(lane_head == head, rows, 0.0) for head in range(heads)], axis=0
    ).astype(BF16)


def diagonal(stacked, heads):
    return jnp.concatenate(
        [
            stacked[head * HD : (head + 1) * HD, head * BLK : (head + 1) * BLK]
            for head in range(heads)
        ],
        axis=0,
    )


def put_pairs(paired, at, width, k_ref, v_ref, kt_ref, vt_ref):
    for index, entry in enumerate(at):
        rows = paired[index * BLK : (index + 1) * BLK]
        keys, values = rows[:, :width], rows[:, width:]
        k_ref[block_at(entry), :] = keys.astype(BF16)
        v_ref[block_at(entry), :] = values.astype(BF16)
        kt_ref[entry] = keys.T.astype(BF16)
        vt_ref[entry] = values.T.astype(BF16)


def own_kernel(*refs):
    sources = refs[:6]
    unit_ref, q_ref, g_ref, k_ref, v_ref, kt_ref, vt_ref, slab_ref, inverse_ref = refs[6:15]
    held, states_ref, sems = refs[15:20], refs[20], refs[21]
    cot_ref, wq_ref, wk_ref, wv_ref, wo_ref = held
    copies = []
    for index, (source, target) in enumerate(zip(sources, (states_ref,) + tuple(held))):
        copies.append(pltpu.make_async_copy(source, target, sems.at[index]))
        copies[-1].start()
    rows, feats = states_ref.shape
    width = wq_ref.shape[1]
    heads = width // HD
    tall = heads * BLK
    rank = lax.axis_index("tensor")
    copies[0].wait()
    for start in range(0, rows, CHUNK):
        values = states_ref[start : start + CHUNK, :].astype(F32)
        inverse = lax.rsqrt(jnp.mean(values * values, axis=-1, keepdims=True) + EPS)
        normed = values * inverse
        unit_ref[start : start + CHUNK, :] = normed.astype(BF16)
        slab = normed[:, :width]
        for index in range(1, feats // width):
            slab = jnp.where(rank == index, normed[:, index * width : (index + 1) * width], slab)
        slab_ref[start : start + CHUNK, :] = slab
        inverse_ref[start : start + CHUNK, :] = jnp.broadcast_to(inverse, slab.shape)
    for copy in copies[1:]:
        copy.wait()
    unit = unit_ref[...]
    queries = nn(unit, wq_ref[...])
    grads = nt(cot_ref[...], wo_ref[...])
    for block in range(rows // BLK):
        q_ref[block * tall : (block + 1) * tall, :] = by_head(
            queries[block * BLK : (block + 1) * BLK], heads
        )
        g_ref[block * tall : (block + 1) * tall, :] = by_head(
            grads[block * BLK : (block + 1) * BLK], heads
        )
    paired = nn(unit, jnp.concatenate([wk_ref[...], wv_ref[...]], axis=1))
    put_pairs(paired, range(rows // BLK), width, k_ref, v_ref, kt_ref, vt_ref)


def run_own(states, cot, weights):
    rows, feats = states.shape
    width = weights[0].shape[1]
    blocks = rows // BLK
    tall = blocks * (width // HD) * BLK
    vmem = pl.BlockSpec(memory_space=pltpu.VMEM)
    far = pl.BlockSpec(memory_space=pltpu.HBM)
    shape = jax.ShapeDtypeStruct
    return pl.pallas_call(
        own_kernel,
        out_shape=(
            shape((rows, feats), BF16),
            shape((tall, width), BF16),
            shape((tall, width), BF16),
            shape((rows, width), BF16),
            shape((rows, width), BF16),
            shape((blocks, width, BLK), BF16),
            shape((blocks, width, BLK), BF16),
            shape((rows, width), F32),
            shape((rows, width), F32),
            shape(cot.shape, BF16),
            *[shape(w.shape, BF16) for w in weights],
        ),
        in_specs=[far] * 6,
        out_specs=[vmem] * 14,
        scratch_shapes=[pltpu.VMEM((rows, feats), BF16), pltpu.SemaphoreType.DMA((6,))],
        compiler_params=pltpu.CompilerParams(vmem_limit_bytes=LIMIT),
        cost_estimate=BRIEF,
        name="own_rows",
    )(*in_hbm(states, cot, *weights))


def attend_kernel(cfg, near_ref, *refs):
    ranks, share, blocks, offsets, width, explicit = cfg
    count = ranks * share
    piece_refs = refs[:count]
    own_refs = refs[count : count + 7]
    cot_ref, wk_ref, wv_ref = refs[count + 7 : count + 10]
    refs = refs[count + 10 :]
    both_ref, dq_ref, mixed_ref = refs[:3]
    far_refs, half_refs = refs[3:5], refs[5:9]
    pool_ref, refs = refs[9], refs[10:]
    k_ref, v_ref, kt_ref, vt_ref, ka_ref, va_ref, dk_ref, dv_ref, near_table, near_sem = refs
    fetch = pltpu.make_async_copy(near_ref, near_table, near_sem)
    fetch.start()
    q_ref, g_ref, k_own, v_own, kt_own, vt_own = own_refs[1:]
    heads = width // HD
    tall = heads * BLK
    entries = blocks + offsets * SEND
    rank = lax.axis_index("tensor")

    own_rows = blocks * BLK
    k_ref[:own_rows, :] = k_own[...]
    v_ref[:own_rows, :] = v_own[...]
    kt_ref[:blocks] = kt_own[...]
    vt_ref[:blocks] = vt_own[...]
    wkv = jnp.concatenate([wk_ref[...], wv_ref[...]], axis=1)
    for slot in range(ranks):
        for inner in range(share):
            entry = rank_piece(rank ^ slot, ranks, share, inner)
            base = pl.multiple_of(entry * BLK, BLK)
            source = piece_refs[slot * share + inner]
            for start in range(0, BLK, CHUNK):
                rows = unit_of(source[start : start + CHUNK, :])
                pool_ref[pl.ds(pl.multiple_of(base + start, CHUNK), CHUNK), :] = rows
    for start in range(blocks, entries, blocks):
        first = (start - blocks) * BLK
        paired = nn(pool_ref[first : first + blocks * BLK, :], wkv)
        put_pairs(
            paired, range(start, start + blocks), width, k_ref, v_ref, kt_ref, vt_ref
        )

    shrink = 1.0 / math.sqrt(HD)
    near = near_ref.shape[1]
    fetch.wait()
    for block in range(blocks):
        listed = [block] + [near_table[block, n] for n in range(near)]
        keys = jnp.concatenate([k_ref[block_at(e), :] for e in listed], axis=0)
        values = jnp.concatenate([v_ref[block_at(e), :] for e in listed], axis=0)
        keys_t = jnp.concatenate([kt_ref[e] for e in listed], axis=1)
        values_t = jnp.concatenate([vt_ref[e] for e in listed], axis=1)
        q_all = q_ref[block * tall : (block + 1) * tall, :]
        g_all = g_ref[block * tall : (block + 1) * tall, :]
        scores = nt(keys, q_all) * shrink
        powers = jnp.exp(scores - jnp.max(scores, axis=0, keepdims=True))
        weights = powers * (1.0 / jnp.sum(powers, axis=0, keepdims=True))
        low = weights.astype(BF16)
        mix = diagonal(nn(values_t, low), heads)
        mixed_ref[block * BLK : (block + 1) * BLK, :] = mix.T.astype(BF16)
        prob = nt(values, g_all)
        drop = jnp.sum(weights * prob, axis=0, keepdims=True)
        score_low = (weights * (prob - drop) * shrink).astype(BF16)
        dq = diagonal(nn(keys_t, score_low), heads)
        dq_ref[block * BLK : (block + 1) * BLK, :] = dq.T.astype(BF16)
        dk = nn(score_low, q_all)
        dv = nn(low, g_all)
        ka_ref[block * BLK : (block + 1) * BLK, :] = dk[:BLK]
        va_ref[block * BLK : (block + 1) * BLK, :] = dv[:BLK]
        dk_ref[block] = dk[BLK:]
        dv_ref[block] = dv[BLK:]

    ka_ref[own_rows:, :] = jnp.zeros((entries * BLK - own_rows, width), F32)
    va_ref[own_rows:, :] = jnp.zeros((entries * BLK - own_rows, width), F32)
    for block in range(blocks):
        for n in range(near):
            entry = block_at(near_table[block, n])
            ka_ref[entry, :] += dk_ref[block, n * BLK : (n + 1) * BLK]
            va_ref[entry, :] += dv_ref[block, n * BLK : (n + 1) * BLK]

    both_ref[:, :width] = ka_ref[...].astype(BF16)
    both_ref[:, width:] = va_ref[...].astype(BF16)
    grad_terms(explicit, own_refs[0], pool_ref, both_ref, dq_ref, mixed_ref, cot_ref, *half_refs)
    far_terms(blocks, pool_ref, both_ref, wk_ref, wv_ref, *far_refs)


def grad_terms(explicit, unit_ref, pool_ref, both_ref, dq_ref, mixed_ref, cot_ref, *refs):
    first_keep, first_send, second_keep, second_send = refs
    rows, width = dq_ref.shape

    def turned(ref, first, last):
        parts = [
            ref[start : start + BLK, :].astype(F32).T.astype(BF16)
            for start in range(first, last, BLK)
        ]
        return jnp.concatenate(parts, axis=1)

    unit = unit_ref[...]
    grad_q = nn(turned(dq_ref, 0, rows), unit)
    grad_out = nn(turned(mixed_ref, 0, rows), cot_ref[...])
    grad_kv = nn(turned(both_ref, 0, rows), unit)
    grad_kv = grad_kv + nn(turned(both_ref, rows, both_ref.shape[0]), pool_ref[...])
    grad_k, grad_v = grad_kv[:width], grad_kv[width:]
    by_dp = jnp.equal(lax.axis_index("dp") if explicit else 0, 1)
    by_dom = jnp.equal(lax.axis_index("dom") & 1 if explicit else 0, 1)
    first_keep[...] = jnp.where(by_dp, grad_k, grad_q).astype(BF16)
    first_send[...] = jnp.where(by_dp, grad_q, grad_k).astype(BF16)
    second_keep[...] = jnp.where(by_dom, grad_out, grad_v).astype(BF16)
    second_send[...] = jnp.where(by_dom, grad_v, grad_out).astype(BF16)


def run_attend(explicit, ranks, share, offsets, near, pieces, own, cot, w_key, w_value):
    rows, feats = own[0].shape
    blocks = rows // BLK
    width = w_key.shape[1]
    received = offsets * SEND
    entries = blocks + received
    vmem = pl.BlockSpec(memory_space=pltpu.VMEM)
    far = pl.BlockSpec(memory_space=pltpu.HBM)
    cfg = (ranks, share, blocks, offsets, width, explicit)
    shape = jax.ShapeDtypeStruct
    return pl.pallas_call(
        functools.partial(attend_kernel, cfg),
        out_shape=[
            shape((entries * BLK, 2 * width), BF16),
            shape((rows, width), BF16),
            shape((rows, width), BF16),
            *[shape((feats // width // 2, offsets * (SEND * BLK + PAD), width), BF16)] * 2,
            *[shape((width, feats), BF16)] * 4,
        ],
        in_specs=[far] + [vmem] * (len(pieces) + 10),
        out_specs=[vmem] * 9,
        scratch_shapes=[
            pltpu.VMEM((received * BLK, feats), BF16),
            pltpu.VMEM((entries * BLK, width), BF16),
            pltpu.VMEM((entries * BLK, width), BF16),
            pltpu.VMEM((entries, width, BLK), BF16),
            pltpu.VMEM((entries, width, BLK), BF16),
            pltpu.VMEM((entries * BLK, width), F32),
            pltpu.VMEM((entries * BLK, width), F32),
            pltpu.VMEM((blocks, near.shape[1] * BLK, width), F32),
            pltpu.VMEM((blocks, near.shape[1] * BLK, width), F32),
            pltpu.SMEM(near.shape, jnp.int32),
            pltpu.SemaphoreType.DMA(()),
        ],
        compiler_params=pltpu.CompilerParams(vmem_limit_bytes=LIMIT),
        cost_estimate=BRIEF,
        name="attention",
    )(*in_hbm(near), *pieces, *own, cot, w_key, w_value)


def put(odd, upper, keep_ref, send_ref, row, values):
    count, width = values.shape[0], keep_ref.shape[2]
    for pair in range(values.shape[1] // width // 2):
        left = values[:, 2 * pair * width : (2 * pair + 1) * width]
        right = values[:, (2 * pair + 1) * width : (2 * pair + 2) * width]
        at = upper ^ pair
        keep_ref[at, row : row + count, :] = jnp.where(odd, right, left).astype(BF16)
        send_ref[at, row : row + count, :] = jnp.where(odd, left, right).astype(BF16)


def put_dots(keep_ref, send_ref, row, dots):
    width = keep_ref.shape[2]
    parts = []
    for dot in dots:
        for piece in range(BLK // width):
            parts.append(dot[:1, piece * width : (piece + 1) * width])
    parts.append(jnp.zeros((PAD - len(parts), width), F32))
    rows = jnp.concatenate(parts, axis=0).astype(BF16)
    for pair in range(keep_ref.shape[0]):
        keep_ref[pair, row : row + PAD, :] = rows
        send_ref[pair, row : row + PAD, :] = rows


def row_dot(term, ref, first):
    ones = jnp.ones((16, ref.shape[1]), BF16)
    product = (term * ref[first : first + BLK, :].astype(F32)).astype(BF16)
    return nt(ones, product)


def far_terms(blocks, pool_ref, both_ref, wk_ref, wv_ref, far_keep, far_send):
    rank = lax.axis_index("tensor")
    odd, upper = (rank & 1) == 1, rank >> 1
    rows, step = blocks * BLK, SEND * BLK
    wkv = jnp.concatenate([wk_ref[...], wv_ref[...]], axis=1)
    for index in range(pool_ref.shape[0] // step):
        first, at = index * step, index * (step + PAD)
        term = nt(both_ref[rows + first : rows + first + step, :], wkv)
        put(odd, upper, far_keep, far_send, at, term)
        dots = [
            row_dot(term[c * BLK : (c + 1) * BLK], pool_ref, first + c * BLK) for c in range(SEND)
        ]
        put_dots(far_keep, far_send, at + step, dots)


def own_terms_kernel(both_ref, unit_ref, dq_ref, mixed_ref, *refs):
    wq_ref, wk_ref, wv_ref, wo_ref, own_keep, own_send = refs
    rank = lax.axis_index("tensor")
    odd, upper = (rank & 1) == 1, rank >> 1
    rows, step = unit_ref.shape[0], 2 * BLK
    wkv = jnp.concatenate([wk_ref[...], wv_ref[...]], axis=1)
    dots = []
    for first in range(0, rows, step):
        last = first + step
        term = nt(both_ref[first:last, :], wkv) + nt(dq_ref[first:last, :], wq_ref[...])
        put(odd, upper, own_keep, own_send, first, term)
        dots += [row_dot(term[c * BLK : (c + 1) * BLK], unit_ref, first + c * BLK) for c in (0, 1)]
        update = nn(mixed_ref[first:last, :], wo_ref[...])
        put(odd, upper, own_keep, own_send, rows + PAD + first, update)
    put_dots(own_keep, own_send, rows, dots)


def run_own_terms(both, unit, dq, mixed, weights):
    rows, feats = unit.shape
    width = dq.shape[1]
    vmem = pl.BlockSpec(memory_space=pltpu.VMEM)
    own = jax.ShapeDtypeStruct((feats // width // 2, 2 * rows + PAD, width), BF16)
    return pl.pallas_call(
        own_terms_kernel,
        out_shape=(own, own),
        in_specs=[vmem] * 8,
        out_specs=[vmem] * 2,
        compiler_params=pltpu.CompilerParams(vmem_limit_bytes=LIMIT),
        cost_estimate=BRIEF,
        name="own_terms",
    )(both, unit, dq, mixed, *weights)


def returns_kernel(bounds, keep_ref, got_ref, last_ref, *outs):
    for (first, last), out_ref in zip(bounds, outs):
        total = keep_ref[0, first:last, :].astype(F32) + got_ref[0, first:last, :].astype(F32)
        out_ref[...] = (total + last_ref[first:last, :].astype(F32)).astype(BF16)


def run_returns(bounds, keep, got, last):
    vmem = pl.BlockSpec(memory_space=pltpu.VMEM)
    width = keep.shape[2]
    return pl.pallas_call(
        functools.partial(returns_kernel, bounds),
        out_shape=[jax.ShapeDtypeStruct((b - a, width), BF16) for a, b in bounds],
        in_specs=[vmem] * 3,
        out_specs=[vmem] * len(bounds),
        compiler_params=pltpu.CompilerParams(vmem_limit_bytes=SMALL),
        cost_estimate=BRIEF,
        name="returned_terms",
    )(keep, got, last)


def my_bits():
    dom = lax.axis_index("dom")
    return lax.axis_index("dp"), dom & 1, dom >> 1


def halve_kernel(bits, *refs):
    count = len(bits)
    ins, outs = refs[: 2 * count], refs[2 * count :]
    mine = my_bits()
    size = outs[0].shape[0]
    for index, bit in enumerate(bits):
        keep_ref, got_ref = ins[2 * index : 2 * index + 2]
        for side, name in enumerate((mine[bit], 1 - mine[bit])):
            at = block_at(name, size)
            total = keep_ref[at, :].astype(F32) + got_ref[at, :].astype(F32)
            outs[2 * index + side][...] = total.astype(BF16)


def run_halve(bits, *arrays):
    vmem = pl.BlockSpec(memory_space=pltpu.VMEM)
    rows, feats = arrays[0].shape
    return pl.pallas_call(
        functools.partial(halve_kernel, bits),
        out_shape=[jax.ShapeDtypeStruct((rows // 2, feats), BF16)] * len(arrays),
        in_specs=[vmem] * len(arrays),
        out_specs=[vmem] * len(arrays),
        compiler_params=pltpu.CompilerParams(vmem_limit_bytes=SMALL),
        cost_estimate=BRIEF,
        name="halve_grads",
    )(*arrays)


def total_kernel(*refs):
    out_ref = refs[-1]
    size = refs[0].shape[0]
    for index in range(len(refs) // 2):
        total = refs[2 * index][...].astype(F32) + refs[2 * index + 1][...].astype(F32)
        out_ref[index * size : (index + 1) * size, :] = total.astype(BF16)


def run_total(*arrays):
    vmem = pl.BlockSpec(memory_space=pltpu.VMEM)
    rows, feats = arrays[0].shape
    return pl.pallas_call(
        total_kernel,
        out_shape=jax.ShapeDtypeStruct((len(arrays) // 2 * rows, feats), BF16),
        in_specs=[vmem] * len(arrays),
        out_specs=vmem,
        compiler_params=pltpu.CompilerParams(vmem_limit_bytes=SMALL),
        cost_estimate=BRIEF,
        name="total_grads",
    )(*arrays)


def settle_kernel(mine_ref, got_ref, *outs):
    size = outs[0].shape[0]
    for index, out_ref in enumerate(outs):
        rows = slice(index * size, (index + 1) * size)
        total = mine_ref[rows, :].astype(F32) + got_ref[rows, :].astype(F32)
        out_ref[...] = total.astype(BF16)


def run_settle(mine, got):
    vmem = pl.BlockSpec(memory_space=pltpu.VMEM)
    rows, feats = mine.shape
    return pl.pallas_call(
        settle_kernel,
        out_shape=[jax.ShapeDtypeStruct((rows // 2, feats), BF16)] * 2,
        in_specs=[vmem] * 2,
        out_specs=[vmem] * 2,
        compiler_params=pltpu.CompilerParams(vmem_limit_bytes=SMALL),
        cost_estimate=BRIEF,
        name="settle_grads",
    )(mine, got)


def join_kernel(bits, *refs):
    count = len(bits)
    outs = refs[-count:]
    mine = my_bits()
    size = refs[0].shape[0]
    for index, bit in enumerate(bits):
        outs[index][block_at(mine[bit], size), :] = refs[2 * index][...]
        outs[index][block_at(1 - mine[bit], size), :] = refs[2 * index + 1][...]


def run_join(bits, *arrays):
    vmem = pl.BlockSpec(memory_space=pltpu.VMEM)
    rows, feats = arrays[0].shape
    return pl.pallas_call(
        functools.partial(join_kernel, bits),
        out_shape=[jax.ShapeDtypeStruct((2 * rows, feats), BF16)] * len(bits),
        in_specs=[vmem] * len(arrays),
        out_specs=[vmem] * len(bits),
        compiler_params=pltpu.CompilerParams(vmem_limit_bytes=SMALL),
        cost_estimate=BRIEF,
        name="join_grads",
    )(*arrays)


def own_sum_kernel(keep_ref, got_ref, last_ref, update_ref, unit_ref):
    rows = update_ref.shape[0]

    def total(first, last):
        both = keep_ref[0, first:last, :].astype(F32) + got_ref[0, first:last, :].astype(F32)
        return both + last_ref[first:last, :].astype(F32)

    unit_ref[...] = total(0, rows + PAD)
    update_ref[...] = total(rows + PAD, 2 * rows + PAD).astype(BF16)


def run_own_sum(rows, keep, got, last):
    width = last.shape[1]
    vmem = pl.BlockSpec(memory_space=pltpu.VMEM)
    shape = jax.ShapeDtypeStruct
    return pl.pallas_call(
        own_sum_kernel,
        out_shape=(shape((rows, width), BF16), shape((rows + PAD, width), F32)),
        in_specs=[vmem] * 3,
        out_specs=[vmem] * 2,
        compiler_params=pltpu.CompilerParams(vmem_limit_bytes=SMALL),
        cost_estimate=BRIEF,
        name="own_sum",
    )(keep, got, last)


def finish_kernel(cfg, *refs):
    blocks, offsets, width, feats, spread = cfg
    send_ref, sum_ref, slab_ref, inverse_ref = refs[:4]
    far_refs = refs[4 : 4 + len(spread)]
    branch_ref, unit_ref, table, sem = refs[4 + len(spread) :]
    fetch = pltpu.make_async_copy(send_ref, table, sem)
    fetch.start()
    own_rows = blocks * BLK
    sub = BLK // width
    group = SEND * BLK + PAD

    unit_ref[...] = sum_ref[:own_rows, :]
    dots = sum_ref[own_rows:, :]
    at_row = lax.broadcasted_iota(jnp.int32, (PAD, width), 0)
    fetch.wait()
    for ref, members in zip(far_refs, spread):
        for position, offset in enumerate(members):
            first = position * group
            extra = ref[first + SEND * BLK : first + group, :].astype(F32)
            for c in range(SEND):
                block = table[c, offset]
                rows = ref[first + c * BLK : first + (c + 1) * BLK, :].astype(F32)
                unit_ref[block_at(block), :] += rows
                for piece in range(sub):
                    line = extra[c * sub + piece : c * sub + piece + 1, :]
                    dots = dots + jnp.where(at_row == block * sub + piece, line, 0.0)
    for block in range(blocks):
        rows = slice(block * BLK, (block + 1) * BLK)
        line = jnp.concatenate(
            [dots[block * sub + piece : block * sub + piece + 1, :] for piece in range(sub)], axis=1
        )
        mean = jnp.broadcast_to(line * (1.0 / feats), (BLK, BLK)).T[:, :width]
        branch = inverse_ref[rows, :] * (unit_ref[rows, :] - slab_ref[rows, :] * mean)
        branch_ref[rows, :] = branch.astype(BF16)


def run_finish(feats, send, own_sum, slab, inverse, far, spread):
    rows, width = slab.shape
    vmem = pl.BlockSpec(memory_space=pltpu.VMEM)
    hbm = pl.BlockSpec(memory_space=pltpu.HBM)
    cfg = (rows // BLK, send.shape[1], width, feats, spread)
    return pl.pallas_call(
        functools.partial(finish_kernel, cfg),
        out_shape=jax.ShapeDtypeStruct((rows, width), BF16),
        in_specs=[hbm] + [vmem] * (3 + len(far)),
        out_specs=vmem,
        scratch_shapes=[
            pltpu.VMEM((rows, width), F32),
            pltpu.SMEM(send.shape, jnp.int32),
            pltpu.SemaphoreType.DMA(()),
        ],
        compiler_params=pltpu.CompilerParams(vmem_limit_bytes=SMALL),
        cost_estimate=BRIEF,
        name="finish",
    )(*in_hbm(send), own_sum, slab, inverse, *far)


def grads_kernel(factor, *refs):
    first_held, first_got, second_held, second_got, q_ref, k_ref, v_ref, o_ref = refs
    dp, low, _ = my_bits()
    first, second = jnp.equal(dp, 1), jnp.equal(low, 1)

    def picked(flag, left, right, start):
        columns = slice(start, start + BLK)
        return jnp.where(flag, left[:, columns].astype(F32), right[:, columns].astype(F32)) * factor

    for start in range(0, q_ref.shape[0], BLK):
        rows = slice(start, start + BLK)
        q_ref[rows, :] = picked(first, first_got, first_held, start).T
        k_ref[rows, :] = picked(first, first_held, first_got, start).T
        v_ref[rows, :] = picked(second, second_got, second_held, start).T
        o_ref[:, rows] = picked(second, second_held, second_got, start)


def run_grads(factor, *arrays):
    width, feats = arrays[0].shape
    vmem = pl.BlockSpec(memory_space=pltpu.VMEM)
    tall = jax.ShapeDtypeStruct((feats, width), F32)
    return pl.pallas_call(
        functools.partial(grads_kernel, factor),
        out_shape=(tall, tall, tall, jax.ShapeDtypeStruct((width, feats), F32)),
        in_specs=[vmem] * 4,
        out_specs=[vmem] * 4,
        compiler_params=pltpu.CompilerParams(vmem_limit_bytes=SMALL),
        cost_estimate=BRIEF,
        name="weight_grads",
    )(*arrays)


def swap(array, axis, bit):
    return lax.ppermute(array, axis, [(i, i ^ bit) for i in range(lax.axis_size(axis))])


def shifted(array, axis, distance):
    size = lax.axis_size(axis)
    return lax.ppermute(array, axis, [(i, (i + distance) % size) for i in range(size)])


def added(left, right):
    return (left.astype(F32) + right.astype(F32)).astype(BF16)


def after(values, *earlier):
    held = lax.optimization_barrier((values, earlier))
    return held[0]


def narrow(keep, got, bit):
    while keep.shape[0] > 2:
        summed = added(keep, got)
        keep, send = summed[0::2], summed[1::2]
        got = swap(send, "tensor", bit)
        bit *= 2
    return keep, got, bit


def body(states, w_query, w_key, w_value, w_out, send_blocks, neighbor_blocks, cotangent):
    replicas, node_count, feats = states.shape
    width = w_query.shape[1]
    ranks = lax.axis_size("tensor")
    parts = lax.axis_size("dom")
    explicit = parts == 4 and lax.axis_size("dp") == 2
    offsets = offset_list(HOPS)
    order, share = piece_order(ranks, len(offsets))
    send = send_blocks[0].T
    weights = (w_query, w_key, w_value, w_out)
    flat_states = states.reshape(-1, feats)
    flat_cot = cotangent.reshape(-1, feats)

    leaving = pick_blocks(flat_states, send, ranks, share)
    route = []
    for p in range(parts):
        for r in range(ranks):
            distance = offsets[order[r * share] // SEND]
            route.append((p * ranks + r, ((p + distance) % parts) * ranks + r))
    levels = []
    bit = 1
    while bit < ranks:
        levels.append(bit)
        bit *= 2
    arrived = [lax.ppermute(block, ("dom", "tensor"), route) for block in leaving]
    own = run_own(flat_states, flat_cot, weights)
    arrived[0] = after(arrived[0], own[0])
    pieces = [None] * (ranks * share)
    for inner in range(share):
        if inner:
            arrived[inner] = after(arrived[inner], pieces[share + inner - 1])
        held = {0: arrived[inner]}
        for bit in reversed(levels):
            for slot in list(held):
                held[slot ^ bit] = swap(held[slot], "tensor", bit)
        for slot in range(ranks):
            pieces[slot * share + inner] = held[slot]
    unit, slab, inverse, cot = own[0], own[7], own[8], own[9]
    weights = own[10:]
    count = len(offsets)
    both, dq, mixed, far_keep, far_send, *halves = run_attend(
        explicit,
        ranks,
        share,
        count,
        neighbor_blocks,
        pieces,
        own[:7],
        cot,
        weights[1],
        weights[2],
    )
    total_rows = replicas * node_count * lax.axis_size("dp") * parts
    factor = 1.0 / math.sqrt(total_rows)

    if explicit:
        first, second = swap(halves[1], "dp", 1), swap(halves[3], "dom", 1)
    far_keep, far_got, bit = narrow(far_keep, swap(far_send, "tensor", 1), 2)
    own_keep, own_send = run_own_terms(both, unit, dq, mixed, weights)
    own_keep, own_got, bit = narrow(own_keep, swap(own_send, "tensor", 1), 2)
    far_out = added(far_keep[1], after(far_got, own_send)[1])
    far_last = swap(far_out, "tensor", bit)
    if explicit:
        first, second = after(first, far_out), after(second, far_out)
        halves = run_halve((1, 0), halves[0], first, halves[2], second)
        first, second = swap(halves[1], "dom", 1), swap(halves[3], "dp", 1)
        own_got = after(own_got, halves[0])
    own_out = added(own_keep[1], own_got[1])
    own_last = swap(own_out, "tensor", bit)
    if explicit:
        first = after(first, own_out)
        total = run_total(halves[0], first, halves[2], second)
        got = swap(total, "dom", 2)
        far_last = after(far_last, total)

    group = SEND * BLK + PAD
    spread = []
    for index, distance in enumerate(offsets):
        for members in spread:
            if (offsets[members[0]] - distance) % parts == 0 and members[-1] == index - 1:
                members.append(index)
                break
        else:
            spread.append([index])
    spread = tuple(tuple(members) for members in spread)
    bounds = tuple((members[0] * group, (members[-1] + 1) * group) for members in spread)
    far_sums = run_returns(bounds, far_keep, far_got, far_last)
    returned = [
        shifted(part, "dom", -offsets[members[0]]) for part, members in zip(far_sums, spread)
    ]
    own_last = after(own_last, far_sums)
    update, own_sum = run_own_sum(replicas * node_count, own_keep, own_got, own_last)
    if explicit:
        held = run_settle(total, after(got, own_sum))
        first, second = swap(held[0], "dom", 1), swap(held[1], "dp", 1)
        first = after(first, returned)
        held = run_join((1, 0), held[0], first, held[1], second)
        first, second = swap(held[0], "dp", 1), swap(held[1], "dom", 1)
    branch = run_finish(feats, send, own_sum, slab, inverse, returned, spread)
    if explicit:
        first = after(first, branch)
        grads = run_grads(factor, held[0], first, held[1], second)
    else:
        summed = [lax.psum(half.astype(F32), ("dp", "dom")) * factor for half in halves]
        grads = (summed[0].T, summed[1].T, summed[2].T, summed[3])
    shape = (replicas, node_count, width)
    return (update.reshape(shape), branch.reshape(shape), *grads)


def solution(mesh):
    placed = (
        P("dp", "dom", None),
        P(None, "tensor"),
        P(None, "tensor"),
        P(None, "tensor"),
        P("tensor", None),
        P("dom", None, None),
        P("dom", None),
        P("dp", "dom", None),
    )
    return jax.shard_map(
        body,
        mesh=mesh,
        in_specs=placed,
        out_specs=(
            P("dp", "dom", "tensor"),
            P("dp", "dom", "tensor"),
            P(None, "tensor"),
            P(None, "tensor"),
            P(None, "tensor"),
            P("tensor", None),
        ),
        check_vma=False,
    )
```

```python
import functools
import math

import jax
import jax.numpy as jnp
from jax import lax
from jax.experimental import pallas as pl
from jax.experimental.pallas import tpu as pltpu
from jax.sharding import PartitionSpec as P

BLK = 128
HOPS = 2
SEND = 2
HD = 64
PAD = 16
EPS = 1e-05
LIMIT = 24 * 1024 * 1024
SMALL = 8 * 1024 * 1024
CHUNK = 64
BRIEF = pl.CostEstimate(flops=1, bytes_accessed=1, transcendentals=0)
F32 = jnp.float32
BF16 = jnp.bfloat16


def offset_list(hops):
    result = []
    for section in range(1, hops + 1):
        result.append(section)
        result.append(-section)
    return result


def piece_order(ranks, offsets):
    count = offsets * SEND
    share = count // ranks
    if share == SEND and offsets == 4:
        return [0, 1, 4, 5, 2, 3, 6, 7], share
    return list(range(count)), share


def nt(left, right):
    return lax.dot_general(left, right, (((1,), (1,)), ((), ())), preferred_element_type=F32)


def nn(left, right):
    return jnp.dot(left, right, preferred_element_type=F32)


def unit_of(rows):
    values = rows.astype(F32)
    return (values * lax.rsqrt(jnp.mean(values * values, axis=-1, keepdims=True) + EPS)).astype(BF16)


def block_at(index, size=BLK):
    return pl.ds(pl.multiple_of(index * size, size), size)


def rank_piece(rank, ranks, share, inner):
    if share == SEND and ranks == 4:
        return ((rank & 1) * 2 + (rank >> 1)) * SEND + inner
    return rank * share + inner


def in_hbm(*arrays):
    return [pltpu.with_memory_space_constraint(array, pltpu.HBM) for array in arrays]


def pick_kernel(ranks, share, send_ref, states_ref, *refs):
    outs, table, sems = refs[:share], refs[share], refs[share + 1]
    rank = lax.axis_index("tensor")
    fetch = pltpu.make_async_copy(send_ref, table, sems.at[share])
    fetch.start()
    fetch.wait()
    copies = []
    for inner, out_ref in enumerate(outs):
        piece = rank_piece(rank, ranks, share, inner)
        block = table[piece % SEND, piece // SEND]
        copies.append(
            pltpu.make_async_copy(states_ref.at[block_at(block), :], out_ref, sems.at[inner])
        )
        copies[-1].start()
    for copy in copies:
        copy.wait()


def pick_blocks(states, send, ranks, share):
    far = pl.BlockSpec(memory_space=pltpu.HBM)
    vmem = pl.BlockSpec(memory_space=pltpu.VMEM)
    return pl.pallas_call(
        functools.partial(pick_kernel, ranks, share),
        out_shape=[jax.ShapeDtypeStruct((BLK, states.shape[1]), BF16)] * share,
        in_specs=[far, far],
        out_specs=[vmem] * share,
        scratch_shapes=[
            pltpu.SMEM(send.shape, jnp.int32),
            pltpu.SemaphoreType.DMA((share + 1,)),
        ],
        compiler_params=pltpu.CompilerParams(vmem_limit_bytes=SMALL),
        cost_estimate=BRIEF,
        name="pick_blocks",
    )(*in_hbm(send, states))


def by_head(rows, heads):
    if heads == 1:
        return rows.astype(BF16)
    lane_head = lax.broadcasted_iota(jnp.int32, rows.shape, 1) // HD
    return jnp.concatenate(
        [jnp.where(lane_head == head, rows, 0.0) for head in range(heads)], axis=0
    ).astype(BF16)


def diagonal(stacked, heads):
    return jnp.concatenate(
        [
            stacked[head * HD : (head + 1) * HD, head * BLK : (head + 1) * BLK]
            for head in range(heads)
        ],
        axis=0,
    )


def put_pairs(paired, at, width, k_ref, v_ref, kt_ref, vt_ref):
    for index, entry in enumerate(at):
        rows = paired[index * BLK : (index + 1) * BLK]
        keys, values = rows[:, :width], rows[:, width:]
        k_ref[block_at(entry), :] = keys.astype(BF16)
        v_ref[block_at(entry), :] = values.astype(BF16)
        kt_ref[entry] = keys.T.astype(BF16)
        vt_ref[entry] = values.T.astype(BF16)


def own_kernel(*refs):
    sources = refs[:6]
    unit_ref, q_ref, g_ref, k_ref, v_ref, kt_ref, vt_ref, slab_ref, inverse_ref = refs[6:15]
    held, states_ref, sems = refs[15:20], refs[20], refs[21]
    cot_ref, wq_ref, wk_ref, wv_ref, wo_ref = held
    copies = []
    for index, (source, target) in enumerate(zip(sources, (states_ref,) + tuple(held))):
        copies.append(pltpu.make_async_copy(source, target, sems.at[index]))
        copies[-1].start()
    rows, feats = states_ref.shape
    width = wq_ref.shape[1]
    heads = width // HD
    tall = heads * BLK
    rank = lax.axis_index("tensor")
    copies[0].wait()
    for start in range(0, rows, CHUNK):
        values = states_ref[start : start + CHUNK, :].astype(F32)
        inverse = lax.rsqrt(jnp.mean(values * values, axis=-1, keepdims=True) + EPS)
        normed = values * inverse
        unit_ref[start : start + CHUNK, :] = normed.astype(BF16)
        slab = normed[:, :width]
        for index in range(1, feats // width):
            slab = jnp.where(rank == index, normed[:, index * width : (index + 1) * width], slab)
        slab_ref[start : start + CHUNK, :] = slab
        inverse_ref[start : start + CHUNK, :] = jnp.broadcast_to(inverse, slab.shape)
    for copy in copies[1:]:
        copy.wait()
    unit = unit_ref[...]
    queries = nn(unit, wq_ref[...])
    grads = nt(cot_ref[...], wo_ref[...])
    for block in range(rows // BLK):
        q_ref[block * tall : (block + 1) * tall, :] = by_head(
            queries[block * BLK : (block + 1) * BLK], heads
        )
        g_ref[block * tall : (block + 1) * tall, :] = by_head(
            grads[block * BLK : (block + 1) * BLK], heads
        )
    paired = nn(unit, jnp.concatenate([wk_ref[...], wv_ref[...]], axis=1))
    put_pairs(paired, range(rows // BLK), width, k_ref, v_ref, kt_ref, vt_ref)


def run_own(states, cot, weights):
    rows, feats = states.shape
    width = weights[0].shape[1]
    blocks = rows // BLK
    tall = blocks * (width // HD) * BLK
    vmem = pl.BlockSpec(memory_space=pltpu.VMEM)
    far = pl.BlockSpec(memory_space=pltpu.HBM)
    shape = jax.ShapeDtypeStruct
    return pl.pallas_call(
        own_kernel,
        out_shape=(
            shape((rows, feats), BF16),
            shape((tall, width), BF16),
            shape((tall, width), BF16),
            shape((rows, width), BF16),
            shape((rows, width), BF16),
            shape((blocks, width, BLK), BF16),
            shape((blocks, width, BLK), BF16),
            shape((rows, width), F32),
            shape((rows, width), F32),
            shape(cot.shape, BF16),
            *[shape(w.shape, BF16) for w in weights],
        ),
        in_specs=[far] * 6,
        out_specs=[vmem] * 14,
        scratch_shapes=[pltpu.VMEM((rows, feats), BF16), pltpu.SemaphoreType.DMA((6,))],
        compiler_params=pltpu.CompilerParams(vmem_limit_bytes=LIMIT),
        cost_estimate=BRIEF,
        name="own_rows",
    )(*in_hbm(states, cot, *weights))


def attend_kernel(cfg, near_ref, *refs):
    ranks, share, blocks, offsets, width, explicit = cfg
    count = ranks * share
    piece_refs = refs[:count]
    own_refs = refs[count : count + 7]
    cot_ref, wk_ref, wv_ref = refs[count + 7 : count + 10]
    refs = refs[count + 10 :]
    both_ref, dq_ref, mixed_ref = refs[:3]
    far_refs, half_refs = refs[3:5], refs[5:9]
    pool_ref, refs = refs[9], refs[10:]
    k_ref, v_ref, kt_ref, vt_ref, ka_ref, va_ref, dk_ref, dv_ref, near_table, near_sem = refs
    fetch = pltpu.make_async_copy(near_ref, near_table, near_sem)
    fetch.start()
    q_ref, g_ref, k_own, v_own, kt_own, vt_own = own_refs[1:]
    heads = width // HD
    tall = heads * BLK
    entries = blocks + offsets * SEND
    rank = lax.axis_index("tensor")

    own_rows = blocks * BLK
    k_ref[:own_rows, :] = k_own[...]
    v_ref[:own_rows, :] = v_own[...]
    kt_ref[:blocks] = kt_own[...]
    vt_ref[:blocks] = vt_own[...]
    wkv = jnp.concatenate([wk_ref[...], wv_ref[...]], axis=1)
    for slot in range(ranks):
        for inner in range(share):
            entry = rank_piece(rank ^ slot, ranks, share, inner)
            base = pl.multiple_of(entry * BLK, BLK)
            source = piece_refs[slot * share + inner]
            for start in range(0, BLK, CHUNK):
                rows = unit_of(source[start : start + CHUNK, :])
                pool_ref[pl.ds(pl.multiple_of(base + start, CHUNK), CHUNK), :] = rows
    for start in range(blocks, entries, blocks):
        first = (start - blocks) * BLK
        paired = nn(pool_ref[first : first + blocks * BLK, :], wkv)
        put_pairs(
            paired, range(start, start + blocks), width, k_ref, v_ref, kt_ref, vt_ref
        )

    shrink = 1.0 / math.sqrt(HD)
    near = near_ref.shape[1]
    fetch.wait()
    for block in range(blocks):
        listed = [block] + [near_table[block, n] for n in range(near)]
        keys = jnp.concatenate([k_ref[block_at(e), :] for e in listed], axis=0)
        values = jnp.concatenate([v_ref[block_at(e), :] for e in listed], axis=0)
        keys_t = jnp.concatenate([kt_ref[e] for e in listed], axis=1)
        values_t = jnp.concatenate([vt_ref[e] for e in listed], axis=1)
        q_all = q_ref[block * tall : (block + 1) * tall, :]
        g_all = g_ref[block * tall : (block + 1) * tall, :]
        scores = nt(keys, q_all) * shrink
        powers = jnp.exp(scores - jnp.max(scores, axis=0, keepdims=True))
        weights = powers * (1.0 / jnp.sum(powers, axis=0, keepdims=True))
        low = weights.astype(BF16)
        mix = diagonal(nn(values_t, low), heads)
        mixed_ref[block * BLK : (block + 1) * BLK, :] = mix.T.astype(BF16)
        prob = nt(values, g_all)
        drop = jnp.sum(weights * prob, axis=0, keepdims=True)
        score_low = (weights * (prob - drop) * shrink).astype(BF16)
        dq = diagonal(nn(keys_t, score_low), heads)
        dq_ref[block * BLK : (block + 1) * BLK, :] = dq.T.astype(BF16)
        dk = nn(score_low, q_all)
        dv = nn(low, g_all)
        ka_ref[block * BLK : (block + 1) * BLK, :] = dk[:BLK]
        va_ref[block * BLK : (block + 1) * BLK, :] = dv[:BLK]
        dk_ref[block] = dk[BLK:]
        dv_ref[block] = dv[BLK:]

    ka_ref[own_rows:, :] = jnp.zeros((entries * BLK - own_rows, width), F32)
    va_ref[own_rows:, :] = jnp.zeros((entries * BLK - own_rows, width), F32)
    for block in range(blocks):
        for n in range(near):
            entry = block_at(near_table[block, n])
            ka_ref[entry, :] += dk_ref[block, n * BLK : (n + 1) * BLK]
            va_ref[entry, :] += dv_ref[block, n * BLK : (n + 1) * BLK]

    both_ref[:, :width] = ka_ref[...].astype(BF16)
    both_ref[:, width:] = va_ref[...].astype(BF16)
    grad_terms(explicit, own_refs[0], pool_ref, both_ref, dq_ref, mixed_ref, cot_ref, *half_refs)
    far_terms(blocks, pool_ref, both_ref, wk_ref, wv_ref, *far_refs)


def grad_terms(explicit, unit_ref, pool_ref, both_ref, dq_ref, mixed_ref, cot_ref, *refs):
    first_keep, first_send, second_keep, second_send = refs
    rows, width = dq_ref.shape

    def turned(ref, first, last):
        parts = [
            ref[start : start + BLK, :].astype(F32).T.astype(BF16)
            for start in range(first, last, BLK)
        ]
        return jnp.concatenate(parts, axis=1)

    unit = unit_ref[...]
    grad_q = nn(turned(dq_ref, 0, rows), unit)
    grad_out = nn(turned(mixed_ref, 0, rows), cot_ref[...])
    grad_kv = nn(turned(both_ref, 0, rows), unit)
    grad_kv = grad_kv + nn(turned(both_ref, rows, both_ref.shape[0]), pool_ref[...])
    grad_k, grad_v = grad_kv[:width], grad_kv[width:]
    by_dp = jnp.equal(lax.axis_index("dp") if explicit else 0, 1)
    by_dom = jnp.equal(lax.axis_index("dom") & 1 if explicit else 0, 1)
    first_keep[...] = jnp.where(by_dp, grad_k, grad_q).astype(BF16)
    first_send[...] = jnp.where(by_dp, grad_q, grad_k).astype(BF16)
    second_keep[...] = jnp.where(by_dom, grad_out, grad_v).astype(BF16)
    second_send[...] = jnp.where(by_dom, grad_v, grad_out).astype(BF16)


def run_attend(explicit, ranks, share, offsets, near, pieces, own, cot, w_key, w_value):
    rows, feats = own[0].shape
    blocks = rows // BLK
    width = w_key.shape[1]
    received = offsets * SEND
    entries = blocks + received
    vmem = pl.BlockSpec(memory_space=pltpu.VMEM)
    far = pl.BlockSpec(memory_space=pltpu.HBM)
    cfg = (ranks, share, blocks, offsets, width, explicit)
    shape = jax.ShapeDtypeStruct
    return pl.pallas_call(
        functools.partial(attend_kernel, cfg),
        out_shape=[
            shape((entries * BLK, 2 * width), BF16),
            shape((rows, width), BF16),
            shape((rows, width), BF16),
            *[shape((feats // width // 2, offsets * (SEND * BLK + PAD), width), BF16)] * 2,
            *[shape((width, feats), BF16)] * 4,
        ],
        in_specs=[far] + [vmem] * (len(pieces) + 10),
        out_specs=[vmem] * 9,
        scratch_shapes=[
            pltpu.VMEM((received * BLK, feats), BF16),
            pltpu.VMEM((entries * BLK, width), BF16),
            pltpu.VMEM((entries * BLK, width), BF16),
            pltpu.VMEM((entries, width, BLK), BF16),
            pltpu.VMEM((entries, width, BLK), BF16),
            pltpu.VMEM((entries * BLK, width), F32),
            pltpu.VMEM((entries * BLK, width), F32),
            pltpu.VMEM((blocks, near.shape[1] * BLK, width), F32),
            pltpu.VMEM((blocks, near.shape[1] * BLK, width), F32),
            pltpu.SMEM(near.shape, jnp.int32),
            pltpu.SemaphoreType.DMA(()),
        ],
        compiler_params=pltpu.CompilerParams(vmem_limit_bytes=LIMIT),
        cost_estimate=BRIEF,
        name="attention",
    )(*in_hbm(near), *pieces, *own, cot, w_key, w_value)


def put(odd, upper, keep_ref, send_ref, row, values):
    count, width = values.shape[0], keep_ref.shape[2]
    for pair in range(values.shape[1] // width // 2):
        left = values[:, 2 * pair * width : (2 * pair + 1) * width]
        right = values[:, (2 * pair + 1) * width : (2 * pair + 2) * width]
        at = upper ^ pair
        keep_ref[at, row : row + count, :] = jnp.where(odd, right, left).astype(BF16)
        send_ref[at, row : row + count, :] = jnp.where(odd, left, right).astype(BF16)


def put_dots(keep_ref, send_ref, row, dots):
    width = keep_ref.shape[2]
    parts = []
    for dot in dots:
        for piece in range(BLK // width):
            parts.append(dot[:1, piece * width : (piece + 1) * width])
    parts.append(jnp.zeros((PAD - len(parts), width), F32))
    rows = jnp.concatenate(parts, axis=0).astype(BF16)
    for pair in range(keep_ref.shape[0]):
        keep_ref[pair, row : row + PAD, :] = rows
        send_ref[pair, row : row + PAD, :] = rows


def row_dot(term, ref, first):
    ones = jnp.ones((16, ref.shape[1]), BF16)
    product = (term * ref[first : first + BLK, :].astype(F32)).astype(BF16)
    return nt(ones, product)


def far_terms(blocks, pool_ref, both_ref, wk_ref, wv_ref, far_keep, far_send):
    rank = lax.axis_index("tensor")
    odd, upper = (rank & 1) == 1, rank >> 1
    rows, step = blocks * BLK, SEND * BLK
    wkv = jnp.concatenate([wk_ref[...], wv_ref[...]], axis=1)
    for index in range(pool_ref.shape[0] // step):
        first, at = index * step, index * (step + PAD)
        term = nt(both_ref[rows + first : rows + first + step, :], wkv)
        put(odd, upper, far_keep, far_send, at, term)
        dots = [
            row_dot(term[c * BLK : (c + 1) * BLK], pool_ref, first + c * BLK) for c in range(SEND)
        ]
        put_dots(far_keep, far_send, at + step, dots)


def own_terms_kernel(both_ref, unit_ref, dq_ref, mixed_ref, *refs):
    wq_ref, wk_ref, wv_ref, wo_ref, own_keep, own_send = refs
    rank = lax.axis_index("tensor")
    odd, upper = (rank & 1) == 1, rank >> 1
    rows, step = unit_ref.shape[0], 2 * BLK
    wkv = jnp.concatenate([wk_ref[...], wv_ref[...]], axis=1)
    dots = []
    for first in range(0, rows, step):
        last = first + step
        term = nt(both_ref[first:last, :], wkv) + nt(dq_ref[first:last, :], wq_ref[...])
        put(odd, upper, own_keep, own_send, first, term)
        dots += [row_dot(term[c * BLK : (c + 1) * BLK], unit_ref, first + c * BLK) for c in (0, 1)]
        update = nn(mixed_ref[first:last, :], wo_ref[...])
        put(odd, upper, own_keep, own_send, rows + PAD + first, update)
    put_dots(own_keep, own_send, rows, dots)


def run_own_terms(both, unit, dq, mixed, weights):
    rows, feats = unit.shape
    width = dq.shape[1]
    vmem = pl.BlockSpec(memory_space=pltpu.VMEM)
    own = jax.ShapeDtypeStruct((feats // width // 2, 2 * rows + PAD, width), BF16)
    return pl.pallas_call(
        own_terms_kernel,
        out_shape=(own, own),
        in_specs=[vmem] * 8,
        out_specs=[vmem] * 2,
        compiler_params=pltpu.CompilerParams(vmem_limit_bytes=LIMIT),
        cost_estimate=BRIEF,
        name="own_terms",
    )(both, unit, dq, mixed, *weights)


def returns_kernel(bounds, keep_ref, got_ref, last_ref, *outs):
    for (first, last), out_ref in zip(bounds, outs):
        total = keep_ref[0, first:last, :].astype(F32) + got_ref[0, first:last, :].astype(F32)
        out_ref[...] = (total + last_ref[first:last, :].astype(F32)).astype(BF16)


def run_returns(bounds, keep, got, last):
    vmem = pl.BlockSpec(memory_space=pltpu.VMEM)
    width = keep.shape[2]
    return pl.pallas_call(
        functools.partial(returns_kernel, bounds),
        out_shape=[jax.ShapeDtypeStruct((b - a, width), BF16) for a, b in bounds],
        in_specs=[vmem] * 3,
        out_specs=[vmem] * len(bounds),
        compiler_params=pltpu.CompilerParams(vmem_limit_bytes=SMALL),
        cost_estimate=BRIEF,
        name="returned_terms",
    )(keep, got, last)


def my_bits():
    dom = lax.axis_index("dom")
    return lax.axis_index("dp"), dom & 1, dom >> 1


def halve_kernel(bits, *refs):
    count = len(bits)
    ins, outs = refs[: 2 * count], refs[2 * count :]
    mine = my_bits()
    size = outs[0].shape[0]
    for index, bit in enumerate(bits):
        keep_ref, got_ref = ins[2 * index : 2 * index + 2]
        for side, name in enumerate((mine[bit], 1 - mine[bit])):
            at = block_at(name, size)
            total = keep_ref[at, :].astype(F32) + got_ref[at, :].astype(F32)
            outs[2 * index + side][...] = total.astype(BF16)


def run_halve(bits, *arrays):
    vmem = pl.BlockSpec(memory_space=pltpu.VMEM)
    rows, feats = arrays[0].shape
    return pl.pallas_call(
        functools.partial(halve_kernel, bits),
        out_shape=[jax.ShapeDtypeStruct((rows // 2, feats), BF16)] * len(arrays),
        in_specs=[vmem] * len(arrays),
        out_specs=[vmem] * len(arrays),
        compiler_params=pltpu.CompilerParams(vmem_limit_bytes=SMALL),
        cost_estimate=BRIEF,
        name="halve_grads",
    )(*arrays)


def total_kernel(*refs):
    out_ref = refs[-1]
    size = refs[0].shape[0]
    for index in range(len(refs) // 2):
        total = refs[2 * index][...].astype(F32) + refs[2 * index + 1][...].astype(F32)
        out_ref[index * size : (index + 1) * size, :] = total.astype(BF16)


def run_total(*arrays):
    vmem = pl.BlockSpec(memory_space=pltpu.VMEM)
    rows, feats = arrays[0].shape
    return pl.pallas_call(
        total_kernel,
        out_shape=jax.ShapeDtypeStruct((len(arrays) // 2 * rows, feats), BF16),
        in_specs=[vmem] * len(arrays),
        out_specs=vmem,
        compiler_params=pltpu.CompilerParams(vmem_limit_bytes=SMALL),
        cost_estimate=BRIEF,
        name="total_grads",
    )(*arrays)


def settle_kernel(mine_ref, got_ref, *outs):
    size = outs[0].shape[0]
    for index, out_ref in enumerate(outs):
        rows = slice(index * size, (index + 1) * size)
        total = mine_ref[rows, :].astype(F32) + got_ref[rows, :].astype(F32)
        out_ref[...] = total.astype(BF16)


def run_settle(mine, got):
    vmem = pl.BlockSpec(memory_space=pltpu.VMEM)
    rows, feats = mine.shape
    return pl.pallas_call(
        settle_kernel,
        out_shape=[jax.ShapeDtypeStruct((rows // 2, feats), BF16)] * 2,
        in_specs=[vmem] * 2,
        out_specs=[vmem] * 2,
        compiler_params=pltpu.CompilerParams(vmem_limit_bytes=SMALL),
        cost_estimate=BRIEF,
        name="settle_grads",
    )(mine, got)


def join_kernel(bits, *refs):
    count = len(bits)
    outs = refs[-count:]
    mine = my_bits()
    size = refs[0].shape[0]
    for index, bit in enumerate(bits):
        outs[index][block_at(mine[bit], size), :] = refs[2 * index][...]
        outs[index][block_at(1 - mine[bit], size), :] = refs[2 * index + 1][...]


def run_join(bits, *arrays):
    vmem = pl.BlockSpec(memory_space=pltpu.VMEM)
    rows, feats = arrays[0].shape
    return pl.pallas_call(
        functools.partial(join_kernel, bits),
        out_shape=[jax.ShapeDtypeStruct((2 * rows, feats), BF16)] * len(bits),
        in_specs=[vmem] * len(arrays),
        out_specs=[vmem] * len(bits),
        compiler_params=pltpu.CompilerParams(vmem_limit_bytes=SMALL),
        cost_estimate=BRIEF,
        name="join_grads",
    )(*arrays)


def own_sum_kernel(keep_ref, got_ref, last_ref, update_ref, unit_ref):
    rows = update_ref.shape[0]

    def total(first, last):
        both = keep_ref[0, first:last, :].astype(F32) + got_ref[0, first:last, :].astype(F32)
        return both + last_ref[first:last, :].astype(F32)

    unit_ref[...] = total(0, rows + PAD)
    update_ref[...] = total(rows + PAD, 2 * rows + PAD).astype(BF16)


def run_own_sum(rows, keep, got, last):
    width = last.shape[1]
    vmem = pl.BlockSpec(memory_space=pltpu.VMEM)
    shape = jax.ShapeDtypeStruct
    return pl.pallas_call(
        own_sum_kernel,
        out_shape=(shape((rows, width), BF16), shape((rows + PAD, width), F32)),
        in_specs=[vmem] * 3,
        out_specs=[vmem] * 2,
        compiler_params=pltpu.CompilerParams(vmem_limit_bytes=SMALL),
        cost_estimate=BRIEF,
        name="own_sum",
    )(keep, got, last)


def finish_kernel(cfg, *refs):
    blocks, offsets, width, feats, spread = cfg
    send_ref, sum_ref, slab_ref, inverse_ref = refs[:4]
    far_refs = refs[4 : 4 + len(spread)]
    branch_ref, unit_ref, table, sem = refs[4 + len(spread) :]
    fetch = pltpu.make_async_copy(send_ref, table, sem)
    fetch.start()
    own_rows = blocks * BLK
    sub = BLK // width
    group = SEND * BLK + PAD

    unit_ref[...] = sum_ref[:own_rows, :]
    dots = sum_ref[own_rows:, :]
    at_row = lax.broadcasted_iota(jnp.int32, (PAD, width), 0)
    fetch.wait()
    for ref, members in zip(far_refs, spread):
        for position, offset in enumerate(members):
            first = position * group
            extra = ref[first + SEND * BLK : first + group, :].astype(F32)
            for c in range(SEND):
                block = table[c, offset]
                rows = ref[first + c * BLK : first + (c + 1) * BLK, :].astype(F32)
                unit_ref[block_at(block), :] += rows
                for piece in range(sub):
                    line = extra[c * sub + piece : c * sub + piece + 1, :]
                    dots = dots + jnp.where(at_row == block * sub + piece, line, 0.0)
    for block in range(blocks):
        rows = slice(block * BLK, (block + 1) * BLK)
        line = jnp.concatenate(
            [dots[block * sub + piece : block * sub + piece + 1, :] for piece in range(sub)], axis=1
        )
        mean = jnp.broadcast_to(line * (1.0 / feats), (BLK, BLK)).T[:, :width]
        branch = inverse_ref[rows, :] * (unit_ref[rows, :] - slab_ref[rows, :] * mean)
        branch_ref[rows, :] = branch.astype(BF16)


def run_finish(feats, send, own_sum, slab, inverse, far, spread):
    rows, width = slab.shape
    vmem = pl.BlockSpec(memory_space=pltpu.VMEM)
    hbm = pl.BlockSpec(memory_space=pltpu.HBM)
    cfg = (rows // BLK, send.shape[1], width, feats, spread)
    return pl.pallas_call(
        functools.partial(finish_kernel, cfg),
        out_shape=jax.ShapeDtypeStruct((rows, width), BF16),
        in_specs=[hbm] + [vmem] * (3 + len(far)),
        out_specs=vmem,
        scratch_shapes=[
            pltpu.VMEM((rows, width), F32),
            pltpu.SMEM(send.shape, jnp.int32),
            pltpu.SemaphoreType.DMA(()),
        ],
        compiler_params=pltpu.CompilerParams(vmem_limit_bytes=SMALL),
        cost_estimate=BRIEF,
        name="finish",
    )(*in_hbm(send), own_sum, slab, inverse, *far)


def grads_kernel(factor, *refs):
    first_held, first_got, second_held, second_got, q_ref, k_ref, v_ref, o_ref = refs
    dp, low, _ = my_bits()
    first, second = jnp.equal(dp, 1), jnp.equal(low, 1)

    def picked(flag, left, right, start):
        columns = slice(start, start + BLK)
        return jnp.where(flag, left[:, columns].astype(F32), right[:, columns].astype(F32)) * factor

    for start in range(0, q_ref.shape[0], BLK):
        rows = slice(start, start + BLK)
        q_ref[rows, :] = picked(first, first_got, first_held, start).T
        k_ref[rows, :] = picked(first, first_held, first_got, start).T
        v_ref[rows, :] = picked(second, second_got, second_held, start).T
        o_ref[:, rows] = picked(second, second_held, second_got, start)


def run_grads(factor, *arrays):
    width, feats = arrays[0].shape
    vmem = pl.BlockSpec(memory_space=pltpu.VMEM)
    tall = jax.ShapeDtypeStruct((feats, width), F32)
    return pl.pallas_call(
        functools.partial(grads_kernel, factor),
        out_shape=(tall, tall, tall, jax.ShapeDtypeStruct((width, feats), F32)),
        in_specs=[vmem] * 4,
        out_specs=[vmem] * 4,
        compiler_params=pltpu.CompilerParams(vmem_limit_bytes=SMALL),
        cost_estimate=BRIEF,
        name="weight_grads",
    )(*arrays)


def swap(array, axis, bit):
    return lax.ppermute(array, axis, [(i, i ^ bit) for i in range(lax.axis_size(axis))])


def shifted(array, axis, distance):
    size = lax.axis_size(axis)
    return lax.ppermute(array, axis, [(i, (i + distance) % size) for i in range(size)])


def added(left, right):
    return (left.astype(F32) + right.astype(F32)).astype(BF16)


def after(values, *earlier):
    held = lax.optimization_barrier((values, earlier))
    return held[0]


def narrow(keep, got, bit):
    while keep.shape[0] > 2:
        summed = added(keep, got)
        keep, send = summed[0::2], summed[1::2]
        got = swap(send, "tensor", bit)
        bit *= 2
    return keep, got, bit


def body(states, w_query, w_key, w_value, w_out, send_blocks, neighbor_blocks, cotangent):
    replicas, node_count, feats = states.shape
    width = w_query.shape[1]
    ranks = lax.axis_size("tensor")
    parts = lax.axis_size("dom")
    explicit = parts == 4 and lax.axis_size("dp") == 2
    offsets = offset_list(HOPS)
    order, share = piece_order(ranks, len(offsets))
    send = send_blocks[0].T
    weights = (w_query, w_key, w_value, w_out)
    flat_states = states.reshape(-1, feats)
    flat_cot = cotangent.reshape(-1, feats)

    leaving = pick_blocks(flat_states, send, ranks, share)
    route = []
    for p in range(parts):
        for r in range(ranks):
            distance = offsets[order[r * share] // SEND]
            route.append((p * ranks + r, ((p + distance) % parts) * ranks + r))
    levels = []
    bit = 1
    while bit < ranks:
        levels.append(bit)
        bit *= 2
    arrived = [lax.ppermute(block, ("dom", "tensor"), route) for block in leaving]
    own = run_own(flat_states, flat_cot, weights)
    arrived[0] = after(arrived[0], own[0])
    pieces = [None] * (ranks * share)
    for inner in range(share):
        if inner:
            arrived[inner] = after(arrived[inner], pieces[share + inner - 1])
        held = {0: arrived[inner]}
        for bit in reversed(levels):
            for slot in list(held):
                held[slot ^ bit] = swap(held[slot], "tensor", bit)
        for slot in range(ranks):
            pieces[slot * share + inner] = held[slot]
    unit, slab, inverse, cot = own[0], own[7], own[8], own[9]
    weights = own[10:]
    count = len(offsets)
    both, dq, mixed, far_keep, far_send, *halves = run_attend(
        explicit,
        ranks,
        share,
        count,
        neighbor_blocks,
        pieces,
        own[:7],
        cot,
        weights[1],
        weights[2],
    )
    total_rows = replicas * node_count * lax.axis_size("dp") * parts
    factor = 1.0 / math.sqrt(total_rows)

    if explicit:
        first, second = swap(halves[1], "dp", 1), swap(halves[3], "dom", 1)
    far_keep, far_got, bit = narrow(far_keep, swap(far_send, "tensor", 1), 2)
    own_keep, own_send = run_own_terms(both, unit, dq, mixed, weights)
    own_keep, own_got, bit = narrow(own_keep, swap(own_send, "tensor", 1), 2)
    far_out = added(far_keep[1], far_got[1])
    far_last = swap(far_out, "tensor", bit)
    if explicit:
        first, second = after(first, far_out, own_send), after(second, far_out, own_send)
        halves = run_halve((1, 0), halves[0], first, halves[2], second)
        first, second = swap(halves[1], "dom", 1), swap(halves[3], "dp", 1)
        total = run_total(halves[0], first, halves[2], second)
        got = swap(total, "dom", 2)
        own_got = after(own_got, total)
    own_out = added(own_keep[1], own_got[1])
    own_last = swap(own_out, "tensor", bit)
    far_last = after(far_last, own_out)

    group = SEND * BLK + PAD
    spread = []
    for index, distance in enumerate(offsets):
        for members in spread:
            if (offsets[members[0]] - distance) % parts == 0 and members[-1] == index - 1:
                members.append(index)
                break
        else:
            spread.append([index])
    spread = tuple(tuple(members) for members in spread)
    bounds = tuple((members[0] * group, (members[-1] + 1) * group) for members in spread)
    far_sums = run_returns(bounds, far_keep, far_got, far_last)
    returned = [
        shifted(part, "dom", -offsets[members[0]]) for part, members in zip(far_sums, spread)
    ]
    own_last = after(own_last, far_sums)
    update, own_sum = run_own_sum(replicas * node_count, own_keep, own_got, own_last)
    if explicit:
        held = run_settle(total, after(got, own_sum))
        first, second = swap(held[0], "dom", 1), swap(held[1], "dp", 1)
        first = after(first, returned)
        held = run_join((1, 0), held[0], first, held[1], second)
        first, second = swap(held[0], "dp", 1), swap(held[1], "dom", 1)
    branch = run_finish(feats, send, own_sum, slab, inverse, returned, spread)
    if explicit:
        first = after(first, branch)
        grads = run_grads(factor, held[0], first, held[1], second)
    else:
        summed = [lax.psum(half.astype(F32), ("dp", "dom")) * factor for half in halves]
        grads = (summed[0].T, summed[1].T, summed[2].T, summed[3])
    shape = (replicas, node_count, width)
    return (update.reshape(shape), branch.reshape(shape), *grads)


def solution(mesh):
    placed = (
        P("dp", "dom", None),
        P(None, "tensor"),
        P(None, "tensor"),
        P(None, "tensor"),
        P("tensor", None),
        P("dom", None, None),
        P("dom", None),
        P("dp", "dom", None),
    )
    return jax.shard_map(
        body,
        mesh=mesh,
        in_specs=placed,
        out_specs=(
            P("dp", "dom", "tensor"),
            P("dp", "dom", "tensor"),
            P(None, "tensor"),
            P(None, "tensor"),
            P(None, "tensor"),
            P("tensor", None),
        ),
        check_vma=False,
    )
```

```python
import functools
import math

import jax
import jax.numpy as jnp
from jax import lax
from jax.experimental import pallas as pl
from jax.experimental.pallas import tpu as pltpu
from jax.sharding import PartitionSpec as P

BLK = 128
HOPS = 2
SEND = 2
HD = 64
PAD = 16
EARLY = 2
EPS = 1e-05
LIMIT = 24 * 1024 * 1024
SMALL = 8 * 1024 * 1024
CHUNK = 64
BRIEF = pl.CostEstimate(flops=1, bytes_accessed=1, transcendentals=0)
F32 = jnp.float32
BF16 = jnp.bfloat16


def offset_list(hops):
    result = []
    for section in range(1, hops + 1):
        result.append(section)
        result.append(-section)
    return result


def piece_order(ranks, offsets):
    count = offsets * SEND
    share = count // ranks
    if share == SEND and offsets == 4:
        return [0, 1, 4, 5, 2, 3, 6, 7], share
    return list(range(count)), share


def nt(left, right):
    return lax.dot_general(left, right, (((1,), (1,)), ((), ())), preferred_element_type=F32)


def nn(left, right):
    return jnp.dot(left, right, preferred_element_type=F32)


def unit_of(rows):
    values = rows.astype(F32)
    return (values * lax.rsqrt(jnp.mean(values * values, axis=-1, keepdims=True) + EPS)).astype(BF16)


def block_at(index, size=BLK):
    return pl.ds(pl.multiple_of(index * size, size), size)


def rank_piece(rank, ranks, share, inner):
    if share == SEND and ranks == 4:
        return ((rank & 1) * 2 + (rank >> 1)) * SEND + inner
    return rank * share + inner


def in_hbm(*arrays):
    return [pltpu.with_memory_space_constraint(array, pltpu.HBM) for array in arrays]


def pick_kernel(ranks, share, send_ref, states_ref, *refs):
    outs, table, sems = refs[:share], refs[share], refs[share + 1]
    rank = lax.axis_index("tensor")
    fetch = pltpu.make_async_copy(send_ref, table, sems.at[share])
    fetch.start()
    fetch.wait()
    copies = []
    for inner, out_ref in enumerate(outs):
        piece = rank_piece(rank, ranks, share, inner)
        block = table[piece % SEND, piece // SEND]
        copies.append(
            pltpu.make_async_copy(states_ref.at[block_at(block), :], out_ref, sems.at[inner])
        )
        copies[-1].start()
    for copy in copies:
        copy.wait()


def pick_blocks(states, send, ranks, share):
    far = pl.BlockSpec(memory_space=pltpu.HBM)
    vmem = pl.BlockSpec(memory_space=pltpu.VMEM)
    return pl.pallas_call(
        functools.partial(pick_kernel, ranks, share),
        out_shape=[jax.ShapeDtypeStruct((BLK, states.shape[1]), BF16)] * share,
        in_specs=[far, far],
        out_specs=[vmem] * share,
        scratch_shapes=[
            pltpu.SMEM(send.shape, jnp.int32),
            pltpu.SemaphoreType.DMA((share + 1,)),
        ],
        compiler_params=pltpu.CompilerParams(vmem_limit_bytes=SMALL),
        cost_estimate=BRIEF,
        name="pick_blocks",
    )(*in_hbm(send, states))


def by_head(rows, heads):
    if heads == 1:
        return rows.astype(BF16)
    lane_head = lax.broadcasted_iota(jnp.int32, rows.shape, 1) // HD
    return jnp.concatenate(
        [jnp.where(lane_head == head, rows, 0.0) for head in range(heads)], axis=0
    ).astype(BF16)


def diagonal(stacked, heads):
    return jnp.concatenate(
        [
            stacked[head * HD : (head + 1) * HD, head * BLK : (head + 1) * BLK]
            for head in range(heads)
        ],
        axis=0,
    )


def put_pairs(paired, at, width, k_ref, v_ref, kt_ref, vt_ref):
    for index, entry in enumerate(at):
        rows = paired[index * BLK : (index + 1) * BLK]
        keys, values = rows[:, :width], rows[:, width:]
        k_ref[block_at(entry), :] = keys.astype(BF16)
        v_ref[block_at(entry), :] = values.astype(BF16)
        kt_ref[entry] = keys.T.astype(BF16)
        vt_ref[entry] = values.T.astype(BF16)


def own_kernel(*refs):
    sources = refs[:6]
    unit_ref, q_ref, g_ref, k_ref, v_ref, kt_ref, vt_ref, slab_ref, inverse_ref = refs[6:15]
    held, states_ref, sems = refs[15:20], refs[20], refs[21]
    cot_ref, wq_ref, wk_ref, wv_ref, wo_ref = held
    copies = []
    for index, (source, target) in enumerate(zip(sources, (states_ref,) + tuple(held))):
        copies.append(pltpu.make_async_copy(source, target, sems.at[index]))
        copies[-1].start()
    rows, feats = states_ref.shape
    width = wq_ref.shape[1]
    heads = width // HD
    tall = heads * BLK
    rank = lax.axis_index("tensor")
    copies[0].wait()
    for start in range(0, rows, CHUNK):
        values = states_ref[start : start + CHUNK, :].astype(F32)
        inverse = lax.rsqrt(jnp.mean(values * values, axis=-1, keepdims=True) + EPS)
        normed = values * inverse
        unit_ref[start : start + CHUNK, :] = normed.astype(BF16)
        slab = normed[:, :width]
        for index in range(1, feats // width):
            slab = jnp.where(rank == index, normed[:, index * width : (index + 1) * width], slab)
        slab_ref[start : start + CHUNK, :] = slab
        inverse_ref[start : start + CHUNK, :] = jnp.broadcast_to(inverse, slab.shape)
    for copy in copies[1:]:
        copy.wait()
    unit = unit_ref[...]
    queries = nn(unit, wq_ref[...])
    grads = nt(cot_ref[...], wo_ref[...])
    for block in range(rows // BLK):
        q_ref[block * tall : (block + 1) * tall, :] = by_head(
            queries[block * BLK : (block + 1) * BLK], heads
        )
        g_ref[block * tall : (block + 1) * tall, :] = by_head(
            grads[block * BLK : (block + 1) * BLK], heads
        )
    paired = nn(unit, jnp.concatenate([wk_ref[...], wv_ref[...]], axis=1))
    put_pairs(paired, range(rows // BLK), width, k_ref, v_ref, kt_ref, vt_ref)


def run_own(states, cot, weights):
    rows, feats = states.shape
    width = weights[0].shape[1]
    blocks = rows // BLK
    tall = blocks * (width // HD) * BLK
    vmem = pl.BlockSpec(memory_space=pltpu.VMEM)
    far = pl.BlockSpec(memory_space=pltpu.HBM)
    shape = jax.ShapeDtypeStruct
    return pl.pallas_call(
        own_kernel,
        out_shape=(
            shape((rows, feats), BF16),
            shape((tall, width), BF16),
            shape((tall, width), BF16),
            shape((rows, width), BF16),
            shape((rows, width), BF16),
            shape((blocks, width, BLK), BF16),
            shape((blocks, width, BLK), BF16),
            shape((rows, width), F32),
            shape((rows, width), F32),
            shape(cot.shape, BF16),
            *[shape(w.shape, BF16) for w in weights],
        ),
        in_specs=[far] * 6,
        out_specs=[vmem] * 14,
        scratch_shapes=[pltpu.VMEM((rows, feats), BF16), pltpu.SemaphoreType.DMA((6,))],
        compiler_params=pltpu.CompilerParams(vmem_limit_bytes=LIMIT),
        cost_estimate=BRIEF,
        name="own_rows",
    )(*in_hbm(states, cot, *weights))


def early_kernel(count, *refs):
    piece_refs, (wk_ref, wv_ref) = refs[:count], refs[count : count + 2]
    unit_ref, k_ref, v_ref, kt_ref, vt_ref = refs[count + 2 :]
    width = wk_ref.shape[1]
    at = 0
    for source in piece_refs:
        for start in range(0, source.shape[0], CHUNK):
            unit_ref[at : at + CHUNK, :] = unit_of(source[start : start + CHUNK, :])
            at += CHUNK
    wkv = jnp.concatenate([wk_ref[...], wv_ref[...]], axis=1)
    paired = nn(unit_ref[...], wkv)
    blocks = range(unit_ref.shape[0] // BLK)
    put_pairs(paired, blocks, width, k_ref, v_ref, kt_ref, vt_ref)


def run_early(pieces, w_key, w_value):
    inputs, count = len(pieces), sum(piece.shape[0] for piece in pieces) // BLK
    feats, width = w_key.shape
    vmem = pl.BlockSpec(memory_space=pltpu.VMEM)
    shape = jax.ShapeDtypeStruct
    return pl.pallas_call(
        functools.partial(early_kernel, inputs),
        out_shape=(
            shape((count * BLK, feats), BF16),
            shape((count * BLK, width), BF16),
            shape((count * BLK, width), BF16),
            shape((count, width, BLK), BF16),
            shape((count, width, BLK), BF16),
        ),
        in_specs=[vmem] * (inputs + 2),
        out_specs=[vmem] * 5,
        compiler_params=pltpu.CompilerParams(vmem_limit_bytes=LIMIT),
        cost_estimate=BRIEF,
        name="early_rows",
    )(*pieces, w_key, w_value)


def attend_kernel(cfg, near_ref, *refs):
    ranks, share, blocks, offsets, width, explicit, early = cfg
    early_refs, refs = refs[:5], refs[5:]
    count = (ranks - early) * share
    piece_refs = refs[:count]
    own_refs = refs[count : count + 7]
    cot_ref, wk_ref, wv_ref = refs[count + 7 : count + 10]
    refs = refs[count + 10 :]
    both_ref, dq_ref, mixed_ref = refs[:3]
    far_refs, half_refs = refs[3:5], refs[5:9]
    pool_ref, refs = refs[9], refs[10:]
    k_ref, v_ref, kt_ref, vt_ref, ka_ref, va_ref, dk_ref, dv_ref, near_table, near_sem = refs
    fetch = pltpu.make_async_copy(near_ref, near_table, near_sem)
    fetch.start()
    q_ref, g_ref, k_own, v_own, kt_own, vt_own = own_refs[1:]
    heads = width // HD
    tall = heads * BLK
    entries = blocks + offsets * SEND
    rank = lax.axis_index("tensor")

    own_rows = blocks * BLK
    k_ref[:own_rows, :] = k_own[...]
    v_ref[:own_rows, :] = v_own[...]
    kt_ref[:blocks] = kt_own[...]
    vt_ref[:blocks] = vt_own[...]
    wkv = jnp.concatenate([wk_ref[...], wv_ref[...]], axis=1)
    unit_e, k_e, v_e, kt_e, vt_e = early_refs
    for slot in range(early):
        for inner in range(share):
            entry = rank_piece(rank ^ slot, ranks, share, inner)
            index = slot * share + inner
            rows = slice(index * BLK, (index + 1) * BLK)
            pool_ref[block_at(entry), :] = unit_e[rows, :]
            k_ref[block_at(entry + blocks), :] = k_e[rows, :]
            v_ref[block_at(entry + blocks), :] = v_e[rows, :]
            kt_ref[entry + blocks] = kt_e[index]
            vt_ref[entry + blocks] = vt_e[index]
    late, places = [], []
    for slot in range(early, ranks):
        for inner in range(share):
            entry = rank_piece(rank ^ slot, ranks, share, inner)
            base = pl.multiple_of(entry * BLK, BLK)
            places.append(entry + blocks)
            source = piece_refs[(slot - early) * share + inner]
            for start in range(0, BLK, CHUNK):
                rows = unit_of(source[start : start + CHUNK, :])
                pool_ref[pl.ds(pl.multiple_of(base + start, CHUNK), CHUNK), :] = rows
                late.append(rows)
    paired = nn(jnp.concatenate(late, axis=0), wkv)
    put_pairs(paired, places, width, k_ref, v_ref, kt_ref, vt_ref)

    shrink = 1.0 / math.sqrt(HD)
    near = near_ref.shape[1]
    fetch.wait()
    for block in range(blocks):
        listed = [block] + [near_table[block, n] for n in range(near)]
        keys = jnp.concatenate([k_ref[block_at(e), :] for e in listed], axis=0)
        values = jnp.concatenate([v_ref[block_at(e), :] for e in listed], axis=0)
        keys_t = jnp.concatenate([kt_ref[e] for e in listed], axis=1)
        values_t = jnp.concatenate([vt_ref[e] for e in listed], axis=1)
        q_all = q_ref[block * tall : (block + 1) * tall, :]
        g_all = g_ref[block * tall : (block + 1) * tall, :]
        scores = nt(keys, q_all) * shrink
        powers = jnp.exp(scores - jnp.max(scores, axis=0, keepdims=True))
        weights = powers * (1.0 / jnp.sum(powers, axis=0, keepdims=True))
        low = weights.astype(BF16)
        mix = diagonal(nn(values_t, low), heads)
        mixed_ref[block * BLK : (block + 1) * BLK, :] = mix.T.astype(BF16)
        prob = nt(values, g_all)
        drop = jnp.sum(weights * prob, axis=0, keepdims=True)
        score_low = (weights * (prob - drop) * shrink).astype(BF16)
        dq = diagonal(nn(keys_t, score_low), heads)
        dq_ref[block * BLK : (block + 1) * BLK, :] = dq.T.astype(BF16)
        dk = nn(score_low, q_all)
        dv = nn(low, g_all)
        ka_ref[block * BLK : (block + 1) * BLK, :] = dk[:BLK]
        va_ref[block * BLK : (block + 1) * BLK, :] = dv[:BLK]
        dk_ref[block] = dk[BLK:]
        dv_ref[block] = dv[BLK:]

    ka_ref[own_rows:, :] = jnp.zeros((entries * BLK - own_rows, width), F32)
    va_ref[own_rows:, :] = jnp.zeros((entries * BLK - own_rows, width), F32)
    for block in range(blocks):
        for n in range(near):
            entry = block_at(near_table[block, n])
            ka_ref[entry, :] += dk_ref[block, n * BLK : (n + 1) * BLK]
            va_ref[entry, :] += dv_ref[block, n * BLK : (n + 1) * BLK]

    both_ref[:, :width] = ka_ref[...].astype(BF16)
    both_ref[:, width:] = va_ref[...].astype(BF16)
    grad_terms(explicit, own_refs[0], pool_ref, both_ref, dq_ref, mixed_ref, cot_ref, *half_refs)
    far_terms(blocks, pool_ref, both_ref, wk_ref, wv_ref, *far_refs)


def grad_terms(explicit, unit_ref, pool_ref, both_ref, dq_ref, mixed_ref, cot_ref, *refs):
    first_keep, first_send, second_keep, second_send = refs
    rows, width = dq_ref.shape

    def turned(ref, first, last):
        parts = [
            ref[start : start + BLK, :].astype(F32).T.astype(BF16)
            for start in range(first, last, BLK)
        ]
        return jnp.concatenate(parts, axis=1)

    unit = unit_ref[...]
    grad_q = nn(turned(dq_ref, 0, rows), unit)
    grad_out = nn(turned(mixed_ref, 0, rows), cot_ref[...])
    grad_kv = nn(turned(both_ref, 0, rows), unit)
    grad_kv = grad_kv + nn(turned(both_ref, rows, both_ref.shape[0]), pool_ref[...])
    grad_k, grad_v = grad_kv[:width], grad_kv[width:]
    by_dp = jnp.equal(lax.axis_index("dp") if explicit else 0, 1)
    by_dom = jnp.equal(lax.axis_index("dom") & 1 if explicit else 0, 1)
    first_keep[...] = jnp.where(by_dp, grad_k, grad_q).astype(BF16)
    first_send[...] = jnp.where(by_dp, grad_q, grad_k).astype(BF16)
    second_keep[...] = jnp.where(by_dom, grad_out, grad_v).astype(BF16)
    second_send[...] = jnp.where(by_dom, grad_v, grad_out).astype(BF16)


def run_attend(explicit, early, ranks, share, offsets, near, pieces, own, cot, w_key, w_value):
    rows, feats = own[0].shape
    blocks = rows // BLK
    width = w_key.shape[1]
    received = offsets * SEND
    entries = blocks + received
    vmem = pl.BlockSpec(memory_space=pltpu.VMEM)
    far = pl.BlockSpec(memory_space=pltpu.HBM)
    cfg = (ranks, share, blocks, offsets, width, explicit, EARLY)
    shape = jax.ShapeDtypeStruct
    return pl.pallas_call(
        functools.partial(attend_kernel, cfg),
        out_shape=[
            shape((entries * BLK, 2 * width), BF16),
            shape((rows, width), BF16),
            shape((rows, width), BF16),
            *[shape((feats // width // 2, offsets * (SEND * BLK + PAD), width), BF16)] * 2,
            *[shape((width, feats), BF16)] * 4,
        ],
        in_specs=[far] + [vmem] * (len(early) + len(pieces) + 10),
        out_specs=[vmem] * 9,
        scratch_shapes=[
            pltpu.VMEM((received * BLK, feats), BF16),
            pltpu.VMEM((entries * BLK, width), BF16),
            pltpu.VMEM((entries * BLK, width), BF16),
            pltpu.VMEM((entries, width, BLK), BF16),
            pltpu.VMEM((entries, width, BLK), BF16),
            pltpu.VMEM((entries * BLK, width), F32),
            pltpu.VMEM((entries * BLK, width), F32),
            pltpu.VMEM((blocks, near.shape[1] * BLK, width), F32),
            pltpu.VMEM((blocks, near.shape[1] * BLK, width), F32),
            pltpu.SMEM(near.shape, jnp.int32),
            pltpu.SemaphoreType.DMA(()),
        ],
        compiler_params=pltpu.CompilerParams(vmem_limit_bytes=LIMIT),
        cost_estimate=BRIEF,
        name="attention",
    )(*in_hbm(near), *early, *pieces, *own, cot, w_key, w_value)


def put(odd, upper, keep_ref, send_ref, row, values):
    count, width = values.shape[0], keep_ref.shape[2]
    for pair in range(values.shape[1] // width // 2):
        left = values[:, 2 * pair * width : (2 * pair + 1) * width]
        right = values[:, (2 * pair + 1) * width : (2 * pair + 2) * width]
        at = upper ^ pair
        keep_ref[at, row : row + count, :] = jnp.where(odd, right, left).astype(BF16)
        send_ref[at, row : row + count, :] = jnp.where(odd, left, right).astype(BF16)


def put_dots(keep_ref, send_ref, row, dots):
    width = keep_ref.shape[2]
    parts = []
    for dot in dots:
        for piece in range(BLK // width):
            parts.append(dot[:1, piece * width : (piece + 1) * width])
    parts.append(jnp.zeros((PAD - len(parts), width), F32))
    rows = jnp.concatenate(parts, axis=0).astype(BF16)
    for pair in range(keep_ref.shape[0]):
        keep_ref[pair, row : row + PAD, :] = rows
        send_ref[pair, row : row + PAD, :] = rows


def row_dot(term, ref, first):
    ones = jnp.ones((16, ref.shape[1]), BF16)
    product = (term * ref[first : first + BLK, :].astype(F32)).astype(BF16)
    return nt(ones, product)


def far_terms(blocks, pool_ref, both_ref, wk_ref, wv_ref, far_keep, far_send):
    rank = lax.axis_index("tensor")
    odd, upper = (rank & 1) == 1, rank >> 1
    rows, step = blocks * BLK, SEND * BLK
    wkv = jnp.concatenate([wk_ref[...], wv_ref[...]], axis=1)
    for index in range(pool_ref.shape[0] // step):
        first, at = index * step, index * (step + PAD)
        term = nt(both_ref[rows + first : rows + first + step, :], wkv)
        put(odd, upper, far_keep, far_send, at, term)
        dots = [
            row_dot(term[c * BLK : (c + 1) * BLK], pool_ref, first + c * BLK) for c in range(SEND)
        ]
        put_dots(far_keep, far_send, at + step, dots)


def own_terms_kernel(both_ref, unit_ref, dq_ref, mixed_ref, *refs):
    wq_ref, wk_ref, wv_ref, wo_ref, own_keep, own_send = refs
    rank = lax.axis_index("tensor")
    odd, upper = (rank & 1) == 1, rank >> 1
    rows, step = unit_ref.shape[0], 2 * BLK
    wkv = jnp.concatenate([wk_ref[...], wv_ref[...]], axis=1)
    dots = []
    for first in range(0, rows, step):
        last = first + step
        term = nt(both_ref[first:last, :], wkv) + nt(dq_ref[first:last, :], wq_ref[...])
        put(odd, upper, own_keep, own_send, first, term)
        dots += [row_dot(term[c * BLK : (c + 1) * BLK], unit_ref, first + c * BLK) for c in (0, 1)]
        update = nn(mixed_ref[first:last, :], wo_ref[...])
        put(odd, upper, own_keep, own_send, rows + PAD + first, update)
    put_dots(own_keep, own_send, rows, dots)


def run_own_terms(both, unit, dq, mixed, weights):
    rows, feats = unit.shape
    width = dq.shape[1]
    vmem = pl.BlockSpec(memory_space=pltpu.VMEM)
    own = jax.ShapeDtypeStruct((feats // width // 2, 2 * rows + PAD, width), BF16)
    return pl.pallas_call(
        own_terms_kernel,
        out_shape=(own, own),
        in_specs=[vmem] * 8,
        out_specs=[vmem] * 2,
        compiler_params=pltpu.CompilerParams(vmem_limit_bytes=LIMIT),
        cost_estimate=BRIEF,
        name="own_terms",
    )(both, unit, dq, mixed, *weights)


def returns_kernel(bounds, keep_ref, got_ref, last_ref, *outs):
    for (first, last), out_ref in zip(bounds, outs):
        total = keep_ref[0, first:last, :].astype(F32) + got_ref[0, first:last, :].astype(F32)
        out_ref[...] = (total + last_ref[first:last, :].astype(F32)).astype(BF16)


def run_returns(bounds, keep, got, last):
    vmem = pl.BlockSpec(memory_space=pltpu.VMEM)
    width = keep.shape[2]
    return pl.pallas_call(
        functools.partial(returns_kernel, bounds),
        out_shape=[jax.ShapeDtypeStruct((b - a, width), BF16) for a, b in bounds],
        in_specs=[vmem] * 3,
        out_specs=[vmem] * len(bounds),
        compiler_params=pltpu.CompilerParams(vmem_limit_bytes=SMALL),
        cost_estimate=BRIEF,
        name="returned_terms",
    )(keep, got, last)


def my_bits():
    dom = lax.axis_index("dom")
    return lax.axis_index("dp"), dom & 1, dom >> 1


def halve_kernel(bits, *refs):
    count = len(bits)
    ins, outs = refs[: 2 * count], refs[2 * count :]
    mine = my_bits()
    size = outs[0].shape[0]
    for index, bit in enumerate(bits):
        keep_ref, got_ref = ins[2 * index : 2 * index + 2]
        for side, name in enumerate((mine[bit], 1 - mine[bit])):
            at = block_at(name, size)
            total = keep_ref[at, :].astype(F32) + got_ref[at, :].astype(F32)
            outs[2 * index + side][...] = total.astype(BF16)


def run_halve(bits, *arrays):
    vmem = pl.BlockSpec(memory_space=pltpu.VMEM)
    rows, feats = arrays[0].shape
    return pl.pallas_call(
        functools.partial(halve_kernel, bits),
        out_shape=[jax.ShapeDtypeStruct((rows // 2, feats), BF16)] * len(arrays),
        in_specs=[vmem] * len(arrays),
        out_specs=[vmem] * len(arrays),
        compiler_params=pltpu.CompilerParams(vmem_limit_bytes=SMALL),
        cost_estimate=BRIEF,
        name="halve_grads",
    )(*arrays)


def total_kernel(*refs):
    out_ref = refs[-1]
    size = refs[0].shape[0]
    for index in range(len(refs) // 2):
        total = refs[2 * index][...].astype(F32) + refs[2 * index + 1][...].astype(F32)
        out_ref[index * size : (index + 1) * size, :] = total.astype(BF16)


def run_total(*arrays):
    vmem = pl.BlockSpec(memory_space=pltpu.VMEM)
    rows, feats = arrays[0].shape
    return pl.pallas_call(
        total_kernel,
        out_shape=jax.ShapeDtypeStruct((len(arrays) // 2 * rows, feats), BF16),
        in_specs=[vmem] * len(arrays),
        out_specs=vmem,
        compiler_params=pltpu.CompilerParams(vmem_limit_bytes=SMALL),
        cost_estimate=BRIEF,
        name="total_grads",
    )(*arrays)


def settle_kernel(mine_ref, got_ref, *outs):
    size = outs[0].shape[0]
    for index, out_ref in enumerate(outs):
        rows = slice(index * size, (index + 1) * size)
        total = mine_ref[rows, :].astype(F32) + got_ref[rows, :].astype(F32)
        out_ref[...] = total.astype(BF16)


def run_settle(mine, got):
    vmem = pl.BlockSpec(memory_space=pltpu.VMEM)
    rows, feats = mine.shape
    return pl.pallas_call(
        settle_kernel,
        out_shape=[jax.ShapeDtypeStruct((rows // 2, feats), BF16)] * 2,
        in_specs=[vmem] * 2,
        out_specs=[vmem] * 2,
        compiler_params=pltpu.CompilerParams(vmem_limit_bytes=SMALL),
        cost_estimate=BRIEF,
        name="settle_grads",
    )(mine, got)


def join_kernel(bits, *refs):
    count = len(bits)
    outs = refs[-count:]
    mine = my_bits()
    size = refs[0].shape[0]
    for index, bit in enumerate(bits):
        outs[index][block_at(mine[bit], size), :] = refs[2 * index][...]
        outs[index][block_at(1 - mine[bit], size), :] = refs[2 * index + 1][...]


def run_join(bits, *arrays):
    vmem = pl.BlockSpec(memory_space=pltpu.VMEM)
    rows, feats = arrays[0].shape
    return pl.pallas_call(
        functools.partial(join_kernel, bits),
        out_shape=[jax.ShapeDtypeStruct((2 * rows, feats), BF16)] * len(bits),
        in_specs=[vmem] * len(arrays),
        out_specs=[vmem] * len(bits),
        compiler_params=pltpu.CompilerParams(vmem_limit_bytes=SMALL),
        cost_estimate=BRIEF,
        name="join_grads",
    )(*arrays)


def own_sum_kernel(keep_ref, got_ref, last_ref, update_ref, unit_ref):
    rows = update_ref.shape[0]

    def total(first, last):
        both = keep_ref[0, first:last, :].astype(F32) + got_ref[0, first:last, :].astype(F32)
        return both + last_ref[first:last, :].astype(F32)

    unit_ref[...] = total(0, rows + PAD)
    update_ref[...] = total(rows + PAD, 2 * rows + PAD).astype(BF16)


def run_own_sum(rows, keep, got, last):
    width = last.shape[1]
    vmem = pl.BlockSpec(memory_space=pltpu.VMEM)
    shape = jax.ShapeDtypeStruct
    return pl.pallas_call(
        own_sum_kernel,
        out_shape=(shape((rows, width), BF16), shape((rows + PAD, width), F32)),
        in_specs=[vmem] * 3,
        out_specs=[vmem] * 2,
        compiler_params=pltpu.CompilerParams(vmem_limit_bytes=SMALL),
        cost_estimate=BRIEF,
        name="own_sum",
    )(keep, got, last)


def finish_kernel(cfg, *refs):
    blocks, offsets, width, feats, spread = cfg
    send_ref, sum_ref, slab_ref, inverse_ref = refs[:4]
    far_refs = refs[4 : 4 + len(spread)]
    branch_ref, unit_ref, table, sem = refs[4 + len(spread) :]
    fetch = pltpu.make_async_copy(send_ref, table, sem)
    fetch.start()
    own_rows = blocks * BLK
    sub = BLK // width
    group = SEND * BLK + PAD

    unit_ref[...] = sum_ref[:own_rows, :]
    dots = sum_ref[own_rows:, :]
    at_row = lax.broadcasted_iota(jnp.int32, (PAD, width), 0)
    fetch.wait()
    for ref, members in zip(far_refs, spread):
        for position, offset in enumerate(members):
            first = position * group
            extra = ref[first + SEND * BLK : first + group, :].astype(F32)
            for c in range(SEND):
                block = table[c, offset]
                rows = ref[first + c * BLK : first + (c + 1) * BLK, :].astype(F32)
                unit_ref[block_at(block), :] += rows
                for piece in range(sub):
                    line = extra[c * sub + piece : c * sub + piece + 1, :]
                    dots = dots + jnp.where(at_row == block * sub + piece, line, 0.0)
    for block in range(blocks):
        rows = slice(block * BLK, (block + 1) * BLK)
        line = jnp.concatenate(
            [dots[block * sub + piece : block * sub + piece + 1, :] for piece in range(sub)], axis=1
        )
        mean = jnp.broadcast_to(line * (1.0 / feats), (BLK, BLK)).T[:, :width]
        branch = inverse_ref[rows, :] * (unit_ref[rows, :] - slab_ref[rows, :] * mean)
        branch_ref[rows, :] = branch.astype(BF16)


def run_finish(feats, send, own_sum, slab, inverse, far, spread):
    rows, width = slab.shape
    vmem = pl.BlockSpec(memory_space=pltpu.VMEM)
    hbm = pl.BlockSpec(memory_space=pltpu.HBM)
    cfg = (rows // BLK, send.shape[1], width, feats, spread)
    return pl.pallas_call(
        functools.partial(finish_kernel, cfg),
        out_shape=jax.ShapeDtypeStruct((rows, width), BF16),
        in_specs=[hbm] + [vmem] * (3 + len(far)),
        out_specs=vmem,
        scratch_shapes=[
            pltpu.VMEM((rows, width), F32),
            pltpu.SMEM(send.shape, jnp.int32),
            pltpu.SemaphoreType.DMA(()),
        ],
        compiler_params=pltpu.CompilerParams(vmem_limit_bytes=SMALL),
        cost_estimate=BRIEF,
        name="finish",
    )(*in_hbm(send), own_sum, slab, inverse, *far)


def grads_kernel(factor, *refs):
    first_held, first_got, second_held, second_got, q_ref, k_ref, v_ref, o_ref = refs
    dp, low, _ = my_bits()
    first, second = jnp.equal(dp, 1), jnp.equal(low, 1)

    def picked(flag, left, right, start):
        columns = slice(start, start + BLK)
        return jnp.where(flag, left[:, columns].astype(F32), right[:, columns].astype(F32)) * factor

    for start in range(0, q_ref.shape[0], BLK):
        rows = slice(start, start + BLK)
        q_ref[rows, :] = picked(first, first_got, first_held, start).T
        k_ref[rows, :] = picked(first, first_held, first_got, start).T
        v_ref[rows, :] = picked(second, second_got, second_held, start).T
        o_ref[:, rows] = picked(second, second_held, second_got, start)


def run_grads(factor, *arrays):
    width, feats = arrays[0].shape
    vmem = pl.BlockSpec(memory_space=pltpu.VMEM)
    tall = jax.ShapeDtypeStruct((feats, width), F32)
    return pl.pallas_call(
        functools.partial(grads_kernel, factor),
        out_shape=(tall, tall, tall, jax.ShapeDtypeStruct((width, feats), F32)),
        in_specs=[vmem] * 4,
        out_specs=[vmem] * 4,
        compiler_params=pltpu.CompilerParams(vmem_limit_bytes=SMALL),
        cost_estimate=BRIEF,
        name="weight_grads",
    )(*arrays)


def swap(array, axis, bit):
    return lax.ppermute(array, axis, [(i, i ^ bit) for i in range(lax.axis_size(axis))])


def shifted(array, axis, distance):
    size = lax.axis_size(axis)
    return lax.ppermute(array, axis, [(i, (i + distance) % size) for i in range(size)])


def added(left, right):
    return (left.astype(F32) + right.astype(F32)).astype(BF16)


def after(values, *earlier):
    held = lax.optimization_barrier((values, earlier))
    return held[0]


def narrow(keep, got, bit):
    while keep.shape[0] > 2:
        summed = added(keep, got)
        keep, send = summed[0::2], summed[1::2]
        got = swap(send, "tensor", bit)
        bit *= 2
    return keep, got, bit


def body(states, w_query, w_key, w_value, w_out, send_blocks, neighbor_blocks, cotangent):
    replicas, node_count, feats = states.shape
    width = w_query.shape[1]
    ranks = lax.axis_size("tensor")
    parts = lax.axis_size("dom")
    explicit = parts == 4 and lax.axis_size("dp") == 2
    offsets = offset_list(HOPS)
    order, share = piece_order(ranks, len(offsets))
    send = send_blocks[0].T
    weights = (w_query, w_key, w_value, w_out)
    flat_states = states.reshape(-1, feats)
    flat_cot = cotangent.reshape(-1, feats)

    leaving = pick_blocks(flat_states, send, ranks, share)
    route = []
    for p in range(parts):
        for r in range(ranks):
            distance = offsets[order[r * share] // SEND]
            route.append((p * ranks + r, ((p + distance) % parts) * ranks + r))
    levels = []
    bit = 1
    while bit < ranks:
        levels.append(bit)
        bit *= 2
    arrived = [lax.ppermute(block, ("dom", "tensor"), route) for block in leaving]
    own = run_own(flat_states, flat_cot, weights)
    arrived[0] = after(arrived[0], own[0])
    unit, slab, inverse, cot = own[0], own[7], own[8], own[9]
    weights = own[10:]
    first_pieces = list(arrived)
    wide = [swap(block, "tensor", levels[-1]) for block in arrived]
    close = after(first_pieces, *arrived)
    close = [swap(half, "tensor", 1) for block in close for half in jnp.split(block, 2)]
    early = run_early(first_pieces + close, weights[1], weights[2])
    held = {levels[-1]: after(wide, early[0])}
    for bit in reversed(levels[:-1]):
        for slot in list(held):
            held[slot ^ bit] = [swap(block, "tensor", bit) for block in held[slot]]
    for bit in levels[1:-1]:
        held[bit] = [swap(block, "tensor", bit) for block in first_pieces]
        held[bit ^ 1] = [swap(block, "tensor", 1) for block in held[bit]]
    pieces = [block for slot in range(EARLY, ranks) for block in held[slot]]
    count = len(offsets)
    both, dq, mixed, far_keep, far_send, *halves = run_attend(
        explicit,
        early,
        ranks,
        share,
        count,
        neighbor_blocks,
        pieces,
        own[:7],
        cot,
        weights[1],
        weights[2],
    )
    total_rows = replicas * node_count * lax.axis_size("dp") * parts
    factor = 1.0 / math.sqrt(total_rows)

    if explicit:
        first, second = swap(halves[1], "dp", 1), swap(halves[3], "dom", 1)
    far_keep, far_got, bit = narrow(far_keep, swap(far_send, "tensor", 1), 2)
    own_keep, own_send = run_own_terms(both, unit, dq, mixed, weights)
    own_keep, own_got, bit = narrow(own_keep, swap(own_send, "tensor", 1), 2)
    far_out = added(far_keep[1], far_got[1])
    far_last = swap(far_out, "tensor", bit)
    if explicit:
        first, second = after(first, far_out, own_send), after(second, far_out, own_send)
        halves = run_halve((1, 0), halves[0], first, halves[2], second)
        first, second = swap(halves[1], "dom", 1), swap(halves[3], "dp", 1)
        total = run_total(halves[0], first, halves[2], second)
        got = swap(total, "dom", 2)
        own_got = after(own_got, total)
    own_out = added(own_keep[1], own_got[1])
    own_last = swap(own_out, "tensor", bit)
    far_last = after(far_last, own_out)

    group = SEND * BLK + PAD
    spread = []
    for index, distance in enumerate(offsets):
        for members in spread:
            if (offsets[members[0]] - distance) % parts == 0 and members[-1] == index - 1:
                members.append(index)
                break
        else:
            spread.append([index])
    spread = tuple(tuple(members) for members in spread)
    bounds = tuple((members[0] * group, (members[-1] + 1) * group) for members in spread)
    far_sums = run_returns(bounds, far_keep, far_got, far_last)
    returned = [
        shifted(part, "dom", -offsets[members[0]]) for part, members in zip(far_sums, spread)
    ]
    own_last = after(own_last, far_sums)
    update, own_sum = run_own_sum(replicas * node_count, own_keep, own_got, own_last)
    if explicit:
        held = run_settle(total, after(got, own_sum))
        first, second = swap(held[0], "dom", 1), swap(held[1], "dp", 1)
        first = after(first, returned)
        held = run_join((1, 0), held[0], first, held[1], second)
        first, second = swap(held[0], "dp", 1), swap(held[1], "dom", 1)
    branch = run_finish(feats, send, own_sum, slab, inverse, returned, spread)
    if explicit:
        first = after(first, branch)
        grads = run_grads(factor, held[0], first, held[1], second)
    else:
        summed = [lax.psum(half.astype(F32), ("dp", "dom")) * factor for half in halves]
        grads = (summed[0].T, summed[1].T, summed[2].T, summed[3])
    shape = (replicas, node_count, width)
    return (update.reshape(shape), branch.reshape(shape), *grads)


def solution(mesh):
    placed = (
        P("dp", "dom", None),
        P(None, "tensor"),
        P(None, "tensor"),
        P(None, "tensor"),
        P("tensor", None),
        P("dom", None, None),
        P("dom", None),
        P("dp", "dom", None),
    )
    return jax.shard_map(
        body,
        mesh=mesh,
        in_specs=placed,
        out_specs=(
            P("dp", "dom", "tensor"),
            P("dp", "dom", "tensor"),
            P(None, "tensor"),
            P(None, "tensor"),
            P(None, "tensor"),
            P("tensor", None),
        ),
        check_vma=False,
    )
```

```python
import functools
import math

import jax
import jax.numpy as jnp
from jax import lax
from jax.experimental import pallas as pl
from jax.experimental.pallas import tpu as pltpu
from jax.sharding import PartitionSpec as P

BLK = 128
HOPS = 2
SEND = 2
HD = 64
PAD = 16
EARLY = 2
EPS = 1e-05
LIMIT = 24 * 1024 * 1024
SMALL = 8 * 1024 * 1024
CHUNK = 64
BRIEF = pl.CostEstimate(flops=1, bytes_accessed=1, transcendentals=0)
F32 = jnp.float32
BF16 = jnp.bfloat16


def offset_list(hops):
    result = []
    for section in range(1, hops + 1):
        result.append(section)
        result.append(-section)
    return result


def piece_order(ranks, offsets):
    count = offsets * SEND
    share = count // ranks
    if share == SEND and offsets == 4:
        return [0, 1, 4, 5, 2, 3, 6, 7], share
    return list(range(count)), share


def nt(left, right):
    return lax.dot_general(left, right, (((1,), (1,)), ((), ())), preferred_element_type=F32)


def nn(left, right):
    return jnp.dot(left, right, preferred_element_type=F32)


def unit_of(rows):
    values = rows.astype(F32)
    return (values * lax.rsqrt(jnp.mean(values * values, axis=-1, keepdims=True) + EPS)).astype(BF16)


def block_at(index, size=BLK):
    return pl.ds(pl.multiple_of(index * size, size), size)


def rank_piece(rank, ranks, share, inner):
    if share == SEND and ranks == 4:
        return ((rank & 1) * 2 + (rank >> 1)) * SEND + inner
    return rank * share + inner


def in_hbm(*arrays):
    return [pltpu.with_memory_space_constraint(array, pltpu.HBM) for array in arrays]


def pick_kernel(ranks, share, send_ref, states_ref, *refs):
    outs, table, sems = refs[:share], refs[share], refs[share + 1]
    rank = lax.axis_index("tensor")
    fetch = pltpu.make_async_copy(send_ref, table, sems.at[share])
    fetch.start()
    fetch.wait()
    copies = []
    for inner, out_ref in enumerate(outs):
        piece = rank_piece(rank, ranks, share, inner)
        block = table[piece % SEND, piece // SEND]
        copies.append(
            pltpu.make_async_copy(states_ref.at[block_at(block), :], out_ref, sems.at[inner])
        )
        copies[-1].start()
    for copy in copies:
        copy.wait()


def pick_blocks(states, send, ranks, share):
    far = pl.BlockSpec(memory_space=pltpu.HBM)
    vmem = pl.BlockSpec(memory_space=pltpu.VMEM)
    return pl.pallas_call(
        functools.partial(pick_kernel, ranks, share),
        out_shape=[jax.ShapeDtypeStruct((BLK, states.shape[1]), BF16)] * share,
        in_specs=[far, far],
        out_specs=[vmem] * share,
        scratch_shapes=[
            pltpu.SMEM(send.shape, jnp.int32),
            pltpu.SemaphoreType.DMA((share + 1,)),
        ],
        compiler_params=pltpu.CompilerParams(vmem_limit_bytes=SMALL),
        cost_estimate=BRIEF,
        name="pick_blocks",
    )(*in_hbm(send, states))


def by_head(rows, heads):
    if heads == 1:
        return rows.astype(BF16)
    lane_head = lax.broadcasted_iota(jnp.int32, rows.shape, 1) // HD
    return jnp.concatenate(
        [jnp.where(lane_head == head, rows, 0.0) for head in range(heads)], axis=0
    ).astype(BF16)


def diagonal(stacked, heads):
    return jnp.concatenate(
        [
            stacked[head * HD : (head + 1) * HD, head * BLK : (head + 1) * BLK]
            for head in range(heads)
        ],
        axis=0,
    )


def put_pairs(paired, at, width, k_ref, v_ref, kt_ref, vt_ref):
    for index, entry in enumerate(at):
        rows = paired[index * BLK : (index + 1) * BLK]
        keys, values = rows[:, :width], rows[:, width:]
        k_ref[block_at(entry), :] = keys.astype(BF16)
        v_ref[block_at(entry), :] = values.astype(BF16)
        kt_ref[entry] = keys.T.astype(BF16)
        vt_ref[entry] = values.T.astype(BF16)


def own_kernel(*refs):
    sources = refs[:6]
    unit_ref, q_ref, g_ref, k_ref, v_ref, kt_ref, vt_ref, slab_ref, inverse_ref = refs[6:15]
    held, states_ref, sems = refs[15:20], refs[20], refs[21]
    cot_ref, wq_ref, wk_ref, wv_ref, wo_ref = held
    copies = []
    for index, (source, target) in enumerate(zip(sources, (states_ref,) + tuple(held))):
        copies.append(pltpu.make_async_copy(source, target, sems.at[index]))
        copies[-1].start()
    rows, feats = states_ref.shape
    width = wq_ref.shape[1]
    heads = width // HD
    tall = heads * BLK
    rank = lax.axis_index("tensor")
    copies[0].wait()
    for start in range(0, rows, CHUNK):
        values = states_ref[start : start + CHUNK, :].astype(F32)
        inverse = lax.rsqrt(jnp.mean(values * values, axis=-1, keepdims=True) + EPS)
        normed = values * inverse
        unit_ref[start : start + CHUNK, :] = normed.astype(BF16)
        slab = normed[:, :width]
        for index in range(1, feats // width):
            slab = jnp.where(rank == index, normed[:, index * width : (index + 1) * width], slab)
        slab_ref[start : start + CHUNK, :] = slab
        inverse_ref[start : start + CHUNK, :] = jnp.broadcast_to(inverse, slab.shape)
    for copy in copies[1:]:
        copy.wait()
    unit = unit_ref[...]
    queries = nn(unit, wq_ref[...])
    grads = nt(cot_ref[...], wo_ref[...])
    for block in range(rows // BLK):
        q_ref[block * tall : (block + 1) * tall, :] = by_head(
            queries[block * BLK : (block + 1) * BLK], heads
        )
        g_ref[block * tall : (block + 1) * tall, :] = by_head(
            grads[block * BLK : (block + 1) * BLK], heads
        )
    paired = nn(unit, jnp.concatenate([wk_ref[...], wv_ref[...]], axis=1))
    put_pairs(paired, range(rows // BLK), width, k_ref, v_ref, kt_ref, vt_ref)


def run_own(states, cot, weights):
    rows, feats = states.shape
    width = weights[0].shape[1]
    blocks = rows // BLK
    tall = blocks * (width // HD) * BLK
    vmem = pl.BlockSpec(memory_space=pltpu.VMEM)
    far = pl.BlockSpec(memory_space=pltpu.HBM)
    shape = jax.ShapeDtypeStruct
    return pl.pallas_call(
        own_kernel,
        out_shape=(
            shape((rows, feats), BF16),
            shape((tall, width), BF16),
            shape((tall, width), BF16),
            shape((rows, width), BF16),
            shape((rows, width), BF16),
            shape((blocks, width, BLK), BF16),
            shape((blocks, width, BLK), BF16),
            shape((rows, width), F32),
            shape((rows, width), F32),
            shape(cot.shape, BF16),
            *[shape(w.shape, BF16) for w in weights],
        ),
        in_specs=[far] * 6,
        out_specs=[vmem] * 14,
        scratch_shapes=[pltpu.VMEM((rows, feats), BF16), pltpu.SemaphoreType.DMA((6,))],
        compiler_params=pltpu.CompilerParams(vmem_limit_bytes=LIMIT),
        cost_estimate=BRIEF,
        name="own_rows",
    )(*in_hbm(states, cot, *weights))


def early_kernel(count, *refs):
    piece_refs, (wk_ref, wv_ref) = refs[:count], refs[count : count + 2]
    unit_ref, k_ref, v_ref, kt_ref, vt_ref = refs[count + 2 :]
    width = wk_ref.shape[1]
    at = 0
    for source in piece_refs:
        for start in range(0, source.shape[0], CHUNK):
            unit_ref[at : at + CHUNK, :] = unit_of(source[start : start + CHUNK, :])
            at += CHUNK
    wkv = jnp.concatenate([wk_ref[...], wv_ref[...]], axis=1)
    paired = nn(unit_ref[...], wkv)
    blocks = range(unit_ref.shape[0] // BLK)
    put_pairs(paired, blocks, width, k_ref, v_ref, kt_ref, vt_ref)


def run_early(pieces, w_key, w_value):
    inputs, count = len(pieces), sum(piece.shape[0] for piece in pieces) // BLK
    feats, width = w_key.shape
    vmem = pl.BlockSpec(memory_space=pltpu.VMEM)
    shape = jax.ShapeDtypeStruct
    return pl.pallas_call(
        functools.partial(early_kernel, inputs),
        out_shape=(
            shape((count * BLK, feats), BF16),
            shape((count * BLK, width), BF16),
            shape((count * BLK, width), BF16),
            shape((count, width, BLK), BF16),
            shape((count, width, BLK), BF16),
        ),
        in_specs=[vmem] * (inputs + 2),
        out_specs=[vmem] * 5,
        compiler_params=pltpu.CompilerParams(vmem_limit_bytes=LIMIT),
        cost_estimate=BRIEF,
        name="early_rows",
    )(*pieces, w_key, w_value)


def attend_kernel(cfg, near_ref, *refs):
    ranks, share, blocks, offsets, width, explicit, early = cfg
    early_refs, refs = refs[:5], refs[5:]
    count = (ranks - early) * share
    piece_refs = refs[:count]
    own_refs = refs[count : count + 7]
    cot_ref, wk_ref, wv_ref = refs[count + 7 : count + 10]
    refs = refs[count + 10 :]
    both_ref, dq_ref, mixed_ref = refs[:3]
    far_refs, half_refs = refs[3:5], refs[5:9]
    pool_ref, refs = refs[9], refs[10:]
    k_ref, v_ref, kt_ref, vt_ref, ka_ref, va_ref, dk_ref, dv_ref = refs[:8]
    score_ref, prob_ref, low_ref, change_ref, near_table, near_sem = refs[8:]
    fetch = pltpu.make_async_copy(near_ref, near_table, near_sem)
    fetch.start()
    q_ref, g_ref, k_own, v_own, kt_own, vt_own = own_refs[1:]
    heads = width // HD
    tall = heads * BLK
    entries = blocks + offsets * SEND
    rank = lax.axis_index("tensor")

    own_rows = blocks * BLK
    k_ref[:own_rows, :] = k_own[...]
    v_ref[:own_rows, :] = v_own[...]
    kt_ref[:blocks] = kt_own[...]
    vt_ref[:blocks] = vt_own[...]
    wkv = jnp.concatenate([wk_ref[...], wv_ref[...]], axis=1)
    unit_e, k_e, v_e, kt_e, vt_e = early_refs
    for slot in range(early):
        for inner in range(share):
            entry = rank_piece(rank ^ slot, ranks, share, inner)
            index = slot * share + inner
            rows = slice(index * BLK, (index + 1) * BLK)
            pool_ref[block_at(entry), :] = unit_e[rows, :]
            k_ref[block_at(entry + blocks), :] = k_e[rows, :]
            v_ref[block_at(entry + blocks), :] = v_e[rows, :]
            kt_ref[entry + blocks] = kt_e[index]
            vt_ref[entry + blocks] = vt_e[index]
    late, places = [], []
    for slot in range(early, ranks):
        for inner in range(share):
            entry = rank_piece(rank ^ slot, ranks, share, inner)
            base = pl.multiple_of(entry * BLK, BLK)
            places.append(entry + blocks)
            source = piece_refs[(slot - early) * share + inner]
            for start in range(0, BLK, CHUNK):
                rows = unit_of(source[start : start + CHUNK, :])
                pool_ref[pl.ds(pl.multiple_of(base + start, CHUNK), CHUNK), :] = rows
                late.append(rows)
    paired = nn(jnp.concatenate(late, axis=0), wkv)
    put_pairs(paired, places, width, k_ref, v_ref, kt_ref, vt_ref)

    shrink = 1.0 / math.sqrt(HD)
    near = near_ref.shape[1]
    fetch.wait()
    listed = [[block] + [near_table[block, n] for n in range(near)] for block in range(blocks)]

    def open_block(block):
        keys = jnp.concatenate([k_ref[block_at(e), :] for e in listed[block]], axis=0)
        values = jnp.concatenate([v_ref[block_at(e), :] for e in listed[block]], axis=0)
        score_ref[block] = nt(keys, q_ref[block * tall : (block + 1) * tall, :]) * shrink
        prob_ref[block] = nt(values, g_ref[block * tall : (block + 1) * tall, :])

    def weigh_block(block):
        spans = [slice(n * CHUNK, (n + 1) * CHUNK) for n in range((near + 1) * BLK // CHUNK)]
        highest = jnp.max(score_ref[block, spans[0], :], axis=0, keepdims=True)
        for span in spans[1:]:
            rows = jnp.max(score_ref[block, span, :], axis=0, keepdims=True)
            highest = jnp.maximum(highest, rows)
        total, drop = jnp.zeros_like(highest), jnp.zeros_like(highest)
        for span in spans:
            powers = jnp.exp(score_ref[block, span, :] - highest)
            score_ref[block, span, :] = powers
            total = total + jnp.sum(powers, axis=0, keepdims=True)
            drop = drop + jnp.sum(powers * prob_ref[block, span, :], axis=0, keepdims=True)
        scale = 1.0 / total
        drop = drop * scale
        for span in spans:
            weights = score_ref[block, span, :] * scale
            low_ref[block, span, :] = weights.astype(BF16)
            change = weights * (prob_ref[block, span, :] - drop) * shrink
            change_ref[block, span, :] = change.astype(BF16)

    def close_block(block):
        rows = slice(block * BLK, (block + 1) * BLK)
        keys_t = jnp.concatenate([kt_ref[e] for e in listed[block]], axis=1)
        values_t = jnp.concatenate([vt_ref[e] for e in listed[block]], axis=1)
        low, change = low_ref[block], change_ref[block]
        mixed_ref[rows, :] = diagonal(nn(values_t, low), heads).T.astype(BF16)
        dq_ref[rows, :] = diagonal(nn(keys_t, change), heads).T.astype(BF16)
        dk = nn(change, q_ref[block * tall : (block + 1) * tall, :])
        dv = nn(low, g_ref[block * tall : (block + 1) * tall, :])
        ka_ref[rows, :] = dk[:BLK]
        va_ref[rows, :] = dv[:BLK]
        dk_ref[block] = dk[BLK:]
        dv_ref[block] = dv[BLK:]

    open_block(0)
    for block in range(blocks):
        if block + 1 < blocks:
            open_block(block + 1)
        weigh_block(block)
        if block:
            close_block(block - 1)
    close_block(blocks - 1)

    ka_ref[own_rows:, :] = jnp.zeros((entries * BLK - own_rows, width), F32)
    va_ref[own_rows:, :] = jnp.zeros((entries * BLK - own_rows, width), F32)
    for block in range(blocks):
        for n in range(near):
            entry = block_at(listed[block][n + 1])
            ka_ref[entry, :] += dk_ref[block, n * BLK : (n + 1) * BLK]
            va_ref[entry, :] += dv_ref[block, n * BLK : (n + 1) * BLK]

    both_ref[:, :width] = ka_ref[...].astype(BF16)
    both_ref[:, width:] = va_ref[...].astype(BF16)
    grad_terms(explicit, own_refs[0], pool_ref, both_ref, dq_ref, mixed_ref, cot_ref, *half_refs)
    far_terms(blocks, pool_ref, both_ref, wk_ref, wv_ref, *far_refs)


def grad_terms(explicit, unit_ref, pool_ref, both_ref, dq_ref, mixed_ref, cot_ref, *refs):
    first_keep, first_send, second_keep, second_send = refs
    rows, width = dq_ref.shape

    def turned(ref, first, last):
        parts = [
            ref[start : start + BLK, :].astype(F32).T.astype(BF16)
            for start in range(first, last, BLK)
        ]
        return jnp.concatenate(parts, axis=1)

    unit = unit_ref[...]
    grad_q = nn(turned(dq_ref, 0, rows), unit)
    grad_out = nn(turned(mixed_ref, 0, rows), cot_ref[...])
    grad_kv = nn(turned(both_ref, 0, rows), unit)
    grad_kv = grad_kv + nn(turned(both_ref, rows, both_ref.shape[0]), pool_ref[...])
    grad_k, grad_v = grad_kv[:width], grad_kv[width:]
    by_dp = jnp.equal(lax.axis_index("dp") if explicit else 0, 1)
    by_dom = jnp.equal(lax.axis_index("dom") & 1 if explicit else 0, 1)
    first_keep[...] = jnp.where(by_dp, grad_k, grad_q).astype(BF16)
    first_send[...] = jnp.where(by_dp, grad_q, grad_k).astype(BF16)
    second_keep[...] = jnp.where(by_dom, grad_out, grad_v).astype(BF16)
    second_send[...] = jnp.where(by_dom, grad_v, grad_out).astype(BF16)


def run_attend(explicit, early, ranks, share, offsets, near, pieces, own, cot, w_key, w_value):
    rows, feats = own[0].shape
    blocks = rows // BLK
    width = w_key.shape[1]
    received = offsets * SEND
    entries = blocks + received
    listed, tall = (near.shape[1] + 1) * BLK, width // HD * BLK
    vmem = pl.BlockSpec(memory_space=pltpu.VMEM)
    far = pl.BlockSpec(memory_space=pltpu.HBM)
    cfg = (ranks, share, blocks, offsets, width, explicit, EARLY)
    shape = jax.ShapeDtypeStruct
    return pl.pallas_call(
        functools.partial(attend_kernel, cfg),
        out_shape=[
            shape((entries * BLK, 2 * width), BF16),
            shape((rows, width), BF16),
            shape((rows, width), BF16),
            *[shape((feats // width // 2, offsets * (SEND * BLK + PAD), width), BF16)] * 2,
            *[shape((width, feats), BF16)] * 4,
        ],
        in_specs=[far] + [vmem] * (len(early) + len(pieces) + 10),
        out_specs=[vmem] * 9,
        scratch_shapes=[
            pltpu.VMEM((received * BLK, feats), BF16),
            pltpu.VMEM((entries * BLK, width), BF16),
            pltpu.VMEM((entries * BLK, width), BF16),
            pltpu.VMEM((entries, width, BLK), BF16),
            pltpu.VMEM((entries, width, BLK), BF16),
            pltpu.VMEM((entries * BLK, width), F32),
            pltpu.VMEM((entries * BLK, width), F32),
            pltpu.VMEM((blocks, near.shape[1] * BLK, width), F32),
            pltpu.VMEM((blocks, near.shape[1] * BLK, width), F32),
            *[pltpu.VMEM((blocks, listed, tall), F32)] * 2,
            *[pltpu.VMEM((blocks, listed, tall), BF16)] * 2,
            pltpu.SMEM(near.shape, jnp.int32),
            pltpu.SemaphoreType.DMA(()),
        ],
        compiler_params=pltpu.CompilerParams(vmem_limit_bytes=LIMIT),
        cost_estimate=BRIEF,
        name="attention",
    )(*in_hbm(near), *early, *pieces, *own, cot, w_key, w_value)


def put(odd, upper, keep_ref, send_ref, row, values):
    count, width = values.shape[0], keep_ref.shape[2]
    for pair in range(values.shape[1] // width // 2):
        left = values[:, 2 * pair * width : (2 * pair + 1) * width]
        right = values[:, (2 * pair + 1) * width : (2 * pair + 2) * width]
        at = upper ^ pair
        keep_ref[at, row : row + count, :] = jnp.where(odd, right, left).astype(BF16)
        send_ref[at, row : row + count, :] = jnp.where(odd, left, right).astype(BF16)


def put_dots(keep_ref, send_ref, row, dots):
    width = keep_ref.shape[2]
    parts = []
    for dot in dots:
        for piece in range(BLK // width):
            parts.append(dot[:1, piece * width : (piece + 1) * width])
    parts.append(jnp.zeros((PAD - len(parts), width), F32))
    rows = jnp.concatenate(parts, axis=0).astype(BF16)
    for pair in range(keep_ref.shape[0]):
        keep_ref[pair, row : row + PAD, :] = rows
        send_ref[pair, row : row + PAD, :] = rows


def row_dot(term, ref, first):
    ones = jnp.ones((16, ref.shape[1]), BF16)
    product = (term * ref[first : first + BLK, :].astype(F32)).astype(BF16)
    return nt(ones, product)


def far_terms(blocks, pool_ref, both_ref, wk_ref, wv_ref, far_keep, far_send):
    rank = lax.axis_index("tensor")
    odd, upper = (rank & 1) == 1, rank >> 1
    rows, step = blocks * BLK, SEND * BLK
    wkv = jnp.concatenate([wk_ref[...], wv_ref[...]], axis=1)
    for index in range(pool_ref.shape[0] // step):
        first, at = index * step, index * (step + PAD)
        term = nt(both_ref[rows + first : rows + first + step, :], wkv)
        put(odd, upper, far_keep, far_send, at, term)
        dots = [
            row_dot(term[c * BLK : (c + 1) * BLK], pool_ref, first + c * BLK) for c in range(SEND)
        ]
        put_dots(far_keep, far_send, at + step, dots)


def own_terms_kernel(both_ref, unit_ref, dq_ref, mixed_ref, *refs):
    wq_ref, wk_ref, wv_ref, wo_ref, own_keep, own_send = refs
    rank = lax.axis_index("tensor")
    odd, upper = (rank & 1) == 1, rank >> 1
    rows, step = unit_ref.shape[0], 2 * BLK
    wkv = jnp.concatenate([wk_ref[...], wv_ref[...]], axis=1)
    dots = []
    for first in range(0, rows, step):
        last = first + step
        term = nt(both_ref[first:last, :], wkv) + nt(dq_ref[first:last, :], wq_ref[...])
        put(odd, upper, own_keep, own_send, first, term)
        dots += [row_dot(term[c * BLK : (c + 1) * BLK], unit_ref, first + c * BLK) for c in (0, 1)]
        update = nn(mixed_ref[first:last, :], wo_ref[...])
        put(odd, upper, own_keep, own_send, rows + PAD + first, update)
    put_dots(own_keep, own_send, rows, dots)


def run_own_terms(both, unit, dq, mixed, weights):
    rows, feats = unit.shape
    width = dq.shape[1]
    vmem = pl.BlockSpec(memory_space=pltpu.VMEM)
    own = jax.ShapeDtypeStruct((feats // width // 2, 2 * rows + PAD, width), BF16)
    return pl.pallas_call(
        own_terms_kernel,
        out_shape=(own, own),
        in_specs=[vmem] * 8,
        out_specs=[vmem] * 2,
        compiler_params=pltpu.CompilerParams(vmem_limit_bytes=LIMIT),
        cost_estimate=BRIEF,
        name="own_terms",
    )(both, unit, dq, mixed, *weights)


def returns_kernel(bounds, keep_ref, got_ref, last_ref, *outs):
    for (first, last), out_ref in zip(bounds, outs):
        total = keep_ref[0, first:last, :].astype(F32) + got_ref[0, first:last, :].astype(F32)
        out_ref[...] = (total + last_ref[first:last, :].astype(F32)).astype(BF16)


def run_returns(bounds, keep, got, last):
    vmem = pl.BlockSpec(memory_space=pltpu.VMEM)
    width = keep.shape[2]
    return pl.pallas_call(
        functools.partial(returns_kernel, bounds),
        out_shape=[jax.ShapeDtypeStruct((b - a, width), BF16) for a, b in bounds],
        in_specs=[vmem] * 3,
        out_specs=[vmem] * len(bounds),
        compiler_params=pltpu.CompilerParams(vmem_limit_bytes=SMALL),
        cost_estimate=BRIEF,
        name="returned_terms",
    )(keep, got, last)


def my_bits():
    dom = lax.axis_index("dom")
    return lax.axis_index("dp"), dom & 1, dom >> 1


def halve_kernel(bits, *refs):
    count = len(bits)
    ins, outs = refs[: 2 * count], refs[2 * count :]
    mine = my_bits()
    size = outs[0].shape[0]
    for index, bit in enumerate(bits):
        keep_ref, got_ref = ins[2 * index : 2 * index + 2]
        for side, name in enumerate((mine[bit], 1 - mine[bit])):
            at = block_at(name, size)
            total = keep_ref[at, :].astype(F32) + got_ref[at, :].astype(F32)
            outs[2 * index + side][...] = total.astype(BF16)


def run_halve(bits, *arrays):
    vmem = pl.BlockSpec(memory_space=pltpu.VMEM)
    rows, feats = arrays[0].shape
    return pl.pallas_call(
        functools.partial(halve_kernel, bits),
        out_shape=[jax.ShapeDtypeStruct((rows // 2, feats), BF16)] * len(arrays),
        in_specs=[vmem] * len(arrays),
        out_specs=[vmem] * len(arrays),
        compiler_params=pltpu.CompilerParams(vmem_limit_bytes=SMALL),
        cost_estimate=BRIEF,
        name="halve_grads",
    )(*arrays)


def total_kernel(*refs):
    out_ref = refs[-1]
    size = refs[0].shape[0]
    for index in range(len(refs) // 2):
        total = refs[2 * index][...].astype(F32) + refs[2 * index + 1][...].astype(F32)
        out_ref[index * size : (index + 1) * size, :] = total.astype(BF16)


def run_total(*arrays):
    vmem = pl.BlockSpec(memory_space=pltpu.VMEM)
    rows, feats = arrays[0].shape
    return pl.pallas_call(
        total_kernel,
        out_shape=jax.ShapeDtypeStruct((len(arrays) // 2 * rows, feats), BF16),
        in_specs=[vmem] * len(arrays),
        out_specs=vmem,
        compiler_params=pltpu.CompilerParams(vmem_limit_bytes=SMALL),
        cost_estimate=BRIEF,
        name="total_grads",
    )(*arrays)


def settle_kernel(mine_ref, got_ref, *outs):
    size = outs[0].shape[0]
    for index, out_ref in enumerate(outs):
        rows = slice(index * size, (index + 1) * size)
        total = mine_ref[rows, :].astype(F32) + got_ref[rows, :].astype(F32)
        out_ref[...] = total.astype(BF16)


def run_settle(mine, got):
    vmem = pl.BlockSpec(memory_space=pltpu.VMEM)
    rows, feats = mine.shape
    return pl.pallas_call(
        settle_kernel,
        out_shape=[jax.ShapeDtypeStruct((rows // 2, feats), BF16)] * 2,
        in_specs=[vmem] * 2,
        out_specs=[vmem] * 2,
        compiler_params=pltpu.CompilerParams(vmem_limit_bytes=SMALL),
        cost_estimate=BRIEF,
        name="settle_grads",
    )(mine, got)


def join_kernel(bits, *refs):
    count = len(bits)
    outs = refs[-count:]
    mine = my_bits()
    size = refs[0].shape[0]
    for index, bit in enumerate(bits):
        outs[index][block_at(mine[bit], size), :] = refs[2 * index][...]
        outs[index][block_at(1 - mine[bit], size), :] = refs[2 * index + 1][...]


def run_join(bits, *arrays):
    vmem = pl.BlockSpec(memory_space=pltpu.VMEM)
    rows, feats = arrays[0].shape
    return pl.pallas_call(
        functools.partial(join_kernel, bits),
        out_shape=[jax.ShapeDtypeStruct((2 * rows, feats), BF16)] * len(bits),
        in_specs=[vmem] * len(arrays),
        out_specs=[vmem] * len(bits),
        compiler_params=pltpu.CompilerParams(vmem_limit_bytes=SMALL),
        cost_estimate=BRIEF,
        name="join_grads",
    )(*arrays)


def own_sum_kernel(keep_ref, got_ref, last_ref, update_ref, unit_ref):
    rows = update_ref.shape[0]

    def total(first, last):
        both = keep_ref[0, first:last, :].astype(F32) + got_ref[0, first:last, :].astype(F32)
        return both + last_ref[first:last, :].astype(F32)

    unit_ref[...] = total(0, rows + PAD)
    update_ref[...] = total(rows + PAD, 2 * rows + PAD).astype(BF16)


def run_own_sum(rows, keep, got, last):
    width = last.shape[1]
    vmem = pl.BlockSpec(memory_space=pltpu.VMEM)
    shape = jax.ShapeDtypeStruct
    return pl.pallas_call(
        own_sum_kernel,
        out_shape=(shape((rows, width), BF16), shape((rows + PAD, width), F32)),
        in_specs=[vmem] * 3,
        out_specs=[vmem] * 2,
        compiler_params=pltpu.CompilerParams(vmem_limit_bytes=SMALL),
        cost_estimate=BRIEF,
        name="own_sum",
    )(keep, got, last)


def finish_kernel(cfg, *refs):
    blocks, offsets, width, feats, spread = cfg
    send_ref, sum_ref, slab_ref, inverse_ref = refs[:4]
    far_refs = refs[4 : 4 + len(spread)]
    branch_ref, unit_ref, table, sem = refs[4 + len(spread) :]
    fetch = pltpu.make_async_copy(send_ref, table, sem)
    fetch.start()
    own_rows = blocks * BLK
    sub = BLK // width
    group = SEND * BLK + PAD

    unit_ref[...] = sum_ref[:own_rows, :]
    dots = sum_ref[own_rows:, :]
    at_row = lax.broadcasted_iota(jnp.int32, (PAD, width), 0)
    fetch.wait()
    for ref, members in zip(far_refs, spread):
        for position, offset in enumerate(members):
            first = position * group
            extra = ref[first + SEND * BLK : first + group, :].astype(F32)
            for c in range(SEND):
                block = table[c, offset]
                rows = ref[first + c * BLK : first + (c + 1) * BLK, :].astype(F32)
                unit_ref[block_at(block), :] += rows
                for piece in range(sub):
                    line = extra[c * sub + piece : c * sub + piece + 1, :]
                    dots = dots + jnp.where(at_row == block * sub + piece, line, 0.0)
    for block in range(blocks):
        rows = slice(block * BLK, (block + 1) * BLK)
        line = jnp.concatenate(
            [dots[block * sub + piece : block * sub + piece + 1, :] for piece in range(sub)], axis=1
        )
        mean = jnp.broadcast_to(line * (1.0 / feats), (BLK, BLK)).T[:, :width]
        branch = inverse_ref[rows, :] * (unit_ref[rows, :] - slab_ref[rows, :] * mean)
        branch_ref[rows, :] = branch.astype(BF16)


def run_finish(feats, send, own_sum, slab, inverse, far, spread):
    rows, width = slab.shape
    vmem = pl.BlockSpec(memory_space=pltpu.VMEM)
    hbm = pl.BlockSpec(memory_space=pltpu.HBM)
    cfg = (rows // BLK, send.shape[1], width, feats, spread)
    return pl.pallas_call(
        functools.partial(finish_kernel, cfg),
        out_shape=jax.ShapeDtypeStruct((rows, width), BF16),
        in_specs=[hbm] + [vmem] * (3 + len(far)),
        out_specs=vmem,
        scratch_shapes=[
            pltpu.VMEM((rows, width), F32),
            pltpu.SMEM(send.shape, jnp.int32),
            pltpu.SemaphoreType.DMA(()),
        ],
        compiler_params=pltpu.CompilerParams(vmem_limit_bytes=SMALL),
        cost_estimate=BRIEF,
        name="finish",
    )(*in_hbm(send), own_sum, slab, inverse, *far)


def grads_kernel(factor, *refs):
    first_held, first_got, second_held, second_got, q_ref, k_ref, v_ref, o_ref = refs
    dp, low, _ = my_bits()
    first, second = jnp.equal(dp, 1), jnp.equal(low, 1)

    def picked(flag, left, right, start):
        columns = slice(start, start + BLK)
        return jnp.where(flag, left[:, columns].astype(F32), right[:, columns].astype(F32)) * factor

    for start in range(0, q_ref.shape[0], BLK):
        rows = slice(start, start + BLK)
        q_ref[rows, :] = picked(first, first_got, first_held, start).T
        k_ref[rows, :] = picked(first, first_held, first_got, start).T
        v_ref[rows, :] = picked(second, second_got, second_held, start).T
        o_ref[:, rows] = picked(second, second_held, second_got, start)


def run_grads(factor, *arrays):
    width, feats = arrays[0].shape
    vmem = pl.BlockSpec(memory_space=pltpu.VMEM)
    tall = jax.ShapeDtypeStruct((feats, width), F32)
    return pl.pallas_call(
        functools.partial(grads_kernel, factor),
        out_shape=(tall, tall, tall, jax.ShapeDtypeStruct((width, feats), F32)),
        in_specs=[vmem] * 4,
        out_specs=[vmem] * 4,
        compiler_params=pltpu.CompilerParams(vmem_limit_bytes=SMALL),
        cost_estimate=BRIEF,
        name="weight_grads",
    )(*arrays)


def swap(array, axis, bit):
    return lax.ppermute(array, axis, [(i, i ^ bit) for i in range(lax.axis_size(axis))])


def shifted(array, axis, distance):
    size = lax.axis_size(axis)
    return lax.ppermute(array, axis, [(i, (i + distance) % size) for i in range(size)])


def added(left, right):
    return (left.astype(F32) + right.astype(F32)).astype(BF16)


def after(values, *earlier):
    held = lax.optimization_barrier((values, earlier))
    return held[0]


def narrow(keep, got, bit):
    while keep.shape[0] > 2:
        summed = added(keep, got)
        keep, send = summed[0::2], summed[1::2]
        got = swap(send, "tensor", bit)
        bit *= 2
    return keep, got, bit


def body(states, w_query, w_key, w_value, w_out, send_blocks, neighbor_blocks, cotangent):
    replicas, node_count, feats = states.shape
    width = w_query.shape[1]
    ranks = lax.axis_size("tensor")
    parts = lax.axis_size("dom")
    explicit = parts == 4 and lax.axis_size("dp") == 2
    offsets = offset_list(HOPS)
    order, share = piece_order(ranks, len(offsets))
    send = send_blocks[0].T
    weights = (w_query, w_key, w_value, w_out)
    flat_states = states.reshape(-1, feats)
    flat_cot = cotangent.reshape(-1, feats)

    leaving = pick_blocks(flat_states, send, ranks, share)
    route = []
    for p in range(parts):
        for r in range(ranks):
            distance = offsets[order[r * share] // SEND]
            route.append((p * ranks + r, ((p + distance) % parts) * ranks + r))
    levels = []
    bit = 1
    while bit < ranks:
        levels.append(bit)
        bit *= 2
    arrived = [lax.ppermute(block, ("dom", "tensor"), route) for block in leaving]
    own = run_own(flat_states, flat_cot, weights)
    arrived[0] = after(arrived[0], own[0])
    unit, slab, inverse, cot = own[0], own[7], own[8], own[9]
    weights = own[10:]
    first_pieces = list(arrived)
    wide = [swap(block, "tensor", levels[-1]) for block in arrived]
    close = after(first_pieces, *arrived)
    close = [swap(half, "tensor", 1) for block in close for half in jnp.split(block, 2)]
    early = run_early(first_pieces + close, weights[1], weights[2])
    held = {levels[-1]: after(wide, early[0])}
    for bit in reversed(levels[:-1]):
        for slot in list(held):
            held[slot ^ bit] = [swap(block, "tensor", bit) for block in held[slot]]
    for bit in levels[1:-1]:
        held[bit] = [swap(block, "tensor", bit) for block in first_pieces]
        held[bit ^ 1] = [swap(block, "tensor", 1) for block in held[bit]]
    pieces = [block for slot in range(EARLY, ranks) for block in held[slot]]
    count = len(offsets)
    both, dq, mixed, far_keep, far_send, *halves = run_attend(
        explicit,
        early,
        ranks,
        share,
        count,
        neighbor_blocks,
        pieces,
        own[:7],
        cot,
        weights[1],
        weights[2],
    )
    total_rows = replicas * node_count * lax.axis_size("dp") * parts
    factor = 1.0 / math.sqrt(total_rows)

    if explicit:
        first, second = swap(halves[1], "dp", 1), swap(halves[3], "dom", 1)
    far_keep, far_got, bit = narrow(far_keep, swap(far_send, "tensor", 1), 2)
    own_keep, own_send = run_own_terms(both, unit, dq, mixed, weights)
    own_keep, own_got, bit = narrow(own_keep, swap(own_send, "tensor", 1), 2)
    far_out = added(far_keep[1], far_got[1])
    far_last = swap(far_out, "tensor", bit)
    if explicit:
        first, second = after(first, far_out, own_send), after(second, far_out, own_send)
        halves = run_halve((1, 0), halves[0], first, halves[2], second)
        first, second = swap(halves[1], "dom", 1), swap(halves[3], "dp", 1)
        total = run_total(halves[0], first, halves[2], second)
        got = swap(total, "dom", 2)
        own_got = after(own_got, total)
    own_out = added(own_keep[1], own_got[1])
    own_last = swap(own_out, "tensor", bit)
    far_last = after(far_last, own_out)

    group = SEND * BLK + PAD
    spread = []
    for index, distance in enumerate(offsets):
        for members in spread:
            if (offsets[members[0]] - distance) % parts == 0 and members[-1] == index - 1:
                members.append(index)
                break
        else:
            spread.append([index])
    spread = tuple(tuple(members) for members in spread)
    bounds = tuple((members[0] * group, (members[-1] + 1) * group) for members in spread)
    far_sums = run_returns(bounds, far_keep, far_got, far_last)
    returned = [
        shifted(part, "dom", -offsets[members[0]]) for part, members in zip(far_sums, spread)
    ]
    own_last = after(own_last, far_sums)
    update, own_sum = run_own_sum(replicas * node_count, own_keep, own_got, own_last)
    if explicit:
        held = run_settle(total, after(got, own_sum))
        first, second = swap(held[0], "dom", 1), swap(held[1], "dp", 1)
        first = after(first, returned)
        held = run_join((1, 0), held[0], first, held[1], second)
        first, second = swap(held[0], "dp", 1), swap(held[1], "dom", 1)
    branch = run_finish(feats, send, own_sum, slab, inverse, returned, spread)
    if explicit:
        first = after(first, branch)
        grads = run_grads(factor, held[0], first, held[1], second)
    else:
        summed = [lax.psum(half.astype(F32), ("dp", "dom")) * factor for half in halves]
        grads = (summed[0].T, summed[1].T, summed[2].T, summed[3])
    shape = (replicas, node_count, width)
    return (update.reshape(shape), branch.reshape(shape), *grads)


def solution(mesh):
    placed = (
        P("dp", "dom", None),
        P(None, "tensor"),
        P(None, "tensor"),
        P(None, "tensor"),
        P("tensor", None),
        P("dom", None, None),
        P("dom", None),
        P("dp", "dom", None),
    )
    return jax.shard_map(
        body,
        mesh=mesh,
        in_specs=placed,
        out_specs=(
            P("dp", "dom", "tensor"),
            P("dp", "dom", "tensor"),
            P(None, "tensor"),
            P(None, "tensor"),
            P(None, "tensor"),
            P("tensor", None),
        ),
        check_vma=False,
    )
```

```python
import functools
import math

import jax
import jax.numpy as jnp
from jax import lax
from jax.experimental import pallas as pl
from jax.experimental.pallas import tpu as pltpu
from jax.sharding import PartitionSpec as P

BLK = 128
HOPS = 2
SEND = 2
HD = 64
PAD = 16
EARLY = 2
EPS = 1e-05
LIMIT = 24 * 1024 * 1024
SMALL = 8 * 1024 * 1024
CHUNK = 64
BRIEF = pl.CostEstimate(flops=1, bytes_accessed=1, transcendentals=0)
F32 = jnp.float32
BF16 = jnp.bfloat16


def offset_list(hops):
    result = []
    for section in range(1, hops + 1):
        result.append(section)
        result.append(-section)
    return result


def piece_order(ranks, offsets):
    count = offsets * SEND
    share = count // ranks
    if share == SEND and offsets == 4:
        return [0, 1, 4, 5, 2, 3, 6, 7], share
    return list(range(count)), share


def nt(left, right):
    return lax.dot_general(left, right, (((1,), (1,)), ((), ())), preferred_element_type=F32)


def nn(left, right):
    return jnp.dot(left, right, preferred_element_type=F32)


def unit_of(rows):
    values = rows.astype(F32)
    return (values * lax.rsqrt(jnp.mean(values * values, axis=-1, keepdims=True) + EPS)).astype(BF16)


def block_at(index, size=BLK):
    return pl.ds(pl.multiple_of(index * size, size), size)


def rank_piece(rank, ranks, share, inner):
    if share == SEND and ranks == 4:
        return ((rank & 1) * 2 + (rank >> 1)) * SEND + inner
    return rank * share + inner


def in_hbm(*arrays):
    return [pltpu.with_memory_space_constraint(array, pltpu.HBM) for array in arrays]


def pick_kernel(ranks, share, send_ref, states_ref, *refs):
    outs, (table, held, sems) = refs[:share], refs[share:]
    rank = lax.axis_index("tensor")
    copies = [
        pltpu.make_async_copy(send_ref, table, sems.at[0]),
        pltpu.make_async_copy(states_ref, held, sems.at[1]),
    ]
    for copy in copies:
        copy.start()
    for copy in copies:
        copy.wait()
    for inner, out_ref in enumerate(outs):
        piece = rank_piece(rank, ranks, share, inner)
        out_ref[...] = held[block_at(table[piece % SEND, piece // SEND]), :]


def pick_blocks(states, send, ranks, share):
    far = pl.BlockSpec(memory_space=pltpu.HBM)
    vmem = pl.BlockSpec(memory_space=pltpu.VMEM)
    return pl.pallas_call(
        functools.partial(pick_kernel, ranks, share),
        out_shape=[jax.ShapeDtypeStruct((BLK, states.shape[1]), BF16)] * share,
        in_specs=[far, far],
        out_specs=[vmem] * share,
        scratch_shapes=[
            pltpu.SMEM(send.shape, jnp.int32),
            pltpu.VMEM(states.shape, BF16),
            pltpu.SemaphoreType.DMA((2,)),
        ],
        compiler_params=pltpu.CompilerParams(vmem_limit_bytes=SMALL),
        cost_estimate=BRIEF,
        name="pick_blocks",
    )(*in_hbm(send, states))


def by_head(rows, heads):
    if heads == 1:
        return rows.astype(BF16)
    lane_head = lax.broadcasted_iota(jnp.int32, rows.shape, 1) // HD
    return jnp.concatenate(
        [jnp.where(lane_head == head, rows, 0.0) for head in range(heads)], axis=0
    ).astype(BF16)


def diagonal(stacked, heads):
    return jnp.concatenate(
        [
            stacked[head * HD : (head + 1) * HD, head * BLK : (head + 1) * BLK]
            for head in range(heads)
        ],
        axis=0,
    )


def put_pairs(paired, at, width, k_ref, v_ref, kt_ref, vt_ref):
    for index, entry in enumerate(at):
        rows = paired[index * BLK : (index + 1) * BLK]
        keys, values = rows[:, :width], rows[:, width:]
        k_ref[block_at(entry), :] = keys.astype(BF16)
        v_ref[block_at(entry), :] = values.astype(BF16)
        kt_ref[entry] = keys.T.astype(BF16)
        vt_ref[entry] = values.T.astype(BF16)


def own_kernel(*refs):
    sources = refs[:6]
    unit_ref, q_ref, g_ref, k_ref, v_ref, kt_ref, vt_ref, slab_ref, inverse_ref = refs[6:15]
    held, states_ref, sems = refs[15:20], refs[20], refs[21]
    cot_ref, wq_ref, wk_ref, wv_ref, wo_ref = held
    copies = []
    for index, (source, target) in enumerate(zip(sources, (states_ref,) + tuple(held))):
        copies.append(pltpu.make_async_copy(source, target, sems.at[index]))
        copies[-1].start()
    rows, feats = states_ref.shape
    width = wq_ref.shape[1]
    heads = width // HD
    tall = heads * BLK
    rank = lax.axis_index("tensor")
    copies[0].wait()
    for start in range(0, rows, CHUNK):
        values = states_ref[start : start + CHUNK, :].astype(F32)
        inverse = lax.rsqrt(jnp.mean(values * values, axis=-1, keepdims=True) + EPS)
        normed = values * inverse
        unit_ref[start : start + CHUNK, :] = normed.astype(BF16)
        slab = normed[:, :width]
        for index in range(1, feats // width):
            slab = jnp.where(rank == index, normed[:, index * width : (index + 1) * width], slab)
        slab_ref[start : start + CHUNK, :] = slab
        inverse_ref[start : start + CHUNK, :] = jnp.broadcast_to(inverse, slab.shape)
    for copy in copies[1:]:
        copy.wait()
    unit = unit_ref[...]
    queries = nn(unit, wq_ref[...])
    grads = nt(cot_ref[...], wo_ref[...])
    for block in range(rows // BLK):
        q_ref[block * tall : (block + 1) * tall, :] = by_head(
            queries[block * BLK : (block + 1) * BLK], heads
        )
        g_ref[block * tall : (block + 1) * tall, :] = by_head(
            grads[block * BLK : (block + 1) * BLK], heads
        )
    paired = nn(unit, jnp.concatenate([wk_ref[...], wv_ref[...]], axis=1))
    put_pairs(paired, range(rows // BLK), width, k_ref, v_ref, kt_ref, vt_ref)


def run_own(states, cot, weights):
    rows, feats = states.shape
    width = weights[0].shape[1]
    blocks = rows // BLK
    tall = blocks * (width // HD) * BLK
    vmem = pl.BlockSpec(memory_space=pltpu.VMEM)
    far = pl.BlockSpec(memory_space=pltpu.HBM)
    shape = jax.ShapeDtypeStruct
    return pl.pallas_call(
        own_kernel,
        out_shape=(
            shape((rows, feats), BF16),
            shape((tall, width), BF16),
            shape((tall, width), BF16),
            shape((rows, width), BF16),
            shape((rows, width), BF16),
            shape((blocks, width, BLK), BF16),
            shape((blocks, width, BLK), BF16),
            shape((rows, width), F32),
            shape((rows, width), F32),
            shape(cot.shape, BF16),
            *[shape(w.shape, BF16) for w in weights],
        ),
        in_specs=[far] * 6,
        out_specs=[vmem] * 14,
        scratch_shapes=[pltpu.VMEM((rows, feats), BF16), pltpu.SemaphoreType.DMA((6,))],
        compiler_params=pltpu.CompilerParams(vmem_limit_bytes=LIMIT),
        cost_estimate=BRIEF,
        name="own_rows",
    )(*in_hbm(states, cot, *weights))


def early_kernel(count, *refs):
    piece_refs, (wk_ref, wv_ref) = refs[:count], refs[count : count + 2]
    unit_ref, k_ref, v_ref, kt_ref, vt_ref = refs[count + 2 :]
    width = wk_ref.shape[1]
    at = 0
    for source in piece_refs:
        for start in range(0, source.shape[0], CHUNK):
            unit_ref[at : at + CHUNK, :] = unit_of(source[start : start + CHUNK, :])
            at += CHUNK
    wkv = jnp.concatenate([wk_ref[...], wv_ref[...]], axis=1)
    paired = nn(unit_ref[...], wkv)
    blocks = range(unit_ref.shape[0] // BLK)
    put_pairs(paired, blocks, width, k_ref, v_ref, kt_ref, vt_ref)


def run_early(pieces, w_key, w_value):
    inputs, count = len(pieces), sum(piece.shape[0] for piece in pieces) // BLK
    feats, width = w_key.shape
    vmem = pl.BlockSpec(memory_space=pltpu.VMEM)
    shape = jax.ShapeDtypeStruct
    return pl.pallas_call(
        functools.partial(early_kernel, inputs),
        out_shape=(
            shape((count * BLK, feats), BF16),
            shape((count * BLK, width), BF16),
            shape((count * BLK, width), BF16),
            shape((count, width, BLK), BF16),
            shape((count, width, BLK), BF16),
        ),
        in_specs=[vmem] * (inputs + 2),
        out_specs=[vmem] * 5,
        compiler_params=pltpu.CompilerParams(vmem_limit_bytes=LIMIT),
        cost_estimate=BRIEF,
        name="early_rows",
    )(*pieces, w_key, w_value)


def attend_kernel(cfg, near_ref, *refs):
    ranks, share, blocks, offsets, width, explicit, early = cfg
    early_refs, refs = refs[:5], refs[5:]
    count = (ranks - early) * share
    piece_refs = refs[:count]
    own_refs = refs[count : count + 7]
    cot_ref, wk_ref, wv_ref = refs[count + 7 : count + 10]
    refs = refs[count + 10 :]
    both_ref, dq_ref, mixed_ref = refs[:3]
    far_refs, half_refs = refs[3:5], refs[5:9]
    pool_ref, refs = refs[9], refs[10:]
    k_ref, v_ref, kt_ref, vt_ref, ka_ref, va_ref, dk_ref, dv_ref = refs[:8]
    score_ref, prob_ref, low_ref, change_ref, near_table, near_sem = refs[8:]
    fetch = pltpu.make_async_copy(near_ref, near_table, near_sem)
    fetch.start()
    q_ref, g_ref, k_own, v_own, kt_own, vt_own = own_refs[1:]
    heads = width // HD
    tall = heads * BLK
    entries = blocks + offsets * SEND
    rank = lax.axis_index("tensor")

    own_rows = blocks * BLK
    k_ref[:own_rows, :] = k_own[...]
    v_ref[:own_rows, :] = v_own[...]
    kt_ref[:blocks] = kt_own[...]
    vt_ref[:blocks] = vt_own[...]
    wkv = jnp.concatenate([wk_ref[...], wv_ref[...]], axis=1)
    unit_e, k_e, v_e, kt_e, vt_e = early_refs
    for slot in range(early):
        for inner in range(share):
            entry = rank_piece(rank ^ slot, ranks, share, inner)
            index = slot * share + inner
            rows = slice(index * BLK, (index + 1) * BLK)
            pool_ref[block_at(entry), :] = unit_e[rows, :]
            k_ref[block_at(entry + blocks), :] = k_e[rows, :]
            v_ref[block_at(entry + blocks), :] = v_e[rows, :]
            kt_ref[entry + blocks] = kt_e[index]
            vt_ref[entry + blocks] = vt_e[index]
    late, places = [], []
    for slot in range(early, ranks):
        for inner in range(share):
            entry = rank_piece(rank ^ slot, ranks, share, inner)
            base = pl.multiple_of(entry * BLK, BLK)
            places.append(entry + blocks)
            source = piece_refs[(slot - early) * share + inner]
            for start in range(0, BLK, CHUNK):
                rows = unit_of(source[start : start + CHUNK, :])
                pool_ref[pl.ds(pl.multiple_of(base + start, CHUNK), CHUNK), :] = rows
                late.append(rows)
    paired = nn(jnp.concatenate(late, axis=0), wkv)
    put_pairs(paired, places, width, k_ref, v_ref, kt_ref, vt_ref)

    shrink = 1.0 / math.sqrt(HD)
    near = near_ref.shape[1]
    fetch.wait()
    listed = [[block] + [near_table[block, n] for n in range(near)] for block in range(blocks)]

    def open_block(block):
        keys = jnp.concatenate([k_ref[block_at(e), :] for e in listed[block]], axis=0)
        values = jnp.concatenate([v_ref[block_at(e), :] for e in listed[block]], axis=0)
        score_ref[block] = nt(keys, q_ref[block * tall : (block + 1) * tall, :]) * shrink
        prob_ref[block] = nt(values, g_ref[block * tall : (block + 1) * tall, :])

    def weigh_block(block):
        spans = [slice(n * CHUNK, (n + 1) * CHUNK) for n in range((near + 1) * BLK // CHUNK)]
        highest = jnp.max(score_ref[block, spans[0], :], axis=0, keepdims=True)
        for span in spans[1:]:
            rows = jnp.max(score_ref[block, span, :], axis=0, keepdims=True)
            highest = jnp.maximum(highest, rows)
        total, drop = jnp.zeros_like(highest), jnp.zeros_like(highest)
        for span in spans:
            powers = jnp.exp(score_ref[block, span, :] - highest)
            score_ref[block, span, :] = powers
            total = total + jnp.sum(powers, axis=0, keepdims=True)
            drop = drop + jnp.sum(powers * prob_ref[block, span, :], axis=0, keepdims=True)
        scale = 1.0 / total
        drop = drop * scale
        for span in spans:
            weights = score_ref[block, span, :] * scale
            low_ref[block, span, :] = weights.astype(BF16)
            change = weights * (prob_ref[block, span, :] - drop) * shrink
            change_ref[block, span, :] = change.astype(BF16)

    def close_block(block):
        rows = slice(block * BLK, (block + 1) * BLK)
        keys_t = jnp.concatenate([kt_ref[e] for e in listed[block]], axis=1)
        values_t = jnp.concatenate([vt_ref[e] for e in listed[block]], axis=1)
        low, change = low_ref[block], change_ref[block]
        mixed_ref[rows, :] = diagonal(nn(values_t, low), heads).T.astype(BF16)
        dq_ref[rows, :] = diagonal(nn(keys_t, change), heads).T.astype(BF16)
        dk = nn(change, q_ref[block * tall : (block + 1) * tall, :])
        dv = nn(low, g_ref[block * tall : (block + 1) * tall, :])
        ka_ref[rows, :] = dk[:BLK]
        va_ref[rows, :] = dv[:BLK]
        dk_ref[block] = dk[BLK:]
        dv_ref[block] = dv[BLK:]

    open_block(0)
    for block in range(blocks):
        if block + 1 < blocks:
            open_block(block + 1)
        weigh_block(block)
        if block:
            close_block(block - 1)
    close_block(blocks - 1)

    ka_ref[own_rows:, :] = jnp.zeros((entries * BLK - own_rows, width), F32)
    va_ref[own_rows:, :] = jnp.zeros((entries * BLK - own_rows, width), F32)
    for block in range(blocks):
        for n in range(near):
            entry = block_at(listed[block][n + 1])
            ka_ref[entry, :] += dk_ref[block, n * BLK : (n + 1) * BLK]
            va_ref[entry, :] += dv_ref[block, n * BLK : (n + 1) * BLK]

    both_ref[:, :width] = ka_ref[...].astype(BF16)
    both_ref[:, width:] = va_ref[...].astype(BF16)
    grad_terms(explicit, own_refs[0], pool_ref, both_ref, dq_ref, mixed_ref, cot_ref, *half_refs)
    far_terms(blocks, pool_ref, both_ref, wk_ref, wv_ref, *far_refs)


def grad_terms(explicit, unit_ref, pool_ref, both_ref, dq_ref, mixed_ref, cot_ref, *refs):
    first_keep, first_send, second_keep, second_send = refs
    rows, width = dq_ref.shape

    def turned(ref, first, last):
        parts = [
            ref[start : start + BLK, :].astype(F32).T.astype(BF16)
            for start in range(first, last, BLK)
        ]
        return jnp.concatenate(parts, axis=1)

    unit = unit_ref[...]
    grad_q = nn(turned(dq_ref, 0, rows), unit)
    grad_out = nn(turned(mixed_ref, 0, rows), cot_ref[...])
    grad_kv = nn(turned(both_ref, 0, rows), unit)
    grad_kv = grad_kv + nn(turned(both_ref, rows, both_ref.shape[0]), pool_ref[...])
    grad_k, grad_v = grad_kv[:width], grad_kv[width:]
    by_dp = jnp.equal(lax.axis_index("dp") if explicit else 0, 1)
    by_dom = jnp.equal(lax.axis_index("dom") & 1 if explicit else 0, 1)
    first_keep[...] = jnp.where(by_dp, grad_k, grad_q).astype(BF16)
    first_send[...] = jnp.where(by_dp, grad_q, grad_k).astype(BF16)
    second_keep[...] = jnp.where(by_dom, grad_out, grad_v).astype(BF16)
    second_send[...] = jnp.where(by_dom, grad_v, grad_out).astype(BF16)


def run_attend(explicit, early, ranks, share, offsets, near, pieces, own, cot, w_key, w_value):
    rows, feats = own[0].shape
    blocks = rows // BLK
    width = w_key.shape[1]
    received = offsets * SEND
    entries = blocks + received
    listed, tall = (near.shape[1] + 1) * BLK, width // HD * BLK
    vmem = pl.BlockSpec(memory_space=pltpu.VMEM)
    far = pl.BlockSpec(memory_space=pltpu.HBM)
    cfg = (ranks, share, blocks, offsets, width, explicit, EARLY)
    shape = jax.ShapeDtypeStruct
    return pl.pallas_call(
        functools.partial(attend_kernel, cfg),
        out_shape=[
            shape((entries * BLK, 2 * width), BF16),
            shape((rows, width), BF16),
            shape((rows, width), BF16),
            *[shape((feats // width // 2, offsets * (SEND * BLK + PAD), width), BF16)] * 2,
            *[shape((width, feats), BF16)] * 4,
        ],
        in_specs=[far] + [vmem] * (len(early) + len(pieces) + 10),
        out_specs=[vmem] * 9,
        scratch_shapes=[
            pltpu.VMEM((received * BLK, feats), BF16),
            pltpu.VMEM((entries * BLK, width), BF16),
            pltpu.VMEM((entries * BLK, width), BF16),
            pltpu.VMEM((entries, width, BLK), BF16),
            pltpu.VMEM((entries, width, BLK), BF16),
            pltpu.VMEM((entries * BLK, width), F32),
            pltpu.VMEM((entries * BLK, width), F32),
            pltpu.VMEM((blocks, near.shape[1] * BLK, width), F32),
            pltpu.VMEM((blocks, near.shape[1] * BLK, width), F32),
            *[pltpu.VMEM((blocks, listed, tall), F32)] * 2,
            *[pltpu.VMEM((blocks, listed, tall), BF16)] * 2,
            pltpu.SMEM(near.shape, jnp.int32),
            pltpu.SemaphoreType.DMA(()),
        ],
        compiler_params=pltpu.CompilerParams(vmem_limit_bytes=LIMIT),
        cost_estimate=BRIEF,
        name="attention",
    )(*in_hbm(near), *early, *pieces, *own, cot, w_key, w_value)


def put(odd, upper, keep_ref, send_ref, row, values):
    count, width = values.shape[0], keep_ref.shape[2]
    for pair in range(values.shape[1] // width // 2):
        left = values[:, 2 * pair * width : (2 * pair + 1) * width]
        right = values[:, (2 * pair + 1) * width : (2 * pair + 2) * width]
        at = upper ^ pair
        keep_ref[at, row : row + count, :] = jnp.where(odd, right, left).astype(BF16)
        send_ref[at, row : row + count, :] = jnp.where(odd, left, right).astype(BF16)


def put_dots(keep_ref, send_ref, row, dots):
    width = keep_ref.shape[2]
    parts = []
    for dot in dots:
        for piece in range(BLK // width):
            parts.append(dot[:1, piece * width : (piece + 1) * width])
    parts.append(jnp.zeros((PAD - len(parts), width), F32))
    rows = jnp.concatenate(parts, axis=0).astype(BF16)
    for pair in range(keep_ref.shape[0]):
        keep_ref[pair, row : row + PAD, :] = rows
        send_ref[pair, row : row + PAD, :] = rows


def row_dot(term, ref, first):
    ones = jnp.ones((16, ref.shape[1]), BF16)
    product = (term * ref[first : first + BLK, :].astype(F32)).astype(BF16)
    return nt(ones, product)


def far_terms(blocks, pool_ref, both_ref, wk_ref, wv_ref, far_keep, far_send):
    rank = lax.axis_index("tensor")
    odd, upper = (rank & 1) == 1, rank >> 1
    rows, step = blocks * BLK, SEND * BLK
    wkv = jnp.concatenate([wk_ref[...], wv_ref[...]], axis=1)
    for index in range(pool_ref.shape[0] // step):
        first, at = index * step, index * (step + PAD)
        term = nt(both_ref[rows + first : rows + first + step, :], wkv)
        put(odd, upper, far_keep, far_send, at, term)
        dots = [
            row_dot(term[c * BLK : (c + 1) * BLK], pool_ref, first + c * BLK) for c in range(SEND)
        ]
        put_dots(far_keep, far_send, at + step, dots)


def own_terms_kernel(both_ref, unit_ref, dq_ref, mixed_ref, *refs):
    wq_ref, wk_ref, wv_ref, wo_ref, own_keep, own_send = refs
    rank = lax.axis_index("tensor")
    odd, upper = (rank & 1) == 1, rank >> 1
    rows, step = unit_ref.shape[0], 2 * BLK
    wkv = jnp.concatenate([wk_ref[...], wv_ref[...]], axis=1)
    dots = []
    for first in range(0, rows, step):
        last = first + step
        term = nt(both_ref[first:last, :], wkv) + nt(dq_ref[first:last, :], wq_ref[...])
        put(odd, upper, own_keep, own_send, first, term)
        dots += [row_dot(term[c * BLK : (c + 1) * BLK], unit_ref, first + c * BLK) for c in (0, 1)]
        update = nn(mixed_ref[first:last, :], wo_ref[...])
        put(odd, upper, own_keep, own_send, rows + PAD + first, update)
    put_dots(own_keep, own_send, rows, dots)


def run_own_terms(both, unit, dq, mixed, weights):
    rows, feats = unit.shape
    width = dq.shape[1]
    vmem = pl.BlockSpec(memory_space=pltpu.VMEM)
    own = jax.ShapeDtypeStruct((feats // width // 2, 2 * rows + PAD, width), BF16)
    return pl.pallas_call(
        own_terms_kernel,
        out_shape=(own, own),
        in_specs=[vmem] * 8,
        out_specs=[vmem] * 2,
        compiler_params=pltpu.CompilerParams(vmem_limit_bytes=LIMIT),
        cost_estimate=BRIEF,
        name="own_terms",
    )(both, unit, dq, mixed, *weights)


def returns_kernel(bounds, keep_ref, got_ref, last_ref, *outs):
    for (first, last), out_ref in zip(bounds, outs):
        total = keep_ref[0, first:last, :].astype(F32) + got_ref[0, first:last, :].astype(F32)
        out_ref[...] = (total + last_ref[first:last, :].astype(F32)).astype(BF16)


def run_returns(bounds, keep, got, last):
    vmem = pl.BlockSpec(memory_space=pltpu.VMEM)
    width = keep.shape[2]
    return pl.pallas_call(
        functools.partial(returns_kernel, bounds),
        out_shape=[jax.ShapeDtypeStruct((b - a, width), BF16) for a, b in bounds],
        in_specs=[vmem] * 3,
        out_specs=[vmem] * len(bounds),
        compiler_params=pltpu.CompilerParams(vmem_limit_bytes=SMALL),
        cost_estimate=BRIEF,
        name="returned_terms",
    )(keep, got, last)


def my_bits():
    dom = lax.axis_index("dom")
    return lax.axis_index("dp"), dom & 1, dom >> 1


def halve_kernel(bits, *refs):
    count = len(bits)
    ins, outs = refs[: 2 * count], refs[2 * count :]
    mine = my_bits()
    size = outs[0].shape[0]
    for index, bit in enumerate(bits):
        keep_ref, got_ref = ins[2 * index : 2 * index + 2]
        for side, name in enumerate((mine[bit], 1 - mine[bit])):
            at = block_at(name, size)
            total = keep_ref[at, :].astype(F32) + got_ref[at, :].astype(F32)
            outs[2 * index + side][...] = total.astype(BF16)


def run_halve(bits, *arrays):
    vmem = pl.BlockSpec(memory_space=pltpu.VMEM)
    rows, feats = arrays[0].shape
    return pl.pallas_call(
        functools.partial(halve_kernel, bits),
        out_shape=[jax.ShapeDtypeStruct((rows // 2, feats), BF16)] * len(arrays),
        in_specs=[vmem] * len(arrays),
        out_specs=[vmem] * len(arrays),
        compiler_params=pltpu.CompilerParams(vmem_limit_bytes=SMALL),
        cost_estimate=BRIEF,
        name="halve_grads",
    )(*arrays)


def total_kernel(*refs):
    out_ref = refs[-1]
    size = refs[0].shape[0]
    for index in range(len(refs) // 2):
        total = refs[2 * index][...].astype(F32) + refs[2 * index + 1][...].astype(F32)
        out_ref[index * size : (index + 1) * size, :] = total.astype(BF16)


def run_total(*arrays):
    vmem = pl.BlockSpec(memory_space=pltpu.VMEM)
    rows, feats = arrays[0].shape
    return pl.pallas_call(
        total_kernel,
        out_shape=jax.ShapeDtypeStruct((len(arrays) // 2 * rows, feats), BF16),
        in_specs=[vmem] * len(arrays),
        out_specs=vmem,
        compiler_params=pltpu.CompilerParams(vmem_limit_bytes=SMALL),
        cost_estimate=BRIEF,
        name="total_grads",
    )(*arrays)


def settle_kernel(mine_ref, got_ref, *outs):
    size = outs[0].shape[0]
    for index, out_ref in enumerate(outs):
        rows = slice(index * size, (index + 1) * size)
        total = mine_ref[rows, :].astype(F32) + got_ref[rows, :].astype(F32)
        out_ref[...] = total.astype(BF16)


def run_settle(mine, got):
    vmem = pl.BlockSpec(memory_space=pltpu.VMEM)
    rows, feats = mine.shape
    return pl.pallas_call(
        settle_kernel,
        out_shape=[jax.ShapeDtypeStruct((rows // 2, feats), BF16)] * 2,
        in_specs=[vmem] * 2,
        out_specs=[vmem] * 2,
        compiler_params=pltpu.CompilerParams(vmem_limit_bytes=SMALL),
        cost_estimate=BRIEF,
        name="settle_grads",
    )(mine, got)


def join_kernel(bits, *refs):
    count = len(bits)
    outs = refs[-count:]
    mine = my_bits()
    size = refs[0].shape[0]
    for index, bit in enumerate(bits):
        outs[index][block_at(mine[bit], size), :] = refs[2 * index][...]
        outs[index][block_at(1 - mine[bit], size), :] = refs[2 * index + 1][...]


def run_join(bits, *arrays):
    vmem = pl.BlockSpec(memory_space=pltpu.VMEM)
    rows, feats = arrays[0].shape
    return pl.pallas_call(
        functools.partial(join_kernel, bits),
        out_shape=[jax.ShapeDtypeStruct((2 * rows, feats), BF16)] * len(bits),
        in_specs=[vmem] * len(arrays),
        out_specs=[vmem] * len(bits),
        compiler_params=pltpu.CompilerParams(vmem_limit_bytes=SMALL),
        cost_estimate=BRIEF,
        name="join_grads",
    )(*arrays)


def own_sum_kernel(keep_ref, got_ref, last_ref, update_ref, unit_ref):
    rows = update_ref.shape[0]

    def total(first, last):
        both = keep_ref[0, first:last, :].astype(F32) + got_ref[0, first:last, :].astype(F32)
        return both + last_ref[first:last, :].astype(F32)

    unit_ref[...] = total(0, rows + PAD)
    update_ref[...] = total(rows + PAD, 2 * rows + PAD).astype(BF16)


def run_own_sum(rows, keep, got, last):
    width = last.shape[1]
    vmem = pl.BlockSpec(memory_space=pltpu.VMEM)
    shape = jax.ShapeDtypeStruct
    return pl.pallas_call(
        own_sum_kernel,
        out_shape=(shape((rows, width), BF16), shape((rows + PAD, width), F32)),
        in_specs=[vmem] * 3,
        out_specs=[vmem] * 2,
        compiler_params=pltpu.CompilerParams(vmem_limit_bytes=SMALL),
        cost_estimate=BRIEF,
        name="own_sum",
    )(keep, got, last)


def finish_kernel(cfg, *refs):
    blocks, offsets, width, feats, spread = cfg
    send_ref, sum_ref, slab_ref, inverse_ref = refs[:4]
    far_refs = refs[4 : 4 + len(spread)]
    branch_ref, unit_ref, table, sem = refs[4 + len(spread) :]
    fetch = pltpu.make_async_copy(send_ref, table, sem)
    fetch.start()
    own_rows = blocks * BLK
    sub = BLK // width
    group = SEND * BLK + PAD

    unit_ref[...] = sum_ref[:own_rows, :]
    dots = sum_ref[own_rows:, :]
    at_row = lax.broadcasted_iota(jnp.int32, (PAD, width), 0)
    fetch.wait()
    for ref, members in zip(far_refs, spread):
        for position, offset in enumerate(members):
            first = position * group
            extra = ref[first + SEND * BLK : first + group, :].astype(F32)
            for c in range(SEND):
                block = table[c, offset]
                rows = ref[first + c * BLK : first + (c + 1) * BLK, :].astype(F32)
                unit_ref[block_at(block), :] += rows
                for piece in range(sub):
                    line = extra[c * sub + piece : c * sub + piece + 1, :]
                    dots = dots + jnp.where(at_row == block * sub + piece, line, 0.0)
    for block in range(blocks):
        rows = slice(block * BLK, (block + 1) * BLK)
        line = jnp.concatenate(
            [dots[block * sub + piece : block * sub + piece + 1, :] for piece in range(sub)], axis=1
        )
        mean = jnp.broadcast_to(line * (1.0 / feats), (BLK, BLK)).T[:, :width]
        branch = inverse_ref[rows, :] * (unit_ref[rows, :] - slab_ref[rows, :] * mean)
        branch_ref[rows, :] = branch.astype(BF16)


def run_finish(feats, send, own_sum, slab, inverse, far, spread):
    rows, width = slab.shape
    vmem = pl.BlockSpec(memory_space=pltpu.VMEM)
    hbm = pl.BlockSpec(memory_space=pltpu.HBM)
    cfg = (rows // BLK, send.shape[1], width, feats, spread)
    return pl.pallas_call(
        functools.partial(finish_kernel, cfg),
        out_shape=jax.ShapeDtypeStruct((rows, width), BF16),
        in_specs=[hbm] + [vmem] * (3 + len(far)),
        out_specs=vmem,
        scratch_shapes=[
            pltpu.VMEM((rows, width), F32),
            pltpu.SMEM(send.shape, jnp.int32),
            pltpu.SemaphoreType.DMA(()),
        ],
        compiler_params=pltpu.CompilerParams(vmem_limit_bytes=SMALL),
        cost_estimate=BRIEF,
        name="finish",
    )(*in_hbm(send), own_sum, slab, inverse, *far)


def grads_kernel(factor, *refs):
    first_held, first_got, second_held, second_got = refs[:4]
    results, made, sems = refs[4:8], refs[8:12], refs[12]
    dp, low, _ = my_bits()
    first, second = jnp.equal(dp, 1), jnp.equal(low, 1)
    copies = [
        pltpu.make_async_copy(source, target, sems.at[index])
        for index, (source, target) in enumerate(zip(made, results))
    ]

    def picked(flag, left, right, start):
        columns = slice(start, start + BLK)
        return jnp.where(flag, left[:, columns].astype(F32), right[:, columns].astype(F32)) * factor

    picks = (
        (first, first_got, first_held),
        (first, first_held, first_got),
        (second, second_got, second_held),
        (second, second_held, second_got),
    )
    for index in (3, 0, 1, 2):
        for start in range(0, first_held.shape[1], BLK):
            rows = slice(start, start + BLK)
            block = picked(*picks[index], start)
            if index == 3:
                made[index][:, rows] = block
            else:
                made[index][rows, :] = block.T
        copies[index].start()
    for copy in copies:
        copy.wait()


def run_grads(factor, *arrays):
    width, feats = arrays[0].shape
    vmem = pl.BlockSpec(memory_space=pltpu.VMEM)
    hbm = pl.BlockSpec(memory_space=pltpu.HBM)
    shapes = [(feats, width)] * 3 + [(width, feats)]
    return pl.pallas_call(
        functools.partial(grads_kernel, factor),
        out_shape=[jax.ShapeDtypeStruct(shape, F32) for shape in shapes],
        in_specs=[vmem] * 4,
        out_specs=[hbm] * 4,
        scratch_shapes=[
            *[pltpu.VMEM(shape, F32) for shape in shapes],
            pltpu.SemaphoreType.DMA((4,)),
        ],
        compiler_params=pltpu.CompilerParams(vmem_limit_bytes=SMALL),
        cost_estimate=BRIEF,
        name="weight_grads",
    )(*arrays)


def swap(array, axis, bit):
    return lax.ppermute(array, axis, [(i, i ^ bit) for i in range(lax.axis_size(axis))])


def shifted(array, axis, distance):
    size = lax.axis_size(axis)
    return lax.ppermute(array, axis, [(i, (i + distance) % size) for i in range(size)])


def added(left, right):
    return (left.astype(F32) + right.astype(F32)).astype(BF16)


def after(values, *earlier):
    held = lax.optimization_barrier((values, earlier))
    return held[0]


def narrow(keep, got, bit):
    while keep.shape[0] > 2:
        summed = added(keep, got)
        keep, send = summed[0::2], summed[1::2]
        got = swap(send, "tensor", bit)
        bit *= 2
    return keep, got, bit


def body(states, w_query, w_key, w_value, w_out, send_blocks, neighbor_blocks, cotangent):
    replicas, node_count, feats = states.shape
    width = w_query.shape[1]
    ranks = lax.axis_size("tensor")
    parts = lax.axis_size("dom")
    explicit = parts == 4 and lax.axis_size("dp") == 2
    offsets = offset_list(HOPS)
    order, share = piece_order(ranks, len(offsets))
    send = send_blocks[0].T
    weights = (w_query, w_key, w_value, w_out)
    flat_states = states.reshape(-1, feats)
    flat_cot = cotangent.reshape(-1, feats)

    leaving = pick_blocks(flat_states, send, ranks, share)
    route = []
    for p in range(parts):
        for r in range(ranks):
            distance = offsets[order[r * share] // SEND]
            route.append((p * ranks + r, ((p + distance) % parts) * ranks + r))
    levels = []
    bit = 1
    while bit < ranks:
        levels.append(bit)
        bit *= 2
    arrived = [lax.ppermute(block, ("dom", "tensor"), route) for block in leaving]
    own = run_own(flat_states, flat_cot, weights)
    arrived[0] = after(arrived[0], own[0])
    unit, slab, inverse, cot = own[0], own[7], own[8], own[9]
    weights = own[10:]
    first_pieces = list(arrived)
    wide = [swap(block, "tensor", levels[-1]) for block in arrived]
    close = after(first_pieces, *arrived)
    close = [swap(half, "tensor", 1) for block in close for half in jnp.split(block, 2)]
    early = run_early(first_pieces + close, weights[1], weights[2])
    held = {levels[-1]: after(wide, early[0])}
    for bit in reversed(levels[:-1]):
        for slot in list(held):
            held[slot ^ bit] = [swap(block, "tensor", bit) for block in held[slot]]
    for bit in levels[1:-1]:
        held[bit] = [swap(block, "tensor", bit) for block in first_pieces]
        held[bit ^ 1] = [swap(block, "tensor", 1) for block in held[bit]]
    pieces = [block for slot in range(EARLY, ranks) for block in held[slot]]
    count = len(offsets)
    both, dq, mixed, far_keep, far_send, *halves = run_attend(
        explicit,
        early,
        ranks,
        share,
        count,
        neighbor_blocks,
        pieces,
        own[:7],
        cot,
        weights[1],
        weights[2],
    )
    total_rows = replicas * node_count * lax.axis_size("dp") * parts
    factor = 1.0 / math.sqrt(total_rows)

    if explicit:
        first, second = swap(halves[1], "dp", 1), swap(halves[3], "dom", 1)
    far_keep, far_got, bit = narrow(far_keep, swap(far_send, "tensor", 1), 2)
    own_keep, own_send = run_own_terms(both, unit, dq, mixed, weights)
    own_keep, own_got, bit = narrow(own_keep, swap(own_send, "tensor", 1), 2)
    far_out = added(far_keep[1], far_got[1])
    far_last = swap(far_out, "tensor", bit)
    if explicit:
        first, second = after(first, far_out, own_send), after(second, far_out, own_send)
        halves = run_halve((1, 0), halves[0], first, halves[2], second)
        first, second = swap(halves[1], "dom", 1), swap(halves[3], "dp", 1)
        total = run_total(halves[0], first, halves[2], second)
        got = swap(total, "dom", 2)
        own_got = after(own_got, total)
    own_out = added(own_keep[1], own_got[1])
    own_last = swap(own_out, "tensor", bit)
    far_last = after(far_last, own_out)

    group = SEND * BLK + PAD
    spread = []
    for index, distance in enumerate(offsets):
        for members in spread:
            if (offsets[members[0]] - distance) % parts == 0 and members[-1] == index - 1:
                members.append(index)
                break
        else:
            spread.append([index])
    spread = tuple(tuple(members) for members in spread)
    bounds = tuple((members[0] * group, (members[-1] + 1) * group) for members in spread)
    far_sums = run_returns(bounds, far_keep, far_got, far_last)
    returned = [
        shifted(part, "dom", -offsets[members[0]]) for part, members in zip(far_sums, spread)
    ]
    own_last = after(own_last, far_sums)
    update, own_sum = run_own_sum(replicas * node_count, own_keep, own_got, own_last)
    if explicit:
        held = run_settle(total, after(got, own_sum))
        first, second = swap(held[0], "dom", 1), swap(held[1], "dp", 1)
        first = after(first, returned)
        held = run_join((1, 0), held[0], first, held[1], second)
        first, second = swap(held[0], "dp", 1), swap(held[1], "dom", 1)
    branch = run_finish(feats, send, own_sum, slab, inverse, returned, spread)
    if explicit:
        first = after(first, branch)
        grads = run_grads(factor, held[0], first, held[1], second)
    else:
        summed = [lax.psum(half.astype(F32), ("dp", "dom")) * factor for half in halves]
        grads = (summed[0].T, summed[1].T, summed[2].T, summed[3])
    shape = (replicas, node_count, width)
    return (update.reshape(shape), branch.reshape(shape), *grads)


def solution(mesh):
    placed = (
        P("dp", "dom", None),
        P(None, "tensor"),
        P(None, "tensor"),
        P(None, "tensor"),
        P("tensor", None),
        P("dom", None, None),
        P("dom", None),
        P("dp", "dom", None),
    )
    return jax.shard_map(
        body,
        mesh=mesh,
        in_specs=placed,
        out_specs=(
            P("dp", "dom", "tensor"),
            P("dp", "dom", "tensor"),
            P(None, "tensor"),
            P(None, "tensor"),
            P(None, "tensor"),
            P("tensor", None),
        ),
        check_vma=False,
    )
```

```python
import functools
import math

import jax
import jax.numpy as jnp
from jax import lax
from jax.experimental import pallas as pl
from jax.experimental.pallas import tpu as pltpu
from jax.sharding import PartitionSpec as P

BLK = 128
HOPS = 2
SEND = 2
HD = 64
PAD = 16
EARLY = 2
EPS = 1e-05
LIMIT = 24 * 1024 * 1024
SMALL = 8 * 1024 * 1024
CHUNK = 64
BRIEF = pl.CostEstimate(flops=1, bytes_accessed=1, transcendentals=0)
F32 = jnp.float32
BF16 = jnp.bfloat16


def offset_list(hops):
    result = []
    for section in range(1, hops + 1):
        result.append(section)
        result.append(-section)
    return result


def piece_order(ranks, offsets):
    count = offsets * SEND
    share = count // ranks
    if share == SEND and offsets == 4:
        return [0, 1, 4, 5, 2, 3, 6, 7], share
    return list(range(count)), share


def nt(left, right):
    return lax.dot_general(left, right, (((1,), (1,)), ((), ())), preferred_element_type=F32)


def nn(left, right):
    return jnp.dot(left, right, preferred_element_type=F32)


def unit_of(rows):
    values = rows.astype(F32)
    return (values * lax.rsqrt(jnp.mean(values * values, axis=-1, keepdims=True) + EPS)).astype(BF16)


def block_at(index, size=BLK):
    return pl.ds(pl.multiple_of(index * size, size), size)


def rank_piece(rank, ranks, share, inner):
    if share == SEND and ranks == 4:
        return ((rank & 1) * 2 + (rank >> 1)) * SEND + inner
    return rank * share + inner


def in_hbm(*arrays):
    return [pltpu.with_memory_space_constraint(array, pltpu.HBM) for array in arrays]


def pick_kernel(ranks, share, send_ref, states_ref, *refs):
    outs, (table, held, sems) = refs[:share], refs[share:]
    rank = lax.axis_index("tensor")
    copies = [
        pltpu.make_async_copy(send_ref, table, sems.at[0]),
        pltpu.make_async_copy(states_ref, held, sems.at[1]),
    ]
    for copy in copies:
        copy.start()
    for copy in copies:
        copy.wait()
    for inner, out_ref in enumerate(outs):
        piece = rank_piece(rank, ranks, share, inner)
        out_ref[...] = held[block_at(table[piece % SEND, piece // SEND]), :]


def pick_blocks(states, send, ranks, share):
    far = pl.BlockSpec(memory_space=pltpu.HBM)
    vmem = pl.BlockSpec(memory_space=pltpu.VMEM)
    return pl.pallas_call(
        functools.partial(pick_kernel, ranks, share),
        out_shape=[jax.ShapeDtypeStruct((BLK, states.shape[1]), BF16)] * share,
        in_specs=[far, far],
        out_specs=[vmem] * share,
        scratch_shapes=[
            pltpu.SMEM(send.shape, jnp.int32),
            pltpu.VMEM(states.shape, BF16),
            pltpu.SemaphoreType.DMA((2,)),
        ],
        compiler_params=pltpu.CompilerParams(vmem_limit_bytes=SMALL),
        cost_estimate=BRIEF,
        name="pick_blocks",
    )(*in_hbm(send, states))


def by_head(rows, heads):
    if heads == 1:
        return rows.astype(BF16)
    lane_head = lax.broadcasted_iota(jnp.int32, rows.shape, 1) // HD
    return jnp.concatenate(
        [jnp.where(lane_head == head, rows, 0.0) for head in range(heads)], axis=0
    ).astype(BF16)


def diagonal(stacked, heads):
    return jnp.concatenate(
        [
            stacked[head * HD : (head + 1) * HD, head * BLK : (head + 1) * BLK]
            for head in range(heads)
        ],
        axis=0,
    )


def put_pairs(paired, at, width, k_ref, v_ref, kt_ref, vt_ref):
    for index, entry in enumerate(at):
        rows = paired[index * BLK : (index + 1) * BLK]
        keys, values = rows[:, :width], rows[:, width:]
        k_ref[block_at(entry), :] = keys.astype(BF16)
        v_ref[block_at(entry), :] = values.astype(BF16)
        kt_ref[entry] = keys.T.astype(BF16)
        vt_ref[entry] = values.T.astype(BF16)


def own_kernel(*refs):
    sources = refs[:6]
    unit_ref, q_ref, g_ref, k_ref, v_ref, kt_ref, vt_ref, slab_ref, inverse_ref = refs[6:15]
    held, states_ref, sems = refs[15:20], refs[20], refs[21]
    cot_ref, wq_ref, wk_ref, wv_ref, wo_ref = held
    copies = []
    for index, (source, target) in enumerate(zip(sources, (states_ref,) + tuple(held))):
        copies.append(pltpu.make_async_copy(source, target, sems.at[index]))
        copies[-1].start()
    rows, feats = states_ref.shape
    width = wq_ref.shape[1]
    heads = width // HD
    tall = heads * BLK
    rank = lax.axis_index("tensor")
    copies[0].wait()
    for start in range(0, rows, CHUNK):
        values = states_ref[start : start + CHUNK, :].astype(F32)
        inverse = lax.rsqrt(jnp.mean(values * values, axis=-1, keepdims=True) + EPS)
        normed = values * inverse
        unit_ref[start : start + CHUNK, :] = normed.astype(BF16)
        slab = normed[:, :width]
        for index in range(1, feats // width):
            slab = jnp.where(rank == index, normed[:, index * width : (index + 1) * width], slab)
        slab_ref[start : start + CHUNK, :] = slab
        inverse_ref[start : start + CHUNK, :] = jnp.broadcast_to(inverse, slab.shape)
    for copy in copies[1:]:
        copy.wait()
    unit = unit_ref[...]
    queries = nn(unit, wq_ref[...])
    grads = nt(cot_ref[...], wo_ref[...])
    for block in range(rows // BLK):
        q_ref[block * tall : (block + 1) * tall, :] = by_head(
            queries[block * BLK : (block + 1) * BLK], heads
        )
        g_ref[block * tall : (block + 1) * tall, :] = by_head(
            grads[block * BLK : (block + 1) * BLK], heads
        )
    paired = nn(unit, jnp.concatenate([wk_ref[...], wv_ref[...]], axis=1))
    put_pairs(paired, range(rows // BLK), width, k_ref, v_ref, kt_ref, vt_ref)


def run_own(states, cot, weights):
    rows, feats = states.shape
    width = weights[0].shape[1]
    blocks = rows // BLK
    tall = blocks * (width // HD) * BLK
    vmem = pl.BlockSpec(memory_space=pltpu.VMEM)
    far = pl.BlockSpec(memory_space=pltpu.HBM)
    shape = jax.ShapeDtypeStruct
    return pl.pallas_call(
        own_kernel,
        out_shape=(
            shape((rows, feats), BF16),
            shape((tall, width), BF16),
            shape((tall, width), BF16),
            shape((rows, width), BF16),
            shape((rows, width), BF16),
            shape((blocks, width, BLK), BF16),
            shape((blocks, width, BLK), BF16),
            shape((rows, width), F32),
            shape((rows, width), F32),
            shape(cot.shape, BF16),
            *[shape(w.shape, BF16) for w in weights],
        ),
        in_specs=[far] * 6,
        out_specs=[vmem] * 14,
        scratch_shapes=[pltpu.VMEM((rows, feats), BF16), pltpu.SemaphoreType.DMA((6,))],
        compiler_params=pltpu.CompilerParams(vmem_limit_bytes=LIMIT),
        cost_estimate=BRIEF,
        name="own_rows",
    )(*in_hbm(states, cot, *weights))


def early_kernel(count, *refs):
    piece_refs, (wk_ref, wv_ref) = refs[:count], refs[count : count + 2]
    unit_ref, k_ref, v_ref, kt_ref, vt_ref = refs[count + 2 :]
    width = wk_ref.shape[1]
    at = 0
    for source in piece_refs:
        for start in range(0, source.shape[0], CHUNK):
            unit_ref[at : at + CHUNK, :] = unit_of(source[start : start + CHUNK, :])
            at += CHUNK
    wkv = jnp.concatenate([wk_ref[...], wv_ref[...]], axis=1)
    paired = nn(unit_ref[...], wkv)
    blocks = range(unit_ref.shape[0] // BLK)
    put_pairs(paired, blocks, width, k_ref, v_ref, kt_ref, vt_ref)


def run_early(pieces, w_key, w_value):
    inputs, count = len(pieces), sum(piece.shape[0] for piece in pieces) // BLK
    feats, width = w_key.shape
    vmem = pl.BlockSpec(memory_space=pltpu.VMEM)
    shape = jax.ShapeDtypeStruct
    return pl.pallas_call(
        functools.partial(early_kernel, inputs),
        out_shape=(
            shape((count * BLK, feats), BF16),
            shape((count * BLK, width), BF16),
            shape((count * BLK, width), BF16),
            shape((count, width, BLK), BF16),
            shape((count, width, BLK), BF16),
        ),
        in_specs=[vmem] * (inputs + 2),
        out_specs=[vmem] * 5,
        compiler_params=pltpu.CompilerParams(vmem_limit_bytes=LIMIT),
        cost_estimate=BRIEF,
        name="early_rows",
    )(*pieces, w_key, w_value)


def attend_kernel(cfg, near_ref, *refs):
    ranks, share, blocks, offsets, width, explicit, early = cfg
    early_refs, refs = refs[:5], refs[5:]
    count = (ranks - early) * share
    piece_refs = refs[:count]
    own_refs = refs[count : count + 7]
    cot_ref, wk_ref, wv_ref = refs[count + 7 : count + 10]
    refs = refs[count + 10 :]
    both_ref, dq_ref, mixed_ref = refs[:3]
    far_refs, half_refs = refs[3:5], refs[5:9]
    pool_ref, refs = refs[9], refs[10:]
    k_ref, v_ref, kt_ref, vt_ref, ka_ref, va_ref, dk_ref, dv_ref = refs[:8]
    score_ref, prob_ref, low_ref, change_ref, near_table, near_sem = refs[8:]
    fetch = pltpu.make_async_copy(near_ref, near_table, near_sem)
    fetch.start()
    q_ref, g_ref, k_own, v_own, kt_own, vt_own = own_refs[1:]
    heads = width // HD
    tall = heads * BLK
    entries = blocks + offsets * SEND
    rank = lax.axis_index("tensor")

    own_rows = blocks * BLK
    k_ref[:own_rows, :] = k_own[...]
    v_ref[:own_rows, :] = v_own[...]
    kt_ref[:blocks] = kt_own[...]
    vt_ref[:blocks] = vt_own[...]
    wkv = jnp.concatenate([wk_ref[...], wv_ref[...]], axis=1)
    unit_e, k_e, v_e, kt_e, vt_e = early_refs
    for slot in range(early):
        for inner in range(share):
            entry = rank_piece(rank ^ slot, ranks, share, inner)
            index = slot * share + inner
            rows = slice(index * BLK, (index + 1) * BLK)
            pool_ref[block_at(entry), :] = unit_e[rows, :]
            k_ref[block_at(entry + blocks), :] = k_e[rows, :]
            v_ref[block_at(entry + blocks), :] = v_e[rows, :]
            kt_ref[entry + blocks] = kt_e[index]
            vt_ref[entry + blocks] = vt_e[index]
    late, places = [], []
    for slot in range(early, ranks):
        for inner in range(share):
            entry = rank_piece(rank ^ slot, ranks, share, inner)
            base = pl.multiple_of(entry * BLK, BLK)
            places.append(entry + blocks)
            source = piece_refs[(slot - early) * share + inner]
            for start in range(0, BLK, CHUNK):
                rows = unit_of(source[start : start + CHUNK, :])
                pool_ref[pl.ds(pl.multiple_of(base + start, CHUNK), CHUNK), :] = rows
                late.append(rows)
    paired = nn(jnp.concatenate(late, axis=0), wkv)
    put_pairs(paired, places, width, k_ref, v_ref, kt_ref, vt_ref)

    shrink = 1.0 / math.sqrt(HD)
    steep = shrink / math.log(2.0)
    near = near_ref.shape[1]
    fetch.wait()
    listed = [[block] + [near_table[block, n] for n in range(near)] for block in range(blocks)]

    def open_block(block):
        keys = jnp.concatenate([k_ref[block_at(e), :] for e in listed[block]], axis=0)
        values = jnp.concatenate([v_ref[block_at(e), :] for e in listed[block]], axis=0)
        score_ref[block] = nt(keys, q_ref[block * tall : (block + 1) * tall, :])
        prob_ref[block] = nt(values, g_ref[block * tall : (block + 1) * tall, :])

    def weigh_block(block):
        spans = [slice(n * CHUNK, (n + 1) * CHUNK) for n in range((near + 1) * BLK // CHUNK)]
        highest = jnp.max(score_ref[block, spans[0], :], axis=0, keepdims=True)
        for span in spans[1:]:
            rows = jnp.max(score_ref[block, span, :], axis=0, keepdims=True)
            highest = jnp.maximum(highest, rows)
        total, drop = jnp.zeros_like(highest), jnp.zeros_like(highest)
        for span in spans:
            powers = jnp.exp2((score_ref[block, span, :] - highest) * steep)
            score_ref[block, span, :] = powers
            total = total + jnp.sum(powers, axis=0, keepdims=True)
            drop = drop + jnp.sum(powers * prob_ref[block, span, :], axis=0, keepdims=True)
        scale = 1.0 / total
        drop = drop * scale
        for span in spans:
            weights = score_ref[block, span, :] * scale
            low_ref[block, span, :] = weights.astype(BF16)
            change = weights * (prob_ref[block, span, :] - drop) * shrink
            change_ref[block, span, :] = change.astype(BF16)

    def close_block(block):
        rows = slice(block * BLK, (block + 1) * BLK)
        keys_t = jnp.concatenate([kt_ref[e] for e in listed[block]], axis=1)
        values_t = jnp.concatenate([vt_ref[e] for e in listed[block]], axis=1)
        low, change = low_ref[block], change_ref[block]
        mixed_ref[rows, :] = diagonal(nn(values_t, low), heads).T.astype(BF16)
        dq_ref[rows, :] = diagonal(nn(keys_t, change), heads).T.astype(BF16)
        dk = nn(change, q_ref[block * tall : (block + 1) * tall, :])
        dv = nn(low, g_ref[block * tall : (block + 1) * tall, :])
        ka_ref[rows, :] = dk[:BLK]
        va_ref[rows, :] = dv[:BLK]
        dk_ref[block] = dk[BLK:]
        dv_ref[block] = dv[BLK:]

    open_block(0)
    for block in range(blocks):
        if block + 1 < blocks:
            open_block(block + 1)
        if block:
            close_block(block - 1)
        weigh_block(block)
    close_block(blocks - 1)

    ka_ref[own_rows:, :] = jnp.zeros((entries * BLK - own_rows, width), F32)
    va_ref[own_rows:, :] = jnp.zeros((entries * BLK - own_rows, width), F32)
    for block in range(blocks):
        for n in range(near):
            entry = block_at(listed[block][n + 1])
            ka_ref[entry, :] += dk_ref[block, n * BLK : (n + 1) * BLK]
            va_ref[entry, :] += dv_ref[block, n * BLK : (n + 1) * BLK]

    both_ref[:, :width] = ka_ref[...].astype(BF16)
    both_ref[:, width:] = va_ref[...].astype(BF16)
    grad_terms(explicit, own_refs[0], pool_ref, both_ref, dq_ref, mixed_ref, cot_ref, *half_refs)
    far_terms(blocks, pool_ref, both_ref, wk_ref, wv_ref, *far_refs)


def grad_terms(explicit, unit_ref, pool_ref, both_ref, dq_ref, mixed_ref, cot_ref, *refs):
    first_keep, first_send, second_keep, second_send = refs
    rows, width = dq_ref.shape

    def turned(ref, first, last):
        parts = [
            ref[start : start + BLK, :].astype(F32).T.astype(BF16)
            for start in range(first, last, BLK)
        ]
        return jnp.concatenate(parts, axis=1)

    unit = unit_ref[...]
    grad_q = nn(turned(dq_ref, 0, rows), unit)
    grad_out = nn(turned(mixed_ref, 0, rows), cot_ref[...])
    grad_kv = nn(turned(both_ref, 0, rows), unit)
    grad_kv = grad_kv + nn(turned(both_ref, rows, both_ref.shape[0]), pool_ref[...])
    grad_k, grad_v = grad_kv[:width], grad_kv[width:]
    by_dp = jnp.equal(lax.axis_index("dp") if explicit else 0, 1)
    by_dom = jnp.equal(lax.axis_index("dom") & 1 if explicit else 0, 1)
    first_keep[...] = jnp.where(by_dp, grad_k, grad_q).astype(BF16)
    first_send[...] = jnp.where(by_dp, grad_q, grad_k).astype(BF16)
    second_keep[...] = jnp.where(by_dom, grad_out, grad_v).astype(BF16)
    second_send[...] = jnp.where(by_dom, grad_v, grad_out).astype(BF16)


def run_attend(explicit, early, ranks, share, offsets, near, pieces, own, cot, w_key, w_value):
    rows, feats = own[0].shape
    blocks = rows // BLK
    width = w_key.shape[1]
    received = offsets * SEND
    entries = blocks + received
    listed, tall = (near.shape[1] + 1) * BLK, width // HD * BLK
    vmem = pl.BlockSpec(memory_space=pltpu.VMEM)
    far = pl.BlockSpec(memory_space=pltpu.HBM)
    cfg = (ranks, share, blocks, offsets, width, explicit, EARLY)
    shape = jax.ShapeDtypeStruct
    return pl.pallas_call(
        functools.partial(attend_kernel, cfg),
        out_shape=[
            shape((entries * BLK, 2 * width), BF16),
            shape((rows, width), BF16),
            shape((rows, width), BF16),
            *[shape((feats // width // 2, offsets * (SEND * BLK + PAD), width), BF16)] * 2,
            *[shape((width, feats), BF16)] * 4,
        ],
        in_specs=[far] + [vmem] * (len(early) + len(pieces) + 10),
        out_specs=[vmem] * 9,
        scratch_shapes=[
            pltpu.VMEM((received * BLK, feats), BF16),
            pltpu.VMEM((entries * BLK, width), BF16),
            pltpu.VMEM((entries * BLK, width), BF16),
            pltpu.VMEM((entries, width, BLK), BF16),
            pltpu.VMEM((entries, width, BLK), BF16),
            pltpu.VMEM((entries * BLK, width), F32),
            pltpu.VMEM((entries * BLK, width), F32),
            pltpu.VMEM((blocks, near.shape[1] * BLK, width), F32),
            pltpu.VMEM((blocks, near.shape[1] * BLK, width), F32),
            *[pltpu.VMEM((blocks, listed, tall), F32)] * 2,
            *[pltpu.VMEM((blocks, listed, tall), BF16)] * 2,
            pltpu.SMEM(near.shape, jnp.int32),
            pltpu.SemaphoreType.DMA(()),
        ],
        compiler_params=pltpu.CompilerParams(vmem_limit_bytes=LIMIT),
        cost_estimate=BRIEF,
        name="attention",
    )(*in_hbm(near), *early, *pieces, *own, cot, w_key, w_value)


def put(odd, upper, keep_ref, send_ref, row, values):
    count, width = values.shape[0], keep_ref.shape[2]
    for pair in range(values.shape[1] // width // 2):
        left = values[:, 2 * pair * width : (2 * pair + 1) * width]
        right = values[:, (2 * pair + 1) * width : (2 * pair + 2) * width]
        at = upper ^ pair
        keep_ref[at, row : row + count, :] = jnp.where(odd, right, left).astype(BF16)
        send_ref[at, row : row + count, :] = jnp.where(odd, left, right).astype(BF16)


def put_dots(keep_ref, send_ref, row, dots):
    width = keep_ref.shape[2]
    parts = []
    for dot in dots:
        for piece in range(BLK // width):
            parts.append(dot[:1, piece * width : (piece + 1) * width])
    parts.append(jnp.zeros((PAD - len(parts), width), F32))
    rows = jnp.concatenate(parts, axis=0).astype(BF16)
    for pair in range(keep_ref.shape[0]):
        keep_ref[pair, row : row + PAD, :] = rows
        send_ref[pair, row : row + PAD, :] = rows


def row_dot(term, ref, first):
    ones = jnp.ones((16, ref.shape[1]), BF16)
    product = (term * ref[first : first + BLK, :].astype(F32)).astype(BF16)
    return nt(ones, product)


def far_terms(blocks, pool_ref, both_ref, wk_ref, wv_ref, far_keep, far_send):
    rank = lax.axis_index("tensor")
    odd, upper = (rank & 1) == 1, rank >> 1
    rows, step = blocks * BLK, SEND * BLK
    wkv = jnp.concatenate([wk_ref[...], wv_ref[...]], axis=1)
    for index in range(pool_ref.shape[0] // step):
        first, at = index * step, index * (step + PAD)
        term = nt(both_ref[rows + first : rows + first + step, :], wkv)
        put(odd, upper, far_keep, far_send, at, term)
        dots = [
            row_dot(term[c * BLK : (c + 1) * BLK], pool_ref, first + c * BLK) for c in range(SEND)
        ]
        put_dots(far_keep, far_send, at + step, dots)


def own_terms_kernel(both_ref, unit_ref, dq_ref, mixed_ref, *refs):
    wq_ref, wk_ref, wv_ref, wo_ref, own_keep, own_send = refs
    rank = lax.axis_index("tensor")
    odd, upper = (rank & 1) == 1, rank >> 1
    rows, step = unit_ref.shape[0], 2 * BLK
    wkv = jnp.concatenate([wk_ref[...], wv_ref[...]], axis=1)
    dots = []
    for first in range(0, rows, step):
        last = first + step
        term = nt(both_ref[first:last, :], wkv) + nt(dq_ref[first:last, :], wq_ref[...])
        put(odd, upper, own_keep, own_send, first, term)
        dots += [row_dot(term[c * BLK : (c + 1) * BLK], unit_ref, first + c * BLK) for c in (0, 1)]
        update = nn(mixed_ref[first:last, :], wo_ref[...])
        put(odd, upper, own_keep, own_send, rows + PAD + first, update)
    put_dots(own_keep, own_send, rows, dots)


def run_own_terms(both, unit, dq, mixed, weights):
    rows, feats = unit.shape
    width = dq.shape[1]
    vmem = pl.BlockSpec(memory_space=pltpu.VMEM)
    own = jax.ShapeDtypeStruct((feats // width // 2, 2 * rows + PAD, width), BF16)
    return pl.pallas_call(
        own_terms_kernel,
        out_shape=(own, own),
        in_specs=[vmem] * 8,
        out_specs=[vmem] * 2,
        compiler_params=pltpu.CompilerParams(vmem_limit_bytes=LIMIT),
        cost_estimate=BRIEF,
        name="own_terms",
    )(both, unit, dq, mixed, *weights)


def returns_kernel(bounds, keep_ref, got_ref, last_ref, *outs):
    for (first, last), out_ref in zip(bounds, outs):
        total = keep_ref[0, first:last, :].astype(F32) + got_ref[0, first:last, :].astype(F32)
        out_ref[...] = (total + last_ref[first:last, :].astype(F32)).astype(BF16)


def run_returns(bounds, keep, got, last):
    vmem = pl.BlockSpec(memory_space=pltpu.VMEM)
    width = keep.shape[2]
    return pl.pallas_call(
        functools.partial(returns_kernel, bounds),
        out_shape=[jax.ShapeDtypeStruct((b - a, width), BF16) for a, b in bounds],
        in_specs=[vmem] * 3,
        out_specs=[vmem] * len(bounds),
        compiler_params=pltpu.CompilerParams(vmem_limit_bytes=SMALL),
        cost_estimate=BRIEF,
        name="returned_terms",
    )(keep, got, last)


def my_bits():
    dom = lax.axis_index("dom")
    return lax.axis_index("dp"), dom & 1, dom >> 1


def halve_kernel(bits, *refs):
    count = len(bits)
    ins, outs = refs[: 2 * count], refs[2 * count :]
    mine = my_bits()
    size = outs[0].shape[0]
    for index, bit in enumerate(bits):
        keep_ref, got_ref = ins[2 * index : 2 * index + 2]
        for side, name in enumerate((mine[bit], 1 - mine[bit])):
            at = block_at(name, size)
            total = keep_ref[at, :].astype(F32) + got_ref[at, :].astype(F32)
            outs[2 * index + side][...] = total.astype(BF16)


def run_halve(bits, *arrays):
    vmem = pl.BlockSpec(memory_space=pltpu.VMEM)
    rows, feats = arrays[0].shape
    return pl.pallas_call(
        functools.partial(halve_kernel, bits),
        out_shape=[jax.ShapeDtypeStruct((rows // 2, feats), BF16)] * len(arrays),
        in_specs=[vmem] * len(arrays),
        out_specs=[vmem] * len(arrays),
        compiler_params=pltpu.CompilerParams(vmem_limit_bytes=SMALL),
        cost_estimate=BRIEF,
        name="halve_grads",
    )(*arrays)


def total_kernel(*refs):
    out_ref = refs[-1]
    size = refs[0].shape[0]
    for index in range(len(refs) // 2):
        total = refs[2 * index][...].astype(F32) + refs[2 * index + 1][...].astype(F32)
        out_ref[index * size : (index + 1) * size, :] = total.astype(BF16)


def run_total(*arrays):
    vmem = pl.BlockSpec(memory_space=pltpu.VMEM)
    rows, feats = arrays[0].shape
    return pl.pallas_call(
        total_kernel,
        out_shape=jax.ShapeDtypeStruct((len(arrays) // 2 * rows, feats), BF16),
        in_specs=[vmem] * len(arrays),
        out_specs=vmem,
        compiler_params=pltpu.CompilerParams(vmem_limit_bytes=SMALL),
        cost_estimate=BRIEF,
        name="total_grads",
    )(*arrays)


def settle_kernel(mine_ref, got_ref, *outs):
    size = outs[0].shape[0]
    for index, out_ref in enumerate(outs):
        rows = slice(index * size, (index + 1) * size)
        total = mine_ref[rows, :].astype(F32) + got_ref[rows, :].astype(F32)
        out_ref[...] = total.astype(BF16)


def run_settle(mine, got):
    vmem = pl.BlockSpec(memory_space=pltpu.VMEM)
    rows, feats = mine.shape
    return pl.pallas_call(
        settle_kernel,
        out_shape=[jax.ShapeDtypeStruct((rows // 2, feats), BF16)] * 2,
        in_specs=[vmem] * 2,
        out_specs=[vmem] * 2,
        compiler_params=pltpu.CompilerParams(vmem_limit_bytes=SMALL),
        cost_estimate=BRIEF,
        name="settle_grads",
    )(mine, got)


def join_kernel(bits, *refs):
    count = len(bits)
    outs = refs[-count:]
    mine = my_bits()
    size = refs[0].shape[0]
    for index, bit in enumerate(bits):
        outs[index][block_at(mine[bit], size), :] = refs[2 * index][...]
        outs[index][block_at(1 - mine[bit], size), :] = refs[2 * index + 1][...]


def run_join(bits, *arrays):
    vmem = pl.BlockSpec(memory_space=pltpu.VMEM)
    rows, feats = arrays[0].shape
    return pl.pallas_call(
        functools.partial(join_kernel, bits),
        out_shape=[jax.ShapeDtypeStruct((2 * rows, feats), BF16)] * len(bits),
        in_specs=[vmem] * len(arrays),
        out_specs=[vmem] * len(bits),
        compiler_params=pltpu.CompilerParams(vmem_limit_bytes=SMALL),
        cost_estimate=BRIEF,
        name="join_grads",
    )(*arrays)


def own_sum_kernel(keep_ref, got_ref, last_ref, update_ref, unit_ref):
    rows = update_ref.shape[0]

    def total(first, last):
        both = keep_ref[0, first:last, :].astype(F32) + got_ref[0, first:last, :].astype(F32)
        return both + last_ref[first:last, :].astype(F32)

    unit_ref[...] = total(0, rows + PAD)
    update_ref[...] = total(rows + PAD, 2 * rows + PAD).astype(BF16)


def run_own_sum(rows, keep, got, last):
    width = last.shape[1]
    vmem = pl.BlockSpec(memory_space=pltpu.VMEM)
    shape = jax.ShapeDtypeStruct
    return pl.pallas_call(
        own_sum_kernel,
        out_shape=(shape((rows, width), BF16), shape((rows + PAD, width), F32)),
        in_specs=[vmem] * 3,
        out_specs=[vmem] * 2,
        compiler_params=pltpu.CompilerParams(vmem_limit_bytes=SMALL),
        cost_estimate=BRIEF,
        name="own_sum",
    )(keep, got, last)


def finish_kernel(cfg, *refs):
    blocks, offsets, width, feats, spread = cfg
    send_ref, sum_ref, slab_ref, inverse_ref = refs[:4]
    far_refs = refs[4 : 4 + len(spread)]
    branch_ref, unit_ref, table, sem = refs[4 + len(spread) :]
    fetch = pltpu.make_async_copy(send_ref, table, sem)
    fetch.start()
    own_rows = blocks * BLK
    sub = BLK // width
    group = SEND * BLK + PAD

    unit_ref[...] = sum_ref[:own_rows, :]
    dots = sum_ref[own_rows:, :]
    at_row = lax.broadcasted_iota(jnp.int32, (PAD, width), 0)
    fetch.wait()
    for ref, members in zip(far_refs, spread):
        for position, offset in enumerate(members):
            first = position * group
            extra = ref[first + SEND * BLK : first + group, :].astype(F32)
            for c in range(SEND):
                block = table[c, offset]
                rows = ref[first + c * BLK : first + (c + 1) * BLK, :].astype(F32)
                unit_ref[block_at(block), :] += rows
                for piece in range(sub):
                    line = extra[c * sub + piece : c * sub + piece + 1, :]
                    dots = dots + jnp.where(at_row == block * sub + piece, line, 0.0)
    for block in range(blocks):
        rows = slice(block * BLK, (block + 1) * BLK)
        line = jnp.concatenate(
            [dots[block * sub + piece : block * sub + piece + 1, :] for piece in range(sub)], axis=1
        )
        mean = jnp.broadcast_to(line * (1.0 / feats), (BLK, BLK)).T[:, :width]
        branch = inverse_ref[rows, :] * (unit_ref[rows, :] - slab_ref[rows, :] * mean)
        branch_ref[rows, :] = branch.astype(BF16)


def run_finish(feats, send, own_sum, slab, inverse, far, spread):
    rows, width = slab.shape
    vmem = pl.BlockSpec(memory_space=pltpu.VMEM)
    hbm = pl.BlockSpec(memory_space=pltpu.HBM)
    cfg = (rows // BLK, send.shape[1], width, feats, spread)
    return pl.pallas_call(
        functools.partial(finish_kernel, cfg),
        out_shape=jax.ShapeDtypeStruct((rows, width), BF16),
        in_specs=[hbm] + [vmem] * (3 + len(far)),
        out_specs=vmem,
        scratch_shapes=[
            pltpu.VMEM((rows, width), F32),
            pltpu.SMEM(send.shape, jnp.int32),
            pltpu.SemaphoreType.DMA(()),
        ],
        compiler_params=pltpu.CompilerParams(vmem_limit_bytes=SMALL),
        cost_estimate=BRIEF,
        name="finish",
    )(*in_hbm(send), own_sum, slab, inverse, *far)


def grads_kernel(factor, *refs):
    first_held, first_got, second_held, second_got = refs[:4]
    results, made, sems = refs[4:8], refs[8:12], refs[12]
    dp, low, _ = my_bits()
    first, second = jnp.equal(dp, 1), jnp.equal(low, 1)
    copies = [
        pltpu.make_async_copy(source, target, sems.at[index])
        for index, (source, target) in enumerate(zip(made, results))
    ]

    def picked(flag, left, right, start):
        columns = slice(start, start + BLK)
        return jnp.where(flag, left[:, columns].astype(F32), right[:, columns].astype(F32)) * factor

    picks = (
        (first, first_got, first_held),
        (first, first_held, first_got),
        (second, second_got, second_held),
        (second, second_held, second_got),
    )
    for index in (3, 0, 1, 2):
        for start in range(0, first_held.shape[1], BLK):
            rows = slice(start, start + BLK)
            block = picked(*picks[index], start)
            if index == 3:
                made[index][:, rows] = block
            else:
                made[index][rows, :] = block.T
        copies[index].start()
    for copy in copies:
        copy.wait()


def run_grads(factor, *arrays):
    width, feats = arrays[0].shape
    vmem = pl.BlockSpec(memory_space=pltpu.VMEM)
    hbm = pl.BlockSpec(memory_space=pltpu.HBM)
    shapes = [(feats, width)] * 3 + [(width, feats)]
    return pl.pallas_call(
        functools.partial(grads_kernel, factor),
        out_shape=[jax.ShapeDtypeStruct(shape, F32) for shape in shapes],
        in_specs=[vmem] * 4,
        out_specs=[hbm] * 4,
        scratch_shapes=[
            *[pltpu.VMEM(shape, F32) for shape in shapes],
            pltpu.SemaphoreType.DMA((4,)),
        ],
        compiler_params=pltpu.CompilerParams(vmem_limit_bytes=SMALL),
        cost_estimate=BRIEF,
        name="weight_grads",
    )(*arrays)


def swap(array, axis, bit):
    return lax.ppermute(array, axis, [(i, i ^ bit) for i in range(lax.axis_size(axis))])


def shifted(array, axis, distance):
    size = lax.axis_size(axis)
    return lax.ppermute(array, axis, [(i, (i + distance) % size) for i in range(size)])


def added(left, right):
    return (left.astype(F32) + right.astype(F32)).astype(BF16)


def after(values, *earlier):
    held = lax.optimization_barrier((values, earlier))
    return held[0]


def narrow(keep, got, bit):
    while keep.shape[0] > 2:
        summed = added(keep, got)
        keep, send = summed[0::2], summed[1::2]
        got = swap(send, "tensor", bit)
        bit *= 2
    return keep, got, bit


def body(states, w_query, w_key, w_value, w_out, send_blocks, neighbor_blocks, cotangent):
    replicas, node_count, feats = states.shape
    width = w_query.shape[1]
    ranks = lax.axis_size("tensor")
    parts = lax.axis_size("dom")
    explicit = parts == 4 and lax.axis_size("dp") == 2
    offsets = offset_list(HOPS)
    order, share = piece_order(ranks, len(offsets))
    send = send_blocks[0].T
    weights = (w_query, w_key, w_value, w_out)
    flat_states = states.reshape(-1, feats)
    flat_cot = cotangent.reshape(-1, feats)

    leaving = pick_blocks(flat_states, send, ranks, share)
    route = []
    for p in range(parts):
        for r in range(ranks):
            distance = offsets[order[r * share] // SEND]
            route.append((p * ranks + r, ((p + distance) % parts) * ranks + r))
    levels = []
    bit = 1
    while bit < ranks:
        levels.append(bit)
        bit *= 2
    arrived = [lax.ppermute(block, ("dom", "tensor"), route) for block in leaving]
    own = run_own(flat_states, flat_cot, weights)
    arrived[0] = after(arrived[0], own[0])
    unit, slab, inverse, cot = own[0], own[7], own[8], own[9]
    weights = own[10:]
    first_pieces = list(arrived)
    wide = [swap(block, "tensor", levels[-1]) for block in arrived]
    close = after(first_pieces, *arrived)
    close = [swap(half, "tensor", 1) for block in close for half in jnp.split(block, 2)]
    early = run_early(first_pieces + close, weights[1], weights[2])
    held = {levels[-1]: after(wide, early[0])}
    for bit in reversed(levels[:-1]):
        for slot in list(held):
            held[slot ^ bit] = [swap(block, "tensor", bit) for block in held[slot]]
    for bit in levels[1:-1]:
        held[bit] = [swap(block, "tensor", bit) for block in first_pieces]
        held[bit ^ 1] = [swap(block, "tensor", 1) for block in held[bit]]
    pieces = [block for slot in range(EARLY, ranks) for block in held[slot]]
    count = len(offsets)
    both, dq, mixed, far_keep, far_send, *halves = run_attend(
        explicit,
        early,
        ranks,
        share,
        count,
        neighbor_blocks,
        pieces,
        own[:7],
        cot,
        weights[1],
        weights[2],
    )
    total_rows = replicas * node_count * lax.axis_size("dp") * parts
    factor = 1.0 / math.sqrt(total_rows)

    if explicit:
        first, second = swap(halves[1], "dp", 1), swap(halves[3], "dom", 1)
    far_keep, far_got, bit = narrow(far_keep, swap(far_send, "tensor", 1), 2)
    own_keep, own_send = run_own_terms(both, unit, dq, mixed, weights)
    own_keep, own_got, bit = narrow(own_keep, swap(own_send, "tensor", 1), 2)
    far_out = added(far_keep[1], far_got[1])
    far_last = swap(far_out, "tensor", bit)
    if explicit:
        first, second = after(first, far_out, own_send), after(second, far_out, own_send)
        halves = run_halve((1, 0), halves[0], first, halves[2], second)
        first, second = swap(halves[1], "dom", 1), swap(halves[3], "dp", 1)
        total = run_total(halves[0], first, halves[2], second)
        got = swap(total, "dom", 2)
        own_got = after(own_got, total)
    own_out = added(own_keep[1], own_got[1])
    own_last = swap(own_out, "tensor", bit)
    far_last = after(far_last, own_out)

    group = SEND * BLK + PAD
    spread = []
    for index, distance in enumerate(offsets):
        for members in spread:
            if (offsets[members[0]] - distance) % parts == 0 and members[-1] == index - 1:
                members.append(index)
                break
        else:
            spread.append([index])
    spread = tuple(tuple(members) for members in spread)
    bounds = tuple((members[0] * group, (members[-1] + 1) * group) for members in spread)
    far_sums = run_returns(bounds, far_keep, far_got, far_last)
    returned = [
        shifted(part, "dom", -offsets[members[0]]) for part, members in zip(far_sums, spread)
    ]
    own_last = after(own_last, far_sums)
    update, own_sum = run_own_sum(replicas * node_count, own_keep, own_got, own_last)
    if explicit:
        held = run_settle(total, after(got, own_sum))
        first, second = swap(held[0], "dom", 1), swap(held[1], "dp", 1)
        first = after(first, returned)
        held = run_join((1, 0), held[0], first, held[1], second)
        first, second = swap(held[0], "dp", 1), swap(held[1], "dom", 1)
    branch = run_finish(feats, send, own_sum, slab, inverse, returned, spread)
    if explicit:
        first = after(first, branch)
        grads = run_grads(factor, held[0], first, held[1], second)
    else:
        summed = [lax.psum(half.astype(F32), ("dp", "dom")) * factor for half in halves]
        grads = (summed[0].T, summed[1].T, summed[2].T, summed[3])
    shape = (replicas, node_count, width)
    return (update.reshape(shape), branch.reshape(shape), *grads)


def solution(mesh):
    placed = (
        P("dp", "dom", None),
        P(None, "tensor"),
        P(None, "tensor"),
        P(None, "tensor"),
        P("tensor", None),
        P("dom", None, None),
        P("dom", None),
        P("dp", "dom", None),
    )
    return jax.shard_map(
        body,
        mesh=mesh,
        in_specs=placed,
        out_specs=(
            P("dp", "dom", "tensor"),
            P("dp", "dom", "tensor"),
            P(None, "tensor"),
            P(None, "tensor"),
            P(None, "tensor"),
            P("tensor", None),
        ),
        check_vma=False,
    )
```

```python
import functools
import math

import jax
import jax.numpy as jnp
from jax import lax
from jax.experimental import pallas as pl
from jax.experimental.pallas import tpu as pltpu
from jax.sharding import PartitionSpec as P

BLK = 128
HOPS = 2
SEND = 2
HD = 64
PAD = 16
EARLY = 2
EPS = 1e-05
LIMIT = 24 * 1024 * 1024
SMALL = 8 * 1024 * 1024
CHUNK = 64
BRIEF = pl.CostEstimate(flops=1, bytes_accessed=1, transcendentals=0)
F32 = jnp.float32
BF16 = jnp.bfloat16


def offset_list(hops):
    result = []
    for section in range(1, hops + 1):
        result.append(section)
        result.append(-section)
    return result


def piece_order(ranks, offsets):
    count = offsets * SEND
    share = count // ranks
    if share == SEND and offsets == 4:
        return [0, 1, 4, 5, 2, 3, 6, 7], share
    return list(range(count)), share


def nt(left, right):
    return lax.dot_general(left, right, (((1,), (1,)), ((), ())), preferred_element_type=F32)


def nn(left, right):
    return jnp.dot(left, right, preferred_element_type=F32)


def unit_of(rows):
    values = rows.astype(F32)
    return (values * lax.rsqrt(jnp.mean(values * values, axis=-1, keepdims=True) + EPS)).astype(BF16)


def block_at(index, size=BLK):
    return pl.ds(pl.multiple_of(index * size, size), size)


def rank_piece(rank, ranks, share, inner):
    if share == SEND and ranks == 4:
        return ((rank & 1) * 2 + (rank >> 1)) * SEND + inner
    return rank * share + inner


def in_hbm(*arrays):
    return [pltpu.with_memory_space_constraint(array, pltpu.HBM) for array in arrays]


def pick_kernel(ranks, share, send_ref, states_ref, *refs):
    outs, (table, held, sems) = refs[:share], refs[share:]
    rank = lax.axis_index("tensor")
    copies = [
        pltpu.make_async_copy(send_ref, table, sems.at[0]),
        pltpu.make_async_copy(states_ref, held, sems.at[1]),
    ]
    for copy in copies:
        copy.start()
    for copy in copies:
        copy.wait()
    for inner, out_ref in enumerate(outs):
        piece = rank_piece(rank, ranks, share, inner)
        out_ref[...] = held[block_at(table[piece % SEND, piece // SEND]), :]


def pick_blocks(states, send, ranks, share):
    far = pl.BlockSpec(memory_space=pltpu.HBM)
    vmem = pl.BlockSpec(memory_space=pltpu.VMEM)
    return pl.pallas_call(
        functools.partial(pick_kernel, ranks, share),
        out_shape=[jax.ShapeDtypeStruct((BLK, states.shape[1]), BF16)] * share,
        in_specs=[far, far],
        out_specs=[vmem] * share,
        scratch_shapes=[
            pltpu.SMEM(send.shape, jnp.int32),
            pltpu.VMEM(states.shape, BF16),
            pltpu.SemaphoreType.DMA((2,)),
        ],
        compiler_params=pltpu.CompilerParams(vmem_limit_bytes=SMALL),
        cost_estimate=BRIEF,
        name="pick_blocks",
    )(*in_hbm(send, states))


def by_head(rows, heads):
    if heads == 1:
        return rows.astype(BF16)
    lane_head = lax.broadcasted_iota(jnp.int32, rows.shape, 1) // HD
    return jnp.concatenate(
        [jnp.where(lane_head == head, rows, 0.0) for head in range(heads)], axis=0
    ).astype(BF16)


def diagonal(stacked, heads):
    return jnp.concatenate(
        [
            stacked[head * HD : (head + 1) * HD, head * BLK : (head + 1) * BLK]
            for head in range(heads)
        ],
        axis=0,
    )


def put_pairs(paired, at, width, k_ref, v_ref, kt_ref, vt_ref):
    for index, entry in enumerate(at):
        rows = paired[index * BLK : (index + 1) * BLK]
        keys, values = rows[:, :width], rows[:, width:]
        k_ref[block_at(entry), :] = keys.astype(BF16)
        v_ref[block_at(entry), :] = values.astype(BF16)
        kt_ref[entry] = keys.T.astype(BF16)
        vt_ref[entry] = values.T.astype(BF16)


def own_kernel(*refs):
    sources = refs[:6]
    unit_ref, q_ref, g_ref, k_ref, v_ref, kt_ref, vt_ref, slab_ref, inverse_ref = refs[6:15]
    held, states_ref, sems = refs[15:20], refs[20], refs[21]
    cot_ref, wq_ref, wk_ref, wv_ref, wo_ref = held
    copies = []
    for index, (source, target) in enumerate(zip(sources, (states_ref,) + tuple(held))):
        copies.append(pltpu.make_async_copy(source, target, sems.at[index]))
        copies[-1].start()
    rows, feats = states_ref.shape
    width = wq_ref.shape[1]
    heads = width // HD
    tall = heads * BLK
    rank = lax.axis_index("tensor")
    copies[0].wait()
    for start in range(0, rows, CHUNK):
        values = states_ref[start : start + CHUNK, :].astype(F32)
        inverse = lax.rsqrt(jnp.mean(values * values, axis=-1, keepdims=True) + EPS)
        normed = values * inverse
        unit_ref[start : start + CHUNK, :] = normed.astype(BF16)
        slab = normed[:, :width]
        for index in range(1, feats // width):
            slab = jnp.where(rank == index, normed[:, index * width : (index + 1) * width], slab)
        slab_ref[start : start + CHUNK, :] = slab
        inverse_ref[start : start + CHUNK, :] = jnp.broadcast_to(inverse, slab.shape)
    for copy in copies[1:]:
        copy.wait()
    unit = unit_ref[...]
    queries = nn(unit, wq_ref[...])
    grads = nt(cot_ref[...], wo_ref[...])
    for block in range(rows // BLK):
        q_ref[block * tall : (block + 1) * tall, :] = by_head(
            queries[block * BLK : (block + 1) * BLK], heads
        )
        g_ref[block * tall : (block + 1) * tall, :] = by_head(
            grads[block * BLK : (block + 1) * BLK], heads
        )
    paired = nn(unit, jnp.concatenate([wk_ref[...], wv_ref[...]], axis=1))
    put_pairs(paired, range(rows // BLK), width, k_ref, v_ref, kt_ref, vt_ref)


def run_own(states, cot, weights):
    rows, feats = states.shape
    width = weights[0].shape[1]
    blocks = rows // BLK
    tall = blocks * (width // HD) * BLK
    vmem = pl.BlockSpec(memory_space=pltpu.VMEM)
    far = pl.BlockSpec(memory_space=pltpu.HBM)
    shape = jax.ShapeDtypeStruct
    return pl.pallas_call(
        own_kernel,
        out_shape=(
            shape((rows, feats), BF16),
            shape((tall, width), BF16),
            shape((tall, width), BF16),
            shape((rows, width), BF16),
            shape((rows, width), BF16),
            shape((blocks, width, BLK), BF16),
            shape((blocks, width, BLK), BF16),
            shape((rows, width), F32),
            shape((rows, width), F32),
            shape(cot.shape, BF16),
            *[shape(w.shape, BF16) for w in weights],
        ),
        in_specs=[far] * 6,
        out_specs=[vmem] * 14,
        scratch_shapes=[pltpu.VMEM((rows, feats), BF16), pltpu.SemaphoreType.DMA((6,))],
        compiler_params=pltpu.CompilerParams(vmem_limit_bytes=LIMIT),
        cost_estimate=BRIEF,
        name="own_rows",
    )(*in_hbm(states, cot, *weights))


def early_kernel(count, *refs):
    piece_refs, (wk_ref, wv_ref) = refs[:count], refs[count : count + 2]
    unit_ref, k_ref, v_ref, kt_ref, vt_ref = refs[count + 2 :]
    width = wk_ref.shape[1]
    at = 0
    for source in piece_refs:
        for start in range(0, source.shape[0], CHUNK):
            unit_ref[at : at + CHUNK, :] = unit_of(source[start : start + CHUNK, :])
            at += CHUNK
    wkv = jnp.concatenate([wk_ref[...], wv_ref[...]], axis=1)
    paired = nn(unit_ref[...], wkv)
    blocks = range(unit_ref.shape[0] // BLK)
    put_pairs(paired, blocks, width, k_ref, v_ref, kt_ref, vt_ref)


def run_early(pieces, w_key, w_value):
    inputs, count = len(pieces), sum(piece.shape[0] for piece in pieces) // BLK
    feats, width = w_key.shape
    vmem = pl.BlockSpec(memory_space=pltpu.VMEM)
    shape = jax.ShapeDtypeStruct
    return pl.pallas_call(
        functools.partial(early_kernel, inputs),
        out_shape=(
            shape((count * BLK, feats), BF16),
            shape((count * BLK, width), BF16),
            shape((count * BLK, width), BF16),
            shape((count, width, BLK), BF16),
            shape((count, width, BLK), BF16),
        ),
        in_specs=[vmem] * (inputs + 2),
        out_specs=[vmem] * 5,
        compiler_params=pltpu.CompilerParams(vmem_limit_bytes=LIMIT),
        cost_estimate=BRIEF,
        name="early_rows",
    )(*pieces, w_key, w_value)


def attend_kernel(cfg, near_ref, *refs):
    ranks, share, blocks, offsets, width, explicit, early = cfg
    early_refs, refs = refs[:5], refs[5:]
    count = (ranks - early) * share
    piece_refs = refs[:count]
    own_refs = refs[count : count + 7]
    cot_ref, wk_ref, wv_ref = refs[count + 7 : count + 10]
    refs = refs[count + 10 :]
    both_ref, dq_ref, mixed_ref = refs[:3]
    far_refs, half_refs = refs[3:5], refs[5:9]
    pool_ref, refs = refs[9], refs[10:]
    k_ref, v_ref, kt_ref, vt_ref, ka_ref, va_ref, dk_ref, dv_ref = refs[:8]
    score_ref, prob_ref, low_ref, change_ref, near_table, near_sem = refs[8:]
    fetch = pltpu.make_async_copy(near_ref, near_table, near_sem)
    fetch.start()
    q_ref, g_ref, k_own, v_own, kt_own, vt_own = own_refs[1:]
    heads = width // HD
    tall = heads * BLK
    entries = blocks + offsets * SEND
    rank = lax.axis_index("tensor")

    own_rows = blocks * BLK
    k_ref[:own_rows, :] = k_own[...]
    v_ref[:own_rows, :] = v_own[...]
    kt_ref[:blocks] = kt_own[...]
    vt_ref[:blocks] = vt_own[...]
    wkv = jnp.concatenate([wk_ref[...], wv_ref[...]], axis=1)
    unit_e, k_e, v_e, kt_e, vt_e = early_refs
    for slot in range(early):
        for inner in range(share):
            entry = rank_piece(rank ^ slot, ranks, share, inner)
            index = slot * share + inner
            rows = slice(index * BLK, (index + 1) * BLK)
            pool_ref[block_at(entry), :] = unit_e[rows, :]
            k_ref[block_at(entry + blocks), :] = k_e[rows, :]
            v_ref[block_at(entry + blocks), :] = v_e[rows, :]
            kt_ref[entry + blocks] = kt_e[index]
            vt_ref[entry + blocks] = vt_e[index]
    late, places = [], []
    for slot in range(early, ranks):
        for inner in range(share):
            entry = rank_piece(rank ^ slot, ranks, share, inner)
            base = pl.multiple_of(entry * BLK, BLK)
            places.append(entry + blocks)
            source = piece_refs[(slot - early) * share + inner]
            for start in range(0, BLK, CHUNK):
                rows = unit_of(source[start : start + CHUNK, :])
                pool_ref[pl.ds(pl.multiple_of(base + start, CHUNK), CHUNK), :] = rows
                late.append(rows)
    paired = nn(jnp.concatenate(late, axis=0), wkv)
    put_pairs(paired, places, width, k_ref, v_ref, kt_ref, vt_ref)

    shrink = 1.0 / math.sqrt(HD)
    near = near_ref.shape[1]
    fetch.wait()
    listed = [[block] + [near_table[block, n] for n in range(near)] for block in range(blocks)]

    def open_block(block):
        keys = jnp.concatenate([k_ref[block_at(e), :] for e in listed[block]], axis=0)
        values = jnp.concatenate([v_ref[block_at(e), :] for e in listed[block]], axis=0)
        score_ref[block] = nt(keys, q_ref[block * tall : (block + 1) * tall, :]) * shrink
        prob_ref[block] = nt(values, g_ref[block * tall : (block + 1) * tall, :])

    def weigh_block(block):
        spans = [slice(n * BLK, (n + 1) * BLK) for n in range(near + 1)]
        highest = jnp.max(score_ref[block, spans[0], :], axis=0, keepdims=True)
        for span in spans[1:]:
            rows = jnp.max(score_ref[block, span, :], axis=0, keepdims=True)
            highest = jnp.maximum(highest, rows)
        total, drop = jnp.zeros_like(highest), jnp.zeros_like(highest)
        for span in spans:
            powers = jnp.exp(score_ref[block, span, :] - highest)
            score_ref[block, span, :] = powers
            total = total + jnp.sum(powers, axis=0, keepdims=True)
            drop = drop + jnp.sum(powers * prob_ref[block, span, :], axis=0, keepdims=True)
        scale = 1.0 / total
        drop = drop * scale
        for span in spans:
            weights = score_ref[block, span, :] * scale
            low_ref[block, span, :] = weights.astype(BF16)
            change = weights * (prob_ref[block, span, :] - drop) * shrink
            change_ref[block, span, :] = change.astype(BF16)

    def close_block(block):
        rows = slice(block * BLK, (block + 1) * BLK)
        keys_t = jnp.concatenate([kt_ref[e] for e in listed[block]], axis=1)
        values_t = jnp.concatenate([vt_ref[e] for e in listed[block]], axis=1)
        low, change = low_ref[block], change_ref[block]
        mixed_ref[rows, :] = diagonal(nn(values_t, low), heads).T.astype(BF16)
        dq_ref[rows, :] = diagonal(nn(keys_t, change), heads).T.astype(BF16)
        dk = nn(change, q_ref[block * tall : (block + 1) * tall, :])
        dv = nn(low, g_ref[block * tall : (block + 1) * tall, :])
        ka_ref[rows, :] = dk[:BLK]
        va_ref[rows, :] = dv[:BLK]
        dk_ref[block] = dk[BLK:]
        dv_ref[block] = dv[BLK:]

    open_block(0)
    for block in range(blocks):
        if block + 1 < blocks:
            open_block(block + 1)
        weigh_block(block)
        if block:
            close_block(block - 1)
    close_block(blocks - 1)

    ka_ref[own_rows:, :] = jnp.zeros((entries * BLK - own_rows, width), F32)
    va_ref[own_rows:, :] = jnp.zeros((entries * BLK - own_rows, width), F32)
    for block in range(blocks):
        for n in range(near):
            entry = block_at(listed[block][n + 1])
            ka_ref[entry, :] += dk_ref[block, n * BLK : (n + 1) * BLK]
            va_ref[entry, :] += dv_ref[block, n * BLK : (n + 1) * BLK]

    both_ref[:, :width] = ka_ref[...].astype(BF16)
    both_ref[:, width:] = va_ref[...].astype(BF16)
    grad_terms(explicit, own_refs[0], pool_ref, both_ref, dq_ref, mixed_ref, cot_ref, *half_refs)
    far_terms(blocks, pool_ref, both_ref, wk_ref, wv_ref, *far_refs)


def grad_terms(explicit, unit_ref, pool_ref, both_ref, dq_ref, mixed_ref, cot_ref, *refs):
    first_keep, first_send, second_keep, second_send = refs
    rows, width = dq_ref.shape

    def turned(ref, first, last):
        parts = [
            ref[start : start + BLK, :].astype(F32).T.astype(BF16)
            for start in range(first, last, BLK)
        ]
        return jnp.concatenate(parts, axis=1)

    unit = unit_ref[...]
    grad_q = nn(turned(dq_ref, 0, rows), unit)
    grad_out = nn(turned(mixed_ref, 0, rows), cot_ref[...])
    grad_kv = nn(turned(both_ref, 0, rows), unit)
    grad_kv = grad_kv + nn(turned(both_ref, rows, both_ref.shape[0]), pool_ref[...])
    grad_k, grad_v = grad_kv[:width], grad_kv[width:]
    by_dp = jnp.equal(lax.axis_index("dp") if explicit else 0, 1)
    by_dom = jnp.equal(lax.axis_index("dom") & 1 if explicit else 0, 1)
    first_keep[...] = jnp.where(by_dp, grad_k, grad_q).astype(BF16)
    first_send[...] = jnp.where(by_dp, grad_q, grad_k).astype(BF16)
    second_keep[...] = jnp.where(by_dom, grad_out, grad_v).astype(BF16)
    second_send[...] = jnp.where(by_dom, grad_v, grad_out).astype(BF16)


def run_attend(explicit, early, ranks, share, offsets, near, pieces, own, cot, w_key, w_value):
    rows, feats = own[0].shape
    blocks = rows // BLK
    width = w_key.shape[1]
    received = offsets * SEND
    entries = blocks + received
    listed, tall = (near.shape[1] + 1) * BLK, width // HD * BLK
    vmem = pl.BlockSpec(memory_space=pltpu.VMEM)
    far = pl.BlockSpec(memory_space=pltpu.HBM)
    cfg = (ranks, share, blocks, offsets, width, explicit, EARLY)
    shape = jax.ShapeDtypeStruct
    return pl.pallas_call(
        functools.partial(attend_kernel, cfg),
        out_shape=[
            shape((entries * BLK, 2 * width), BF16),
            shape((rows, width), BF16),
            shape((rows, width), BF16),
            *[shape((feats // width // 2, offsets * (SEND * BLK + PAD), width), BF16)] * 2,
            *[shape((width, feats), BF16)] * 4,
        ],
        in_specs=[far] + [vmem] * (len(early) + len(pieces) + 10),
        out_specs=[vmem] * 9,
        scratch_shapes=[
            pltpu.VMEM((received * BLK, feats), BF16),
            pltpu.VMEM((entries * BLK, width), BF16),
            pltpu.VMEM((entries * BLK, width), BF16),
            pltpu.VMEM((entries, width, BLK), BF16),
            pltpu.VMEM((entries, width, BLK), BF16),
            pltpu.VMEM((entries * BLK, width), F32),
            pltpu.VMEM((entries * BLK, width), F32),
            pltpu.VMEM((blocks, near.shape[1] * BLK, width), F32),
            pltpu.VMEM((blocks, near.shape[1] * BLK, width), F32),
            *[pltpu.VMEM((blocks, listed, tall), F32)] * 2,
            *[pltpu.VMEM((blocks, listed, tall), BF16)] * 2,
            pltpu.SMEM(near.shape, jnp.int32),
            pltpu.SemaphoreType.DMA(()),
        ],
        compiler_params=pltpu.CompilerParams(vmem_limit_bytes=LIMIT),
        cost_estimate=BRIEF,
        name="attention",
    )(*in_hbm(near), *early, *pieces, *own, cot, w_key, w_value)


def put(odd, upper, keep_ref, send_ref, row, values):
    count, width = values.shape[0], keep_ref.shape[2]
    for pair in range(values.shape[1] // width // 2):
        left = values[:, 2 * pair * width : (2 * pair + 1) * width]
        right = values[:, (2 * pair + 1) * width : (2 * pair + 2) * width]
        at = upper ^ pair
        keep_ref[at, row : row + count, :] = jnp.where(odd, right, left).astype(BF16)
        send_ref[at, row : row + count, :] = jnp.where(odd, left, right).astype(BF16)


def put_dots(keep_ref, send_ref, row, dots):
    width = keep_ref.shape[2]
    parts = []
    for dot in dots:
        for piece in range(BLK // width):
            parts.append(dot[:1, piece * width : (piece + 1) * width])
    parts.append(jnp.zeros((PAD - len(parts), width), F32))
    rows = jnp.concatenate(parts, axis=0).astype(BF16)
    for pair in range(keep_ref.shape[0]):
        keep_ref[pair, row : row + PAD, :] = rows
        send_ref[pair, row : row + PAD, :] = rows


def row_dot(term, ref, first):
    ones = jnp.ones((16, ref.shape[1]), BF16)
    product = (term * ref[first : first + BLK, :].astype(F32)).astype(BF16)
    return nt(ones, product)


def far_terms(blocks, pool_ref, both_ref, wk_ref, wv_ref, far_keep, far_send):
    rank = lax.axis_index("tensor")
    odd, upper = (rank & 1) == 1, rank >> 1
    rows, step = blocks * BLK, SEND * BLK
    wkv = jnp.concatenate([wk_ref[...], wv_ref[...]], axis=1)
    for index in range(pool_ref.shape[0] // step):
        first, at = index * step, index * (step + PAD)
        term = nt(both_ref[rows + first : rows + first + step, :], wkv)
        put(odd, upper, far_keep, far_send, at, term)
        dots = [
            row_dot(term[c * BLK : (c + 1) * BLK], pool_ref, first + c * BLK) for c in range(SEND)
        ]
        put_dots(far_keep, far_send, at + step, dots)


def own_terms_kernel(both_ref, unit_ref, dq_ref, mixed_ref, *refs):
    wq_ref, wk_ref, wv_ref, wo_ref, own_keep, own_send = refs
    rank = lax.axis_index("tensor")
    odd, upper = (rank & 1) == 1, rank >> 1
    rows, step = unit_ref.shape[0], 2 * BLK
    wkv = jnp.concatenate([wk_ref[...], wv_ref[...]], axis=1)
    dots = []
    for first in range(0, rows, step):
        last = first + step
        term = nt(both_ref[first:last, :], wkv) + nt(dq_ref[first:last, :], wq_ref[...])
        put(odd, upper, own_keep, own_send, first, term)
        dots += [row_dot(term[c * BLK : (c + 1) * BLK], unit_ref, first + c * BLK) for c in (0, 1)]
        update = nn(mixed_ref[first:last, :], wo_ref[...])
        put(odd, upper, own_keep, own_send, rows + PAD + first, update)
    put_dots(own_keep, own_send, rows, dots)


def run_own_terms(both, unit, dq, mixed, weights):
    rows, feats = unit.shape
    width = dq.shape[1]
    vmem = pl.BlockSpec(memory_space=pltpu.VMEM)
    own = jax.ShapeDtypeStruct((feats // width // 2, 2 * rows + PAD, width), BF16)
    return pl.pallas_call(
        own_terms_kernel,
        out_shape=(own, own),
        in_specs=[vmem] * 8,
        out_specs=[vmem] * 2,
        compiler_params=pltpu.CompilerParams(vmem_limit_bytes=LIMIT),
        cost_estimate=BRIEF,
        name="own_terms",
    )(both, unit, dq, mixed, *weights)


def returns_kernel(bounds, keep_ref, got_ref, last_ref, *outs):
    for (first, last), out_ref in zip(bounds, outs):
        total = keep_ref[0, first:last, :].astype(F32) + got_ref[0, first:last, :].astype(F32)
        out_ref[...] = (total + last_ref[first:last, :].astype(F32)).astype(BF16)


def run_returns(bounds, keep, got, last):
    vmem = pl.BlockSpec(memory_space=pltpu.VMEM)
    width = keep.shape[2]
    return pl.pallas_call(
        functools.partial(returns_kernel, bounds),
        out_shape=[jax.ShapeDtypeStruct((b - a, width), BF16) for a, b in bounds],
        in_specs=[vmem] * 3,
        out_specs=[vmem] * len(bounds),
        compiler_params=pltpu.CompilerParams(vmem_limit_bytes=SMALL),
        cost_estimate=BRIEF,
        name="returned_terms",
    )(keep, got, last)


def my_bits():
    dom = lax.axis_index("dom")
    return lax.axis_index("dp"), dom & 1, dom >> 1


def halve_kernel(bits, *refs):
    count = len(bits)
    ins, outs = refs[: 2 * count], refs[2 * count :]
    mine = my_bits()
    size = outs[0].shape[0]
    for index, bit in enumerate(bits):
        keep_ref, got_ref = ins[2 * index : 2 * index + 2]
        for side, name in enumerate((mine[bit], 1 - mine[bit])):
            at = block_at(name, size)
            total = keep_ref[at, :].astype(F32) + got_ref[at, :].astype(F32)
            outs[2 * index + side][...] = total.astype(BF16)


def run_halve(bits, *arrays):
    vmem = pl.BlockSpec(memory_space=pltpu.VMEM)
    rows, feats = arrays[0].shape
    return pl.pallas_call(
        functools.partial(halve_kernel, bits),
        out_shape=[jax.ShapeDtypeStruct((rows // 2, feats), BF16)] * len(arrays),
        in_specs=[vmem] * len(arrays),
        out_specs=[vmem] * len(arrays),
        compiler_params=pltpu.CompilerParams(vmem_limit_bytes=SMALL),
        cost_estimate=BRIEF,
        name="halve_grads",
    )(*arrays)


def total_kernel(*refs):
    out_ref = refs[-1]
    size = refs[0].shape[0]
    for index in range(len(refs) // 2):
        total = refs[2 * index][...].astype(F32) + refs[2 * index + 1][...].astype(F32)
        out_ref[index * size : (index + 1) * size, :] = total.astype(BF16)


def run_total(*arrays):
    vmem = pl.BlockSpec(memory_space=pltpu.VMEM)
    rows, feats = arrays[0].shape
    return pl.pallas_call(
        total_kernel,
        out_shape=jax.ShapeDtypeStruct((len(arrays) // 2 * rows, feats), BF16),
        in_specs=[vmem] * len(arrays),
        out_specs=vmem,
        compiler_params=pltpu.CompilerParams(vmem_limit_bytes=SMALL),
        cost_estimate=BRIEF,
        name="total_grads",
    )(*arrays)


def settle_kernel(mine_ref, got_ref, *outs):
    size = outs[0].shape[0]
    for index, out_ref in enumerate(outs):
        rows = slice(index * size, (index + 1) * size)
        total = mine_ref[rows, :].astype(F32) + got_ref[rows, :].astype(F32)
        out_ref[...] = total.astype(BF16)


def run_settle(mine, got):
    vmem = pl.BlockSpec(memory_space=pltpu.VMEM)
    rows, feats = mine.shape
    return pl.pallas_call(
        settle_kernel,
        out_shape=[jax.ShapeDtypeStruct((rows // 2, feats), BF16)] * 2,
        in_specs=[vmem] * 2,
        out_specs=[vmem] * 2,
        compiler_params=pltpu.CompilerParams(vmem_limit_bytes=SMALL),
        cost_estimate=BRIEF,
        name="settle_grads",
    )(mine, got)


def join_kernel(bits, *refs):
    count = len(bits)
    outs = refs[-count:]
    mine = my_bits()
    size = refs[0].shape[0]
    for index, bit in enumerate(bits):
        outs[index][block_at(mine[bit], size), :] = refs[2 * index][...]
        outs[index][block_at(1 - mine[bit], size), :] = refs[2 * index + 1][...]


def run_join(bits, *arrays):
    vmem = pl.BlockSpec(memory_space=pltpu.VMEM)
    rows, feats = arrays[0].shape
    return pl.pallas_call(
        functools.partial(join_kernel, bits),
        out_shape=[jax.ShapeDtypeStruct((2 * rows, feats), BF16)] * len(bits),
        in_specs=[vmem] * len(arrays),
        out_specs=[vmem] * len(bits),
        compiler_params=pltpu.CompilerParams(vmem_limit_bytes=SMALL),
        cost_estimate=BRIEF,
        name="join_grads",
    )(*arrays)


def own_sum_kernel(keep_ref, got_ref, last_ref, update_ref, unit_ref):
    rows = update_ref.shape[0]

    def total(first, last):
        both = keep_ref[0, first:last, :].astype(F32) + got_ref[0, first:last, :].astype(F32)
        return both + last_ref[first:last, :].astype(F32)

    unit_ref[...] = total(0, rows + PAD)
    update_ref[...] = total(rows + PAD, 2 * rows + PAD).astype(BF16)


def run_own_sum(rows, keep, got, last):
    width = last.shape[1]
    vmem = pl.BlockSpec(memory_space=pltpu.VMEM)
    shape = jax.ShapeDtypeStruct
    return pl.pallas_call(
        own_sum_kernel,
        out_shape=(shape((rows, width), BF16), shape((rows + PAD, width), F32)),
        in_specs=[vmem] * 3,
        out_specs=[vmem] * 2,
        compiler_params=pltpu.CompilerParams(vmem_limit_bytes=SMALL),
        cost_estimate=BRIEF,
        name="own_sum",
    )(keep, got, last)


def finish_kernel(cfg, *refs):
    blocks, offsets, width, feats, spread = cfg
    send_ref, sum_ref, slab_ref, inverse_ref = refs[:4]
    far_refs = refs[4 : 4 + len(spread)]
    branch_ref, unit_ref, table, sem = refs[4 + len(spread) :]
    fetch = pltpu.make_async_copy(send_ref, table, sem)
    fetch.start()
    own_rows = blocks * BLK
    sub = BLK // width
    group = SEND * BLK + PAD

    unit_ref[...] = sum_ref[:own_rows, :]
    dots = sum_ref[own_rows:, :]
    at_row = lax.broadcasted_iota(jnp.int32, (PAD, width), 0)
    fetch.wait()
    for ref, members in zip(far_refs, spread):
        for position, offset in enumerate(members):
            first = position * group
            extra = ref[first + SEND * BLK : first + group, :].astype(F32)
            for c in range(SEND):
                block = table[c, offset]
                rows = ref[first + c * BLK : first + (c + 1) * BLK, :].astype(F32)
                unit_ref[block_at(block), :] += rows
                for piece in range(sub):
                    line = extra[c * sub + piece : c * sub + piece + 1, :]
                    dots = dots + jnp.where(at_row == block * sub + piece, line, 0.0)
    for block in range(blocks):
        rows = slice(block * BLK, (block + 1) * BLK)
        line = jnp.concatenate(
            [dots[block * sub + piece : block * sub + piece + 1, :] for piece in range(sub)], axis=1
        )
        mean = jnp.broadcast_to(line * (1.0 / feats), (BLK, BLK)).T[:, :width]
        branch = inverse_ref[rows, :] * (unit_ref[rows, :] - slab_ref[rows, :] * mean)
        branch_ref[rows, :] = branch.astype(BF16)


def run_finish(feats, send, own_sum, slab, inverse, far, spread):
    rows, width = slab.shape
    vmem = pl.BlockSpec(memory_space=pltpu.VMEM)
    hbm = pl.BlockSpec(memory_space=pltpu.HBM)
    cfg = (rows // BLK, send.shape[1], width, feats, spread)
    return pl.pallas_call(
        functools.partial(finish_kernel, cfg),
        out_shape=jax.ShapeDtypeStruct((rows, width), BF16),
        in_specs=[hbm] + [vmem] * (3 + len(far)),
        out_specs=vmem,
        scratch_shapes=[
            pltpu.VMEM((rows, width), F32),
            pltpu.SMEM(send.shape, jnp.int32),
            pltpu.SemaphoreType.DMA(()),
        ],
        compiler_params=pltpu.CompilerParams(vmem_limit_bytes=SMALL),
        cost_estimate=BRIEF,
        name="finish",
    )(*in_hbm(send), own_sum, slab, inverse, *far)


def grads_kernel(factor, *refs):
    first_held, first_got, second_held, second_got = refs[:4]
    results, made, sems = refs[4:8], refs[8:12], refs[12]
    dp, low, _ = my_bits()
    first, second = jnp.equal(dp, 1), jnp.equal(low, 1)
    copies = [
        pltpu.make_async_copy(source, target, sems.at[index])
        for index, (source, target) in enumerate(zip(made, results))
    ]

    def picked(flag, left, right, start):
        columns = slice(start, start + BLK)
        return jnp.where(flag, left[:, columns].astype(F32), right[:, columns].astype(F32)) * factor

    picks = (
        (first, first_got, first_held),
        (first, first_held, first_got),
        (second, second_got, second_held),
        (second, second_held, second_got),
    )
    for index in (3, 0, 1, 2):
        for start in range(0, first_held.shape[1], BLK):
            rows = slice(start, start + BLK)
            block = picked(*picks[index], start)
            if index == 3:
                made[index][:, rows] = block
            else:
                made[index][rows, :] = block.T
        copies[index].start()
    for copy in copies:
        copy.wait()


def run_grads(factor, *arrays):
    width, feats = arrays[0].shape
    vmem = pl.BlockSpec(memory_space=pltpu.VMEM)
    hbm = pl.BlockSpec(memory_space=pltpu.HBM)
    shapes = [(feats, width)] * 3 + [(width, feats)]
    return pl.pallas_call(
        functools.partial(grads_kernel, factor),
        out_shape=[jax.ShapeDtypeStruct(shape, F32) for shape in shapes],
        in_specs=[vmem] * 4,
        out_specs=[hbm] * 4,
        scratch_shapes=[
            *[pltpu.VMEM(shape, F32) for shape in shapes],
            pltpu.SemaphoreType.DMA((4,)),
        ],
        compiler_params=pltpu.CompilerParams(vmem_limit_bytes=SMALL),
        cost_estimate=BRIEF,
        name="weight_grads",
    )(*arrays)


def swap(array, axis, bit):
    return lax.ppermute(array, axis, [(i, i ^ bit) for i in range(lax.axis_size(axis))])


def shifted(array, axis, distance):
    size = lax.axis_size(axis)
    return lax.ppermute(array, axis, [(i, (i + distance) % size) for i in range(size)])


def added(left, right):
    return (left.astype(F32) + right.astype(F32)).astype(BF16)


def after(values, *earlier):
    held = lax.optimization_barrier((values, earlier))
    return held[0]


def narrow(keep, got, bit):
    while keep.shape[0] > 2:
        summed = added(keep, got)
        keep, send = summed[0::2], summed[1::2]
        got = swap(send, "tensor", bit)
        bit *= 2
    return keep, got, bit


def body(states, w_query, w_key, w_value, w_out, send_blocks, neighbor_blocks, cotangent):
    replicas, node_count, feats = states.shape
    width = w_query.shape[1]
    ranks = lax.axis_size("tensor")
    parts = lax.axis_size("dom")
    explicit = parts == 4 and lax.axis_size("dp") == 2
    offsets = offset_list(HOPS)
    order, share = piece_order(ranks, len(offsets))
    send = send_blocks[0].T
    weights = (w_query, w_key, w_value, w_out)
    flat_states = states.reshape(-1, feats)
    flat_cot = cotangent.reshape(-1, feats)

    leaving = pick_blocks(flat_states, send, ranks, share)
    route = []
    for p in range(parts):
        for r in range(ranks):
            distance = offsets[order[r * share] // SEND]
            route.append((p * ranks + r, ((p + distance) % parts) * ranks + r))
    levels = []
    bit = 1
    while bit < ranks:
        levels.append(bit)
        bit *= 2
    arrived = [lax.ppermute(block, ("dom", "tensor"), route) for block in leaving]
    own = run_own(flat_states, flat_cot, weights)
    arrived[0] = after(arrived[0], own[0])
    unit, slab, inverse, cot = own[0], own[7], own[8], own[9]
    weights = own[10:]
    first_pieces = list(arrived)
    wide = [swap(block, "tensor", levels[-1]) for block in arrived]
    close = after(first_pieces, *arrived)
    close = [swap(half, "tensor", 1) for block in close for half in jnp.split(block, 2)]
    early = run_early(first_pieces + close, weights[1], weights[2])
    held = {levels[-1]: after(wide, early[0])}
    for bit in reversed(levels[:-1]):
        for slot in list(held):
            held[slot ^ bit] = [swap(block, "tensor", bit) for block in held[slot]]
    for bit in levels[1:-1]:
        held[bit] = [swap(block, "tensor", bit) for block in first_pieces]
        held[bit ^ 1] = [swap(block, "tensor", 1) for block in held[bit]]
    pieces = [block for slot in range(EARLY, ranks) for block in held[slot]]
    count = len(offsets)
    both, dq, mixed, far_keep, far_send, *halves = run_attend(
        explicit,
        early,
        ranks,
        share,
        count,
        neighbor_blocks,
        pieces,
        own[:7],
        cot,
        weights[1],
        weights[2],
    )
    total_rows = replicas * node_count * lax.axis_size("dp") * parts
    factor = 1.0 / math.sqrt(total_rows)

    if explicit:
        first, second = swap(halves[1], "dp", 1), swap(halves[3], "dom", 1)
    far_keep, far_got, bit = narrow(far_keep, swap(far_send, "tensor", 1), 2)
    own_keep, own_send = run_own_terms(both, unit, dq, mixed, weights)
    own_keep, own_got, bit = narrow(own_keep, swap(own_send, "tensor", 1), 2)
    far_out = added(far_keep[1], far_got[1])
    far_last = swap(far_out, "tensor", bit)
    if explicit:
        first, second = after(first, far_out, own_send), after(second, far_out, own_send)
        halves = run_halve((1, 0), halves[0], first, halves[2], second)
        first, second = swap(halves[1], "dom", 1), swap(halves[3], "dp", 1)
        total = run_total(halves[0], first, halves[2], second)
        got = swap(total, "dom", 2)
        own_got = after(own_got, total)
    own_out = added(own_keep[1], own_got[1])
    own_last = swap(own_out, "tensor", bit)
    far_last = after(far_last, own_out)

    group = SEND * BLK + PAD
    spread = []
    for index, distance in enumerate(offsets):
        for members in spread:
            if (offsets[members[0]] - distance) % parts == 0 and members[-1] == index - 1:
                members.append(index)
                break
        else:
            spread.append([index])
    spread = tuple(tuple(members) for members in spread)
    bounds = tuple((members[0] * group, (members[-1] + 1) * group) for members in spread)
    far_sums = run_returns(bounds, far_keep, far_got, far_last)
    returned = [
        shifted(part, "dom", -offsets[members[0]]) for part, members in zip(far_sums, spread)
    ]
    own_last = after(own_last, far_sums)
    update, own_sum = run_own_sum(replicas * node_count, own_keep, own_got, own_last)
    if explicit:
        held = run_settle(total, after(got, own_sum))
        first, second = swap(held[0], "dom", 1), swap(held[1], "dp", 1)
        first = after(first, returned)
        held = run_join((1, 0), held[0], first, held[1], second)
        first, second = swap(held[0], "dp", 1), swap(held[1], "dom", 1)
    branch = run_finish(feats, send, own_sum, slab, inverse, returned, spread)
    if explicit:
        first = after(first, branch)
        grads = run_grads(factor, held[0], first, held[1], second)
    else:
        summed = [lax.psum(half.astype(F32), ("dp", "dom")) * factor for half in halves]
        grads = (summed[0].T, summed[1].T, summed[2].T, summed[3])
    shape = (replicas, node_count, width)
    return (update.reshape(shape), branch.reshape(shape), *grads)


def solution(mesh):
    placed = (
        P("dp", "dom", None),
        P(None, "tensor"),
        P(None, "tensor"),
        P(None, "tensor"),
        P("tensor", None),
        P("dom", None, None),
        P("dom", None),
        P("dp", "dom", None),
    )
    return jax.shard_map(
        body,
        mesh=mesh,
        in_specs=placed,
        out_specs=(
            P("dp", "dom", "tensor"),
            P("dp", "dom", "tensor"),
            P(None, "tensor"),
            P(None, "tensor"),
            P(None, "tensor"),
            P("tensor", None),
        ),
        check_vma=False,
    )
```
